32 devices in a mesh: grp: 4 (over y, core), row: 8 (over z, x).
Axes of the slice: x: 2, y: 2, z: 4, core: 2. Of those that a mesh axis runs over, the one named last changes fastest.
Arguments:
- features: bfloat16 [12288, 2048], P(('grp', 'row'))
- clip_starts: int32 [64], replicated, may hold values from 0 to 12286, as said below
- kernel_one: bfloat16 [576, 128], P('row', 'grp'), may hold values from -0.25 to 0.25
- kernel_two: bfloat16 [1152, 128], P('row', 'grp'), may hold values from -0.1875 to 0.1875
- gain_one: bfloat16 [128], P('grp'), may hold values from 0.099609375 to 1.8984375
- shift_one: bfloat16 [128], P('grp'), may hold values from -3 to 3
- gain_two: bfloat16 [128], P('grp'), may hold values from 0.099609375 to 1.8984375
- shift_two: bfloat16 [128], P('grp'), may hold values from -3 to 3
- cotangent: bfloat16 [6144, 2048], P(('grp', 'row'))
Outputs:
- block_out: bfloat16 [6144, 2048], P(('grp', 'row'))
- grad_features: float32 [12288, 2048], P(('grp', 'row'))
- grad_kernel_one: float32 [576, 128], P('row', 'grp')
- grad_kernel_two: float32 [1152, 128], P('row', 'grp')
- grad_gain_one: float32 [128], P('grp')
- grad_shift_one: float32 [128], P('grp')
- grad_gain_two: float32 [128], P('grp')
- grad_shift_two: float32 [128], P('grp')
The draws below stay inside these ranges and needn't reach their ends.
Inputs may be any that keep to these rules, and one draw needn't show every extreme that they name: `clip_starts`: clip starts increase and are even; the first is 0 and the last is 12286; exactly two fall in each block of 384 frames, and no other lies on a block's first frame.
All inputs are finite; a program needn't handle non-finite values.
Results may differ from the reference program's by a relative error of at most 0.015.
Values may be sent and summed in bfloat16 or wider, within the bound.
No kernel may reach another device: no remote copies, remote signals or barrier semaphores. Data moves between devices by JAX's collectives and lax.ppermute only.
A program may use at most 192 MiB of HBM per device.

```python
import math
from functools import partial
import jax
import jax.numpy as jnp
from jax import lax

MEL = 32
C_IN = 64
C_MID = 128
FR_DEV = 384
FRAMES = 12288
NSEG = 64


def spread_rows(key, row_total, col_total, rise):
    normal_key = jax.random.fold_in(key, 0)
    row_key = jax.random.fold_in(key, 2)
    col_key = jax.random.fold_in(key, 3)
    normal_part = jax.random.normal(normal_key, (row_total, col_total), jnp.float32)
    base = normal_part
    place = jnp.arange(row_total, dtype=jnp.float32) / row_total
    row_scale = jnp.exp(place * math.log(rise) + jax.random.uniform(row_key, (row_total,), jnp.float32, 0.0, math.log(10.0))) / 5.0
    col_scale = jnp.exp(jax.random.uniform(col_key, (col_total,), jnp.float32, 0.0, math.log(10.0))) / 3.0
    return base * row_scale[:, None] * col_scale[None, :]


def draw_features(key, part):
    key = jax.random.fold_in(key, 11)
    return spread_rows(key, FRAMES, MEL * C_IN, 3.0).astype(jnp.bfloat16)


def draw_cotangent(key, part):
    key = jax.random.fold_in(key, 23)
    return spread_rows(key, FRAMES // 2, MEL // 2 * C_MID, 3.0).astype(jnp.bfloat16)


def draw_clip_starts(key, part):
    key = jax.random.fold_in(key, 5)
    halves = NSEG // 2
    first_key, second_key = jax.random.split(key)
    quarter = FR_DEV // 4
    early = jax.random.randint(first_key, (halves,), 1, quarter)
    late = jax.random.randint(second_key, (halves,), quarter + 1, FR_DEV // 2)
    early = jnp.where(jnp.arange(halves) == 0, 0, early)
    late = jnp.where(jnp.arange(halves) == halves - 1, FR_DEV // 2 - 1, late)
    base = jnp.arange(halves, dtype=jnp.int32) * FR_DEV
    starts = jnp.stack([base + 2 * early, base + 2 * late], axis=1).reshape(NSEG)
    return starts.astype(jnp.int32)


def block_scale(stream_key, shape, cuts, least, high):
    def one(position, parts):
        draws = jax.random.uniform(jax.random.fold_in(jax.random.fold_in(stream_key, 6), position), (parts,), jnp.float32, least / len(cuts), high / len(cuts))
        return jnp.repeat(jnp.exp(draws), shape[position] // parts).reshape((-1,) + (1,) * (len(shape) - position - 1))

    factor_of = one(*cuts[0])
    for cut in cuts[1:]:
        factor_of = factor_of * one(*cut)
    return factor_of


def normal_values(rng, dims, scale, limit, cuts=(), kind=jnp.bfloat16):
    entries = jax.random.normal(rng, dims, jnp.float32) * scale
    if len(cuts) > 0:
        entries = block_scale(rng, dims, cuts, -0.22, 0.18) * entries
    return jnp.clip(entries, min=-limit, max=limit).astype(kind)


def setup_inputs(seed: int = 0) -> dict:
    streams_of = jax.random.split(jax.random.key(seed), 10)
    return {
        "features": draw_features(jax.random.fold_in(streams_of[9], 71), 0),
        "clip_starts": draw_clip_starts(jax.random.fold_in(streams_of[9], 71), 0),
        "kernel_one": normal_values(streams_of[2], (9 * C_IN, C_MID), (9 * C_IN) ** -0.5, 0.25, ((0, 8), (1, 4))),
        "kernel_two": normal_values(streams_of[3], (9 * C_MID, C_MID), (9 * C_MID) ** -0.5, 0.1875, ((0, 8), (1, 4))),
        "gain_one": jnp.clip(1.0 + 0.18 * jax.random.normal(streams_of[4], (C_MID,), jnp.float32), 0.099609375, 1.8984375).astype(jnp.bfloat16),
        "shift_one": normal_values(streams_of[5], (C_MID,), 0.5, 3.0, ((0, 4),)),
        "gain_two": jnp.clip(1.0 + 0.18 * jax.random.normal(streams_of[6], (C_MID,), jnp.float32), 0.099609375, 1.8984375).astype(jnp.bfloat16),
        "shift_two": normal_values(streams_of[7], (C_MID,), 0.5, 3.0, ((0, 4),)),
        "cotangent": draw_cotangent(jax.random.fold_in(streams_of[9], 71), 0),
    }


EPS = 1e-05

@jax.custom_vjp
def low(v):
    return lax.optimization_barrier(v.astype(jnp.bfloat16)).astype(jnp.float32)

@jax.custom_vjp
def low_back(v):
    return v

def low_keep(v):
    return (low(v), None)

def low_pass(kept, grad):
    return (grad,)

def back_keep(v):
    return (v, None)

def back_low(kept, grad):
    return (low(grad),)
low.defvjp(low_keep, low_pass)
low_back.defvjp(back_keep, back_low)

def mel_columns(values):
    padded = jnp.pad(values, ((0, 0), (1, 1), (0, 0)))
    mel_count = values.shape[1]
    return jnp.concatenate([padded[:, 0:mel_count], padded[:, 1:mel_count + 1], padded[:, 2:mel_count + 2]], axis=-1)

def conv_block(weight, pieces):
    block, before, after, keep_before, keep_after = pieces
    extended = jnp.concatenate([before[None], block, after[None]], axis=0)
    columns = mel_columns(extended)
    frames = block.shape[0]
    inner_size = columns.shape[2]
    taps = weight.reshape(3, inner_size, weight.shape[1])
    results = [jnp.einsum('fmk,kc->fmc', columns[offset:offset + frames], taps[offset], precision=lax.Precision.HIGHEST) for offset in range(3)]
    return keep_before[:, None, None] * results[0] + results[1] + keep_after[:, None, None] * results[2]

def conv(values, weight, keep_before, keep_after):
    frame_total, mel_count, channels = values.shape
    block_size = math.gcd(frame_total, 4096)
    number = frame_total // block_size
    blocked = values.reshape(number, block_size, mel_count, channels)
    zero_row = jnp.zeros((1, mel_count, channels), jnp.float32)
    before = jnp.concatenate([zero_row, blocked[:-1, -1]], axis=0)
    after = jnp.concatenate([blocked[1:, 0], zero_row], axis=0)
    block_step = jax.checkpoint(partial(conv_block, weight))
    outputs = lax.map(block_step, (blocked, before, after, keep_before.reshape(number, block_size), keep_after.reshape(number, block_size)))
    return outputs.reshape(frame_total, mel_count, weight.shape[1])

def batch_norm(pre, gain, shift):
    mean = lax.optimization_barrier(jnp.mean(pre, axis=(0, 1)))
    square = lax.optimization_barrier(jnp.mean(pre * pre, axis=(0, 1)))
    rstd = lax.rsqrt(square - mean * mean + EPS)
    return gain * ((pre - mean) * rstd) + shift

def forward(features, kernel_one, kernel_two, gain_one, shift_one, gain_two, shift_two, keep_before, keep_after):
    source = low(features).reshape(FRAMES, MEL, C_IN)
    pre_one = low_back(conv(source, low(kernel_one), keep_before, keep_after))
    active_one = jax.nn.silu(batch_norm(pre_one, gain_one, shift_one))
    pre_two = low_back(conv(low(active_one), low(kernel_two), keep_before, keep_after))
    result = jax.nn.silu(batch_norm(pre_two, gain_two, shift_two))
    pooled = lax.optimization_barrier(jnp.mean(result.reshape(FRAMES // 2, 2, MEL // 2, 2, C_MID), axis=(1, 3)))
    return pooled.reshape(FRAMES // 2, MEL // 2 * C_MID)

def reference(features, clip_starts, kernel_one, kernel_two, gain_one, shift_one, gain_two, shift_two, cotangent):
    begins = jnp.zeros((FRAMES,), jnp.float32).at[clip_starts.astype(jnp.int32)].set(1.0)
    keep_before = 1.0 - begins
    keep_after = 1.0 - jnp.concatenate([begins[1:], jnp.ones((1,), jnp.float32)])
    params = (features.astype(jnp.float32), kernel_one.astype(jnp.float32), kernel_two.astype(jnp.float32), gain_one.astype(jnp.float32), shift_one.astype(jnp.float32), gain_two.astype(jnp.float32), shift_two.astype(jnp.float32))

    def wrapped(*values):
        return forward(*values, keep_before, keep_after)
    block_out, pullback = jax.vjp(wrapped, *params)
    grads = pullback(cotangent.astype(jnp.float32))
    return (block_out.astype(jnp.bfloat16), grads[0], grads[1], grads[2], grads[3], grads[4], grads[5], grads[6])
```

```python
import jax
import jax.numpy as jnp
from jax import lax
from jax.experimental import pallas as pl
from jax.experimental.pallas import tpu as pltpu
from jax.sharding import PartitionSpec as P

MEL = 32
C_IN = 64
C_MID = 128
EPS = 1e-05
AXES = ("grp", "row")
LANES = 128
TAIL = 16
F32 = jnp.float32
BF16 = jnp.bfloat16


def call(body, grid, in_specs, out_specs, out_shape, scratch, flops=0, moved=0):
    return pl.pallas_call(
        body,
        grid=grid,
        in_specs=in_specs,
        out_specs=out_specs,
        out_shape=out_shape,
        scratch_shapes=scratch,
        compiler_params=pltpu.CompilerParams(
            dimension_semantics=("arbitrary",) * len(grid), vmem_limit_bytes=56 * 2**20
        ),
        cost_estimate=pl.CostEstimate(flops=flops, bytes_accessed=moved, transcendentals=0),
    )


def whole(shape):
    return pl.BlockSpec(shape, lambda *_: (0,) * len(shape))


SMEM = pl.BlockSpec(memory_space=pltpu.SMEM)


def padded(size):
    return -(-size // LANES) * LANES


def fold(values):
    total = jnp.sum(values.reshape(-1, 8, 2 * C_MID), axis=0)
    total = jnp.sum(total, axis=0, keepdims=True)
    return total[:, :C_MID] + total[:, C_MID:]


def partial_sum(values):
    return jnp.sum(values.reshape(-1, 8, values.shape[-1]), axis=0)


def twice(row):
    return jnp.concatenate([row, row], axis=1)


def rolled(values, step):
    rows = values.shape[0]
    return pltpu.roll(values, step % rows, 0)


def outer_taps(even, odd, before, after):
    return jnp.concatenate(
        [rolled(odd, 1) * before, even, odd, rolled(even, -1) * after], axis=1
    ).astype(BF16)


def stat_sums(stats_ref):
    return jnp.sum(stats_ref[...], axis=0)


def norm_terms(sums, count):
    mean = sums[0:1] / count
    rstd = lax.rsqrt(sums[1:2] / count - mean * mean + EPS)
    return mean, rstd


def setup_body(meta, k1, k2, ga, sa, gb, sb, clips, x_head, x_tail, c_head, c_tail,
               w1_out, w2_out, masks, up, down):
    share = k1.shape[0]
    copies = w1_out.shape[0]
    rows_one = k1.shape[1]
    w1_out[...] = jnp.zeros(w1_out.shape, BF16)
    w2_out[...] = jnp.zeros(w2_out.shape, BF16)
    first = lax.broadcasted_iota(jnp.int32, (share, share), 0)
    second = lax.broadcasted_iota(jnp.int32, (share, share), 1)
    columns = [k1[...].astype(F32)]
    for vector in (ga, sa, gb, sb):
        spread = jnp.broadcast_to(vector[...].astype(F32), (share, share))
        columns.append(
            jnp.sum(jnp.where(first == second, spread, 0.0), axis=1, keepdims=True)
        )
    chunk_one = jnp.concatenate(columns, axis=1).astype(BF16)
    chunk_two = k2[...]
    for i in range(copies):
        w1_out[i, :, 0 : rows_one + 4] = chunk_one
        w2_out[i, :, 0 : k2.shape[1]] = chunk_two
    rows = masks.shape[1]
    half = rows - TAIL
    place = lax.broadcasted_iota(jnp.int32, (rows, clips.shape[1]), 0)
    pair = jnp.where(place >= half + TAIL // 2, place - rows, place)
    frame = meta[0] + 2 * pair
    starts = jnp.broadcast_to(clips[...], (rows, clips.shape[1]))
    for slot, shift in ((0, 0), (1, 2)):
        hit = jnp.where((frame + shift == starts) | (frame + shift >= meta[1]), 1.0, 0.0)
        begins = jnp.max(hit, axis=1, keepdims=True)
        masks[slot] = jnp.broadcast_to(1.0 - begins, (rows, LANES))
    row = lax.broadcasted_iota(jnp.int32, (8, x_head.shape[1]), 0)
    xt = x_tail[...].astype(F32)
    ct = c_tail[...].astype(F32)
    up[...] = jnp.where(
        row < 4, pltpu.roll(xt[8:16], 4, 0), jnp.where(row == 4, ct[15:16], 0.0)
    ).astype(BF16)
    xh = x_head[...].astype(F32)
    ch = c_head[...].astype(F32)
    down[...] = jnp.where(row < 4, xh[0:8], jnp.where(row == 4, ch[0:1], 0.0)).astype(BF16)


def setup(meta, k1t, k2t, vectors, clips, features, cotangent, copies):
    frames, wide = features.shape
    halves = cotangent.shape[0]
    rows = frames // 2 + TAIL
    share = k1t.shape[0]
    w1 = (copies, share, padded(k1t.shape[1] + 4))
    w2 = (copies, share, padded(k2t.shape[1]))
    return call(
        setup_body,
        (1,),
        [
            SMEM,
            whole(k1t.shape),
            whole(k2t.shape),
            *[whole((1, share))] * 4,
            whole(clips.shape),
            pl.BlockSpec((16, wide), lambda i: (0, 0)),
            pl.BlockSpec((16, wide), lambda i: (frames // 16 - 1, 0)),
            pl.BlockSpec((16, wide), lambda i: (0, 0)),
            pl.BlockSpec((16, wide), lambda i: (halves // 16 - 1, 0)),
        ],
        [whole(w1), whole(w2), whole((2, rows, LANES)), whole((8, wide)), whole((8, wide))],
        [
            jax.ShapeDtypeStruct(w1, BF16),
            jax.ShapeDtypeStruct(w2, BF16),
            jax.ShapeDtypeStruct((2, rows, LANES), F32),
            jax.ShapeDtypeStruct((8, wide), BF16),
            jax.ShapeDtypeStruct((8, wide), BF16),
        ],
        [],
    )(meta, k1t, k2t, *vectors, clips, features, features, cotangent, cotangent)


def rows_of(gathered, index, row_count):
    grps = gathered.shape[0] // row_count
    pieces = [gathered[g * row_count + index] for g in range(grps)]
    return jnp.concatenate(pieces, axis=0).astype(F32).T


def conv_one_body(row_count, x, up, down, masks, wg, pre, stats, taps_out, k1_out, vec_out,
                  xs, kf, w_even, w_odd, taps, acc):
    step = pl.program_id(0)
    last = pl.num_programs(0) - 1
    pairs = x.shape[1] // LANES
    rows = masks.shape[1]
    half = rows - TAIL

    @pl.when(step == 0)
    def _():
        rows_one = kf.shape[0] // row_count
        for r in range(row_count):
            shard = rows_of(wg, r, row_count)
            kf[rows_one * r : rows_one * (r + 1)] = shard[0:rows_one]
            if r == 0:
                vec_out[...] = shard[rows_one : rows_one + 4]
        k1_out[...] = kf[...].astype(BF16)
        w_even[...] = jnp.zeros(w_even.shape, BF16)
        w_odd[...] = jnp.zeros(w_odd.shape, BF16)
        placed = (
            (w_even, 0, 1, 0), (w_even, 1, 0, 1), (w_even, 1, 1, 2),
            (w_odd, 0, 0, 0), (w_odd, 0, 1, 1), (w_odd, 1, 0, 2),
        )
        for matrix, piece, side, d in placed:
            for q in range(4):
                for p in range(2):
                    t = q - p
                    if 0 <= t < 3:
                        at = piece * 512 + q * 128 + side * 64
                        matrix[at : at + 64, p * 128 : p * 128 + 128] = kf[
                            (3 * t + d) * C_IN : (3 * t + d + 1) * C_IN
                        ].astype(BF16)
        taps[0] = jnp.zeros(taps.shape[1:], BF16)
        taps[taps.shape[0] - 1] = jnp.zeros(taps.shape[1:], BF16)
        acc[...] = jnp.zeros(acc.shape, F32)

    @pl.when(step < last)
    def _():
        before = masks[0]
        after = masks[1]
        row = lax.broadcasted_iota(jnp.int32, (TAIL, LANES), 0)
        for q in range(pairs):
            lanes = slice(q * LANES, (q + 1) * LANES)
            xs[...] = x[:, lanes].astype(F32)
            u = up[:, lanes].astype(F32)
            d = down[:, lanes].astype(F32)

            def side(k):
                tail = jnp.where(row == 0, d[k : k + 1], 0.0)
                tail = jnp.where(row == 1, d[k + 2 : k + 3], tail)
                tail = jnp.where(row == TAIL - 2, u[k : k + 1], tail)
                tail = jnp.where(row == TAIL - 1, u[k + 2 : k + 3], tail)
                return jnp.concatenate([xs[pl.ds(k, half, stride=2), :], tail], axis=0)

            block = outer_taps(side(0), side(1), before, after)
            taps[1 + step * pairs + q] = block
            taps_out[q] = block[0:half]

    @pl.when(step > 0)
    def _():
        base = (step - 1) * pairs
        left = taps[pl.ds(base, pairs)].reshape(pairs * rows, 512)
        mid = taps[pl.ds(base + 1, pairs)].reshape(pairs * rows, 512)
        right = taps[pl.ds(base + 2, pairs)].reshape(pairs * rows, 512)
        for parity, lhs, matrix in (
            (0, jnp.concatenate([left, mid], axis=1), w_even),
            (1, jnp.concatenate([mid, right], axis=1), w_odd),
        ):
            out = jnp.dot(lhs, matrix[...], preferred_element_type=F32)
            out = out.reshape(pairs, rows, 2 * C_MID)
            for q in range(pairs):
                pre[2 * q + parity] = out[q]
            own = out[:, 0:half]
            acc[0] += partial_sum(own)
            acc[1] += partial_sum(own * own)

    @pl.when(step == last)
    def _():
        sums = jnp.concatenate([fold(acc[0]), fold(acc[1])], axis=0)
        stats[...] = jnp.broadcast_to(sums[None], stats.shape)


def conv_one(features, up, down, masks, wg, row_count, copies):
    frames, wide = features.shape
    rows = masks.shape[1]
    half = rows - TAIL
    pairs = 4
    steps = wide // LANES // pairs
    lead = lambda i: jnp.minimum(i, steps - 1)
    lag = lambda i: jnp.maximum(i - 1, 0)
    return call(
        lambda *refs: conv_one_body(row_count, *refs),
        (steps + 1,),
        [
            pl.BlockSpec((frames, pairs * LANES), lambda i: (0, lead(i))),
            pl.BlockSpec((8, pairs * LANES), lambda i: (0, lead(i))),
            pl.BlockSpec((8, pairs * LANES), lambda i: (0, lead(i))),
            whole(masks.shape),
            whole(wg.shape),
        ],
        [
            pl.BlockSpec((2 * pairs, rows, 2 * C_MID), lambda i: (lag(i), 0, 0)),
            whole((copies, 2, C_MID)),
            pl.BlockSpec((pairs, half, 512), lambda i: (lead(i), 0, 0)),
            whole((9 * C_IN, C_MID)),
            whole((4, C_MID)),
        ],
        [
            jax.ShapeDtypeStruct((MEL, rows, 2 * C_MID), F32),
            jax.ShapeDtypeStruct((copies, 2, C_MID), F32),
            jax.ShapeDtypeStruct((MEL // 2, half, 512), BF16),
            jax.ShapeDtypeStruct((9 * C_IN, C_MID), BF16),
            jax.ShapeDtypeStruct((4, C_MID), F32),
        ],
        [
            pltpu.VMEM((frames, LANES), F32),
            pltpu.VMEM((9 * C_IN, C_MID), F32),
            pltpu.VMEM((1024, 2 * C_MID), BF16),
            pltpu.VMEM((1024, 2 * C_MID), BF16),
            pltpu.VMEM((MEL // 2 + 2, rows, 512), BF16),
            pltpu.VMEM((2, 8, 2 * C_MID), F32),
        ],
        flops=2 * 2 * MEL * rows * 512 * 256,
        moved=16 * 2**20,
    )(features, up, down, masks, wg)


def conv_two_body(row_count, count, pre_one, stats_one, vec, masks, wg,
                  pre, stats, taps_out, k2_out, sums_out, kf, weight, taps, acc):
    step = pl.program_id(0)
    last = pl.num_programs(0) - 1
    mels = pre_one.shape[0]
    rows = masks.shape[1]
    half = rows - TAIL

    @pl.when(step == 0)
    def _():
        rows_two = kf.shape[0] // row_count
        for r in range(row_count):
            kf[rows_two * r : rows_two * (r + 1)] = rows_of(wg, r, row_count)[0:rows_two]
        k2_out[...] = kf[...].astype(BF16)
        weight[...] = jnp.zeros(weight.shape, BF16)
        for d in range(3):
            for q in range(4):
                for p in range(2):
                    t = q - p
                    if 0 <= t < 3:
                        at = d * 512 + q * 128
                        weight[at : at + 128, p * 128 : p * 128 + 128] = kf[
                            (3 * t + d) * C_MID : (3 * t + d + 1) * C_MID
                        ].astype(BF16)
        taps[0] = jnp.zeros(taps.shape[1:], BF16)
        taps[taps.shape[0] - 1] = jnp.zeros(taps.shape[1:], BF16)
        acc[...] = jnp.zeros(acc.shape, F32)
        sums_out[...] = stat_sums(stats_one)

    @pl.when(step < last)
    def _():
        mean, rstd = norm_terms(sums_out[...], count)
        scale = 0.5 * vec[0:1] * rstd
        shift = 0.5 * vec[1:2] - mean * scale
        scale = twice(scale)
        shift = twice(shift)
        before = masks[0]
        after = masks[1]
        for k in range(mels):
            h = pre_one[k] * scale + shift
            active = h + h * jnp.tanh(h)
            block = outer_taps(active[:, :C_MID], active[:, C_MID:], before, after)
            taps[1 + step * mels + k] = block
            taps_out[k] = block[0:half]

    @pl.when(step > 0)
    def _():
        base = (step - 1) * mels
        lhs = jnp.concatenate(
            [taps[pl.ds(base + d, mels)].reshape(mels * rows, 512) for d in range(3)], axis=1
        )
        out = jnp.dot(lhs, weight[...], preferred_element_type=F32)
        out = out.reshape(mels, rows, 2 * C_MID)
        pre[...] = out
        own = out[:, 0:half]
        acc[0] += partial_sum(own)
        acc[1] += partial_sum(own * own)

    @pl.when(step == last)
    def _():
        sums = jnp.concatenate([fold(acc[0]), fold(acc[1])], axis=0)
        stats[...] = jnp.broadcast_to(sums[None], stats.shape)


def conv_two(pre_one, stats_one, vec, masks, wg, row_count, count):
    copies = stats_one.shape[0]
    rows = masks.shape[1]
    half = rows - TAIL
    mels = 4
    steps = MEL // mels
    lead = lambda i: jnp.minimum(i, steps - 1)
    lag = lambda i: jnp.maximum(i - 1, 0)
    return call(
        lambda *refs: conv_two_body(row_count, count, *refs),
        (steps + 1,),
        [
            pl.BlockSpec((mels, rows, 2 * C_MID), lambda i: (lead(i), 0, 0)),
            whole(stats_one.shape),
            whole(vec.shape),
            whole(masks.shape),
            whole(wg.shape),
        ],
        [
            pl.BlockSpec((mels, rows, 2 * C_MID), lambda i: (lag(i), 0, 0)),
            whole((copies, 2, C_MID)),
            pl.BlockSpec((mels, half, 512), lambda i: (lead(i), 0, 0)),
            whole((9 * C_MID, C_MID)),
            whole((2, C_MID)),
        ],
        [
            jax.ShapeDtypeStruct((MEL, rows, 2 * C_MID), F32),
            jax.ShapeDtypeStruct((copies, 2, C_MID), F32),
            jax.ShapeDtypeStruct((MEL, half, 512), BF16),
            jax.ShapeDtypeStruct((9 * C_MID, C_MID), BF16),
            jax.ShapeDtypeStruct((2, C_MID), F32),
        ],
        [
            pltpu.VMEM((9 * C_MID, C_MID), F32),
            pltpu.VMEM((1536, 2 * C_MID), BF16),
            pltpu.VMEM((MEL + 2, rows, 512), BF16),
            pltpu.VMEM((2, 8, 2 * C_MID), F32),
        ],
        flops=2 * MEL * rows * 1536 * 256,
        moved=20 * 2**20,
    )(pre_one, stats_one, vec, masks, wg)


def norm_two_body(count, pre, stats_two, vec, cot, up, down, pooled, lift, back_stats, sums_out, acc):
    step = pl.program_id(0)
    last = pl.num_programs(0) - 1
    pairs = cot.shape[1] // LANES
    half = cot.shape[0]

    @pl.when(step == 0)
    def _():
        acc[...] = jnp.zeros(acc.shape, F32)
        sums_out[...] = stat_sums(stats_two)

    mean, rstd = norm_terms(sums_out[...], count)
    scale = 0.5 * vec[2:3] * rstd
    shift = 0.5 * vec[3:4] - mean * scale
    norm_shift = -mean * rstd
    row = lax.broadcasted_iota(jnp.int32, (TAIL, LANES), 0)
    for q in range(pairs):
        lanes = slice(q * LANES, (q + 1) * LANES)
        u = up[:, lanes].astype(F32)
        d = down[:, lanes].astype(F32)
        tail = jnp.where(row == 0, d[4:5], jnp.where(row == TAIL - 1, u[4:5], 0.0))
        grad = jnp.concatenate([cot[:, lanes].astype(F32), tail], axis=0) * 0.125
        total = jnp.zeros((half, LANES), F32)
        for k in (2 * q, 2 * q + 1):
            for p in range(2):
                side = slice(p * C_MID, (p + 1) * C_MID)
                value = pre[k, :, side]
                h = value * scale + shift
                th = jnp.tanh(h)
                one = 1.0 + th
                gl = grad * (one * (1.0 + (h - h * th)))
                lift[k, :, side] = gl
                total += (h * one)[0:half]
                own = gl[0:half]
                normed = value[0:half] * rstd + norm_shift
                acc[0] += partial_sum(own)
                acc[1] += partial_sum(own * normed)
        pooled[:, lanes] = (total * 0.25).astype(BF16)

    @pl.when(step == last)
    def _():
        sums = jnp.concatenate(
            [jnp.sum(acc[k], axis=0, keepdims=True) for k in range(2)], axis=0
        )
        back_stats[...] = jnp.broadcast_to(sums[None], back_stats.shape)


def norm_two(pre, stats_two, vec, cot, up, down, count):
    copies = stats_two.shape[0]
    half, wide = cot.shape
    rows = half + TAIL
    pairs = 2
    steps = wide // LANES // pairs
    block = pl.BlockSpec((2 * pairs, rows, 2 * C_MID), lambda i: (i, 0, 0))
    return call(
        lambda *refs: norm_two_body(count, *refs),
        (steps,),
        [
            block,
            whole(stats_two.shape),
            whole(vec.shape),
            pl.BlockSpec((half, pairs * LANES), lambda i: (0, i)),
            pl.BlockSpec((8, pairs * LANES), lambda i: (0, i)),
            pl.BlockSpec((8, pairs * LANES), lambda i: (0, i)),
        ],
        [
            pl.BlockSpec((half, pairs * LANES), lambda i: (0, i)),
            block,
            whole((copies, 2, C_MID)),
            whole((2, C_MID)),
        ],
        [
            jax.ShapeDtypeStruct((half, wide), BF16),
            jax.ShapeDtypeStruct((MEL, rows, 2 * C_MID), F32),
            jax.ShapeDtypeStruct((copies, 2, C_MID), F32),
            jax.ShapeDtypeStruct((2, C_MID), F32),
        ],
        [pltpu.VMEM((2, 8, LANES), F32)],
        moved=16 * 2**20,
    )(pre, stats_two, vec, cot, up, down)


def grad_terms(sums, back, gain, count):
    mean, rstd = norm_terms(sums, count)
    a = gain * rstd
    b = -a * rstd * (back[1:2] / count)
    c = -a * (back[0:1] / count) - b * mean
    return twice(a), twice(b), twice(c)


def back_two_body(count, lift, pre_two, sums_two, back_stats, vec, masks, k2, pre_one, sums_one,
                  grad_out, lift_one, back_out, sums_out, weight, taps, acc):
    step = pl.program_id(0)
    last = pl.num_programs(0) - 1
    mels = lift.shape[0]
    rows = masks.shape[1]
    half = rows - TAIL

    @pl.when(step == 0)
    def _():
        weight[...] = jnp.zeros(weight.shape, BF16)
        for d in range(3):
            for q in range(4):
                for p in range(2):
                    t = 2 - q + p
                    if 0 <= t < 3:
                        at = (2 - d) * 512 + q * 128
                        block = k2[(3 * t + d) * C_MID : (3 * t + d + 1) * C_MID]
                        weight[at : at + 128, p * 128 : p * 128 + 128] = (
                            block.astype(F32).T.astype(BF16)
                        )
        taps[0] = jnp.zeros(taps.shape[1:], BF16)
        taps[taps.shape[0] - 1] = jnp.zeros(taps.shape[1:], BF16)
        acc[...] = jnp.zeros(acc.shape, F32)
        sums_out[...] = stat_sums(back_stats)

    @pl.when(step < last)
    def _():
        a, b, c = grad_terms(sums_two[...], sums_out[...], vec[2:3], count)
        before = masks[0]
        after = masks[1]
        for k in range(mels):
            grad = lift[k] * a + (pre_two[k] * b + c)
            block = outer_taps(grad[:, :C_MID], grad[:, C_MID:], before, after)
            taps[1 + step * mels + k] = block
            grad_out[k] = block[0:half, 128:384]

    @pl.when(step > 0)
    def _():
        base = (step - 1) * mels
        lhs = jnp.concatenate(
            [taps[pl.ds(base + d, mels)].reshape(mels * rows, 512) for d in range(3)], axis=1
        )
        out = jnp.dot(lhs, weight[...], preferred_element_type=F32)
        out = out.reshape(mels, rows, 2 * C_MID)
        mean, rstd = norm_terms(sums_one[...], count)
        scale = 0.5 * vec[0:1] * rstd
        shift = twice(0.5 * vec[1:2] - mean * scale)
        scale = twice(scale)
        norm_shift = twice(-mean * rstd)
        rstd = twice(rstd)
        for k in range(mels):
            value = pre_one[k]
            h = value * scale + shift
            th = jnp.tanh(h)
            gl = out[k] * (0.5 * (1.0 + th) * (1.0 + (h - h * th)))
            lift_one[k] = gl
            own = gl[0:half]
            acc[0] += partial_sum(own)
            acc[1] += partial_sum(own * (value[0:half] * rstd + norm_shift))

    @pl.when(step == last)
    def _():
        sums = jnp.concatenate([fold(acc[0]), fold(acc[1])], axis=0)
        back_out[...] = jnp.broadcast_to(sums[None], back_out.shape)


def back_two(lift, pre_two, sums_two, back_stats, vec, masks, k2, pre_one, sums_one, count):
    copies = back_stats.shape[0]
    rows = masks.shape[1]
    half = rows - TAIL
    mels = 4
    steps = MEL // mels
    lead = lambda i: jnp.minimum(i, steps - 1)
    lag = lambda i: jnp.maximum(i - 1, 0)
    lead_block = pl.BlockSpec((mels, rows, 2 * C_MID), lambda i: (lead(i), 0, 0))
    lag_block = pl.BlockSpec((mels, rows, 2 * C_MID), lambda i: (lag(i), 0, 0))
    return call(
        lambda *refs: back_two_body(count, *refs),
        (steps + 1,),
        [
            lead_block,
            lead_block,
            whole(sums_two.shape),
            whole(back_stats.shape),
            whole(vec.shape),
            whole(masks.shape),
            whole(k2.shape),
            lag_block,
            whole(sums_one.shape),
        ],
        [
            pl.BlockSpec((mels, half, 2 * C_MID), lambda i: (lead(i), 0, 0)),
            lag_block,
            whole((copies, 2, C_MID)),
            whole((2, C_MID)),
        ],
        [
            jax.ShapeDtypeStruct((MEL, half, 2 * C_MID), BF16),
            jax.ShapeDtypeStruct((MEL, rows, 2 * C_MID), F32),
            jax.ShapeDtypeStruct((copies, 2, C_MID), F32),
            jax.ShapeDtypeStruct((2, C_MID), F32),
        ],
        [
            pltpu.VMEM((1536, 2 * C_MID), BF16),
            pltpu.VMEM((MEL + 2, rows, 512), BF16),
            pltpu.VMEM((2, 8, 2 * C_MID), F32),
        ],
        flops=2 * MEL * rows * 1536 * 256,
        moved=32 * 2**20,
    )(lift, pre_two, sums_two, back_stats, vec, masks, k2, pre_one, sums_one)


def dot_rows(first, second):
    return lax.dot_general(
        first, second, (((0,), (0,)), ((), ())), preferred_element_type=F32
    )


def scatter_blocks(out, by_channel, rows_in):
    copies, share, wide = out.shape
    grps = by_channel.shape[0] // share
    row_count = copies // grps
    size = rows_in // row_count
    turned = by_channel.T
    for r in range(row_count):
        part = turned[size * r : size * (r + 1)]
        part = jnp.concatenate([part, jnp.zeros((wide - size, part.shape[1]), F32)], axis=0)
        back = part.T.astype(BF16)
        for g in range(grps):
            out[g * row_count + r] = back[share * g : share * (g + 1)]


def kernel_two_body(taps, grads, out, padded_grads, acc):
    step = pl.program_id(0)
    last = pl.num_programs(0) - 1
    mels, half = taps.shape[0], taps.shape[1]

    @pl.when(step == 0)
    def _():
        padded_grads[0] = jnp.zeros(grads.shape[1:], BF16)
        padded_grads[MEL + 1] = jnp.zeros(grads.shape[1:], BF16)
        padded_grads[1 : MEL + 1] = grads[...]
        acc[...] = jnp.zeros(acc.shape, F32)

    block = taps[...].reshape(mels * half, 512)
    for d in range(3):
        chosen = padded_grads[pl.ds(step * mels + 2 - d, mels)].reshape(mels * half, 2 * C_MID)
        acc[d] += dot_rows(chosen, block)

    @pl.when(step == last)
    def _():
        pieces = []
        for t in range(3):
            for d in range(3):
                pieces.append(
                    acc[d, 0:C_MID, t * 128 : t * 128 + 128]
                    + acc[d, C_MID : 2 * C_MID, (t + 1) * 128 : (t + 1) * 128 + 128]
                )
        scatter_blocks(out, jnp.concatenate(pieces, axis=1), 9 * C_MID)


def kernel_two_grad(taps, grads, copies, share, rows_two):
    half = taps.shape[1]
    mels = 4
    shape = (copies, share, padded(rows_two))
    return call(
        kernel_two_body,
        (MEL // mels,),
        [pl.BlockSpec((mels, half, 512), lambda i: (i, 0, 0)), whole(grads.shape)],
        whole(shape),
        jax.ShapeDtypeStruct(shape, BF16),
        [
            pltpu.VMEM((MEL + 2, half, 2 * C_MID), BF16),
            pltpu.VMEM((3, 2 * C_MID, 512), F32),
        ],
        flops=2 * MEL * half * 1536 * 256,
        moved=11 * 2**20,
    )(taps, grads)


def back_one_body(count, lift, pre_one, sums_one, back_stats, vec, masks, k1, taps_x,
                  grad_x, blocks, sums_out, weight, taps, acc, woven):
    step = pl.program_id(0)
    last = pl.num_programs(0) - 1
    mels = lift.shape[0]
    pairs = mels // 2
    rows = masks.shape[1]
    half = rows - TAIL

    @pl.when(step == 0)
    def _():
        weight[...] = jnp.zeros(weight.shape, BF16)
        for mi in range(4):
            for mo in (1, 2):
                d = mo - mi + 1
                for q in range(4):
                    for p in range(2):
                        t = 2 - q + p
                        if 0 <= t < 3 and 0 <= d < 3:
                            at = mi * 512 + q * 128
                            to = p * 128 + (mo - 1) * 64
                            block = k1[(3 * t + d) * C_IN : (3 * t + d + 1) * C_IN]
                            weight[at : at + 128, to : to + 64] = (
                                block.astype(F32).T.astype(BF16)
                            )
        taps[0] = jnp.zeros(taps.shape[1:], BF16)
        taps[taps.shape[0] - 1] = jnp.zeros(taps.shape[1:], BF16)
        acc[...] = jnp.zeros(acc.shape, F32)
        sums_out[...] = stat_sums(back_stats)

    @pl.when(step < last)
    def _():
        a, b, c = grad_terms(sums_one[...], sums_out[...], vec[0:1], count)
        before = masks[0]
        after = masks[1]
        for k in range(mels):
            grad = lift[k] * a + (pre_one[k] * b + c)
            block = outer_taps(grad[:, :C_MID], grad[:, C_MID:], before, after)
            taps[1 + step * mels + k] = block[0:half]

    @pl.when(step > 0)
    def _():
        base = (step - 1) * mels
        near = []
        for q in range(pairs):
            near.append([taps[base + 2 * q + mi] for mi in range(4)])
        lhs = jnp.concatenate([jnp.concatenate(n, axis=1) for n in near], axis=0)
        out = jnp.dot(lhs, weight[...], preferred_element_type=F32)
        for q in range(pairs):
            lanes = slice(q * LANES, (q + 1) * LANES)
            part = out[q * half : (q + 1) * half]
            woven[q, pl.ds(0, half, stride=2), :] = part[:, 0:128]
            woven[q, pl.ds(1, half, stride=2), :] = part[:, 128:256]
            grad_x[:, lanes] = woven[q]
        chosen = jnp.concatenate(
            [jnp.concatenate([m[:, 128:384] for m in n], axis=1) for n in near], axis=0
        )
        acc[...] += dot_rows(chosen, taps_x[...].reshape(pairs * half, 512))

    @pl.when(step == last)
    def _():
        pieces = []
        for t in range(3):
            for d in range(3):
                total = jnp.zeros((C_MID, C_IN), F32)
                for mi in range(4):
                    for side in range(2):
                        if side - mi + 2 == d:
                            for p in range(2):
                                at = (t + p) * 128 + side * 64
                                total += acc[
                                    mi * 256 + p * 128 : mi * 256 + p * 128 + 128, at : at + 64
                                ]
                pieces.append(total)
        scatter_blocks(blocks, jnp.concatenate(pieces, axis=1), 9 * C_IN)


def back_one(lift, pre_one, sums_one, back_stats, vec, masks, k1, taps_x, share, rows_one, count):
    copies = back_stats.shape[0]
    rows = masks.shape[1]
    half = rows - TAIL
    mels = 4
    pairs = mels // 2
    steps = MEL // mels
    lead = lambda i: jnp.minimum(i, steps - 1)
    lag = lambda i: jnp.maximum(i - 1, 0)
    lead_block = pl.BlockSpec((mels, rows, 2 * C_MID), lambda i: (lead(i), 0, 0))
    shape = (copies, share, padded(rows_one))
    return call(
        lambda *refs: back_one_body(count, *refs),
        (steps + 1,),
        [
            lead_block,
            lead_block,
            whole(sums_one.shape),
            whole(back_stats.shape),
            whole(vec.shape),
            whole(masks.shape),
            whole(k1.shape),
            pl.BlockSpec((pairs, half, 512), lambda i: (lag(i), 0, 0)),
        ],
        [
            pl.BlockSpec((2 * half, pairs * LANES), lambda i: (0, lag(i))),
            whole(shape),
            whole((2, C_MID)),
        ],
        [
            jax.ShapeDtypeStruct((2 * half, MEL * C_IN), F32),
            jax.ShapeDtypeStruct(shape, BF16),
            jax.ShapeDtypeStruct((2, C_MID), F32),
        ],
        [
            pltpu.VMEM((2048, 2 * C_MID), BF16),
            pltpu.VMEM((MEL + 2, half, 512), BF16),
            pltpu.VMEM((1024, 512), F32),
            pltpu.VMEM((pairs, 2 * half, LANES), F32),
        ],
        flops=2 * MEL * half * (1024 + 1024) * 256,
        moved=20 * 2**20,
    )(lift, pre_one, sums_one, back_stats, vec, masks, k1, taps_x)


def finish_body(meta, got_one, got_two, back_one_sums, back_two_sums,
                own_one, own_two, ga, sa, gb, sb):
    own_one[...] = jnp.sum(got_one[...].astype(F32), axis=0)[:, 0 : own_one.shape[1]]
    own_two[...] = jnp.sum(got_two[...].astype(F32), axis=0)[:, 0 : own_two.shape[1]]
    share = ga.shape[1]
    lane = lax.broadcasted_iota(jnp.int32, (share, C_MID), 1)
    row = lax.broadcasted_iota(jnp.int32, (share, C_MID), 0)
    chosen = lane == meta[2] * share + row
    first = lax.broadcasted_iota(jnp.int32, (share, share), 0)
    second = lax.broadcasted_iota(jnp.int32, (share, share), 1)
    for out, sums, k in (
        (ga, back_one_sums, 1), (sa, back_one_sums, 0), (gb, back_two_sums, 1), (sb, back_two_sums, 0)
    ):
        wide = jnp.broadcast_to(sums[k : k + 1], (share, C_MID))
        column = jnp.sum(jnp.where(chosen, wide, 0.0), axis=1, keepdims=True)
        spread = jnp.broadcast_to(column, (share, share))
        out[...] = jnp.sum(jnp.where(first == second, spread, 0.0), axis=0, keepdims=True)


def finish(meta, got_one, got_two, back_one_sums, back_two_sums, rows_one, rows_two):
    share = got_one.shape[1]
    shapes = [(share, rows_one), (share, rows_two)] + [(1, share)] * 4
    return call(
        finish_body,
        (1,),
        [
            SMEM,
            whole(got_one.shape),
            whole(got_two.shape),
            whole(back_one_sums.shape),
            whole(back_two_sums.shape),
        ],
        [whole(s) for s in shapes],
        [jax.ShapeDtypeStruct(s, F32) for s in shapes],
        [],
    )(meta, got_one, got_two, back_one_sums, back_two_sums)


def exchange(blocks):
    return lax.all_to_all(blocks, AXES, 0, 0, tiled=True)


def shards(
    features, clip_starts, kernel_one, kernel_two, gain_one, shift_one, gain_two, shift_two, cotangent
):
    frames = features.shape[0]
    copies = lax.axis_size(AXES)
    row_count = lax.axis_size("row")
    count = float(frames * MEL * copies)
    meta = jnp.stack(
        [lax.axis_index(AXES) * frames, jnp.int32(frames * copies), lax.axis_index("grp")]
    ).astype(jnp.int32)
    rows_one, rows_two = kernel_one.shape[0], kernel_two.shape[0]
    share = kernel_one.shape[1]
    vectors = [v.reshape(1, share) for v in (gain_one, shift_one, gain_two, shift_two)]
    w1, w2, masks, up, down = setup(
        meta, kernel_one.T, kernel_two.T, vectors, clip_starts.reshape(1, -1), features, cotangent, copies
    )
    ends = copies - 1
    up = lax.ppermute(up, AXES, [(i, i + 1) for i in range(ends)])
    down = lax.ppermute(down, AXES, [(i + 1, i) for i in range(ends)])
    w1 = exchange(w1)
    w2 = exchange(w2)
    pre_one, stats, taps_x, k1, vec = conv_one(features, up, down, masks, w1, row_count, copies)
    stats = exchange(stats)
    pre_two, stats, taps_a, k2, sums_one = conv_two(
        pre_one, stats, vec, masks, w2, row_count, count
    )
    stats = exchange(stats)
    block_out, lift_two, stats, sums_two = norm_two(
        pre_two, stats, vec, cotangent, up, down, count
    )
    stats = exchange(stats)
    grad_two, lift_one, stats, back_two_sums = back_two(
        lift_two, pre_two, sums_two, stats, vec, masks, k2, pre_one, sums_one, count
    )
    stats = exchange(stats)
    blocks_two = exchange(kernel_two_grad(taps_a, grad_two, copies, share, rows_two))
    grad_features, blocks_one, back_one_sums = back_one(
        lift_one, pre_one, sums_one, stats, vec, masks, k1, taps_x, share, rows_one, count
    )
    blocks_one = exchange(blocks_one)
    own_one, own_two, ga, sa, gb, sb = finish(
        meta, blocks_one, blocks_two, back_one_sums, back_two_sums, rows_one, rows_two
    )
    return (
        block_out,
        grad_features,
        own_one.T,
        own_two.T,
        ga.reshape(share),
        sa.reshape(share),
        gb.reshape(share),
        sb.reshape(share),
    )


def solution(mesh):
    placed = (
        P(AXES, None), P(), P("row", "grp"), P("row", "grp"),
        P("grp"), P("grp"), P("grp"), P("grp"), P(AXES, None),
    )
    return jax.shard_map(
        shards,
        mesh=mesh,
        in_specs=placed,
        out_specs=(
            P(AXES, None), P(AXES, None), P("row", "grp"), P("row", "grp"),
            P("grp"), P("grp"), P("grp"), P("grp"),
        ),
        check_vma=False,
    )
```

```python
import jax
import jax.numpy as jnp
from jax import lax
from jax.experimental import pallas as pl
from jax.experimental.pallas import tpu as pltpu
from jax.sharding import PartitionSpec as P

MEL = 32
C_IN = 64
C_MID = 128
EPS = 1e-05
AXES = ("grp", "row")
LANES = 128
TAIL = 16
F32 = jnp.float32
BF16 = jnp.bfloat16


def call(body, grid, in_specs, out_specs, out_shape, scratch, flops=0, moved=0):
    return pl.pallas_call(
        body,
        grid=grid,
        in_specs=in_specs,
        out_specs=out_specs,
        out_shape=out_shape,
        scratch_shapes=scratch,
        compiler_params=pltpu.CompilerParams(
            dimension_semantics=("arbitrary",) * len(grid), vmem_limit_bytes=24 * 2**20
        ),
        cost_estimate=pl.CostEstimate(flops=flops, bytes_accessed=moved, transcendentals=0),
    )


def whole(shape):
    return pl.BlockSpec(shape, lambda *_: (0,) * len(shape))


SMEM = pl.BlockSpec(memory_space=pltpu.SMEM)


def padded(size):
    return -(-size // LANES) * LANES


def fold(values):
    total = jnp.sum(values.reshape(-1, 8, 2 * C_MID), axis=0)
    total = jnp.sum(total, axis=0, keepdims=True)
    return total[:, :C_MID] + total[:, C_MID:]


def partial_sum(values):
    return jnp.sum(values.reshape(-1, 8, values.shape[-1]), axis=0)


def twice(row):
    return jnp.concatenate([row, row], axis=1)


def rolled(values, step):
    rows = values.shape[0]
    return pltpu.roll(values, step % rows, 0)


def outer_taps(even, odd, before, after):
    return jnp.concatenate(
        [rolled(odd, 1) * before, even, odd, rolled(even, -1) * after], axis=1
    ).astype(BF16)


def stat_sums(stats_ref):
    return jnp.sum(stats_ref[...], axis=0)


def norm_terms(sums, count):
    mean = sums[0:1] / count
    rstd = lax.rsqrt(sums[1:2] / count - mean * mean + EPS)
    return mean, rstd


def setup_body(meta, k1, k2, ga, sa, gb, sb, clips, x_head, x_tail, c_head, c_tail,
               w1_out, w2_out, masks, up, down):
    share = k1.shape[0]
    copies = w1_out.shape[0]
    rows_one = k1.shape[1]
    w1_out[...] = jnp.zeros(w1_out.shape, BF16)
    w2_out[...] = jnp.zeros(w2_out.shape, BF16)
    first = lax.broadcasted_iota(jnp.int32, (share, share), 0)
    second = lax.broadcasted_iota(jnp.int32, (share, share), 1)
    columns = [k1[...].astype(F32)]
    for vector in (ga, sa, gb, sb):
        spread = jnp.broadcast_to(vector[...].astype(F32), (share, share))
        columns.append(
            jnp.sum(jnp.where(first == second, spread, 0.0), axis=1, keepdims=True)
        )
    chunk_one = jnp.concatenate(columns, axis=1).astype(BF16)
    chunk_two = k2[...]
    for i in range(copies):
        w1_out[i, :, 0 : rows_one + 4] = chunk_one
        w2_out[i, :, 0 : k2.shape[1]] = chunk_two
    rows = masks.shape[1]
    half = rows - TAIL
    place = lax.broadcasted_iota(jnp.int32, (rows, clips.shape[1]), 0)
    pair = jnp.where(place >= half + TAIL // 2, place - rows, place)
    frame = meta[0] + 2 * pair
    starts = jnp.broadcast_to(clips[...], (rows, clips.shape[1]))
    for slot, shift in ((0, 0), (1, 2)):
        hit = jnp.where((frame + shift == starts) | (frame + shift >= meta[1]), 1.0, 0.0)
        begins = jnp.max(hit, axis=1, keepdims=True)
        masks[slot] = jnp.broadcast_to(1.0 - begins, (rows, LANES))
    row = lax.broadcasted_iota(jnp.int32, (8, x_head.shape[1]), 0)
    xt = x_tail[...].astype(F32)
    ct = c_tail[...].astype(F32)
    up[...] = jnp.where(
        row < 4, pltpu.roll(xt[8:16], 4, 0), jnp.where(row == 4, ct[15:16], 0.0)
    ).astype(BF16)
    xh = x_head[...].astype(F32)
    ch = c_head[...].astype(F32)
    down[...] = jnp.where(row < 4, xh[0:8], jnp.where(row == 4, ch[0:1], 0.0)).astype(BF16)


def setup(meta, k1t, k2t, vectors, clips, features, cotangent, copies):
    frames, wide = features.shape
    halves = cotangent.shape[0]
    rows = frames // 2 + TAIL
    share = k1t.shape[0]
    w1 = (copies, share, padded(k1t.shape[1] + 4))
    w2 = (copies, share, padded(k2t.shape[1]))
    return call(
        setup_body,
        (1,),
        [
            SMEM,
            whole(k1t.shape),
            whole(k2t.shape),
            *[whole((1, share))] * 4,
            whole(clips.shape),
            pl.BlockSpec((16, wide), lambda i: (0, 0)),
            pl.BlockSpec((16, wide), lambda i: (frames // 16 - 1, 0)),
            pl.BlockSpec((16, wide), lambda i: (0, 0)),
            pl.BlockSpec((16, wide), lambda i: (halves // 16 - 1, 0)),
        ],
        [whole(w1), whole(w2), whole((2, rows, LANES)), whole((8, wide)), whole((8, wide))],
        [
            jax.ShapeDtypeStruct(w1, BF16),
            jax.ShapeDtypeStruct(w2, BF16),
            jax.ShapeDtypeStruct((2, rows, LANES), F32),
            jax.ShapeDtypeStruct((8, wide), BF16),
            jax.ShapeDtypeStruct((8, wide), BF16),
        ],
        [],
    )(meta, k1t, k2t, *vectors, clips, features, features, cotangent, cotangent)


def rows_of(gathered, index, row_count):
    grps = gathered.shape[0] // row_count
    pieces = [gathered[g * row_count + index] for g in range(grps)]
    return jnp.concatenate(pieces, axis=0).astype(F32).T


def conv_one_body(row_count, x, up, down, masks, wg, pre, stats, taps_out, k1_out, vec_out,
                  xs, kf, w_even, w_odd, taps, acc):
    step = pl.program_id(0)
    last = pl.num_programs(0) - 1
    pairs = x.shape[1] // LANES
    rows = masks.shape[1]
    half = rows - TAIL

    @pl.when(step == 0)
    def _():
        rows_one = kf.shape[0] // row_count
        for r in range(row_count):
            shard = rows_of(wg, r, row_count)
            kf[rows_one * r : rows_one * (r + 1)] = shard[0:rows_one]
            if r == 0:
                vec_out[...] = shard[rows_one : rows_one + 4]
        k1_out[...] = kf[...].astype(BF16)
        w_even[...] = jnp.zeros(w_even.shape, BF16)
        w_odd[...] = jnp.zeros(w_odd.shape, BF16)
        placed = (
            (w_even, 0, 1, 0), (w_even, 1, 0, 1), (w_even, 1, 1, 2),
            (w_odd, 0, 0, 0), (w_odd, 0, 1, 1), (w_odd, 1, 0, 2),
        )
        for matrix, piece, side, d in placed:
            for q in range(4):
                for p in range(2):
                    t = q - p
                    if 0 <= t < 3:
                        at = piece * 512 + q * 128 + side * 64
                        matrix[at : at + 64, p * 128 : p * 128 + 128] = kf[
                            (3 * t + d) * C_IN : (3 * t + d + 1) * C_IN
                        ].astype(BF16)
        taps[0] = jnp.zeros(taps.shape[1:], BF16)
        taps[taps.shape[0] - 1] = jnp.zeros(taps.shape[1:], BF16)
        acc[...] = jnp.zeros(acc.shape, F32)

    @pl.when(step < last)
    def _():
        before = masks[0]
        after = masks[1]
        row = lax.broadcasted_iota(jnp.int32, (TAIL, LANES), 0)
        for q in range(pairs):
            lanes = slice(q * LANES, (q + 1) * LANES)
            xs[...] = x[:, lanes].astype(F32)
            u = up[:, lanes].astype(F32)
            d = down[:, lanes].astype(F32)

            def side(k):
                tail = jnp.where(row == 0, d[k : k + 1], 0.0)
                tail = jnp.where(row == 1, d[k + 2 : k + 3], tail)
                tail = jnp.where(row == TAIL - 2, u[k : k + 1], tail)
                tail = jnp.where(row == TAIL - 1, u[k + 2 : k + 3], tail)
                return jnp.concatenate([xs[pl.ds(k, half, stride=2), :], tail], axis=0)

            block = outer_taps(side(0), side(1), before, after)
            taps[1 + step * pairs + q] = block
            taps_out[q] = block[0:half]

    @pl.when(step > 0)
    def _():
        base = (step - 1) * pairs
        left = taps[pl.ds(base, pairs)].reshape(pairs * rows, 512)
        mid = taps[pl.ds(base + 1, pairs)].reshape(pairs * rows, 512)
        right = taps[pl.ds(base + 2, pairs)].reshape(pairs * rows, 512)
        for parity, lhs, matrix in (
            (0, jnp.concatenate([left, mid], axis=1), w_even),
            (1, jnp.concatenate([mid, right], axis=1), w_odd),
        ):
            out = jnp.dot(lhs, matrix[...], preferred_element_type=F32)
            out = out.reshape(pairs, rows, 2 * C_MID)
            for q in range(pairs):
                pre[2 * q + parity] = out[q]
            own = out[:, 0:half]
            acc[0] += partial_sum(own)
            acc[1] += partial_sum(own * own)

    @pl.when(step == last)
    def _():
        sums = jnp.concatenate([fold(acc[0]), fold(acc[1])], axis=0)
        stats[...] = jnp.broadcast_to(sums[None], stats.shape)


def conv_one(features, up, down, masks, wg, row_count, copies):
    frames, wide = features.shape
    rows = masks.shape[1]
    half = rows - TAIL
    pairs = 4
    steps = wide // LANES // pairs
    lead = lambda i: jnp.minimum(i, steps - 1)
    lag = lambda i: jnp.maximum(i - 1, 0)
    return call(
        lambda *refs: conv_one_body(row_count, *refs),
        (steps + 1,),
        [
            pl.BlockSpec((frames, pairs * LANES), lambda i: (0, lead(i))),
            pl.BlockSpec((8, pairs * LANES), lambda i: (0, lead(i))),
            pl.BlockSpec((8, pairs * LANES), lambda i: (0, lead(i))),
            whole(masks.shape),
            whole(wg.shape),
        ],
        [
            pl.BlockSpec((2 * pairs, rows, 2 * C_MID), lambda i: (lag(i), 0, 0)),
            whole((copies, 2, C_MID)),
            pl.BlockSpec((pairs, half, 512), lambda i: (lead(i), 0, 0)),
            whole((9 * C_IN, C_MID)),
            whole((4, C_MID)),
        ],
        [
            jax.ShapeDtypeStruct((MEL, rows, 2 * C_MID), F32),
            jax.ShapeDtypeStruct((copies, 2, C_MID), F32),
            jax.ShapeDtypeStruct((MEL // 2, half, 512), BF16),
            jax.ShapeDtypeStruct((9 * C_IN, C_MID), BF16),
            jax.ShapeDtypeStruct((4, C_MID), F32),
        ],
        [
            pltpu.VMEM((frames, LANES), F32),
            pltpu.VMEM((9 * C_IN, C_MID), F32),
            pltpu.VMEM((1024, 2 * C_MID), BF16),
            pltpu.VMEM((1024, 2 * C_MID), BF16),
            pltpu.VMEM((MEL // 2 + 2, rows, 512), BF16),
            pltpu.VMEM((2, 8, 2 * C_MID), F32),
        ],
        flops=2 * 2 * MEL * rows * 512 * 256,
        moved=16 * 2**20,
    )(features, up, down, masks, wg)


def conv_two_body(row_count, count, pre_one, stats_one, vec, masks, wg,
                  pre, stats, taps_out, k2_out, sums_out, kf, weight, taps, acc):
    step = pl.program_id(0)
    last = pl.num_programs(0) - 1
    mels = pre_one.shape[0]
    rows = masks.shape[1]
    half = rows - TAIL

    @pl.when(step == 0)
    def _():
        rows_two = kf.shape[0] // row_count
        for r in range(row_count):
            kf[rows_two * r : rows_two * (r + 1)] = rows_of(wg, r, row_count)[0:rows_two]
        k2_out[...] = kf[...].astype(BF16)
        weight[...] = jnp.zeros(weight.shape, BF16)
        for d in range(3):
            for q in range(4):
                for p in range(2):
                    t = q - p
                    if 0 <= t < 3:
                        at = d * 512 + q * 128
                        weight[at : at + 128, p * 128 : p * 128 + 128] = kf[
                            (3 * t + d) * C_MID : (3 * t + d + 1) * C_MID
                        ].astype(BF16)
        taps[0] = jnp.zeros(taps.shape[1:], BF16)
        taps[taps.shape[0] - 1] = jnp.zeros(taps.shape[1:], BF16)
        acc[...] = jnp.zeros(acc.shape, F32)
        sums_out[...] = stat_sums(stats_one)

    @pl.when(step < last)
    def _():
        mean, rstd = norm_terms(sums_out[...], count)
        scale = 0.5 * vec[0:1] * rstd
        shift = 0.5 * vec[1:2] - mean * scale
        scale = twice(scale)
        shift = twice(shift)
        before = masks[0]
        after = masks[1]
        for k in range(mels):
            h = pre_one[k] * scale + shift
            active = h + h * jnp.tanh(h)
            block = outer_taps(active[:, :C_MID], active[:, C_MID:], before, after)
            taps[1 + step * mels + k] = block
            taps_out[k] = block[0:half]

    @pl.when(step > 0)
    def _():
        base = (step - 1) * mels
        lhs = jnp.concatenate(
            [taps[pl.ds(base + d, mels)].reshape(mels * rows, 512) for d in range(3)], axis=1
        )
        out = jnp.dot(lhs, weight[...], preferred_element_type=F32)
        out = out.reshape(mels, rows, 2 * C_MID)
        pre[...] = out
        own = out[:, 0:half]
        acc[0] += partial_sum(own)
        acc[1] += partial_sum(own * own)

    @pl.when(step == last)
    def _():
        sums = jnp.concatenate([fold(acc[0]), fold(acc[1])], axis=0)
        stats[...] = jnp.broadcast_to(sums[None], stats.shape)


def conv_two(pre_one, stats_one, vec, masks, wg, row_count, count):
    copies = stats_one.shape[0]
    rows = masks.shape[1]
    half = rows - TAIL
    mels = 4
    steps = MEL // mels
    lead = lambda i: jnp.minimum(i, steps - 1)
    lag = lambda i: jnp.maximum(i - 1, 0)
    return call(
        lambda *refs: conv_two_body(row_count, count, *refs),
        (steps + 1,),
        [
            pl.BlockSpec((mels, rows, 2 * C_MID), lambda i: (lead(i), 0, 0)),
            whole(stats_one.shape),
            whole(vec.shape),
            whole(masks.shape),
            whole(wg.shape),
        ],
        [
            pl.BlockSpec((mels, rows, 2 * C_MID), lambda i: (lag(i), 0, 0)),
            whole((copies, 2, C_MID)),
            pl.BlockSpec((mels, half, 512), lambda i: (lead(i), 0, 0)),
            whole((9 * C_MID, C_MID)),
            whole((2, C_MID)),
        ],
        [
            jax.ShapeDtypeStruct((MEL, rows, 2 * C_MID), F32),
            jax.ShapeDtypeStruct((copies, 2, C_MID), F32),
            jax.ShapeDtypeStruct((MEL, half, 512), BF16),
            jax.ShapeDtypeStruct((9 * C_MID, C_MID), BF16),
            jax.ShapeDtypeStruct((2, C_MID), F32),
        ],
        [
            pltpu.VMEM((9 * C_MID, C_MID), F32),
            pltpu.VMEM((1536, 2 * C_MID), BF16),
            pltpu.VMEM((MEL + 2, rows, 512), BF16),
            pltpu.VMEM((2, 8, 2 * C_MID), F32),
        ],
        flops=2 * MEL * rows * 1536 * 256,
        moved=20 * 2**20,
    )(pre_one, stats_one, vec, masks, wg)


def norm_two_body(count, pre, stats_two, vec, cot, up, down, pooled, lift, back_stats, sums_out, acc):
    step = pl.program_id(0)
    last = pl.num_programs(0) - 1
    pairs = cot.shape[1] // LANES
    half = cot.shape[0]

    @pl.when(step == 0)
    def _():
        acc[...] = jnp.zeros(acc.shape, F32)
        sums_out[...] = stat_sums(stats_two)

    mean, rstd = norm_terms(sums_out[...], count)
    scale = 0.5 * vec[2:3] * rstd
    shift = 0.5 * vec[3:4] - mean * scale
    norm_shift = -mean * rstd
    row = lax.broadcasted_iota(jnp.int32, (TAIL, LANES), 0)
    for q in range(pairs):
        lanes = slice(q * LANES, (q + 1) * LANES)
        u = up[:, lanes].astype(F32)
        d = down[:, lanes].astype(F32)
        tail = jnp.where(row == 0, d[4:5], jnp.where(row == TAIL - 1, u[4:5], 0.0))
        grad = jnp.concatenate([cot[:, lanes].astype(F32), tail], axis=0) * 0.125
        total = jnp.zeros((half, LANES), F32)
        for k in (2 * q, 2 * q + 1):
            for p in range(2):
                side = slice(p * C_MID, (p + 1) * C_MID)
                value = pre[k, :, side]
                h = value * scale + shift
                th = jnp.tanh(h)
                one = 1.0 + th
                gl = grad * (one * (1.0 + (h - h * th)))
                lift[k, :, side] = gl
                total += (h * one)[0:half]
                own = gl[0:half]
                normed = value[0:half] * rstd + norm_shift
                acc[0] += partial_sum(own)
                acc[1] += partial_sum(own * normed)
        pooled[:, lanes] = (total * 0.25).astype(BF16)

    @pl.when(step == last)
    def _():
        sums = jnp.concatenate(
            [jnp.sum(acc[k], axis=0, keepdims=True) for k in range(2)], axis=0
        )
        back_stats[...] = jnp.broadcast_to(sums[None], back_stats.shape)


def norm_two(pre, stats_two, vec, cot, up, down, count):
    copies = stats_two.shape[0]
    half, wide = cot.shape
    rows = half + TAIL
    pairs = 2
    steps = wide // LANES // pairs
    block = pl.BlockSpec((2 * pairs, rows, 2 * C_MID), lambda i: (i, 0, 0))
    return call(
        lambda *refs: norm_two_body(count, *refs),
        (steps,),
        [
            block,
            whole(stats_two.shape),
            whole(vec.shape),
            pl.BlockSpec((half, pairs * LANES), lambda i: (0, i)),
            pl.BlockSpec((8, pairs * LANES), lambda i: (0, i)),
            pl.BlockSpec((8, pairs * LANES), lambda i: (0, i)),
        ],
        [
            pl.BlockSpec((half, pairs * LANES), lambda i: (0, i)),
            block,
            whole((copies, 2, C_MID)),
            whole((2, C_MID)),
        ],
        [
            jax.ShapeDtypeStruct((half, wide), BF16),
            jax.ShapeDtypeStruct((MEL, rows, 2 * C_MID), F32),
            jax.ShapeDtypeStruct((copies, 2, C_MID), F32),
            jax.ShapeDtypeStruct((2, C_MID), F32),
        ],
        [pltpu.VMEM((2, 8, LANES), F32)],
        moved=16 * 2**20,
    )(pre, stats_two, vec, cot, up, down)


def grad_terms(sums, back, gain, count):
    mean, rstd = norm_terms(sums, count)
    a = gain * rstd
    b = -a * rstd * (back[1:2] / count)
    c = -a * (back[0:1] / count) - b * mean
    return twice(a), twice(b), twice(c)


def back_two_body(count, lift, pre_two, sums_two, back_stats, vec, masks, k2, pre_one, sums_one,
                  grad_out, lift_one, back_out, sums_out, weight, taps, acc):
    step = pl.program_id(0)
    last = pl.num_programs(0) - 1
    mels = lift.shape[0]
    rows = masks.shape[1]
    half = rows - TAIL

    @pl.when(step == 0)
    def _():
        weight[...] = jnp.zeros(weight.shape, BF16)
        for d in range(3):
            for q in range(4):
                for p in range(2):
                    t = 2 - q + p
                    if 0 <= t < 3:
                        at = (2 - d) * 512 + q * 128
                        block = k2[(3 * t + d) * C_MID : (3 * t + d + 1) * C_MID]
                        weight[at : at + 128, p * 128 : p * 128 + 128] = (
                            block.astype(F32).T.astype(BF16)
                        )
        taps[0] = jnp.zeros(taps.shape[1:], BF16)
        taps[taps.shape[0] - 1] = jnp.zeros(taps.shape[1:], BF16)
        acc[...] = jnp.zeros(acc.shape, F32)
        sums_out[...] = stat_sums(back_stats)

    @pl.when(step < last)
    def _():
        a, b, c = grad_terms(sums_two[...], sums_out[...], vec[2:3], count)
        before = masks[0]
        after = masks[1]
        for k in range(mels):
            grad = lift[k] * a + (pre_two[k] * b + c)
            block = outer_taps(grad[:, :C_MID], grad[:, C_MID:], before, after)
            taps[1 + step * mels + k] = block
            grad_out[k] = block[0:half, 128:384]

    @pl.when(step > 0)
    def _():
        base = (step - 1) * mels
        lhs = jnp.concatenate(
            [taps[pl.ds(base + d, mels)].reshape(mels * rows, 512) for d in range(3)], axis=1
        )
        out = jnp.dot(lhs, weight[...], preferred_element_type=F32)
        out = out.reshape(mels, rows, 2 * C_MID)
        mean, rstd = norm_terms(sums_one[...], count)
        scale = 0.5 * vec[0:1] * rstd
        shift = twice(0.5 * vec[1:2] - mean * scale)
        scale = twice(scale)
        norm_shift = twice(-mean * rstd)
        rstd = twice(rstd)
        for k in range(mels):
            value = pre_one[k]
            h = value * scale + shift
            th = jnp.tanh(h)
            gl = out[k] * (0.5 * (1.0 + th) * (1.0 + (h - h * th)))
            lift_one[k] = gl
            own = gl[0:half]
            acc[0] += partial_sum(own)
            acc[1] += partial_sum(own * (value[0:half] * rstd + norm_shift))

    @pl.when(step == last)
    def _():
        sums = jnp.concatenate([fold(acc[0]), fold(acc[1])], axis=0)
        back_out[...] = jnp.broadcast_to(sums[None], back_out.shape)


def back_two(lift, pre_two, sums_two, back_stats, vec, masks, k2, pre_one, sums_one, count):
    copies = back_stats.shape[0]
    rows = masks.shape[1]
    half = rows - TAIL
    mels = 4
    steps = MEL // mels
    lead = lambda i: jnp.minimum(i, steps - 1)
    lag = lambda i: jnp.maximum(i - 1, 0)
    lead_block = pl.BlockSpec((mels, rows, 2 * C_MID), lambda i: (lead(i), 0, 0))
    lag_block = pl.BlockSpec((mels, rows, 2 * C_MID), lambda i: (lag(i), 0, 0))
    return call(
        lambda *refs: back_two_body(count, *refs),
        (steps + 1,),
        [
            lead_block,
            lead_block,
            whole(sums_two.shape),
            whole(back_stats.shape),
            whole(vec.shape),
            whole(masks.shape),
            whole(k2.shape),
            lag_block,
            whole(sums_one.shape),
        ],
        [
            pl.BlockSpec((mels, half, 2 * C_MID), lambda i: (lead(i), 0, 0)),
            lag_block,
            whole((copies, 2, C_MID)),
            whole((2, C_MID)),
        ],
        [
            jax.ShapeDtypeStruct((MEL, half, 2 * C_MID), BF16),
            jax.ShapeDtypeStruct((MEL, rows, 2 * C_MID), F32),
            jax.ShapeDtypeStruct((copies, 2, C_MID), F32),
            jax.ShapeDtypeStruct((2, C_MID), F32),
        ],
        [
            pltpu.VMEM((1536, 2 * C_MID), BF16),
            pltpu.VMEM((MEL + 2, rows, 512), BF16),
            pltpu.VMEM((2, 8, 2 * C_MID), F32),
        ],
        flops=2 * MEL * rows * 1536 * 256,
        moved=32 * 2**20,
    )(lift, pre_two, sums_two, back_stats, vec, masks, k2, pre_one, sums_one)


def dot_rows(first, second):
    return lax.dot_general(
        first, second, (((0,), (0,)), ((), ())), preferred_element_type=F32
    )


def scatter_blocks(out, by_channel, rows_in):
    copies, share, wide = out.shape
    grps = by_channel.shape[0] // share
    row_count = copies // grps
    size = rows_in // row_count
    turned = by_channel.T
    for r in range(row_count):
        part = turned[size * r : size * (r + 1)]
        part = jnp.concatenate([part, jnp.zeros((wide - size, part.shape[1]), F32)], axis=0)
        back = part.T.astype(BF16)
        for g in range(grps):
            out[g * row_count + r] = back[share * g : share * (g + 1)]


def kernel_two_body(taps, grads, out, token, padded_grads, acc):
    step = pl.program_id(0)
    last = pl.num_programs(0) - 1
    mels, half = taps.shape[0], taps.shape[1]

    @pl.when(step == 0)
    def _():
        padded_grads[0] = jnp.zeros(grads.shape[1:], BF16)
        padded_grads[MEL + 1] = jnp.zeros(grads.shape[1:], BF16)
        padded_grads[1 : MEL + 1] = grads[...]
        acc[...] = jnp.zeros(acc.shape, F32)
        token[...] = jnp.zeros(token.shape, F32)

    block = taps[...].reshape(mels * half, 512)
    for d in range(3):
        chosen = padded_grads[pl.ds(step * mels + 2 - d, mels)].reshape(mels * half, 2 * C_MID)
        acc[d] += dot_rows(chosen, block)

    @pl.when(step == last)
    def _():
        pieces = []
        for t in range(3):
            for d in range(3):
                pieces.append(
                    acc[d, 0:C_MID, t * 128 : t * 128 + 128]
                    + acc[d, C_MID : 2 * C_MID, (t + 1) * 128 : (t + 1) * 128 + 128]
                )
        scatter_blocks(out, jnp.concatenate(pieces, axis=1), 9 * C_MID)


def kernel_two_grad(taps, grads, copies, share, rows_two):
    half = taps.shape[1]
    mels = 4
    shape = (copies, share, padded(rows_two))
    return call(
        kernel_two_body,
        (MEL // mels,),
        [pl.BlockSpec((mels, half, 512), lambda i: (i, 0, 0)), whole(grads.shape)],
        [whole(shape), whole((8, LANES))],
        [jax.ShapeDtypeStruct(shape, BF16), jax.ShapeDtypeStruct((8, LANES), F32)],
        [
            pltpu.VMEM((MEL + 2, half, 2 * C_MID), BF16),
            pltpu.VMEM((3, 2 * C_MID, 512), F32),
        ],
        flops=2 * MEL * half * 1536 * 256,
        moved=11 * 2**20,
    )(taps, grads)


def back_one_body(count, lift, pre_one, sums_one, back_stats, vec, masks, k1, taps_x, token,
                  grad_x, blocks, sums_out, weight, taps, acc, woven):
    step = pl.program_id(0)
    last = pl.num_programs(0) - 1
    mels = lift.shape[0]
    pairs = mels // 2
    rows = masks.shape[1]
    half = rows - TAIL

    @pl.when(step == 0)
    def _():
        weight[...] = jnp.zeros(weight.shape, BF16)
        for mi in range(4):
            for mo in (1, 2):
                d = mo - mi + 1
                for q in range(4):
                    for p in range(2):
                        t = 2 - q + p
                        if 0 <= t < 3 and 0 <= d < 3:
                            at = mi * 512 + q * 128
                            to = p * 128 + (mo - 1) * 64
                            block = k1[(3 * t + d) * C_IN : (3 * t + d + 1) * C_IN]
                            weight[at : at + 128, to : to + 64] = (
                                block.astype(F32).T.astype(BF16)
                            )
        taps[0] = jnp.zeros(taps.shape[1:], BF16)
        taps[taps.shape[0] - 1] = jnp.zeros(taps.shape[1:], BF16)
        acc[...] = jnp.zeros(acc.shape, F32)
        sums_out[...] = stat_sums(back_stats)

    @pl.when(step < last)
    def _():
        a, b, c = grad_terms(sums_one[...], sums_out[...], vec[0:1], count)
        before = masks[0]
        after = masks[1]
        for k in range(mels):
            grad = lift[k] * a + (pre_one[k] * b + c)
            block = outer_taps(grad[:, :C_MID], grad[:, C_MID:], before, after)
            taps[1 + step * mels + k] = block[0:half]

    @pl.when(step > 0)
    def _():
        base = (step - 1) * mels
        near = []
        for q in range(pairs):
            near.append([taps[base + 2 * q + mi] for mi in range(4)])
        lhs = jnp.concatenate([jnp.concatenate(n, axis=1) for n in near], axis=0)
        out = jnp.dot(lhs, weight[...], preferred_element_type=F32)
        for q in range(pairs):
            lanes = slice(q * LANES, (q + 1) * LANES)
            part = out[q * half : (q + 1) * half]
            woven[q, pl.ds(0, half, stride=2), :] = part[:, 0:128]
            woven[q, pl.ds(1, half, stride=2), :] = part[:, 128:256]
            grad_x[:, lanes] = woven[q]
        chosen = jnp.concatenate(
            [jnp.concatenate([m[:, 128:384] for m in n], axis=1) for n in near], axis=0
        )
        acc[...] += dot_rows(chosen, taps_x[...].reshape(pairs * half, 512))

    @pl.when(step == last)
    def _():
        pieces = []
        for t in range(3):
            for d in range(3):
                total = jnp.zeros((C_MID, C_IN), F32)
                for mi in range(4):
                    for side in range(2):
                        if side - mi + 2 == d:
                            for p in range(2):
                                at = (t + p) * 128 + side * 64
                                total += acc[
                                    mi * 256 + p * 128 : mi * 256 + p * 128 + 128, at : at + 64
                                ]
                pieces.append(total)
        scatter_blocks(blocks, jnp.concatenate(pieces, axis=1), 9 * C_IN)


def back_one(lift, pre_one, sums_one, back_stats, vec, masks, k1, taps_x, token, share, rows_one, count):
    copies = back_stats.shape[0]
    rows = masks.shape[1]
    half = rows - TAIL
    mels = 4
    pairs = mels // 2
    steps = MEL // mels
    lead = lambda i: jnp.minimum(i, steps - 1)
    lag = lambda i: jnp.maximum(i - 1, 0)
    lead_block = pl.BlockSpec((mels, rows, 2 * C_MID), lambda i: (lead(i), 0, 0))
    shape = (copies, share, padded(rows_one))
    return call(
        lambda *refs: back_one_body(count, *refs),
        (steps + 1,),
        [
            lead_block,
            lead_block,
            whole(sums_one.shape),
            whole(back_stats.shape),
            whole(vec.shape),
            whole(masks.shape),
            whole(k1.shape),
            pl.BlockSpec((pairs, half, 512), lambda i: (lag(i), 0, 0)),
            pl.BlockSpec(memory_space=pl.ANY),
        ],
        [
            pl.BlockSpec((2 * half, pairs * LANES), lambda i: (0, lag(i))),
            whole(shape),
            whole((2, C_MID)),
        ],
        [
            jax.ShapeDtypeStruct((2 * half, MEL * C_IN), F32),
            jax.ShapeDtypeStruct(shape, BF16),
            jax.ShapeDtypeStruct((2, C_MID), F32),
        ],
        [
            pltpu.VMEM((2048, 2 * C_MID), BF16),
            pltpu.VMEM((MEL + 2, half, 512), BF16),
            pltpu.VMEM((1024, 512), F32),
            pltpu.VMEM((pairs, 2 * half, LANES), F32),
        ],
        flops=2 * MEL * half * (1024 + 1024) * 256,
        moved=20 * 2**20,
    )(lift, pre_one, sums_one, back_stats, vec, masks, k1, taps_x, token)


def finish_body(meta, got_one, got_two, back_one_sums, back_two_sums,
                own_one, own_two, ga, sa, gb, sb):
    own_one[...] = jnp.sum(got_one[...].astype(F32), axis=0)[:, 0 : own_one.shape[1]]
    own_two[...] = jnp.sum(got_two[...].astype(F32), axis=0)[:, 0 : own_two.shape[1]]
    share = ga.shape[1]
    lane = lax.broadcasted_iota(jnp.int32, (share, C_MID), 1)
    row = lax.broadcasted_iota(jnp.int32, (share, C_MID), 0)
    chosen = lane == meta[2] * share + row
    first = lax.broadcasted_iota(jnp.int32, (share, share), 0)
    second = lax.broadcasted_iota(jnp.int32, (share, share), 1)
    for out, sums, k in (
        (ga, back_one_sums, 1), (sa, back_one_sums, 0), (gb, back_two_sums, 1), (sb, back_two_sums, 0)
    ):
        wide = jnp.broadcast_to(sums[k : k + 1], (share, C_MID))
        column = jnp.sum(jnp.where(chosen, wide, 0.0), axis=1, keepdims=True)
        spread = jnp.broadcast_to(column, (share, share))
        out[...] = jnp.sum(jnp.where(first == second, spread, 0.0), axis=0, keepdims=True)


def finish(meta, got_one, got_two, back_one_sums, back_two_sums, rows_one, rows_two):
    share = got_one.shape[1]
    shapes = [(share, rows_one), (share, rows_two)] + [(1, share)] * 4
    return call(
        finish_body,
        (1,),
        [
            SMEM,
            whole(got_one.shape),
            whole(got_two.shape),
            whole(back_one_sums.shape),
            whole(back_two_sums.shape),
        ],
        [whole(s) for s in shapes],
        [jax.ShapeDtypeStruct(s, F32) for s in shapes],
        [],
    )(meta, got_one, got_two, back_one_sums, back_two_sums)


def exchange(blocks):
    return lax.all_to_all(blocks, AXES, 0, 0, tiled=True)


def shards(
    features, clip_starts, kernel_one, kernel_two, gain_one, shift_one, gain_two, shift_two, cotangent
):
    frames = features.shape[0]
    copies = lax.axis_size(AXES)
    row_count = lax.axis_size("row")
    count = float(frames * MEL * copies)
    meta = jnp.stack(
        [lax.axis_index(AXES) * frames, jnp.int32(frames * copies), lax.axis_index("grp")]
    ).astype(jnp.int32)
    rows_one, rows_two = kernel_one.shape[0], kernel_two.shape[0]
    share = kernel_one.shape[1]
    vectors = [v.reshape(1, share) for v in (gain_one, shift_one, gain_two, shift_two)]
    w1, w2, masks, up, down = setup(
        meta, kernel_one.T, kernel_two.T, vectors, clip_starts.reshape(1, -1), features, cotangent, copies
    )
    ends = copies - 1
    up = lax.ppermute(up, AXES, [(i, i + 1) for i in range(ends)])
    down = lax.ppermute(down, AXES, [(i + 1, i) for i in range(ends)])
    w1 = exchange(w1)
    w2 = exchange(w2)
    pre_one, stats, taps_x, k1, vec = conv_one(features, up, down, masks, w1, row_count, copies)
    stats = exchange(stats)
    pre_two, stats, taps_a, k2, sums_one = conv_two(
        pre_one, stats, vec, masks, w2, row_count, count
    )
    stats = exchange(stats)
    block_out, lift_two, stats, sums_two = norm_two(
        pre_two, stats, vec, cotangent, up, down, count
    )
    stats = exchange(stats)
    grad_two, lift_one, stats, back_two_sums = back_two(
        lift_two, pre_two, sums_two, stats, vec, masks, k2, pre_one, sums_one, count
    )
    stats = exchange(stats)
    blocks_two, token = kernel_two_grad(taps_a, grad_two, copies, share, rows_two)
    blocks_two = exchange(blocks_two)
    grad_features, blocks_one, back_one_sums = back_one(
        lift_one, pre_one, sums_one, stats, vec, masks, k1, taps_x, token, share, rows_one, count
    )
    blocks_one = exchange(blocks_one)
    own_one, own_two, ga, sa, gb, sb = finish(
        meta, blocks_one, blocks_two, back_one_sums, back_two_sums, rows_one, rows_two
    )
    return (
        block_out,
        grad_features,
        own_one.T,
        own_two.T,
        ga.reshape(share),
        sa.reshape(share),
        gb.reshape(share),
        sb.reshape(share),
    )


def solution(mesh):
    placed = (
        P(AXES, None), P(), P("row", "grp"), P("row", "grp"),
        P("grp"), P("grp"), P("grp"), P("grp"), P(AXES, None),
    )
    return jax.shard_map(
        shards,
        mesh=mesh,
        in_specs=placed,
        out_specs=(
            P(AXES, None), P(AXES, None), P("row", "grp"), P("row", "grp"),
            P("grp"), P("grp"), P("grp"), P("grp"),
        ),
        check_vma=False,
    )
```

```python
import jax
import jax.numpy as jnp
from jax import lax
from jax.experimental import pallas as pl
from jax.experimental.pallas import tpu as pltpu
from jax.sharding import PartitionSpec as P

MEL = 32
C_IN = 64
C_MID = 128
EPS = 1e-05
AXES = ("grp", "row")
LANES = 128
TAIL = 16
WIDE = 4 * LANES
BOTH = 2 * C_MID
F32 = jnp.float32
BF16 = jnp.bfloat16
TILE = 16
MIB = 2**20

VMEM = pl.BlockSpec(memory_space=pltpu.VMEM)
ANY = pl.BlockSpec(memory_space=pl.ANY)


def like(shape, dtype):
    return jax.ShapeDtypeStruct(shape, dtype)


def call(body, args, outs, scratch=(), limit=8, flops=0, moved=0, in_specs=None, out_specs=None, **more):
    return pl.pallas_call(
        body,
        in_specs=in_specs or [VMEM] * len(args),
        out_specs=out_specs or [VMEM] * len(outs),
        out_shape=outs,
        scratch_shapes=list(scratch),
        compiler_params=pltpu.CompilerParams(vmem_limit_bytes=limit * MIB),
        cost_estimate=pl.CostEstimate(flops=flops, bytes_accessed=moved, transcendentals=0),
        **more,
    )(*args)


def padded(size):
    return -(-size // LANES) * LANES


def partial_sum(values):
    return jnp.sum(values.reshape(-1, 8, values.shape[-1]), axis=0)


def fold(values):
    total = jnp.sum(values, axis=0, keepdims=True)
    return total[:, :C_MID] + total[:, C_MID:]


def spread(first, second, out):
    sums = jnp.concatenate([first, second], axis=0)
    out[...] = jnp.broadcast_to(sums[None], out.shape)


def twice(row):
    return jnp.concatenate([row, row], axis=1)


def tiles(rows):
    return range(0, rows, TILE)


def emit_taps(taps, slot, masks, evens, odds, tile_of):
    rows = masks.shape[1]
    kept = taps.shape[1]
    for r in tiles(rows):
        even, odd = tile_of(r)
        evens[r : r + TILE] = even
        odds[8 + r : 8 + r + TILE] = odd
        if r == 0:
            evens[rows : rows + 1] = even[0:1]
        if r + TILE == rows:
            odds[7:8] = odd[TILE - 1 : TILE]
        if r < kept:
            taps[slot, r : r + TILE, 128:256] = even.astype(BF16)
            taps[slot, r : r + TILE, 256:384] = odd.astype(BF16)
    for r in tiles(kept):
        span = slice(r, r + TILE)
        before = odds[7 + r : 7 + r + TILE] * masks[0, span]
        after = evens[1 + r : 1 + r + TILE] * masks[1, span]
        taps[slot, span, 0:128] = before.astype(BF16)
        taps[slot, span, 384:512] = after.astype(BF16)


def halves_of(value):
    return value[:, :C_MID], value[:, C_MID:]


def add_sums(acc, first, second):
    acc[0] += first
    acc[1] += second


def side_scratch(rows):
    return [pltpu.VMEM((2, rows + 8, LANES), F32), pltpu.VMEM((2, rows + 8, LANES), F32)]


def stats_of(pre, mels, half, acc):
    first = jnp.zeros((8, BOTH), F32)
    second = jnp.zeros((8, BOTH), F32)
    for m in mels:
        for r in range(0, half, 8):
            value = pre[m, r : r + 8]
            first += value
            second += value * value
    add_sums(acc, first, second)


def stat_sums(stats):
    return jnp.sum(stats[...], axis=0)


def norm_terms(sums, count):
    mean = sums[0:1] / count
    rstd = lax.rsqrt(sums[1:2] / count - mean * mean + EPS)
    return mean, rstd


def clear_ends(taps):
    blank = jnp.zeros(taps.shape[1:], BF16)
    taps[0] = blank
    taps[taps.shape[0] - 1] = blank


def setup_body(k1, k2, ga, sa, gb, sb, clips, x_head, x_tail, c_head, c_tail, w_out, masks, up, down):
    share = k1.shape[0]
    copies = w_out.shape[0]
    w_out[...] = jnp.zeros(w_out.shape, BF16)
    first = lax.broadcasted_iota(jnp.int32, (share, share), 0)
    second = lax.broadcasted_iota(jnp.int32, (share, share), 1)
    columns = [k1[...].astype(F32), k2[...].astype(F32)]
    for vector in (ga, sa, gb, sb):
        wide = jnp.broadcast_to(vector[...].astype(F32), (share, share))
        columns.append(jnp.sum(jnp.where(first == second, wide, 0.0), axis=1, keepdims=True))
    chunk = jnp.concatenate(columns, axis=1).astype(BF16)
    for i in range(copies):
        w_out[i, :, 0 : chunk.shape[1]] = chunk
    rows = masks.shape[1]
    half = rows - TAIL
    frames = 2 * half
    start = lax.axis_index(AXES) * frames
    place = lax.broadcasted_iota(jnp.int32, (rows, clips.shape[1]), 0)
    pair = jnp.where(place >= half + TAIL // 2, place - rows, place)
    frame = start + 2 * pair
    starts = jnp.broadcast_to(clips[...], (rows, clips.shape[1]))
    for slot, shift in ((0, 0), (1, 2)):
        hit = (frame + shift == starts) | (frame + shift >= frames * copies)
        begins = jnp.max(jnp.where(hit, 1.0, 0.0), axis=1, keepdims=True)
        masks[slot] = jnp.broadcast_to(1.0 - begins, (rows, LANES))
    row = lax.broadcasted_iota(jnp.int32, (8, x_head.shape[1]), 0)
    xt = x_tail[...].astype(F32)
    ct = c_tail[...].astype(F32)
    up[...] = jnp.where(
        row < 4, pltpu.roll(xt[8:16], 4, 0), jnp.where(row == 4, ct[15:16], 0.0)
    ).astype(BF16)
    xh = x_head[...].astype(F32)
    ch = c_head[...].astype(F32)
    down[...] = jnp.where(row < 4, xh[0:8], jnp.where(row == 4, ch[0:1], 0.0)).astype(BF16)


def setup(k1t, k2t, vectors, clips, features, cotangent, copies):
    frames, wide = features.shape
    halves = cotangent.shape[0]
    rows = frames // 2 + TAIL
    share = k1t.shape[0]
    w = (copies, share, padded(k1t.shape[1] + k2t.shape[1] + 4))
    whole = lambda shape: pl.BlockSpec(shape, lambda i: (0,) * len(shape))
    outs = [like(w, BF16), like((2, rows, LANES), F32), like((8, wide), BF16), like((8, wide), BF16)]
    return call(
        setup_body,
        (k1t, k2t, *vectors, clips, features, features, cotangent, cotangent),
        outs,
        limit=56,
        in_specs=[
            whole(k1t.shape),
            whole(k2t.shape),
            *[whole((1, share))] * 4,
            whole(clips.shape),
            pl.BlockSpec((16, wide), lambda i: (0, 0)),
            pl.BlockSpec((16, wide), lambda i: (frames // 16 - 1, 0)),
            pl.BlockSpec((16, wide), lambda i: (0, 0)),
            pl.BlockSpec((16, wide), lambda i: (halves // 16 - 1, 0)),
        ],
        out_specs=[whole(o.shape) for o in outs],
        grid=(1,),
    )


def taps_one_body(x, up, down, masks, taps, frames):
    rows = masks.shape[1]
    half = rows - TAIL
    clear_ends(taps)
    row = lax.broadcasted_iota(jnp.int32, (8, LANES), 0)
    lead = 24
    own = 2 * half
    for b in range(2):
        frames[b, 0:16] = jnp.zeros((16, LANES), F32)
        frames[b, lead + own + 8 : lead + own + 24] = jnp.zeros((16, LANES), F32)

    def pair(j, b):
        lanes = pl.ds(pl.multiple_of(j * LANES, LANES), LANES)
        u = up[:, lanes].astype(F32)
        d = down[:, lanes].astype(F32)
        frames[b, lead - 8 : lead] = jnp.where(row >= 4, pltpu.roll(u, 4, 0), 0.0)
        frames[b, lead + own : lead + own + 8] = jnp.where(row < 4, d, 0.0)
        for r in tiles(own):
            frames[b, lead + r : lead + r + TILE] = x[r : r + TILE, lanes].astype(F32)

        def pick(first, count, shift):
            return frames[b, pl.ds(lead + 2 * first + shift, count, stride=2), :]

        for r in tiles(rows):
            parts = []
            for shift in (-1, 0, 1, 2):
                if r < half:
                    parts.append(pick(r, TILE, shift))
                else:
                    parts.append(
                        jnp.concatenate([pick(half, 8, shift), pick(-8, 8, shift)], axis=0)
                    )
            span = slice(r, r + TILE)
            parts[0] = parts[0] * masks[0, span]
            parts[3] = parts[3] * masks[1, span]
            taps[1 + j, span, :] = jnp.concatenate(parts, axis=1).astype(BF16)

    def two_pairs(i, carry):
        pair(2 * i, 0)
        pair(2 * i + 1, 1)
        return carry

    lax.fori_loop(0, MEL // 4, two_pairs, 0)


def taps_one(features, up, down, masks):
    rows = masks.shape[1]
    return call(
        taps_one_body,
        (features, up, down, masks),
        [like((MEL // 2 + 2, rows, WIDE), BF16)],
        [pltpu.VMEM((2, features.shape[0] + 48, LANES), F32)],
        flops=10**9,
        moved=8 * MIB,
    )[0]


def conv_one_body(row_count, taps, wg, pre, stats, k1_out, k2_out, vec_out, kf, w_even, w_odd, acc):
    rows = taps.shape[1]
    half = rows - TAIL
    pairs = 4
    rows_one = 9 * C_IN // row_count
    rows_two = 9 * C_MID // row_count
    grps = wg.shape[0] // row_count
    for r in range(row_count):
        shard = [wg[g * row_count + r] for g in range(grps)]
        shard = jnp.concatenate(shard, axis=0).astype(F32).T
        kf[rows_one * r : rows_one * (r + 1)] = shard[0:rows_one]
        at = 9 * C_IN + rows_two * r
        kf[at : at + rows_two] = shard[rows_one : rows_one + rows_two]
        if r == 0:
            vec_out[...] = shard[rows_one + rows_two : rows_one + rows_two + 4]
    k1_out[...] = kf[0 : 9 * C_IN].astype(BF16)
    k2_out[...] = kf[9 * C_IN :].astype(BF16)
    w_even[...] = jnp.zeros(w_even.shape, BF16)
    w_odd[...] = jnp.zeros(w_odd.shape, BF16)
    placed = (
        (w_even, 0, 1, 0), (w_even, 1, 0, 1), (w_even, 1, 1, 2),
        (w_odd, 0, 0, 0), (w_odd, 0, 1, 1), (w_odd, 1, 0, 2),
    )
    for matrix, piece, side, d in placed:
        for q in range(4):
            for p in range(2):
                t = q - p
                if 0 <= t < 3:
                    at = piece * WIDE + q * 128 + side * 64
                    start = (3 * t + d) * C_IN
                    matrix[at : at + 64, p * 128 : p * 128 + 128] = k1_out[start : start + C_IN]
    acc[...] = jnp.zeros(acc.shape, F32)
    for c in range(MEL // 2 // pairs):
        left, mid, right = [
            taps[c * pairs + k : c * pairs + k + pairs].reshape(pairs * rows, WIDE) for k in range(3)
        ]
        for parity, lhs, matrix in (
            (0, jnp.concatenate([left, mid], axis=1), w_even),
            (1, jnp.concatenate([mid, right], axis=1), w_odd),
        ):
            out = jnp.dot(lhs, matrix[...], preferred_element_type=F32)
            out = out.reshape(pairs, rows, BOTH)
            mels = [2 * (c * pairs + q) + parity for q in range(pairs)]
            for q in range(pairs):
                pre[mels[q]] = out[q]
            stats_of(pre, mels, half, acc)
    spread(fold(acc[0]), fold(acc[1]), stats)


def conv_one(taps, wg, row_count):
    rows = taps.shape[1]
    copies = wg.shape[0]
    return call(
        lambda *refs: conv_one_body(row_count, *refs),
        (taps, wg),
        [
            like((MEL, rows, BOTH), F32),
            like((copies, 2, C_MID), F32),
            like((9 * C_IN, C_MID), BF16),
            like((9 * C_MID, C_MID), BF16),
            like((4, C_MID), F32),
        ],
        [
            pltpu.VMEM((9 * (C_IN + C_MID), C_MID), F32),
            pltpu.VMEM((2 * WIDE, BOTH), BF16),
            pltpu.VMEM((2 * WIDE, BOTH), BF16),
            pltpu.VMEM((2, 8, BOTH), F32),
        ],
        flops=2 * 2 * MEL * rows * WIDE * BOTH,
        moved=16 * MIB,
    )


def weight_two_body(k2, token, weight):
    weight[...] = jnp.zeros(weight.shape, BF16)
    for d in range(3):
        for q in range(4):
            for p in range(2):
                t = q - p
                if 0 <= t < 3:
                    at = d * WIDE + q * 128
                    start = (3 * t + d) * C_MID
                    weight[at : at + 128, p * 128 : p * 128 + 128] = k2[start : start + C_MID]


def weight_two_back_body(k2, token, weight):
    weight[...] = jnp.zeros(weight.shape, BF16)
    for t in range(3):
        for d in range(3):
            start = (3 * t + d) * C_MID
            turned = k2[start : start + C_MID].astype(F32).T.astype(BF16)
            for p in range(2):
                at = (2 - d) * WIDE + (2 - t + p) * 128
                weight[at : at + 128, p * 128 : p * 128 + 128] = turned


def weight_one_back_body(k1, token, weight):
    weight[...] = jnp.zeros(weight.shape, BF16)
    for t in range(3):
        for d in range(3):
            start = (3 * t + d) * C_IN
            turned = k1[start : start + C_IN].astype(F32).T.astype(BF16)
            for mo in (1, 2):
                for p in range(2):
                    at = (mo - d + 1) * WIDE + (2 - t + p) * 128
                    to = p * 128 + (mo - 1) * 64
                    weight[at : at + 128, to : to + 64] = turned


def build(body, kernel, token, taps):
    return call(
        body,
        (kernel, token),
        [like((taps * WIDE, BOTH), BF16)],
        limit=4,
        flops=10**8,
        moved=2 * MIB,
        in_specs=[VMEM, ANY],
    )[0]


def conv_two_body(count, pre_one, stats_one, vec, masks, weight, pre, stats, taps, sums_out, acc, evens, odds):
    rows = masks.shape[1]
    half = rows - TAIL
    mels = 4
    sums = stat_sums(stats_one)
    sums_out[...] = sums
    mean, rstd = norm_terms(sums, count)
    scale = 0.5 * vec[0:1] * rstd
    shift = twice(0.5 * vec[1:2] - mean * scale)
    scale = twice(scale)
    clear_ends(taps)
    acc[...] = jnp.zeros(acc.shape, F32)

    def activate(m):
        def tile(r):
            h = pre_one[m, r : r + TILE] * scale + shift
            return halves_of(h + h * jnp.tanh(h))

        emit_taps(taps, 1 + m, masks, evens.at[m % 2], odds.at[m % 2], tile)

    def convolve(c):
        lhs = [taps[c * mels + d : (c + 1) * mels + d].reshape(mels * rows, WIDE) for d in range(3)]
        out = jnp.dot(jnp.concatenate(lhs, axis=1), weight[...], preferred_element_type=F32)
        pre[c * mels : (c + 1) * mels] = out.reshape(mels, rows, BOTH)
        stats_of(pre, range(c * mels, (c + 1) * mels), half, acc)

    for m in range(MEL):
        activate(m)
        if m >= mels and m % mels == 0:
            convolve(m // mels - 1)
    convolve(MEL // mels - 1)
    spread(fold(acc[0]), fold(acc[1]), stats)


def conv_two(pre_one, stats_one, vec, masks, weight, count):
    copies = stats_one.shape[0]
    rows = masks.shape[1]
    return call(
        lambda *refs: conv_two_body(count, *refs),
        (pre_one, stats_one, vec, masks, weight),
        [
            like((MEL, rows, BOTH), F32),
            like((copies, 2, C_MID), F32),
            like((MEL + 2, rows, WIDE), BF16),
            like((2, C_MID), F32),
        ],
        [pltpu.VMEM((2, 8, BOTH), F32), *side_scratch(rows)],
        flops=2 * MEL * rows * 3 * WIDE * BOTH,
        moved=20 * MIB,
    )


def norm_two_body(count, pre, stats_two, vec, cot, up, down, pooled, lift, back_stats, sums_out, acc):
    half = cot.shape[0]
    sums = stat_sums(stats_two)
    sums_out[...] = sums
    mean, rstd = norm_terms(sums, count)
    scale = 0.5 * vec[2:3] * rstd
    shift = 0.5 * vec[3:4] - mean * scale
    norm_shift = -mean * rstd
    acc[...] = jnp.zeros(acc.shape, F32)
    row = lax.broadcasted_iota(jnp.int32, (TAIL, LANES), 0)

    def pair(j, carry):
        lanes = pl.ds(pl.multiple_of(j * LANES, LANES), LANES)
        u = up[:, lanes].astype(F32)
        d = down[:, lanes].astype(F32)
        first = jnp.zeros((8, LANES), F32)
        second = jnp.zeros((8, LANES), F32)
        for r in tiles(half + TAIL):
            span = slice(r, r + TILE)
            if r < half:
                grad = cot[span, lanes].astype(F32) * 0.125
            else:
                grad = jnp.where(row == 0, d[4:5], jnp.where(row == TAIL - 1, u[4:5], 0.0)) * 0.125
            total = jnp.zeros((TILE, LANES), F32)
            for m in (2 * j, 2 * j + 1):
                for p in range(2):
                    side = slice(p * C_MID, (p + 1) * C_MID)
                    value = pre[m, span, side]
                    h = value * scale + shift
                    th = jnp.tanh(h)
                    one = 1.0 + th
                    gl = grad * (one * (1.0 + (h - h * th)))
                    lift[m, span, side] = gl
                    if r < half:
                        total += h * one
                        first += partial_sum(gl)
                        second += partial_sum(gl * (value * rstd + norm_shift))
            if r < half:
                pooled[span, lanes] = (total * 0.25).astype(BF16)
        add_sums(acc, first, second)
        return carry

    lax.fori_loop(0, MEL // 2, pair, 0)
    first, second = [jnp.sum(acc[k], axis=0, keepdims=True) for k in range(2)]
    spread(first, second, back_stats)


def norm_two(pre, stats_two, vec, cot, up, down, count):
    copies = stats_two.shape[0]
    half, wide = cot.shape
    return call(
        lambda *refs: norm_two_body(count, *refs),
        (pre, stats_two, vec, cot, up, down),
        [
            like((half, wide), BF16),
            like((MEL, half + TAIL, BOTH), F32),
            like((copies, 2, C_MID), F32),
            like((2, C_MID), F32),
        ],
        [pltpu.VMEM((2, 8, LANES), F32)],
        flops=10**9,
        moved=16 * MIB,
    )


def grad_terms(sums, back, gain, count):
    mean, rstd = norm_terms(sums, count)
    a = gain * rstd
    b = -a * rstd * (back[1:2] / count)
    c = -a * (back[0:1] / count) - b * mean
    return twice(a), twice(b), twice(c)


def back_two_body(count, lift, pre_two, sums_two, back_stats, vec, masks, weight, pre_one, sums_one,
                  lift_one, taps, back_out, sums_out, acc, evens, odds):
    rows = masks.shape[1]
    half = rows - TAIL
    mels = 4
    back = stat_sums(back_stats)
    sums_out[...] = back
    a, b, c = grad_terms(sums_two[...], back, vec[2:3], count)
    mean, rstd = norm_terms(sums_one[...], count)
    scale = 0.5 * vec[0:1] * rstd
    shift = twice(0.5 * vec[1:2] - mean * scale)
    scale = twice(scale)
    norm_shift = twice(-mean * rstd)
    rstd = twice(rstd)
    clear_ends(taps)
    acc[...] = jnp.zeros(acc.shape, F32)

    def lower(m):
        def tile(r):
            span = slice(r, r + TILE)
            return halves_of(lift[m, span] * a + (pre_two[m, span] * b + c))

        emit_taps(taps, 1 + m, masks, evens.at[m % 2], odds.at[m % 2], tile)

    def convolve(k):
        lhs = [taps[k * mels + d : (k + 1) * mels + d].reshape(mels * rows, WIDE) for d in range(3)]
        out = jnp.dot(jnp.concatenate(lhs, axis=1), weight[...], preferred_element_type=F32)
        lift_one[k * mels : (k + 1) * mels] = out.reshape(mels, rows, BOTH)
        first = jnp.zeros((8, BOTH), F32)
        second = jnp.zeros((8, BOTH), F32)
        for m in range(k * mels, (k + 1) * mels):
            for r in range(0, rows, 8):
                span = slice(r, r + 8)
                value = pre_one[m, span]
                h = value * scale + shift
                th = jnp.tanh(h)
                gl = lift_one[m, span] * (0.5 * (1.0 + th) * (1.0 + (h - h * th)))
                lift_one[m, span] = gl
                if r < half:
                    first += gl
                    second += gl * (value * rstd + norm_shift)
        add_sums(acc, first, second)

    for m in range(MEL):
        lower(m)
        if m >= mels and m % mels == 0:
            convolve(m // mels - 1)
    convolve(MEL // mels - 1)
    spread(fold(acc[0]), fold(acc[1]), back_out)


def back_two(lift, pre_two, sums_two, back_stats, vec, masks, weight, pre_one, sums_one, count):
    copies = back_stats.shape[0]
    rows = masks.shape[1]
    return call(
        lambda *refs: back_two_body(count, *refs),
        (lift, pre_two, sums_two, back_stats, vec, masks, weight, pre_one, sums_one),
        [
            like((MEL, rows, BOTH), F32),
            like((MEL + 2, rows, WIDE), BF16),
            like((copies, 2, C_MID), F32),
            like((2, C_MID), F32),
        ],
        [pltpu.VMEM((2, 8, BOTH), F32), *side_scratch(rows)],
        flops=2 * MEL * rows * 3 * WIDE * BOTH,
        moved=32 * MIB,
        input_output_aliases={0: 0},
    )


def dot_rows(first, second):
    return lax.dot_general(
        first, second, (((0,), (0,)), ((), ())), preferred_element_type=F32
    )


def scatter_blocks(out, by_channel, rows_in):
    copies, share, wide = out.shape
    grps = by_channel.shape[0] // share
    row_count = copies // grps
    size = rows_in // row_count
    turned = by_channel.T
    for r in range(row_count):
        part = turned[size * r : size * (r + 1)]
        part = jnp.concatenate([part, jnp.zeros((wide - size, part.shape[1]), F32)], axis=0)
        back = part.T.astype(BF16)
        for g in range(grps):
            out[g * row_count + r] = back[share * g : share * (g + 1)]


def kernel_two_body(taps, grads, out, token, acc):
    mels = 8
    half = taps.shape[1] - TAIL
    token[...] = jnp.zeros(token.shape, F32)
    for c in range(MEL // mels):
        chosen = grads[1 + c * mels : 1 + (c + 1) * mels, 0:half, 128:384].reshape(mels * half, BOTH)
        near = [
            taps[c * mels + d : (c + 1) * mels + d, 0:half].reshape(mels * half, WIDE) for d in range(3)
        ]
        total = dot_rows(chosen, jnp.concatenate(near, axis=1))
        if c == 0:
            acc[...] = total
        else:
            acc[...] += total
    pieces = []
    for t in range(3):
        for d in range(3):
            at = d * WIDE + t * 128
            pieces.append(acc[0:C_MID, at : at + 128] + acc[C_MID:BOTH, at + 128 : at + 256])
    scatter_blocks(out, jnp.concatenate(pieces, axis=1), 9 * C_MID)


def kernel_two_grad(taps, grads, copies, share, rows_two):
    half = taps.shape[1] - TAIL
    return call(
        kernel_two_body,
        (taps, grads),
        [like((copies, share, padded(rows_two)), BF16), like((8, LANES), F32)],
        [pltpu.VMEM((BOTH, 3 * WIDE), F32)],
        limit=10,
        flops=2 * MEL * half * 3 * WIDE * BOTH,
        moved=11 * MIB,
    )


def kernel_one_body(count, lift, pre_one, sums_one, back_stats, vec, masks, taps_x, token,
                    taps, blocks, sums_out, acc, evens, odds):
    pairs = 4
    half = masks.shape[1] - TAIL
    back = stat_sums(back_stats)
    sums_out[...] = back
    a, b, c = grad_terms(sums_one[...], back, vec[0:1], count)
    clear_ends(taps)

    def lower(m):
        def tile(r):
            span = slice(r, r + TILE)
            return halves_of(lift[m, span] * a + (pre_one[m, span] * b + c))

        emit_taps(taps, 1 + m, masks, evens.at[m % 2], odds.at[m % 2], tile)

    for k in range(MEL // 2 // pairs):
        for m in range(2 * pairs):
            lower(2 * pairs * k + m)
        near = [
            taps_x[k * pairs + i : (k + 1) * pairs + i, 0:half].reshape(pairs * half, WIDE)
            for i in range(3)
        ]
        for parity in range(2):
            chosen = [
                taps[1 + 2 * (k * pairs + q) + parity, :, 128:384] for q in range(pairs)
            ]
            total = dot_rows(
                jnp.concatenate(chosen, axis=0),
                jnp.concatenate(near[parity : parity + 2], axis=1),
            )
            if k == 0:
                acc[parity] = total
            else:
                acc[parity] += total
    pieces = []
    for t in range(3):
        for d in range(3):
            total = jnp.zeros((C_MID, C_IN), F32)
            for parity in range(2):
                place = 2 * (1 - parity) + parity + d - 1
                for p in range(2):
                    at = (place // 2) * WIDE + (t + p) * 128 + (place % 2) * 64
                    total += acc[parity, p * 128 : p * 128 + 128, at : at + 64]
            pieces.append(total)
    scatter_blocks(blocks, jnp.concatenate(pieces, axis=1), 9 * C_IN)


def kernel_one_grad(lift, pre_one, sums_one, back_stats, vec, masks, taps_x, token, share, rows_one, count):
    copies = back_stats.shape[0]
    half = masks.shape[1] - TAIL
    return call(
        lambda *refs: kernel_one_body(count, *refs),
        (lift, pre_one, sums_one, back_stats, vec, masks, taps_x, token),
        [
            like((MEL + 2, half, WIDE), BF16),
            like((copies, share, padded(rows_one)), BF16),
            like((2, C_MID), F32),
        ],
        [pltpu.VMEM((2, BOTH, 2 * WIDE), F32), *side_scratch(half + TAIL)],
        limit=10,
        flops=2 * MEL * half * 2 * WIDE * BOTH,
        moved=20 * MIB,
        in_specs=[VMEM] * 7 + [ANY],
    )


def features_body(taps, weight, token, out, woven, sems):
    pairs = 4
    half = taps.shape[1]
    copies = []
    for k in range(MEL // 2 // pairs):
        near = []
        for q in range(pairs):
            j = k * pairs + q
            near.append(jnp.concatenate([taps[2 * j + i] for i in range(4)], axis=1))
        part = jnp.dot(jnp.concatenate(near, axis=0), weight[...], preferred_element_type=F32)
        for q in range(pairs):
            j = k * pairs + q
            rows = slice(q * half, (q + 1) * half)
            woven[j, pl.ds(0, half, stride=2), :] = part[rows, 0:128]
            woven[j, pl.ds(1, half, stride=2), :] = part[rows, 128:256]
            copy = pltpu.make_async_copy(
                woven.at[j], out.at[:, pl.ds(j * LANES, LANES)], sems.at[j]
            )
            copy.start()
            copies.append(copy)
    for copy in copies:
        copy.wait()


def features_grad(taps, weight, token):
    half = taps.shape[1]
    return call(
        features_body,
        (taps, weight, token),
        [like((2 * half, MEL * C_IN), F32)],
        [pltpu.VMEM((MEL // 2, 2 * half, LANES), F32), pltpu.SemaphoreType.DMA((MEL // 2,))],
        limit=10,
        flops=MEL * half * 4 * WIDE * BOTH,
        moved=20 * MIB,
        in_specs=[VMEM, VMEM, ANY],
        out_specs=[ANY],
    )[0]


def finish_two_body(got, waiting, own, passed, token):
    own[...] = jnp.sum(got[...].astype(F32), axis=0)[:, 0 : own.shape[1]]
    token[...] = jnp.zeros(token.shape, F32)


def finish_two(got, waiting, rows_two):
    return call(
        finish_two_body,
        (got, waiting),
        [like((got.shape[1], rows_two), F32), like(waiting.shape, BF16), like((8, LANES), F32)],
        in_specs=[VMEM, ANY],
        out_specs=[VMEM, ANY, VMEM],
        input_output_aliases={1: 1},
    )


def finish_one_body(got, back_one_sums, back_two_sums, own, ga, sa, gb, sb):
    own[...] = jnp.sum(got[...].astype(F32), axis=0)[:, 0 : own.shape[1]]
    share = ga.shape[1]
    lane = lax.broadcasted_iota(jnp.int32, (share, C_MID), 1)
    row = lax.broadcasted_iota(jnp.int32, (share, C_MID), 0)
    chosen = lane == lax.axis_index("grp") * share + row
    first = lax.broadcasted_iota(jnp.int32, (share, share), 0)
    second = lax.broadcasted_iota(jnp.int32, (share, share), 1)
    for out, sums, k in (
        (ga, back_one_sums, 1), (sa, back_one_sums, 0), (gb, back_two_sums, 1), (sb, back_two_sums, 0)
    ):
        wide = jnp.broadcast_to(sums[k : k + 1], (share, C_MID))
        column = jnp.sum(jnp.where(chosen, wide, 0.0), axis=1, keepdims=True)
        wide = jnp.broadcast_to(column, (share, share))
        out[...] = jnp.sum(jnp.where(first == second, wide, 0.0), axis=0, keepdims=True)


def finish_one(got, back_one_sums, back_two_sums, rows_one):
    share = got.shape[1]
    shapes = [(share, rows_one)] + [(1, share)] * 4
    return call(
        finish_one_body,
        (got, back_one_sums, back_two_sums),
        [like(s, F32) for s in shapes],
    )


def exchange(blocks):
    return lax.all_to_all(blocks, AXES, 0, 0, tiled=True)


def shards(
    features, clip_starts, kernel_one, kernel_two, gain_one, shift_one, gain_two, shift_two, cotangent
):
    frames = features.shape[0]
    copies = lax.axis_size(AXES)
    row_count = lax.axis_size("row")
    count = float(frames * MEL * copies)
    rows_one, rows_two = kernel_one.shape[0], kernel_two.shape[0]
    share = kernel_one.shape[1]
    vectors = [v.reshape(1, share) for v in (gain_one, shift_one, gain_two, shift_two)]
    weights, masks, up, down = setup(
        kernel_one.T, kernel_two.T, vectors, clip_starts.reshape(1, -1), features, cotangent, copies
    )
    ends = copies - 1
    up = lax.ppermute(up, AXES, [(i, i + 1) for i in range(ends)])
    down = lax.ppermute(down, AXES, [(i + 1, i) for i in range(ends)])
    weights = exchange(weights)
    taps_x = taps_one(features, up, down, masks)
    pre_one, stats, k1, k2, vec = conv_one(taps_x, weights, row_count)
    stats = exchange(stats)
    weight = build(weight_two_body, k2, vec, 3)
    pre_two, stats, taps_a, sums_one = conv_two(pre_one, stats, vec, masks, weight, count)
    stats = exchange(stats)
    weight = build(weight_two_back_body, k2, sums_one, 3)
    block_out, lift, stats, sums_two = norm_two(pre_two, stats, vec, cotangent, up, down, count)
    stats = exchange(stats)
    weight_x = build(weight_one_back_body, k1, sums_two, 4)
    lift, taps_g, stats, back_two_sums = back_two(
        lift, pre_two, sums_two, stats, vec, masks, weight, pre_one, sums_one, count
    )
    stats = exchange(stats)
    blocks_two, token = kernel_two_grad(taps_a, taps_g, copies, share, rows_two)
    blocks_two = exchange(blocks_two)
    taps_g, blocks_one, back_one_sums = kernel_one_grad(
        lift, pre_one, sums_one, stats, vec, masks, taps_x, token, share, rows_one, count
    )
    own_two, blocks_one, token = finish_two(blocks_two, blocks_one, rows_two)
    blocks_one = exchange(blocks_one)
    grad_features = features_grad(taps_g, weight_x, token)
    own_one, ga, sa, gb, sb = finish_one(blocks_one, back_one_sums, back_two_sums, rows_one)
    return (
        block_out,
        grad_features,
        own_one.T,
        own_two.T,
        ga.reshape(share),
        sa.reshape(share),
        gb.reshape(share),
        sb.reshape(share),
    )


def solution(mesh):
    placed = (
        P(AXES, None), P(), P("row", "grp"), P("row", "grp"),
        P("grp"), P("grp"), P("grp"), P("grp"), P(AXES, None),
    )
    return jax.shard_map(
        shards,
        mesh=mesh,
        in_specs=placed,
        out_specs=(
            P(AXES, None), P(AXES, None), P("row", "grp"), P("row", "grp"),
            P("grp"), P("grp"), P("grp"), P("grp"),
        ),
        check_vma=False,
    )
```

```python
import jax
import jax.numpy as jnp
from jax import lax
from jax.experimental import pallas as pl
from jax.experimental.pallas import tpu as pltpu
from jax.sharding import PartitionSpec as P

MEL = 32
C_IN = 64
C_MID = 128
EPS = 1e-05
AXES = ("grp", "row")
LANES = 128
TAIL = 16
WIDE = 4 * LANES
BOTH = 2 * C_MID
F32 = jnp.float32
BF16 = jnp.bfloat16
TILE = 16
MIB = 2**20

VMEM = pl.BlockSpec(memory_space=pltpu.VMEM)
ANY = pl.BlockSpec(memory_space=pl.ANY)


def like(shape, dtype):
    return jax.ShapeDtypeStruct(shape, dtype)


def call(body, args, outs, scratch=(), limit=14, flops=0, moved=0, in_specs=None, out_specs=None, **more):
    return pl.pallas_call(
        body,
        in_specs=in_specs or [VMEM] * len(args),
        out_specs=out_specs or [VMEM] * len(outs),
        out_shape=outs,
        scratch_shapes=list(scratch),
        compiler_params=pltpu.CompilerParams(vmem_limit_bytes=limit * MIB),
        cost_estimate=pl.CostEstimate(flops=flops, bytes_accessed=moved, transcendentals=0),
        **more,
    )(*args)


def padded(size):
    return -(-size // LANES) * LANES


def partial_sum(values):
    return jnp.sum(values.reshape(-1, 8, values.shape[-1]), axis=0)


def fold(values):
    total = jnp.sum(values, axis=0, keepdims=True)
    return total[:, :C_MID] + total[:, C_MID:]


def spread(first, second, out):
    sums = jnp.concatenate([first, second], axis=0)
    out[...] = jnp.broadcast_to(sums[None], out.shape)


def twice(row):
    return jnp.concatenate([row, row], axis=1)


def tiles(rows):
    return range(0, rows, TILE)


def emit_taps(taps, slot, masks, evens, odds, tile_of):
    rows = masks.shape[1]
    kept = taps.shape[1]
    for r in tiles(rows):
        even, odd = tile_of(r)
        evens[r : r + TILE] = even
        odds[8 + r : 8 + r + TILE] = odd
        if r == 0:
            evens[rows : rows + 1] = even[0:1]
        if r + TILE == rows:
            odds[7:8] = odd[TILE - 1 : TILE]
        if r < kept:
            taps[slot, r : r + TILE, 128:256] = even.astype(BF16)
            taps[slot, r : r + TILE, 256:384] = odd.astype(BF16)
    for r in tiles(kept):
        span = slice(r, r + TILE)
        before = odds[7 + r : 7 + r + TILE] * masks[0, span]
        after = evens[1 + r : 1 + r + TILE] * masks[1, span]
        taps[slot, span, 0:128] = before.astype(BF16)
        taps[slot, span, 384:512] = after.astype(BF16)


def halves_of(value):
    return value[:, :C_MID], value[:, C_MID:]


def add_sums(acc, first, second):
    acc[0] += first
    acc[1] += second


def side_scratch(rows):
    return [pltpu.VMEM((2, rows + 8, LANES), F32), pltpu.VMEM((2, rows + 8, LANES), F32)]


def stats_of(pre, mels, half, acc):
    first = jnp.zeros((8, BOTH), F32)
    second = jnp.zeros((8, BOTH), F32)
    for m in mels:
        for r in range(0, half, 8):
            value = pre[m, r : r + 8]
            first += value
            second += value * value
    add_sums(acc, first, second)


def stat_sums(stats):
    return jnp.sum(stats[...], axis=0)


def norm_terms(sums, count):
    mean = sums[0:1] / count
    rstd = lax.rsqrt(sums[1:2] / count - mean * mean + EPS)
    return mean, rstd


def dot_rows(first, second):
    return lax.dot_general(
        first, second, (((0,), (0,)), ((), ())), preferred_element_type=F32
    )


def ring_slot(taps, m):
    last = taps.shape[0] - 1
    return m % last if 0 <= m < MEL else last


def stack(taps, mels, rows, lanes=slice(None)):
    parts = [taps[ring_slot(taps, m), 0:rows, lanes] for m in mels]
    return jnp.concatenate(parts, axis=0)


def clear_ends(taps):
    blank = jnp.zeros(taps.shape[1:], BF16)
    taps[0] = blank
    taps[taps.shape[0] - 1] = blank


def setup_body(k1, k2, ga, sa, gb, sb, clips, x_head, x_tail, c_head, c_tail, w_out, masks, up, down):
    share = k1.shape[0]
    copies = w_out.shape[0]
    w_out[...] = jnp.zeros(w_out.shape, BF16)
    first = lax.broadcasted_iota(jnp.int32, (share, share), 0)
    second = lax.broadcasted_iota(jnp.int32, (share, share), 1)
    columns = [k1[...].astype(F32), k2[...].astype(F32)]
    for vector in (ga, sa, gb, sb):
        wide = jnp.broadcast_to(vector[...].astype(F32), (share, share))
        columns.append(jnp.sum(jnp.where(first == second, wide, 0.0), axis=1, keepdims=True))
    chunk = jnp.concatenate(columns, axis=1).astype(BF16)
    for i in range(copies):
        w_out[i, :, 0 : chunk.shape[1]] = chunk
    rows = masks.shape[1]
    half = rows - TAIL
    frames = 2 * half
    start = lax.axis_index(AXES) * frames
    place = lax.broadcasted_iota(jnp.int32, (rows, clips.shape[1]), 0)
    pair = jnp.where(place >= half + TAIL // 2, place - rows, place)
    frame = start + 2 * pair
    starts = jnp.broadcast_to(clips[...], (rows, clips.shape[1]))
    for slot, shift in ((0, 0), (1, 2)):
        hit = (frame + shift == starts) | (frame + shift >= frames * copies)
        begins = jnp.max(jnp.where(hit, 1.0, 0.0), axis=1, keepdims=True)
        masks[slot] = jnp.broadcast_to(1.0 - begins, (rows, LANES))
    row = lax.broadcasted_iota(jnp.int32, (8, x_head.shape[1]), 0)
    xt = x_tail[...].astype(F32)
    ct = c_tail[...].astype(F32)
    up[...] = jnp.where(
        row < 4, pltpu.roll(xt[8:16], 4, 0), jnp.where(row == 4, ct[15:16], 0.0)
    ).astype(BF16)
    xh = x_head[...].astype(F32)
    ch = c_head[...].astype(F32)
    down[...] = jnp.where(row < 4, xh[0:8], jnp.where(row == 4, ch[0:1], 0.0)).astype(BF16)


def setup(k1t, k2t, vectors, clips, features, cotangent, copies):
    frames, wide = features.shape
    halves = cotangent.shape[0]
    rows = frames // 2 + TAIL
    share = k1t.shape[0]
    w = (copies, share, padded(k1t.shape[1] + k2t.shape[1] + 4))
    whole = lambda shape: pl.BlockSpec(shape, lambda i: (0,) * len(shape))
    outs = [like(w, BF16), like((2, rows, LANES), F32), like((8, wide), BF16), like((8, wide), BF16)]
    return call(
        setup_body,
        (k1t, k2t, *vectors, clips, features, features, cotangent, cotangent),
        outs,
        limit=56,
        in_specs=[
            whole(k1t.shape),
            whole(k2t.shape),
            *[whole((1, share))] * 4,
            whole(clips.shape),
            pl.BlockSpec((16, wide), lambda i: (0, 0)),
            pl.BlockSpec((16, wide), lambda i: (frames // 16 - 1, 0)),
            pl.BlockSpec((16, wide), lambda i: (0, 0)),
            pl.BlockSpec((16, wide), lambda i: (halves // 16 - 1, 0)),
        ],
        out_specs=[whole(o.shape) for o in outs],
        grid=(1,),
    )


def emit_taps_one(x, up, down, masks, taps, frames):
    rows = masks.shape[1]
    half = rows - TAIL
    clear_ends(taps)
    row = lax.broadcasted_iota(jnp.int32, (8, LANES), 0)
    lead = 24
    own = 2 * half
    for b in range(2):
        frames[b, 0:16] = jnp.zeros((16, LANES), F32)
        frames[b, lead + own + 8 : lead + own + 24] = jnp.zeros((16, LANES), F32)

    def pair(j, b):
        lanes = pl.ds(pl.multiple_of(j * LANES, LANES), LANES)
        u = up[:, lanes].astype(F32)
        d = down[:, lanes].astype(F32)
        frames[b, lead - 8 : lead] = jnp.where(row >= 4, pltpu.roll(u, 4, 0), 0.0)
        frames[b, lead + own : lead + own + 8] = jnp.where(row < 4, d, 0.0)
        for r in tiles(own):
            frames[b, lead + r : lead + r + TILE] = x[r : r + TILE, lanes].astype(F32)

        def pick(first, count, shift):
            return frames[b, pl.ds(lead + 2 * first + shift, count, stride=2), :]

        for r in tiles(rows):
            parts = []
            for shift in (-1, 0, 1, 2):
                if r < half:
                    parts.append(pick(r, TILE, shift))
                else:
                    parts.append(
                        jnp.concatenate([pick(half, 8, shift), pick(-8, 8, shift)], axis=0)
                    )
            span = slice(r, r + TILE)
            parts[0] = parts[0] * masks[0, span]
            parts[3] = parts[3] * masks[1, span]
            taps[1 + j, span, :] = jnp.concatenate(parts, axis=1).astype(BF16)

    def two_pairs(i, carry):
        pair(2 * i, 0)
        pair(2 * i + 1, 1)
        return carry

    lax.fori_loop(0, MEL // 4, two_pairs, 0)


def conv_one_body(row_count, x, up, down, masks, wg, pre, stats, taps, k1_out, k2_out, vec_out,
                  kf, w_even, w_odd, acc, frames):
    emit_taps_one(x, up, down, masks, taps, frames)
    rows = taps.shape[1]
    half = rows - TAIL
    pairs = 4
    rows_one = 9 * C_IN // row_count
    rows_two = 9 * C_MID // row_count
    grps = wg.shape[0] // row_count
    for r in range(row_count):
        shard = [wg[g * row_count + r] for g in range(grps)]
        shard = jnp.concatenate(shard, axis=0).astype(F32).T
        kf[rows_one * r : rows_one * (r + 1)] = shard[0:rows_one]
        at = 9 * C_IN + rows_two * r
        kf[at : at + rows_two] = shard[rows_one : rows_one + rows_two]
        if r == 0:
            vec_out[...] = shard[rows_one + rows_two : rows_one + rows_two + 4]
    k1_out[...] = kf[0 : 9 * C_IN].astype(BF16)
    k2_out[...] = kf[9 * C_IN :].astype(BF16)
    w_even[...] = jnp.zeros(w_even.shape, BF16)
    w_odd[...] = jnp.zeros(w_odd.shape, BF16)
    placed = (
        (w_even, 0, 1, 0), (w_even, 1, 0, 1), (w_even, 1, 1, 2),
        (w_odd, 0, 0, 0), (w_odd, 0, 1, 1), (w_odd, 1, 0, 2),
    )
    for matrix, piece, side, d in placed:
        for q in range(4):
            for p in range(2):
                t = q - p
                if 0 <= t < 3:
                    at = piece * WIDE + q * 128 + side * 64
                    start = (3 * t + d) * C_IN
                    matrix[at : at + 64, p * 128 : p * 128 + 128] = k1_out[start : start + C_IN]
    acc[...] = jnp.zeros(acc.shape, F32)
    for c in range(MEL // 2 // pairs):
        left, mid, right = [
            taps[c * pairs + k : c * pairs + k + pairs].reshape(pairs * rows, WIDE) for k in range(3)
        ]
        for parity, lhs, matrix in (
            (0, jnp.concatenate([left, mid], axis=1), w_even),
            (1, jnp.concatenate([mid, right], axis=1), w_odd),
        ):
            out = jnp.dot(lhs, matrix[...], preferred_element_type=F32)
            out = out.reshape(pairs, rows, BOTH)
            mels = [2 * (c * pairs + q) + parity for q in range(pairs)]
            for q in range(pairs):
                pre[mels[q]] = out[q]
            stats_of(pre, mels, half, acc)
    spread(fold(acc[0]), fold(acc[1]), stats)


def conv_one(features, up, down, masks, wg, row_count):
    rows = masks.shape[1]
    copies = wg.shape[0]
    return call(
        lambda *refs: conv_one_body(row_count, *refs),
        (features, up, down, masks, wg),
        [
            like((MEL, rows, BOTH), F32),
            like((copies, 2, C_MID), F32),
            like((MEL // 2 + 2, rows, WIDE), BF16),
            like((9 * C_IN, C_MID), BF16),
            like((9 * C_MID, C_MID), BF16),
            like((4, C_MID), F32),
        ],
        [
            pltpu.VMEM((9 * (C_IN + C_MID), C_MID), F32),
            pltpu.VMEM((2 * WIDE, BOTH), BF16),
            pltpu.VMEM((2 * WIDE, BOTH), BF16),
            pltpu.VMEM((2, 8, BOTH), F32),
            pltpu.VMEM((2, features.shape[0] + 48, LANES), F32),
        ],
        flops=2 * 2 * MEL * rows * WIDE * BOTH,
        moved=16 * MIB,
    )


def place_two(k2, weight):
    weight[...] = jnp.zeros(weight.shape, BF16)
    for d in range(3):
        for q in range(4):
            for p in range(2):
                t = q - p
                if 0 <= t < 3:
                    at = d * WIDE + q * 128
                    start = (3 * t + d) * C_MID
                    weight[at : at + 128, p * 128 : p * 128 + 128] = k2[start : start + C_MID]


def place_two_back(k2, weight):
    weight[...] = jnp.zeros(weight.shape, BF16)
    for t in range(3):
        for d in range(3):
            start = (3 * t + d) * C_MID
            turned = k2[start : start + C_MID].astype(F32).T.astype(BF16)
            for p in range(2):
                at = (2 - d) * WIDE + (2 - t + p) * 128
                weight[at : at + 128, p * 128 : p * 128 + 128] = turned


def place_one_back(k1, weight):
    weight[...] = jnp.zeros(weight.shape, BF16)
    for t in range(3):
        for d in range(3):
            start = (3 * t + d) * C_IN
            turned = k1[start : start + C_IN].astype(F32).T.astype(BF16)
            for mo in (1, 2):
                for p in range(2):
                    at = (mo - d + 1) * WIDE + (2 - t + p) * 128
                    to = p * 128 + (mo - 1) * 64
                    weight[at : at + 128, to : to + 64] = turned


def conv_two_body(count, pre_one, stats_one, vec, masks, k2, pre, stats, taps, sums_out,
                  acc, weight, evens, odds):
    place_two(k2, weight)
    rows = masks.shape[1]
    half = rows - TAIL
    mels = 4
    sums = stat_sums(stats_one)
    sums_out[...] = sums
    mean, rstd = norm_terms(sums, count)
    scale = 0.5 * vec[0:1] * rstd
    shift = twice(0.5 * vec[1:2] - mean * scale)
    scale = twice(scale)
    clear_ends(taps)
    acc[...] = jnp.zeros(acc.shape, F32)

    def activate(m):
        def tile(r):
            h = pre_one[m, r : r + TILE] * scale + shift
            return halves_of(h + h * jnp.tanh(h))

        emit_taps(taps, 1 + m, masks, evens.at[m % 2], odds.at[m % 2], tile)

    def convolve(c):
        lhs = [taps[c * mels + d : (c + 1) * mels + d].reshape(mels * rows, WIDE) for d in range(3)]
        out = jnp.dot(jnp.concatenate(lhs, axis=1), weight[...], preferred_element_type=F32)
        pre[c * mels : (c + 1) * mels] = out.reshape(mels, rows, BOTH)
        stats_of(pre, range(c * mels, (c + 1) * mels), half, acc)

    for m in range(MEL):
        activate(m)
        if m >= mels and m % mels == 0:
            convolve(m // mels - 1)
    convolve(MEL // mels - 1)
    spread(fold(acc[0]), fold(acc[1]), stats)


def conv_two(pre_one, stats_one, vec, masks, k2, count):
    copies = stats_one.shape[0]
    rows = masks.shape[1]
    return call(
        lambda *refs: conv_two_body(count, *refs),
        (pre_one, stats_one, vec, masks, k2),
        [
            like((MEL, rows, BOTH), F32),
            like((copies, 2, C_MID), F32),
            like((MEL + 2, rows, WIDE), BF16),
            like((2, C_MID), F32),
        ],
        [pltpu.VMEM((2, 8, BOTH), F32), pltpu.VMEM((3 * WIDE, BOTH), BF16), *side_scratch(rows)],
        flops=2 * MEL * rows * 3 * WIDE * BOTH,
        moved=20 * MIB,
    )


def norm_two_body(count, pre, stats_two, vec, cot, up, down, pooled, lift, back_stats, sums_out, acc):
    half = cot.shape[0]
    sums = stat_sums(stats_two)
    sums_out[...] = sums
    mean, rstd = norm_terms(sums, count)
    scale = 0.5 * vec[2:3] * rstd
    shift = 0.5 * vec[3:4] - mean * scale
    norm_shift = -mean * rstd
    acc[...] = jnp.zeros(acc.shape, F32)
    row = lax.broadcasted_iota(jnp.int32, (TAIL, LANES), 0)

    def pair(j, carry):
        lanes = pl.ds(pl.multiple_of(j * LANES, LANES), LANES)
        u = up[:, lanes].astype(F32)
        d = down[:, lanes].astype(F32)
        first = jnp.zeros((8, LANES), F32)
        second = jnp.zeros((8, LANES), F32)
        for r in tiles(half + TAIL):
            span = slice(r, r + TILE)
            if r < half:
                grad = cot[span, lanes].astype(F32) * 0.125
            else:
                grad = jnp.where(row == 0, d[4:5], jnp.where(row == TAIL - 1, u[4:5], 0.0)) * 0.125
            total = jnp.zeros((TILE, LANES), F32)
            for m in (2 * j, 2 * j + 1):
                for p in range(2):
                    side = slice(p * C_MID, (p + 1) * C_MID)
                    value = pre[m, span, side]
                    h = value * scale + shift
                    th = jnp.tanh(h)
                    one = 1.0 + th
                    gl = grad * (one * (1.0 + (h - h * th)))
                    lift[m, span, side] = gl
                    if r < half:
                        total += h * one
                        first += partial_sum(gl)
                        second += partial_sum(gl * (value * rstd + norm_shift))
            if r < half:
                pooled[span, lanes] = (total * 0.25).astype(BF16)
        add_sums(acc, first, second)
        return carry

    lax.fori_loop(0, MEL // 2, pair, 0)
    first, second = [jnp.sum(acc[k], axis=0, keepdims=True) for k in range(2)]
    spread(first, second, back_stats)


def norm_two(pre, stats_two, vec, cot, up, down, count):
    copies = stats_two.shape[0]
    half, wide = cot.shape
    return call(
        lambda *refs: norm_two_body(count, *refs),
        (pre, stats_two, vec, cot, up, down),
        [
            like((half, wide), BF16),
            like((MEL, half + TAIL, BOTH), F32),
            like((copies, 2, C_MID), F32),
            like((2, C_MID), F32),
        ],
        [pltpu.VMEM((2, 8, LANES), F32)],
        flops=10**9,
        moved=16 * MIB,
    )


def grad_terms(sums, back, gain, count):
    mean, rstd = norm_terms(sums, count)
    a = gain * rstd
    b = -a * rstd * (back[1:2] / count)
    c = -a * (back[0:1] / count) - b * mean
    return twice(a), twice(b), twice(c)


def back_two_body(count, lift, pre_two, sums_two, back_stats, vec, masks, k2, pre_one, sums_one,
                  taps_a, lift_one, two, back_out, sums_out, acc, acc_two, taps, weight, evens, odds):
    place_two_back(k2, weight)
    rows = masks.shape[1]
    half = rows - TAIL
    mels = 4
    back = stat_sums(back_stats)
    sums_out[...] = back
    a, b, c = grad_terms(sums_two[...], back, vec[2:3], count)
    mean, rstd = norm_terms(sums_one[...], count)
    scale = 0.5 * vec[0:1] * rstd
    shift = twice(0.5 * vec[1:2] - mean * scale)
    scale = twice(scale)
    norm_shift = twice(-mean * rstd)
    rstd = twice(rstd)
    taps[taps.shape[0] - 1] = jnp.zeros(taps.shape[1:], BF16)
    acc[...] = jnp.zeros(acc.shape, F32)

    def lower(m):
        def tile(r):
            span = slice(r, r + TILE)
            return halves_of(lift[m, span] * a + (pre_two[m, span] * b + c))

        emit_taps(taps, ring_slot(taps, m), masks, evens.at[m % 2], odds.at[m % 2], tile)

    def convolve(k):
        lhs = [stack(taps, range(k * mels + d - 1, (k + 1) * mels + d - 1), rows) for d in range(3)]
        out = jnp.dot(jnp.concatenate(lhs, axis=1), weight[...], preferred_element_type=F32)
        lift_one[k * mels : (k + 1) * mels] = out.reshape(mels, rows, BOTH)
        first = jnp.zeros((8, BOTH), F32)
        second = jnp.zeros((8, BOTH), F32)
        for m in range(k * mels, (k + 1) * mels):
            for r in range(0, rows, 8):
                span = slice(r, r + 8)
                value = pre_one[m, span]
                h = value * scale + shift
                th = jnp.tanh(h)
                gl = lift_one[m, span] * (0.5 * (1.0 + th) * (1.0 + (h - h * th)))
                lift_one[m, span] = gl
                if r < half:
                    first += gl
                    second += gl * (value * rstd + norm_shift)
        add_sums(acc, first, second)

    def correlate(k):
        here = range(k * mels, (k + 1) * mels)
        near = [
            taps_a[k * mels + d : (k + 1) * mels + d, 0:half].reshape(mels * half, WIDE) for d in range(3)
        ]
        total = dot_rows(stack(taps, here, half, slice(128, 384)), jnp.concatenate(near, axis=1))
        if k == 0:
            acc_two[...] = total
        else:
            acc_two[...] += total

    for k in range(MEL // mels + 1):
        for m in range(k * mels, (k + 1) * mels):
            if m < MEL:
                lower(m)
        if k > 0:
            convolve(k - 1)
            correlate(k - 1)
    spread(fold(acc[0]), fold(acc[1]), back_out)
    for t in range(3):
        for d in range(3):
            at = d * WIDE + t * 128
            to = (3 * t + d) * 128
            two[:, to : to + 128] = (
                acc_two[0:C_MID, at : at + 128] + acc_two[C_MID:BOTH, at + 128 : at + 256]
            )


def back_two(lift, pre_two, sums_two, back_stats, vec, masks, k2, pre_one, sums_one, taps_a, count):
    copies = back_stats.shape[0]
    rows = masks.shape[1]
    return call(
        lambda *refs: back_two_body(count, *refs),
        (lift, pre_two, sums_two, back_stats, vec, masks, k2, pre_one, sums_one, taps_a),
        [
            like((MEL, rows, BOTH), F32),
            like((C_MID, 9 * C_MID), F32),
            like((copies, 2, C_MID), F32),
            like((2, C_MID), F32),
        ],
        [
            pltpu.VMEM((2, 8, BOTH), F32),
            pltpu.VMEM((BOTH, 3 * WIDE), F32),
            pltpu.VMEM((11, rows, WIDE), BF16),
            pltpu.VMEM((3 * WIDE, BOTH), BF16),
            *side_scratch(rows),
        ],

        flops=2 * MEL * rows * 3 * WIDE * BOTH,
        moved=32 * MIB,
        input_output_aliases={0: 0},
    )


def scatter_blocks(out, parts):
    copies, share, wide = out.shape
    grps = C_MID // share
    row_count = copies // grps
    turned = [part.T for part in parts]
    sizes = [part.shape[1] // row_count for part in parts]
    blank = jnp.zeros((wide - sum(sizes), C_MID), F32)
    for r in range(row_count):
        rows = [t[n * r : n * (r + 1)] for t, n in zip(turned, sizes)]
        back = jnp.concatenate([*rows, blank], axis=0).T.astype(BF16)
        for g in range(grps):
            out[g * row_count + r] = back[share * g : share * (g + 1)]


def kernel_one_step(taps_x, taps, acc, k, pairs):
    half = taps.shape[1]
    near = [
        taps_x[k * pairs + i : (k + 1) * pairs + i, 0:half].reshape(pairs * half, WIDE)
        for i in range(3)
    ]
    for parity in range(2):
        mels = [2 * (k * pairs + q) + parity for q in range(pairs)]
        total = dot_rows(
            stack(taps, mels, half, slice(128, 384)), jnp.concatenate(near[parity : parity + 2], axis=1)
        )
        if k == 0:
            acc[parity] = total
        else:
            acc[parity] += total


def kernel_one_sums(acc):
    pieces = []
    for t in range(3):
        for d in range(3):
            total = jnp.zeros((C_MID, C_IN), F32)
            for parity in range(2):
                place = 2 * (1 - parity) + parity + d - 1
                for p in range(2):
                    at = (place // 2) * WIDE + (t + p) * 128 + (place % 2) * 64
                    total += acc[parity, p * 128 : p * 128 + 128, at : at + 64]
            pieces.append(total)
    return jnp.concatenate(pieces, axis=1)


def features_step(taps, weight, out, woven, sems, k, pairs, copies):
    half = taps.shape[1]
    slots = woven.shape[0]
    near = [
        stack(taps, [2 * (k * pairs + q) + i - 1 for q in range(pairs)], half) for i in range(4)
    ]
    part = jnp.dot(jnp.concatenate(near, axis=1), weight[...], preferred_element_type=F32)
    for q in range(pairs):
        j = k * pairs + q
        b = j % slots
        rows = slice(q * half, (q + 1) * half)
        if j >= slots:
            copies[j - slots].wait()
        woven[b, pl.ds(0, half, stride=2), :] = part[rows, 0:128]
        woven[b, pl.ds(1, half, stride=2), :] = part[rows, 128:256]
        copy = pltpu.make_async_copy(woven.at[b], out.at[:, pl.ds(j * LANES, LANES)], sems.at[b])
        copy.start()
        copies.append(copy)


def grads_body(count, lift, pre_one, sums_one, back_stats, vec, masks, k1, taps_x, two,
               grad_x, blocks, sums_out, weight, taps, acc_one, evens, odds, woven, sems):
    place_one_back(k1, weight)
    back = stat_sums(back_stats)
    sums_out[...] = back
    a, b, c = grad_terms(sums_one[...], back, vec[0:1], count)
    taps[taps.shape[0] - 1] = jnp.zeros(taps.shape[1:], BF16)

    def lower(m):
        def tile(r):
            span = slice(r, r + TILE)
            return halves_of(lift[m, span] * a + (pre_one[m, span] * b + c))

        emit_taps(taps, ring_slot(taps, m), masks, evens.at[m % 2], odds.at[m % 2], tile)

    pairs = 4
    copies = []
    for k in range(MEL // 2 // pairs + 1):
        for m in range(2 * pairs * k, 2 * pairs * (k + 1)):
            if m < MEL:
                lower(m)
        if k > 0:
            kernel_one_step(taps_x, taps, acc_one, k - 1, pairs)
            features_step(taps, weight, grad_x, woven, sems, k - 1, pairs, copies)
    scatter_blocks(blocks, [kernel_one_sums(acc_one), two[...]])
    for copy in copies[-woven.shape[0] :]:
        copy.wait()


def all_grads(lift, pre_one, sums_one, back_stats, vec, masks, k1, taps_x, two, share, count):
    copies = back_stats.shape[0]
    half = masks.shape[1] - TAIL
    row_count = copies * share // C_MID
    wide = padded(9 * (C_IN + C_MID) // row_count)
    args = (lift, pre_one, sums_one, back_stats, vec, masks, k1, taps_x, two)
    return call(
        lambda *refs: grads_body(count, *refs),
        args,
        [
            like((2 * half, MEL * C_IN), F32),
            like((copies, share, wide), BF16),
            like((2, C_MID), F32),
        ],
        [
            pltpu.VMEM((4 * WIDE, BOTH), BF16),
            pltpu.VMEM((19, half, WIDE), BF16),
            pltpu.VMEM((2, BOTH, 2 * WIDE), F32),
            *side_scratch(half + TAIL),
            pltpu.VMEM((8, 2 * half, LANES), F32),
            pltpu.SemaphoreType.DMA((8,)),
        ],

        flops=12 * 10**9,
        moved=32 * MIB,
        out_specs=[ANY, VMEM, VMEM],
    )


def finish_body(got, back_one_sums, back_two_sums, own_one, own_two, ga, sa, gb, sb):
    total = jnp.sum(got[...].astype(F32), axis=0)
    size = own_one.shape[1]
    own_one[...] = total[:, 0:size]
    own_two[...] = total[:, size : size + own_two.shape[1]]
    share = ga.shape[1]
    lane = lax.broadcasted_iota(jnp.int32, (share, C_MID), 1)
    row = lax.broadcasted_iota(jnp.int32, (share, C_MID), 0)
    chosen = lane == lax.axis_index("grp") * share + row
    first = lax.broadcasted_iota(jnp.int32, (share, share), 0)
    second = lax.broadcasted_iota(jnp.int32, (share, share), 1)
    for out, sums, k in (
        (ga, back_one_sums, 1), (sa, back_one_sums, 0), (gb, back_two_sums, 1), (sb, back_two_sums, 0)
    ):
        wide = jnp.broadcast_to(sums[k : k + 1], (share, C_MID))
        column = jnp.sum(jnp.where(chosen, wide, 0.0), axis=1, keepdims=True)
        wide = jnp.broadcast_to(column, (share, share))
        out[...] = jnp.sum(jnp.where(first == second, wide, 0.0), axis=0, keepdims=True)


def finish(got, back_one_sums, back_two_sums, rows_one, rows_two):
    share = got.shape[1]
    shapes = [(share, rows_one), (share, rows_two)] + [(1, share)] * 4
    return call(
        finish_body,
        (got, back_one_sums, back_two_sums),
        [like(s, F32) for s in shapes],
    )


def exchange(blocks):
    return lax.all_to_all(blocks, AXES, 0, 0, tiled=True)


def shards(
    features, clip_starts, kernel_one, kernel_two, gain_one, shift_one, gain_two, shift_two, cotangent
):
    frames = features.shape[0]
    copies = lax.axis_size(AXES)
    row_count = lax.axis_size("row")
    count = float(frames * MEL * copies)
    rows_one, rows_two = kernel_one.shape[0], kernel_two.shape[0]
    share = kernel_one.shape[1]
    vectors = [v.reshape(1, share) for v in (gain_one, shift_one, gain_two, shift_two)]
    weights, masks, up, down = setup(
        kernel_one.T, kernel_two.T, vectors, clip_starts.reshape(1, -1), features, cotangent, copies
    )
    ends = copies - 1
    up = lax.ppermute(up, AXES, [(i, i + 1) for i in range(ends)])
    down = lax.ppermute(down, AXES, [(i + 1, i) for i in range(ends)])
    weights = exchange(weights)
    pre_one, stats, taps_x, k1, k2, vec = conv_one(features, up, down, masks, weights, row_count)
    stats = exchange(stats)
    pre_two, stats, taps_a, sums_one = conv_two(pre_one, stats, vec, masks, k2, count)
    stats = exchange(stats)
    block_out, lift, stats, sums_two = norm_two(pre_two, stats, vec, cotangent, up, down, count)
    stats = exchange(stats)
    lift, two, stats, back_two_sums = back_two(
        lift, pre_two, sums_two, stats, vec, masks, k2, pre_one, sums_one, taps_a, count
    )
    stats = exchange(stats)
    grad_features, blocks, back_one_sums = all_grads(
        lift, pre_one, sums_one, stats, vec, masks, k1, taps_x, two, share, count
    )
    own_one, own_two, ga, sa, gb, sb = finish(
        exchange(blocks), back_one_sums, back_two_sums, rows_one, rows_two
    )
    return (
        block_out,
        grad_features,
        own_one.T,
        own_two.T,
        ga.reshape(share),
        sa.reshape(share),
        gb.reshape(share),
        sb.reshape(share),
    )


def solution(mesh):
    placed = (
        P(AXES, None), P(), P("row", "grp"), P("row", "grp"),
        P("grp"), P("grp"), P("grp"), P("grp"), P(AXES, None),
    )
    return jax.shard_map(
        shards,
        mesh=mesh,
        in_specs=placed,
        out_specs=(
            P(AXES, None), P(AXES, None), P("row", "grp"), P("row", "grp"),
            P("grp"), P("grp"), P("grp"), P("grp"),
        ),
        check_vma=False,
    )
```

```python
import jax
import jax.numpy as jnp
from jax import lax
from jax.experimental import pallas as pl
from jax.experimental.pallas import tpu as pltpu
from jax.sharding import PartitionSpec as P

MEL = 32
C_IN = 64
C_MID = 128
EPS = 1e-05
AXES = ("grp", "row")
LANES = 128
TAIL = 16
WIDE = 4 * LANES
BOTH = 2 * C_MID
F32 = jnp.float32
BF16 = jnp.bfloat16
TILE = 16
MIB = 2**20

VMEM = pl.BlockSpec(memory_space=pltpu.VMEM)
ANY = pl.BlockSpec(memory_space=pl.ANY)


def like(shape, dtype):
    return jax.ShapeDtypeStruct(shape, dtype)


def call(body, args, outs, scratch=(), limit=14, flops=0, moved=0, in_specs=None, out_specs=None, **more):
    return pl.pallas_call(
        body,
        in_specs=in_specs or [VMEM] * len(args),
        out_specs=out_specs or [VMEM] * len(outs),
        out_shape=outs,
        scratch_shapes=list(scratch),
        compiler_params=pltpu.CompilerParams(vmem_limit_bytes=limit * MIB),
        cost_estimate=pl.CostEstimate(flops=flops, bytes_accessed=moved, transcendentals=0),
        **more,
    )(*args)


def padded(size):
    return -(-size // LANES) * LANES


def partial_sum(values):
    return jnp.sum(values.reshape(-1, 8, values.shape[-1]), axis=0)


def fold(values):
    total = jnp.sum(values, axis=0, keepdims=True)
    return total[:, :C_MID] + total[:, C_MID:]


def spread(first, second, out):
    sums = jnp.concatenate([first, second], axis=0)
    out[...] = jnp.broadcast_to(sums[None], out.shape)


def twice(row):
    return jnp.concatenate([row, row], axis=1)


def tiles(rows):
    return range(0, rows, TILE)


def emit_taps(taps, slot, masks, evens, odds, tile_of):
    rows = masks.shape[1]
    kept = taps.shape[1]
    for r in tiles(rows):
        even, odd = tile_of(r)
        evens[r : r + TILE] = even
        odds[8 + r : 8 + r + TILE] = odd
        if r == 0:
            evens[rows : rows + 1] = even[0:1]
        if r + TILE == rows:
            odds[7:8] = odd[TILE - 1 : TILE]
        if r < kept:
            taps[slot, r : r + TILE, 128:256] = even.astype(BF16)
            taps[slot, r : r + TILE, 256:384] = odd.astype(BF16)
    for r in tiles(kept):
        span = slice(r, r + TILE)
        before = odds[7 + r : 7 + r + TILE] * masks[0, span]
        after = evens[1 + r : 1 + r + TILE] * masks[1, span]
        taps[slot, span, 0:128] = before.astype(BF16)
        taps[slot, span, 384:512] = after.astype(BF16)


def halves_of(value):
    return value[:, :C_MID], value[:, C_MID:]


def add_sums(acc, first, second):
    acc[0] += first
    acc[1] += second


def side_scratch(rows):
    return [pltpu.VMEM((2, rows + 8, LANES), F32), pltpu.VMEM((2, rows + 8, LANES), F32)]


def stats_of(pre, mels, half, acc):
    first = jnp.zeros((8, BOTH), F32)
    second = jnp.zeros((8, BOTH), F32)
    for m in mels:
        for r in range(0, half, 8):
            value = pre[m, r : r + 8]
            first += value
            second += value * value
    add_sums(acc, first, second)


def stat_sums(stats):
    return jnp.sum(stats[...], axis=0)


def norm_terms(sums, count):
    mean = sums[0:1] / count
    rstd = lax.rsqrt(sums[1:2] / count - mean * mean + EPS)
    return mean, rstd


def dot_rows(first, second):
    return lax.dot_general(
        first, second, (((0,), (0,)), ((), ())), preferred_element_type=F32
    )


def ring_slot(taps, m):
    last = taps.shape[0] - 1
    return m % last if 0 <= m < MEL else last


def stack(taps, mels, rows, lanes=slice(None)):
    parts = [taps[ring_slot(taps, m), 0:rows, lanes] for m in mels]
    return jnp.concatenate(parts, axis=0)


def clear_ends(taps):
    blank = jnp.zeros(taps.shape[1:], BF16)
    taps[0] = blank
    taps[taps.shape[0] - 1] = blank


def setup_body(copies, k1, k2, ga, sa, gb, sb, clips, x_head, x_tail, c_head, c_tail, w_out, masks, up, down):
    share = k1.shape[0]
    w_out[...] = jnp.zeros(w_out.shape, BF16)
    first = lax.broadcasted_iota(jnp.int32, (share, share), 0)
    second = lax.broadcasted_iota(jnp.int32, (share, share), 1)
    columns = [k1[...].astype(F32), k2[...].astype(F32)]
    for vector in (ga, sa, gb, sb):
        wide = jnp.broadcast_to(vector[...].astype(F32), (share, share))
        columns.append(jnp.sum(jnp.where(first == second, wide, 0.0), axis=1, keepdims=True))
    chunk = jnp.concatenate(columns, axis=1).astype(BF16)
    for i in range(w_out.shape[0]):
        w_out[i, :, 0 : chunk.shape[1]] = chunk
    rows = masks.shape[1]
    half = rows - TAIL
    frames = 2 * half
    start = lax.axis_index(AXES) * frames
    place = lax.broadcasted_iota(jnp.int32, (rows, clips.shape[1]), 0)
    pair = jnp.where(place >= half + TAIL // 2, place - rows, place)
    frame = start + 2 * pair
    starts = jnp.broadcast_to(clips[...], (rows, clips.shape[1]))
    for slot, shift in ((0, 0), (1, 2)):
        hit = (frame + shift == starts) | (frame + shift >= frames * copies)
        begins = jnp.max(jnp.where(hit, 1.0, 0.0), axis=1, keepdims=True)
        masks[slot] = jnp.broadcast_to(1.0 - begins, (rows, LANES))
    row = lax.broadcasted_iota(jnp.int32, (8, x_head.shape[1]), 0)
    xt = x_tail[...].astype(F32)
    ct = c_tail[...].astype(F32)
    up[...] = jnp.where(
        row < 4, pltpu.roll(xt[8:16], 4, 0), jnp.where(row == 4, ct[15:16], 0.0)
    ).astype(BF16)
    xh = x_head[...].astype(F32)
    ch = c_head[...].astype(F32)
    down[...] = jnp.where(row < 4, xh[0:8], jnp.where(row == 4, ch[0:1], 0.0)).astype(BF16)


def setup(k1t, k2t, vectors, clips, features, cotangent, row_count, copies):
    frames, wide = features.shape
    halves = cotangent.shape[0]
    rows = frames // 2 + TAIL
    share = k1t.shape[0]
    w = (row_count, share, padded(k1t.shape[1] + k2t.shape[1] + 4))
    whole = lambda shape: pl.BlockSpec(shape, lambda i: (0,) * len(shape))
    outs = [like(w, BF16), like((2, rows, LANES), F32), like((8, wide), BF16), like((8, wide), BF16)]
    return call(
        lambda *refs: setup_body(copies, *refs),
        (k1t, k2t, *vectors, clips, features, features, cotangent, cotangent),
        outs,
        limit=56,
        in_specs=[
            whole(k1t.shape),
            whole(k2t.shape),
            *[whole((1, share))] * 4,
            whole(clips.shape),
            pl.BlockSpec((16, wide), lambda i: (0, 0)),
            pl.BlockSpec((16, wide), lambda i: (frames // 16 - 1, 0)),
            pl.BlockSpec((16, wide), lambda i: (0, 0)),
            pl.BlockSpec((16, wide), lambda i: (halves // 16 - 1, 0)),
        ],
        out_specs=[whole(o.shape) for o in outs],
        grid=(1,),
    )


def emit_taps_one(x, up, down, masks, taps, frames):
    rows = masks.shape[1]
    half = rows - TAIL
    clear_ends(taps)
    row = lax.broadcasted_iota(jnp.int32, (8, LANES), 0)
    lead = 24
    own = 2 * half
    for b in range(2):
        frames[b, 0:16] = jnp.zeros((16, LANES), F32)
        frames[b, lead + own + 8 : lead + own + 24] = jnp.zeros((16, LANES), F32)

    def pair(j, b):
        lanes = pl.ds(pl.multiple_of(j * LANES, LANES), LANES)
        u = up[:, lanes].astype(F32)
        d = down[:, lanes].astype(F32)
        frames[b, lead - 8 : lead] = jnp.where(row >= 4, pltpu.roll(u, 4, 0), 0.0)
        frames[b, lead + own : lead + own + 8] = jnp.where(row < 4, d, 0.0)
        for r in tiles(own):
            frames[b, lead + r : lead + r + TILE] = x[r : r + TILE, lanes].astype(F32)

        def pick(first, count, shift):
            return frames[b, pl.ds(lead + 2 * first + shift, count, stride=2), :]

        for r in tiles(rows):
            parts = []
            for shift in (-1, 0, 1, 2):
                if r < half:
                    parts.append(pick(r, TILE, shift))
                else:
                    parts.append(
                        jnp.concatenate([pick(half, 8, shift), pick(-8, 8, shift)], axis=0)
                    )
            span = slice(r, r + TILE)
            parts[0] = parts[0] * masks[0, span]
            parts[3] = parts[3] * masks[1, span]
            taps[1 + j, span, :] = jnp.concatenate(parts, axis=1).astype(BF16)

    def two_pairs(i, carry):
        pair(2 * i, 0)
        pair(2 * i + 1, 1)
        return carry

    lax.fori_loop(0, MEL // 4, two_pairs, 0)


def conv_one_body(row_count, x, up, down, masks, wg, pre, stats, taps, k1_out, k2_out, vec_out,
                  kf, w_even, w_odd, acc, frames):
    emit_taps_one(x, up, down, masks, taps, frames)
    rows = taps.shape[1]
    half = rows - TAIL
    pairs = 4
    rows_one = 9 * C_IN // row_count
    rows_two = 9 * C_MID // row_count
    grps = wg.shape[0] // row_count
    for r in range(row_count):
        shard = [wg[g * row_count + r] for g in range(grps)]
        shard = jnp.concatenate(shard, axis=0).astype(F32).T
        kf[rows_one * r : rows_one * (r + 1)] = shard[0:rows_one]
        at = 9 * C_IN + rows_two * r
        kf[at : at + rows_two] = shard[rows_one : rows_one + rows_two]
        if r == 0:
            vec_out[...] = shard[rows_one + rows_two : rows_one + rows_two + 4]
    k1_out[...] = kf[0 : 9 * C_IN].astype(BF16)
    k2_out[...] = kf[9 * C_IN :].astype(BF16)
    w_even[...] = jnp.zeros(w_even.shape, BF16)
    w_odd[...] = jnp.zeros(w_odd.shape, BF16)
    placed = (
        (w_even, 0, 1, 0), (w_even, 1, 0, 1), (w_even, 1, 1, 2),
        (w_odd, 0, 0, 0), (w_odd, 0, 1, 1), (w_odd, 1, 0, 2),
    )
    for matrix, piece, side, d in placed:
        for q in range(4):
            for p in range(2):
                t = q - p
                if 0 <= t < 3:
                    at = piece * WIDE + q * 128 + side * 64
                    start = (3 * t + d) * C_IN
                    matrix[at : at + 64, p * 128 : p * 128 + 128] = k1_out[start : start + C_IN]
    acc[...] = jnp.zeros(acc.shape, F32)
    for c in range(MEL // 2 // pairs):
        left, mid, right = [
            taps[c * pairs + k : c * pairs + k + pairs].reshape(pairs * rows, WIDE) for k in range(3)
        ]
        for parity, lhs, matrix in (
            (0, jnp.concatenate([left, mid], axis=1), w_even),
            (1, jnp.concatenate([mid, right], axis=1), w_odd),
        ):
            out = jnp.dot(lhs, matrix[...], preferred_element_type=F32)
            out = out.reshape(pairs, rows, BOTH)
            mels = [2 * (c * pairs + q) + parity for q in range(pairs)]
            for q in range(pairs):
                pre[mels[q]] = out[q]
            stats_of(pre, mels, half, acc)
    spread(fold(acc[0]), fold(acc[1]), stats)


def conv_one(features, up, down, masks, wg, row_count):
    rows = masks.shape[1]
    return call(
        lambda *refs: conv_one_body(row_count, *refs),
        (features, up, down, masks, wg),
        [
            like((MEL, rows, BOTH), F32),
            like((row_count, 2, C_MID), F32),
            like((MEL // 2 + 2, rows, WIDE), BF16),
            like((9 * C_IN, C_MID), BF16),
            like((9 * C_MID, C_MID), BF16),
            like((4, C_MID), F32),
        ],
        [
            pltpu.VMEM((9 * (C_IN + C_MID), C_MID), F32),
            pltpu.VMEM((2 * WIDE, BOTH), BF16),
            pltpu.VMEM((2 * WIDE, BOTH), BF16),
            pltpu.VMEM((2, 8, BOTH), F32),
            pltpu.VMEM((2, features.shape[0] + 48, LANES), F32),
        ],
        flops=2 * 2 * MEL * rows * WIDE * BOTH,
        moved=16 * MIB,
    )


def place_two(k2, weight):
    weight[...] = jnp.zeros(weight.shape, BF16)
    for d in range(3):
        for q in range(4):
            for p in range(2):
                t = q - p
                if 0 <= t < 3:
                    at = d * WIDE + q * 128
                    start = (3 * t + d) * C_MID
                    weight[at : at + 128, p * 128 : p * 128 + 128] = k2[start : start + C_MID]


def place_two_back(k2, weight):
    weight[...] = jnp.zeros(weight.shape, BF16)
    for t in range(3):
        for d in range(3):
            start = (3 * t + d) * C_MID
            turned = k2[start : start + C_MID].astype(F32).T.astype(BF16)
            for p in range(2):
                at = (2 - d) * WIDE + (2 - t + p) * 128
                weight[at : at + 128, p * 128 : p * 128 + 128] = turned


def place_one_back(k1, weight):
    weight[...] = jnp.zeros(weight.shape, BF16)
    for t in range(3):
        for d in range(3):
            start = (3 * t + d) * C_IN
            turned = k1[start : start + C_IN].astype(F32).T.astype(BF16)
            for mo in (1, 2):
                for p in range(2):
                    at = (mo - d + 1) * WIDE + (2 - t + p) * 128
                    to = p * 128 + (mo - 1) * 64
                    weight[at : at + 128, to : to + 64] = turned


def conv_two_body(count, pre_one, stats_one, vec, masks, k2, pre, stats, taps, sums_out,
                  acc, weight, evens, odds):
    place_two(k2, weight)
    rows = masks.shape[1]
    half = rows - TAIL
    mels = 4
    sums = stat_sums(stats_one)
    sums_out[...] = sums
    mean, rstd = norm_terms(sums, count)
    scale = 0.5 * vec[0:1] * rstd
    shift = twice(0.5 * vec[1:2] - mean * scale)
    scale = twice(scale)
    clear_ends(taps)
    acc[...] = jnp.zeros(acc.shape, F32)

    def activate(m):
        def tile(r):
            h = pre_one[m, r : r + TILE] * scale + shift
            return halves_of(h + h * jnp.tanh(h))

        emit_taps(taps, 1 + m, masks, evens.at[m % 2], odds.at[m % 2], tile)

    def convolve(c):
        lhs = [taps[c * mels + d : (c + 1) * mels + d].reshape(mels * rows, WIDE) for d in range(3)]
        out = jnp.dot(jnp.concatenate(lhs, axis=1), weight[...], preferred_element_type=F32)
        pre[c * mels : (c + 1) * mels] = out.reshape(mels, rows, BOTH)
        stats_of(pre, range(c * mels, (c + 1) * mels), half, acc)

    for m in range(MEL):
        activate(m)
        if m >= mels and m % mels == 0:
            convolve(m // mels - 1)
    convolve(MEL // mels - 1)
    spread(fold(acc[0]), fold(acc[1]), stats)


def conv_two(pre_one, stats_one, vec, masks, k2, row_count, count):
    rows = masks.shape[1]
    return call(
        lambda *refs: conv_two_body(count, *refs),
        (pre_one, stats_one, vec, masks, k2),
        [
            like((MEL, rows, BOTH), F32),
            like((row_count, 2, C_MID), F32),
            like((MEL + 2, rows, WIDE), BF16),
            like((2, C_MID), F32),
        ],
        [pltpu.VMEM((2, 8, BOTH), F32), pltpu.VMEM((3 * WIDE, BOTH), BF16), *side_scratch(rows)],
        flops=2 * MEL * rows * 3 * WIDE * BOTH,
        moved=20 * MIB,
    )


def norm_two_body(count, pre, stats_two, vec, cot, up, down, pooled, lift, back_stats, sums_out, acc):
    half = cot.shape[0]
    sums = stat_sums(stats_two)
    sums_out[...] = sums
    mean, rstd = norm_terms(sums, count)
    scale = 0.5 * vec[2:3] * rstd
    shift = 0.5 * vec[3:4] - mean * scale
    norm_shift = -mean * rstd
    acc[...] = jnp.zeros(acc.shape, F32)
    row = lax.broadcasted_iota(jnp.int32, (TAIL, LANES), 0)

    def pair(j, carry):
        lanes = pl.ds(pl.multiple_of(j * LANES, LANES), LANES)
        u = up[:, lanes].astype(F32)
        d = down[:, lanes].astype(F32)
        first = jnp.zeros((8, LANES), F32)
        second = jnp.zeros((8, LANES), F32)
        for r in tiles(half + TAIL):
            span = slice(r, r + TILE)
            if r < half:
                grad = cot[span, lanes].astype(F32) * 0.125
            else:
                grad = jnp.where(row == 0, d[4:5], jnp.where(row == TAIL - 1, u[4:5], 0.0)) * 0.125
            total = jnp.zeros((TILE, LANES), F32)
            for m in (2 * j, 2 * j + 1):
                for p in range(2):
                    side = slice(p * C_MID, (p + 1) * C_MID)
                    value = pre[m, span, side]
                    h = value * scale + shift
                    th = jnp.tanh(h)
                    one = 1.0 + th
                    gl = grad * (one * (1.0 + (h - h * th)))
                    lift[m, span, side] = gl
                    if r < half:
                        total += h * one
                        first += partial_sum(gl)
                        second += partial_sum(gl * (value * rstd + norm_shift))
            if r < half:
                pooled[span, lanes] = (total * 0.25).astype(BF16)
        add_sums(acc, first, second)
        return carry

    lax.fori_loop(0, MEL // 2, pair, 0)
    first, second = [jnp.sum(acc[k], axis=0, keepdims=True) for k in range(2)]
    spread(first, second, back_stats)


def norm_two(pre, stats_two, vec, cot, up, down, row_count, count):
    half, wide = cot.shape
    return call(
        lambda *refs: norm_two_body(count, *refs),
        (pre, stats_two, vec, cot, up, down),
        [
            like((half, wide), BF16),
            like((MEL, half + TAIL, BOTH), F32),
            like((row_count, 2, C_MID), F32),
            like((2, C_MID), F32),
        ],
        [pltpu.VMEM((2, 8, LANES), F32)],
        flops=10**9,
        moved=16 * MIB,
    )


def grad_terms(sums, back, gain, count):
    mean, rstd = norm_terms(sums, count)
    a = gain * rstd
    b = -a * rstd * (back[1:2] / count)
    c = -a * (back[0:1] / count) - b * mean
    return twice(a), twice(b), twice(c)


def back_two_body(count, lift, pre_two, sums_two, back_stats, vec, masks, k2, pre_one, sums_one,
                  taps_a, lift_one, two, back_out, sums_out, acc, acc_two, taps, weight, evens, odds):
    place_two_back(k2, weight)
    rows = masks.shape[1]
    half = rows - TAIL
    mels = 4
    back = stat_sums(back_stats)
    sums_out[...] = back
    a, b, c = grad_terms(sums_two[...], back, vec[2:3], count)
    mean, rstd = norm_terms(sums_one[...], count)
    scale = 0.5 * vec[0:1] * rstd
    shift = twice(0.5 * vec[1:2] - mean * scale)
    scale = twice(scale)
    norm_shift = twice(-mean * rstd)
    rstd = twice(rstd)
    taps[taps.shape[0] - 1] = jnp.zeros(taps.shape[1:], BF16)
    acc[...] = jnp.zeros(acc.shape, F32)

    def lower(m):
        def tile(r):
            span = slice(r, r + TILE)
            return halves_of(lift[m, span] * a + (pre_two[m, span] * b + c))

        emit_taps(taps, ring_slot(taps, m), masks, evens.at[m % 2], odds.at[m % 2], tile)

    def convolve(k):
        lhs = [stack(taps, range(k * mels + d - 1, (k + 1) * mels + d - 1), rows) for d in range(3)]
        out = jnp.dot(jnp.concatenate(lhs, axis=1), weight[...], preferred_element_type=F32)
        lift_one[k * mels : (k + 1) * mels] = out.reshape(mels, rows, BOTH)
        first = jnp.zeros((8, BOTH), F32)
        second = jnp.zeros((8, BOTH), F32)
        for m in range(k * mels, (k + 1) * mels):
            for r in range(0, rows, 8):
                span = slice(r, r + 8)
                value = pre_one[m, span]
                h = value * scale + shift
                th = jnp.tanh(h)
                gl = lift_one[m, span] * (0.5 * (1.0 + th) * (1.0 + (h - h * th)))
                lift_one[m, span] = gl
                if r < half:
                    first += gl
                    second += gl * (value * rstd + norm_shift)
        add_sums(acc, first, second)

    def correlate(k):
        here = range(k * mels, (k + 1) * mels)
        near = [
            taps_a[k * mels + d : (k + 1) * mels + d, 0:half].reshape(mels * half, WIDE) for d in range(3)
        ]
        total = dot_rows(stack(taps, here, half, slice(128, 384)), jnp.concatenate(near, axis=1))
        if k == 0:
            acc_two[...] = total
        else:
            acc_two[...] += total

    for k in range(MEL // mels + 1):
        for m in range(k * mels, (k + 1) * mels):
            if m < MEL:
                lower(m)
        if k > 0:
            convolve(k - 1)
            correlate(k - 1)
    spread(fold(acc[0]), fold(acc[1]), back_out)
    for t in range(3):
        for d in range(3):
            at = d * WIDE + t * 128
            to = (3 * t + d) * 128
            two[:, to : to + 128] = (
                acc_two[0:C_MID, at : at + 128] + acc_two[C_MID:BOTH, at + 128 : at + 256]
            )


def back_two(lift, pre_two, sums_two, back_stats, vec, masks, k2, pre_one, sums_one, taps_a, row_count, count):
    rows = masks.shape[1]
    return call(
        lambda *refs: back_two_body(count, *refs),
        (lift, pre_two, sums_two, back_stats, vec, masks, k2, pre_one, sums_one, taps_a),
        [
            like((MEL, rows, BOTH), F32),
            like((C_MID, 9 * C_MID), F32),
            like((row_count, 2, C_MID), F32),
            like((2, C_MID), F32),
        ],
        [
            pltpu.VMEM((2, 8, BOTH), F32),
            pltpu.VMEM((BOTH, 3 * WIDE), F32),
            pltpu.VMEM((11, rows, WIDE), BF16),
            pltpu.VMEM((3 * WIDE, BOTH), BF16),
            *side_scratch(rows),
        ],

        flops=2 * MEL * rows * 3 * WIDE * BOTH,
        moved=32 * MIB,
        input_output_aliases={0: 0},
    )


def scatter_blocks(out, parts):
    copies, share, wide = out.shape
    grps = C_MID // share
    row_count = copies // grps
    turned = [part.T for part in parts]
    sizes = [part.shape[1] // row_count for part in parts]
    blank = jnp.zeros((wide - sum(sizes), C_MID), F32)
    for r in range(row_count):
        rows = [t[n * r : n * (r + 1)] for t, n in zip(turned, sizes)]
        back = jnp.concatenate([*rows, blank], axis=0).T.astype(BF16)
        for g in range(grps):
            out[g * row_count + r] = back[share * g : share * (g + 1)]


def kernel_one_step(taps_x, taps, acc, k, pairs):
    half = taps.shape[1]
    near = [
        taps_x[k * pairs + i : (k + 1) * pairs + i, 0:half].reshape(pairs * half, WIDE)
        for i in range(3)
    ]
    for parity in range(2):
        mels = [2 * (k * pairs + q) + parity for q in range(pairs)]
        total = dot_rows(
            stack(taps, mels, half, slice(128, 384)), jnp.concatenate(near[parity : parity + 2], axis=1)
        )
        if k == 0:
            acc[parity] = total
        else:
            acc[parity] += total


def kernel_one_sums(acc):
    pieces = []
    for t in range(3):
        for d in range(3):
            total = jnp.zeros((C_MID, C_IN), F32)
            for parity in range(2):
                place = 2 * (1 - parity) + parity + d - 1
                for p in range(2):
                    at = (place // 2) * WIDE + (t + p) * 128 + (place % 2) * 64
                    total += acc[parity, p * 128 : p * 128 + 128, at : at + 64]
            pieces.append(total)
    return jnp.concatenate(pieces, axis=1)


def features_step(taps, weight, out, woven, sems, k, pairs, copies):
    half = taps.shape[1]
    slots = woven.shape[0]
    near = [
        stack(taps, [2 * (k * pairs + q) + i - 1 for q in range(pairs)], half) for i in range(4)
    ]
    part = jnp.dot(jnp.concatenate(near, axis=1), weight[...], preferred_element_type=F32)
    for q in range(pairs):
        j = k * pairs + q
        b = j % slots
        rows = slice(q * half, (q + 1) * half)
        if j >= slots:
            copies[j - slots].wait()
        woven[b, pl.ds(0, half, stride=2), :] = part[rows, 0:128]
        woven[b, pl.ds(1, half, stride=2), :] = part[rows, 128:256]
        copy = pltpu.make_async_copy(woven.at[b], out.at[:, pl.ds(j * LANES, LANES)], sems.at[b])
        copy.start()
        copies.append(copy)


def grads_body(count, lift, pre_one, sums_one, back_stats, vec, masks, k1, taps_x, two,
               grad_x, blocks, sums_out, weight, taps, acc_one, evens, odds, woven, sems):
    place_one_back(k1, weight)
    back = stat_sums(back_stats)
    sums_out[...] = back
    a, b, c = grad_terms(sums_one[...], back, vec[0:1], count)
    taps[taps.shape[0] - 1] = jnp.zeros(taps.shape[1:], BF16)

    def lower(m):
        def tile(r):
            span = slice(r, r + TILE)
            return halves_of(lift[m, span] * a + (pre_one[m, span] * b + c))

        emit_taps(taps, ring_slot(taps, m), masks, evens.at[m % 2], odds.at[m % 2], tile)

    pairs = 4
    copies = []
    for k in range(MEL // 2 // pairs + 1):
        for m in range(2 * pairs * k, 2 * pairs * (k + 1)):
            if m < MEL:
                lower(m)
        if k > 0:
            kernel_one_step(taps_x, taps, acc_one, k - 1, pairs)
            features_step(taps, weight, grad_x, woven, sems, k - 1, pairs, copies)
    scatter_blocks(blocks, [kernel_one_sums(acc_one), two[...]])
    for copy in copies[-woven.shape[0] :]:
        copy.wait()


def all_grads(lift, pre_one, sums_one, back_stats, vec, masks, k1, taps_x, two, share, count):
    copies = back_stats.shape[0]
    half = masks.shape[1] - TAIL
    row_count = copies * share // C_MID
    wide = padded(9 * (C_IN + C_MID) // row_count)
    args = (lift, pre_one, sums_one, back_stats, vec, masks, k1, taps_x, two)
    return call(
        lambda *refs: grads_body(count, *refs),
        args,
        [
            like((2 * half, MEL * C_IN), F32),
            like((copies, share, wide), BF16),
            like((2, C_MID), F32),
        ],
        [
            pltpu.VMEM((4 * WIDE, BOTH), BF16),
            pltpu.VMEM((19, half, WIDE), BF16),
            pltpu.VMEM((2, BOTH, 2 * WIDE), F32),
            *side_scratch(half + TAIL),
            pltpu.VMEM((8, 2 * half, LANES), F32),
            pltpu.SemaphoreType.DMA((8,)),
        ],

        flops=12 * 10**9,
        moved=32 * MIB,
        out_specs=[ANY, VMEM, VMEM],
    )


def finish_body(got, back_one_sums, back_two_sums, own_one, own_two, ga, sa, gb, sb):
    total = jnp.sum(got[...].astype(F32), axis=0)
    size = own_one.shape[1]
    own_one[...] = total[:, 0:size]
    own_two[...] = total[:, size : size + own_two.shape[1]]
    share = ga.shape[1]
    lane = lax.broadcasted_iota(jnp.int32, (share, C_MID), 1)
    row = lax.broadcasted_iota(jnp.int32, (share, C_MID), 0)
    chosen = lane == lax.axis_index("grp") * share + row
    first = lax.broadcasted_iota(jnp.int32, (share, share), 0)
    second = lax.broadcasted_iota(jnp.int32, (share, share), 1)
    for out, sums, k in (
        (ga, back_one_sums, 1), (sa, back_one_sums, 0), (gb, back_two_sums, 1), (sb, back_two_sums, 0)
    ):
        wide = jnp.broadcast_to(sums[k : k + 1], (share, C_MID))
        column = jnp.sum(jnp.where(chosen, wide, 0.0), axis=1, keepdims=True)
        wide = jnp.broadcast_to(column, (share, share))
        out[...] = jnp.sum(jnp.where(first == second, wide, 0.0), axis=0, keepdims=True)


def finish(got, back_one_sums, back_two_sums, rows_one, rows_two):
    share = got.shape[1]
    shapes = [(share, rows_one), (share, rows_two)] + [(1, share)] * 4
    return call(
        finish_body,
        (got, back_one_sums, back_two_sums),
        [like(s, F32) for s in shapes],
    )


def exchange(blocks):
    return lax.all_to_all(blocks, AXES, 0, 0, tiled=True)


def collect(copies):
    blocks = lax.all_to_all(copies, "row", 0, 0, tiled=True)
    return lax.all_gather(blocks, "grp", axis=0, tiled=True)


def shards(
    features, clip_starts, kernel_one, kernel_two, gain_one, shift_one, gain_two, shift_two, cotangent
):
    frames = features.shape[0]
    copies = lax.axis_size(AXES)
    row_count = lax.axis_size("row")
    count = float(frames * MEL * copies)
    rows_one, rows_two = kernel_one.shape[0], kernel_two.shape[0]
    share = kernel_one.shape[1]
    vectors = [v.reshape(1, share) for v in (gain_one, shift_one, gain_two, shift_two)]
    weights, masks, up, down = setup(
        kernel_one.T, kernel_two.T, vectors, clip_starts.reshape(1, -1), features, cotangent, row_count, copies
    )
    ends = copies - 1
    up = lax.ppermute(up, AXES, [(i, i + 1) for i in range(ends)])
    down = lax.ppermute(down, AXES, [(i + 1, i) for i in range(ends)])
    weights = collect(weights)
    pre_one, stats, taps_x, k1, k2, vec = conv_one(features, up, down, masks, weights, row_count)
    stats = collect(stats)
    pre_two, stats, taps_a, sums_one = conv_two(pre_one, stats, vec, masks, k2, row_count, count)
    stats = collect(stats)
    block_out, lift, stats, sums_two = norm_two(pre_two, stats, vec, cotangent, up, down, row_count, count)
    stats = collect(stats)
    lift, two, stats, back_two_sums = back_two(
        lift, pre_two, sums_two, stats, vec, masks, k2, pre_one, sums_one, taps_a, row_count, count
    )
    stats = collect(stats)
    grad_features, blocks, back_one_sums = all_grads(
        lift, pre_one, sums_one, stats, vec, masks, k1, taps_x, two, share, count
    )
    own_one, own_two, ga, sa, gb, sb = finish(
        exchange(blocks), back_one_sums, back_two_sums, rows_one, rows_two
    )
    return (
        block_out,
        grad_features,
        own_one.T,
        own_two.T,
        ga.reshape(share),
        sa.reshape(share),
        gb.reshape(share),
        sb.reshape(share),
    )


def solution(mesh):
    placed = (
        P(AXES, None), P(), P("row", "grp"), P("row", "grp"),
        P("grp"), P("grp"), P("grp"), P("grp"), P(AXES, None),
    )
    return jax.shard_map(
        shards,
        mesh=mesh,
        in_specs=placed,
        out_specs=(
            P(AXES, None), P(AXES, None), P("row", "grp"), P("row", "grp"),
            P("grp"), P("grp"), P("grp"), P("grp"),
        ),
        check_vma=False,
    )
```

```python
import jax
import jax.numpy as jnp
from jax import lax
from jax.experimental import pallas as pl
from jax.experimental.pallas import tpu as pltpu
from jax.sharding import PartitionSpec as P

MEL = 32
C_IN = 64
C_MID = 128
EPS = 1e-05
AXES = ("grp", "row")
LANES = 128
TAIL = 16
WIDE = 4 * LANES
BOTH = 2 * C_MID
F32 = jnp.float32
BF16 = jnp.bfloat16
TILE = 16
MIB = 2**20

VMEM = pl.BlockSpec(memory_space=pltpu.VMEM)
ANY = pl.BlockSpec(memory_space=pl.ANY)
HBM = pl.BlockSpec(memory_space=pltpu.HBM)


def like(shape, dtype):
    return jax.ShapeDtypeStruct(shape, dtype)


def call(body, args, outs, scratch=(), limit=16, in_specs=None, out_specs=None, **more):
    return pl.pallas_call(
        body,
        in_specs=in_specs or [VMEM] * len(args),
        out_specs=out_specs or [VMEM] * len(outs),
        out_shape=outs,
        scratch_shapes=list(scratch),
        compiler_params=pltpu.CompilerParams(vmem_limit_bytes=limit * MIB),
        **more,
    )(*args)


def padded(size):
    return -(-size // LANES) * LANES


def partial_sum(values):
    return jnp.sum(values.reshape(-1, 8, values.shape[-1]), axis=0)


def fold(values):
    total = jnp.sum(values, axis=0, keepdims=True)
    return total[:, :C_MID] + total[:, C_MID:]


def spread(first, second, out):
    sums = jnp.concatenate([first, second], axis=0)
    out[...] = jnp.broadcast_to(sums[None], out.shape)


def twice(row):
    return jnp.concatenate([row, row], axis=1)


def tiles(rows):
    return range(0, rows, TILE)


def emit_taps(taps, slot, masks, evens, odds, tile_of):
    rows = masks.shape[1]
    kept = taps.shape[1]
    for r in tiles(rows):
        even, odd = tile_of(r)
        evens[r : r + TILE] = even
        odds[8 + r : 8 + r + TILE] = odd
        if r == 0:
            evens[rows : rows + 1] = even[0:1]
        if r + TILE == rows:
            odds[7:8] = odd[TILE - 1 : TILE]
        if r < kept:
            taps[slot, r : r + TILE, 128:256] = even.astype(BF16)
            taps[slot, r : r + TILE, 256:384] = odd.astype(BF16)
    for r in tiles(kept):
        span = slice(r, r + TILE)
        before = odds[7 + r : 7 + r + TILE] * masks[0, span]
        after = evens[1 + r : 1 + r + TILE] * masks[1, span]
        taps[slot, span, 0:128] = before.astype(BF16)
        taps[slot, span, 384:512] = after.astype(BF16)


def halves_of(value):
    return value[:, :C_MID], value[:, C_MID:]


def add_sums(acc, first, second):
    acc[0] += first
    acc[1] += second


def side_scratch(rows):
    return [pltpu.VMEM((2, rows + 8, LANES), F32), pltpu.VMEM((2, rows + 8, LANES), F32)]


def stats_of(pre, mels, half, acc):
    first = jnp.zeros((8, BOTH), F32)
    second = jnp.zeros((8, BOTH), F32)
    for m in mels:
        for r in range(0, half, 8):
            value = pre[m, r : r + 8]
            first += value
            second += value * value
    add_sums(acc, first, second)


def stat_sums(stats):
    return jnp.sum(stats[...], axis=0)


def norm_terms(sums, count):
    mean = sums[0:1] / count
    rstd = lax.rsqrt(sums[1:2] / count - mean * mean + EPS)
    return mean, rstd


def dot_rows(first, second):
    return lax.dot_general(
        first, second, (((0,), (0,)), ((), ())), preferred_element_type=F32
    )


def ring_slot(taps, m):
    last = taps.shape[0] - 1
    return m % last if 0 <= m < MEL else last


def stack(taps, mels, rows, lanes=slice(None)):
    parts = [taps[ring_slot(taps, m), 0:rows, lanes] for m in mels]
    return jnp.concatenate(parts, axis=0)


def clear_ends(taps):
    blank = jnp.zeros(taps.shape[1:], BF16)
    taps[0] = blank
    taps[taps.shape[0] - 1] = blank


def setup_body(k1, k2, ga, sa, gb, sb, clips, x_head, x_tail, c_head, c_tail, w_out, up, down, clips_out):
    clips_out[...] = clips[...]
    share = k1.shape[0]
    copies = w_out.shape[0]
    w_out[...] = jnp.zeros(w_out.shape, BF16)
    first = lax.broadcasted_iota(jnp.int32, (share, share), 0)
    second = lax.broadcasted_iota(jnp.int32, (share, share), 1)
    columns = [k1[...].astype(F32), k2[...].astype(F32)]
    for vector in (ga, sa, gb, sb):
        wide = jnp.broadcast_to(vector[...].astype(F32), (share, share))
        columns.append(jnp.sum(jnp.where(first == second, wide, 0.0), axis=1, keepdims=True))
    chunk = jnp.concatenate(columns, axis=1).astype(BF16)
    for i in range(copies):
        w_out[i, :, 0 : chunk.shape[1]] = chunk
    row = lax.broadcasted_iota(jnp.int32, (8, x_head.shape[1]), 0)
    xt = x_tail[...].astype(F32)
    ct = c_tail[...].astype(F32)
    up[...] = jnp.where(
        row < 4, pltpu.roll(xt[8:16], 4, 0), jnp.where(row == 4, ct[15:16], 0.0)
    ).astype(BF16)
    xh = x_head[...].astype(F32)
    ch = c_head[...].astype(F32)
    down[...] = jnp.where(row < 4, xh[0:8], jnp.where(row == 4, ch[0:1], 0.0)).astype(BF16)


def setup(k1t, k2t, vectors, clips, features, cotangent, copies):
    frames, wide = features.shape
    halves = cotangent.shape[0]
    share = k1t.shape[0]
    w = (copies, share, padded(k1t.shape[1] + k2t.shape[1] + 4))
    whole = lambda shape: pl.BlockSpec(shape, lambda i: (0,) * len(shape))
    outs = [
        like(w, BF16), like((8, wide), BF16), like((8, wide), BF16), like(clips.shape, jnp.int32)
    ]
    return call(
        setup_body,
        (k1t, k2t, *vectors, clips, features, features, cotangent, cotangent),
        outs,
        limit=56,
        in_specs=[
            whole(k1t.shape),
            whole(k2t.shape),
            *[whole((1, share))] * 4,
            whole(clips.shape),
            pl.BlockSpec((16, wide), lambda i: (0, 0)),
            pl.BlockSpec((16, wide), lambda i: (frames // 16 - 1, 0)),
            pl.BlockSpec((16, wide), lambda i: (0, 0)),
            pl.BlockSpec((16, wide), lambda i: (halves // 16 - 1, 0)),
        ],
        out_specs=[whole(o.shape) for o in outs],
        grid=(1,),
    )


def emit_masks(copies, clips, masks):
    rows = masks.shape[1]
    half = rows - TAIL
    frames = 2 * half
    start = lax.axis_index(AXES) * frames
    place = lax.broadcasted_iota(jnp.int32, (rows, clips.shape[1]), 0)
    pair = jnp.where(place >= half + TAIL // 2, place - rows, place)
    frame = start + 2 * pair
    starts = jnp.broadcast_to(clips[...], (rows, clips.shape[1]))
    for slot, shift in ((0, 0), (1, 2)):
        hit = (frame + shift == starts) | (frame + shift >= frames * copies)
        begins = jnp.max(jnp.where(hit, 1.0, 0.0), axis=1, keepdims=True)
        masks[slot] = jnp.broadcast_to(1.0 - begins, (rows, LANES))


def emit_taps_one(fetch, x, up, down, masks, taps, frames):
    rows = masks.shape[1]
    half = rows - TAIL
    clear_ends(taps)
    row = lax.broadcasted_iota(jnp.int32, (8, LANES), 0)
    lead = 24
    own = 2 * half
    for b in range(2):
        frames[b, 0:16] = jnp.zeros((16, LANES), F32)
        frames[b, lead + own + 8 : lead + own + 24] = jnp.zeros((16, LANES), F32)

    def pair(j, b):
        lanes = pl.ds(pl.multiple_of(j * LANES, LANES), LANES)
        u = up[:, lanes].astype(F32)
        d = down[:, lanes].astype(F32)
        frames[b, lead - 8 : lead] = jnp.where(row >= 4, pltpu.roll(u, 4, 0), 0.0)
        frames[b, lead + own : lead + own + 8] = jnp.where(row < 4, d, 0.0)
        for r in tiles(own):
            frames[b, lead + r : lead + r + TILE] = x[r : r + TILE, lanes].astype(F32)

        def pick(first, count, shift):
            return frames[b, pl.ds(lead + 2 * first + shift, count, stride=2), :]

        for r in tiles(rows):
            parts = []
            for shift in (-1, 0, 1, 2):
                if r < half:
                    parts.append(pick(r, TILE, shift))
                else:
                    parts.append(
                        jnp.concatenate([pick(half, 8, shift), pick(-8, 8, shift)], axis=0)
                    )
            span = slice(r, r + TILE)
            parts[0] = parts[0] * masks[0, span]
            parts[3] = parts[3] * masks[1, span]
            taps[1 + j, span, :] = jnp.concatenate(parts, axis=1).astype(BF16)

    def two_pairs(i, carry):
        pair(2 * i, 0)
        pair(2 * i + 1, 1)
        return carry

    each = MEL // 4 // len(fetch)
    for k, copy in enumerate(fetch):
        copy.wait()
        lax.fori_loop(k * each, (k + 1) * each, two_pairs, 0)


def conv_one_body(row_count, features, up_in, down_in, clips_in, wg,
                  pre, stats, taps, masks, k1_out, k2_out, vec_out,
                  kf, w_even, w_odd, acc, frames, x, up, down, clips, sems, side_sems):
    sides = [
        pltpu.make_async_copy(here, there, side_sems.at[k])
        for k, (here, there) in enumerate(((clips_in, clips), (up_in, up), (down_in, down)))
    ]
    for copy in sides:
        copy.start()
    wide = x.shape[1] // sems.shape[0]
    fetch = []
    for k in range(sems.shape[0]):
        lanes = pl.ds(k * wide, wide)
        fetch.append(pltpu.make_async_copy(features.at[:, lanes], x.at[:, lanes], sems.at[k]))
        fetch[k].start()
    for copy in sides:
        copy.wait()
    emit_masks(wg.shape[0], clips, masks)
    emit_taps_one(fetch, x, up, down, masks, taps, frames)
    rows = taps.shape[1]
    half = rows - TAIL
    pairs = 4
    rows_one = 9 * C_IN // row_count
    rows_two = 9 * C_MID // row_count
    grps = wg.shape[0] // row_count
    for r in range(row_count):
        shard = [wg[g * row_count + r] for g in range(grps)]
        shard = jnp.concatenate(shard, axis=0).astype(F32).T
        kf[rows_one * r : rows_one * (r + 1)] = shard[0:rows_one]
        at = 9 * C_IN + rows_two * r
        kf[at : at + rows_two] = shard[rows_one : rows_one + rows_two]
        if r == 0:
            vec_out[...] = shard[rows_one + rows_two : rows_one + rows_two + 4]
    k1_out[...] = kf[0 : 9 * C_IN].astype(BF16)
    k2_out[...] = kf[9 * C_IN :].astype(BF16)
    w_even[...] = jnp.zeros(w_even.shape, BF16)
    w_odd[...] = jnp.zeros(w_odd.shape, BF16)
    placed = (
        (w_even, 0, 1, 0), (w_even, 1, 0, 1), (w_even, 1, 1, 2),
        (w_odd, 0, 0, 0), (w_odd, 0, 1, 1), (w_odd, 1, 0, 2),
    )
    for matrix, piece, side, d in placed:
        for q in range(4):
            for p in range(2):
                t = q - p
                if 0 <= t < 3:
                    at = piece * WIDE + q * 128 + side * 64
                    start = (3 * t + d) * C_IN
                    matrix[at : at + 64, p * 128 : p * 128 + 128] = k1_out[start : start + C_IN]
    acc[...] = jnp.zeros(acc.shape, F32)
    for c in range(MEL // 2 // pairs):
        left, mid, right = [
            taps[c * pairs + k : c * pairs + k + pairs].reshape(pairs * rows, WIDE) for k in range(3)
        ]
        for parity, lhs, matrix in (
            (0, jnp.concatenate([left, mid], axis=1), w_even),
            (1, jnp.concatenate([mid, right], axis=1), w_odd),
        ):
            out = jnp.dot(lhs, matrix[...], preferred_element_type=F32)
            out = out.reshape(pairs, rows, BOTH)
            mels = [2 * (c * pairs + q) + parity for q in range(pairs)]
            for q in range(pairs):
                pre[mels[q]] = out[q]
            stats_of(pre, mels, half, acc)
    spread(fold(acc[0]), fold(acc[1]), stats)


def conv_one(features, up, down, clips, wg, row_count):
    rows = features.shape[0] // 2 + TAIL
    copies = wg.shape[0]
    return call(
        lambda *refs: conv_one_body(row_count, *refs),
        (features, up, down, clips, wg),
        [
            like((MEL, rows, BOTH), F32),
            like((copies, 2, C_MID), F32),
            like((MEL // 2 + 2, rows, WIDE), BF16),
            like((2, rows, LANES), F32),
            like((9 * C_IN, C_MID), BF16),
            like((9 * C_MID, C_MID), BF16),
            like((4, C_MID), F32),
        ],
        [
            pltpu.VMEM((9 * (C_IN + C_MID), C_MID), F32),
            pltpu.VMEM((2 * WIDE, BOTH), BF16),
            pltpu.VMEM((2 * WIDE, BOTH), BF16),
            pltpu.VMEM((2, 8, BOTH), F32),
            pltpu.VMEM((2, features.shape[0] + 48, LANES), F32),
            pltpu.VMEM(features.shape, BF16),
            pltpu.VMEM(up.shape, BF16),
            pltpu.VMEM(down.shape, BF16),
            pltpu.VMEM(clips.shape, jnp.int32),
            pltpu.SemaphoreType.DMA((4,)),
            pltpu.SemaphoreType.DMA((3,)),
        ],
        in_specs=[HBM, HBM, HBM, HBM, VMEM],
    )


def place_two(k2, weight):
    weight[...] = jnp.zeros(weight.shape, BF16)
    for d in range(3):
        for q in range(4):
            for p in range(2):
                t = q - p
                if 0 <= t < 3:
                    at = d * WIDE + q * 128
                    start = (3 * t + d) * C_MID
                    weight[at : at + 128, p * 128 : p * 128 + 128] = k2[start : start + C_MID]


def place_two_back(k2, weight):
    weight[...] = jnp.zeros(weight.shape, BF16)
    for t in range(3):
        for d in range(3):
            start = (3 * t + d) * C_MID
            turned = k2[start : start + C_MID].astype(F32).T.astype(BF16)
            for p in range(2):
                at = (2 - d) * WIDE + (2 - t + p) * 128
                weight[at : at + 128, p * 128 : p * 128 + 128] = turned


def place_one_back(k1, weight):
    weight[...] = jnp.zeros(weight.shape, BF16)
    for t in range(3):
        for d in range(3):
            start = (3 * t + d) * C_IN
            turned = k1[start : start + C_IN].astype(F32).T.astype(BF16)
            for mo in (1, 2):
                for p in range(2):
                    at = (mo - d + 1) * WIDE + (2 - t + p) * 128
                    to = p * 128 + (mo - 1) * 64
                    weight[at : at + 128, to : to + 64] = turned


def conv_two_body(count, pre_one, stats_one, vec, masks, k2, pre, stats, taps, sums_out,
                  acc, weight, evens, odds):
    place_two(k2, weight)
    rows = masks.shape[1]
    half = rows - TAIL
    mels = 4
    sums = stat_sums(stats_one)
    sums_out[...] = sums
    mean, rstd = norm_terms(sums, count)
    scale = 0.5 * vec[0:1] * rstd
    shift = twice(0.5 * vec[1:2] - mean * scale)
    scale = twice(scale)
    clear_ends(taps)
    acc[...] = jnp.zeros(acc.shape, F32)

    def activate(m):
        def tile(r):
            h = pre_one[m, r : r + TILE] * scale + shift
            return halves_of(h + h * jnp.tanh(h))

        emit_taps(taps, 1 + m, masks, evens.at[m % 2], odds.at[m % 2], tile)

    def convolve(c):
        lhs = [taps[c * mels + d : (c + 1) * mels + d].reshape(mels * rows, WIDE) for d in range(3)]
        out = jnp.dot(jnp.concatenate(lhs, axis=1), weight[...], preferred_element_type=F32)
        pre[c * mels : (c + 1) * mels] = out.reshape(mels, rows, BOTH)
        stats_of(pre, range(c * mels, (c + 1) * mels), half, acc)

    for m in range(MEL):
        activate(m)
        if m >= mels and m % mels == 0:
            convolve(m // mels - 1)
    convolve(MEL // mels - 1)
    spread(fold(acc[0]), fold(acc[1]), stats)


def conv_two(pre_one, stats_one, vec, masks, k2, count):
    copies = stats_one.shape[0]
    rows = masks.shape[1]
    return call(
        lambda *refs: conv_two_body(count, *refs),
        (pre_one, stats_one, vec, masks, k2),
        [
            like((MEL, rows, BOTH), F32),
            like((copies, 2, C_MID), F32),
            like((MEL + 2, rows, WIDE), BF16),
            like((2, C_MID), F32),
        ],
        [pltpu.VMEM((2, 8, BOTH), F32), pltpu.VMEM((3 * WIDE, BOTH), BF16), *side_scratch(rows)],
    )


def norm_two_body(count, pre, stats_two, vec, cot, up, down, pooled, lift, back_stats, sums_out, acc):
    half = cot.shape[0]
    sums = stat_sums(stats_two)
    sums_out[...] = sums
    mean, rstd = norm_terms(sums, count)
    scale = 0.5 * vec[2:3] * rstd
    shift = 0.5 * vec[3:4] - mean * scale
    norm_shift = -mean * rstd
    acc[...] = jnp.zeros(acc.shape, F32)
    row = lax.broadcasted_iota(jnp.int32, (TAIL, LANES), 0)

    def pair(j, carry):
        lanes = pl.ds(pl.multiple_of(j * LANES, LANES), LANES)
        u = up[:, lanes].astype(F32)
        d = down[:, lanes].astype(F32)
        first = jnp.zeros((8, LANES), F32)
        second = jnp.zeros((8, LANES), F32)
        for r in tiles(half + TAIL):
            span = slice(r, r + TILE)
            if r < half:
                grad = cot[span, lanes].astype(F32) * 0.125
            else:
                grad = jnp.where(row == 0, d[4:5], jnp.where(row == TAIL - 1, u[4:5], 0.0)) * 0.125
            total = jnp.zeros((TILE, LANES), F32)
            for m in (2 * j, 2 * j + 1):
                for p in range(2):
                    side = slice(p * C_MID, (p + 1) * C_MID)
                    value = pre[m, span, side]
                    h = value * scale + shift
                    th = jnp.tanh(h)
                    one = 1.0 + th
                    gl = grad * (one * (1.0 + (h - h * th)))
                    lift[m, span, side] = gl
                    if r < half:
                        total += h * one
                        first += partial_sum(gl)
                        second += partial_sum(gl * (value * rstd + norm_shift))
            if r < half:
                pooled[span, lanes] = (total * 0.25).astype(BF16)
        add_sums(acc, first, second)
        return carry

    lax.fori_loop(0, MEL // 2, pair, 0)
    first, second = [jnp.sum(acc[k], axis=0, keepdims=True) for k in range(2)]
    spread(first, second, back_stats)


def norm_two(pre, stats_two, vec, cot, up, down, count):
    copies = stats_two.shape[0]
    half, wide = cot.shape
    return call(
        lambda *refs: norm_two_body(count, *refs),
        (pre, stats_two, vec, cot, up, down),
        [
            like((half, wide), BF16),
            like((MEL, half + TAIL, BOTH), F32),
            like((copies, 2, C_MID), F32),
            like((2, C_MID), F32),
        ],
        [pltpu.VMEM((2, 8, LANES), F32)],
    )


def grad_terms(sums, back, gain, count):
    mean, rstd = norm_terms(sums, count)
    a = gain * rstd
    b = -a * rstd * (back[1:2] / count)
    c = -a * (back[0:1] / count) - b * mean
    return twice(a), twice(b), twice(c)


def back_two_body(count, lift, pre_two, sums_two, back_stats, vec, masks, k2, pre_one, sums_one,
                  taps_a, lift_one, two, back_out, sums_out, acc, acc_two, taps, weight, evens, odds):
    place_two_back(k2, weight)
    rows = masks.shape[1]
    half = rows - TAIL
    mels = 4
    back = stat_sums(back_stats)
    sums_out[...] = back
    a, b, c = grad_terms(sums_two[...], back, vec[2:3], count)
    mean, rstd = norm_terms(sums_one[...], count)
    scale = 0.5 * vec[0:1] * rstd
    shift = twice(0.5 * vec[1:2] - mean * scale)
    scale = twice(scale)
    norm_shift = twice(-mean * rstd)
    rstd = twice(rstd)
    taps[taps.shape[0] - 1] = jnp.zeros(taps.shape[1:], BF16)
    acc[...] = jnp.zeros(acc.shape, F32)

    def lower(m):
        def tile(r):
            span = slice(r, r + TILE)
            return halves_of(lift[m, span] * a + (pre_two[m, span] * b + c))

        emit_taps(taps, ring_slot(taps, m), masks, evens.at[m % 2], odds.at[m % 2], tile)

    def convolve(k):
        lhs = [stack(taps, range(k * mels + d - 1, (k + 1) * mels + d - 1), rows) for d in range(3)]
        out = jnp.dot(jnp.concatenate(lhs, axis=1), weight[...], preferred_element_type=F32)
        lift_one[k * mels : (k + 1) * mels] = out.reshape(mels, rows, BOTH)
        first = jnp.zeros((8, BOTH), F32)
        second = jnp.zeros((8, BOTH), F32)
        for m in range(k * mels, (k + 1) * mels):
            for r in range(0, rows, 8):
                span = slice(r, r + 8)
                value = pre_one[m, span]
                h = value * scale + shift
                th = jnp.tanh(h)
                gl = lift_one[m, span] * (0.5 * (1.0 + th) * (1.0 + (h - h * th)))
                lift_one[m, span] = gl
                if r < half:
                    first += gl
                    second += gl * (value * rstd + norm_shift)
        add_sums(acc, first, second)

    def correlate(k):
        here = range(k * mels, (k + 1) * mels)
        near = [
            taps_a[k * mels + d : (k + 1) * mels + d, 0:half].reshape(mels * half, WIDE) for d in range(3)
        ]
        total = dot_rows(stack(taps, here, half, slice(128, 384)), jnp.concatenate(near, axis=1))
        if k == 0:
            acc_two[...] = total
        else:
            acc_two[...] += total

    for k in range(MEL // mels + 1):
        for m in range(k * mels, (k + 1) * mels):
            if m < MEL:
                lower(m)
        if k > 0:
            convolve(k - 1)
            correlate(k - 1)
    spread(fold(acc[0]), fold(acc[1]), back_out)
    for t in range(3):
        for d in range(3):
            at = d * WIDE + t * 128
            to = (3 * t + d) * 128
            two[:, to : to + 128] = (
                acc_two[0:C_MID, at : at + 128] + acc_two[C_MID:BOTH, at + 128 : at + 256]
            )


def back_two(lift, pre_two, sums_two, back_stats, vec, masks, k2, pre_one, sums_one, taps_a, count):
    copies = back_stats.shape[0]
    rows = masks.shape[1]
    return call(
        lambda *refs: back_two_body(count, *refs),
        (lift, pre_two, sums_two, back_stats, vec, masks, k2, pre_one, sums_one, taps_a),
        [
            like((MEL, rows, BOTH), F32),
            like((C_MID, 9 * C_MID), F32),
            like((copies, 2, C_MID), F32),
            like((2, C_MID), F32),
        ],
        [
            pltpu.VMEM((2, 8, BOTH), F32),
            pltpu.VMEM((BOTH, 3 * WIDE), F32),
            pltpu.VMEM((17, rows, WIDE), BF16),
            pltpu.VMEM((3 * WIDE, BOTH), BF16),
            *side_scratch(rows),
        ],

        input_output_aliases={0: 0},
    )


def scatter_blocks(out, parts):
    copies, share, wide = out.shape
    grps = C_MID // share
    row_count = copies // grps
    turned = [part.T for part in parts]
    sizes = [part.shape[1] // row_count for part in parts]
    blank = jnp.zeros((wide - sum(sizes), C_MID), F32)
    for r in range(row_count):
        rows = [t[n * r : n * (r + 1)] for t, n in zip(turned, sizes)]
        back = jnp.concatenate([*rows, blank], axis=0).T.astype(BF16)
        for g in range(grps):
            out[g * row_count + r] = back[share * g : share * (g + 1)]


def kernel_one_step(taps_x, taps, acc, k, pairs):
    half = taps.shape[1]
    near = [
        taps_x[k * pairs + i : (k + 1) * pairs + i, 0:half].reshape(pairs * half, WIDE)
        for i in range(3)
    ]
    for parity in range(2):
        mels = [2 * (k * pairs + q) + parity for q in range(pairs)]
        total = dot_rows(
            stack(taps, mels, half, slice(128, 384)), jnp.concatenate(near[parity : parity + 2], axis=1)
        )
        if k == 0:
            acc[parity] = total
        else:
            acc[parity] += total


def kernel_one_sums(acc):
    pieces = []
    for t in range(3):
        for d in range(3):
            total = jnp.zeros((C_MID, C_IN), F32)
            for parity in range(2):
                place = 2 * (1 - parity) + parity + d - 1
                for p in range(2):
                    at = (place // 2) * WIDE + (t + p) * 128 + (place % 2) * 64
                    total += acc[parity, p * 128 : p * 128 + 128, at : at + 64]
            pieces.append(total)
    return jnp.concatenate(pieces, axis=1)


def features_step(taps, weight, out, woven, sems, k, pairs, copies):
    half = taps.shape[1]
    slots = woven.shape[0]
    near = [
        stack(taps, [2 * (k * pairs + q) + i - 1 for q in range(pairs)], half) for i in range(4)
    ]
    part = jnp.dot(jnp.concatenate(near, axis=1), weight[...], preferred_element_type=F32)
    for q in range(pairs):
        j = k * pairs + q
        b = j % slots
        rows = slice(q * half, (q + 1) * half)
        if j >= slots:
            copies[j - slots].wait()
        woven[b, pl.ds(0, half, stride=2), :] = part[rows, 0:128]
        woven[b, pl.ds(1, half, stride=2), :] = part[rows, 128:256]
        copy = pltpu.make_async_copy(woven.at[b], out.at[:, pl.ds(j * LANES, LANES)], sems.at[b])
        copy.start()
        copies.append(copy)


def grads_body(count, lift, pre_one, sums_one, back_stats, vec, masks, k1, taps_x, two,
               grad_x, blocks, sums_out, weight, taps, acc_one, evens, odds, woven, sems):
    place_one_back(k1, weight)
    back = stat_sums(back_stats)
    sums_out[...] = back
    a, b, c = grad_terms(sums_one[...], back, vec[0:1], count)
    taps[taps.shape[0] - 1] = jnp.zeros(taps.shape[1:], BF16)

    def lower(m):
        def tile(r):
            span = slice(r, r + TILE)
            return halves_of(lift[m, span] * a + (pre_one[m, span] * b + c))

        emit_taps(taps, ring_slot(taps, m), masks, evens.at[m % 2], odds.at[m % 2], tile)

    pairs = 4
    copies = []
    for k in range(MEL // 2 // pairs + 1):
        for m in range(2 * pairs * k, 2 * pairs * (k + 1)):
            if m < MEL:
                lower(m)
        if k > 0:
            kernel_one_step(taps_x, taps, acc_one, k - 1, pairs)
            features_step(taps, weight, grad_x, woven, sems, k - 1, pairs, copies)
    scatter_blocks(blocks, [kernel_one_sums(acc_one), two[...]])
    for copy in copies[-woven.shape[0] :]:
        copy.wait()


def all_grads(lift, pre_one, sums_one, back_stats, vec, masks, k1, taps_x, two, share, count):
    copies = back_stats.shape[0]
    half = masks.shape[1] - TAIL
    row_count = copies * share // C_MID
    wide = padded(9 * (C_IN + C_MID) // row_count)
    args = (lift, pre_one, sums_one, back_stats, vec, masks, k1, taps_x, two)
    return call(
        lambda *refs: grads_body(count, *refs),
        args,
        [
            like((2 * half, MEL * C_IN), F32),
            like((copies, share, wide), BF16),
            like((2, C_MID), F32),
        ],
        [
            pltpu.VMEM((4 * WIDE, BOTH), BF16),
            pltpu.VMEM((27, half, WIDE), BF16),
            pltpu.VMEM((2, BOTH, 2 * WIDE), F32),
            *side_scratch(half + TAIL),
            pltpu.VMEM((8, 2 * half, LANES), F32),
            pltpu.SemaphoreType.DMA((8,)),
        ],

        out_specs=[ANY, VMEM, VMEM],
    )


def finish_body(got, back_one_sums, back_two_sums, own_one, own_two, ga, sa, gb, sb):
    total = jnp.sum(got[...].astype(F32), axis=0)
    size = own_one.shape[1]
    own_one[...] = total[:, 0:size]
    own_two[...] = total[:, size : size + own_two.shape[1]]
    share = ga.shape[1]
    lane = lax.broadcasted_iota(jnp.int32, (share, C_MID), 1)
    row = lax.broadcasted_iota(jnp.int32, (share, C_MID), 0)
    chosen = lane == lax.axis_index("grp") * share + row
    first = lax.broadcasted_iota(jnp.int32, (share, share), 0)
    second = lax.broadcasted_iota(jnp.int32, (share, share), 1)
    for out, sums, k in (
        (ga, back_one_sums, 1), (sa, back_one_sums, 0), (gb, back_two_sums, 1), (sb, back_two_sums, 0)
    ):
        wide = jnp.broadcast_to(sums[k : k + 1], (share, C_MID))
        column = jnp.sum(jnp.where(chosen, wide, 0.0), axis=1, keepdims=True)
        wide = jnp.broadcast_to(column, (share, share))
        out[...] = jnp.sum(jnp.where(first == second, wide, 0.0), axis=0, keepdims=True)


def finish(got, back_one_sums, back_two_sums, rows_one, rows_two):
    share = got.shape[1]
    shapes = [(share, rows_one), (share, rows_two)] + [(1, share)] * 4
    return call(
        finish_body,
        (got, back_one_sums, back_two_sums),
        [like(s, F32) for s in shapes],
    )


def exchange(blocks):
    return lax.all_to_all(blocks, AXES, 0, 0, tiled=True)


def shards(
    features, clip_starts, kernel_one, kernel_two, gain_one, shift_one, gain_two, shift_two, cotangent
):
    frames = features.shape[0]
    copies = lax.axis_size(AXES)
    row_count = lax.axis_size("row")
    count = float(frames * MEL * copies)
    rows_one, rows_two = kernel_one.shape[0], kernel_two.shape[0]
    share = kernel_one.shape[1]
    vectors = [v.reshape(1, share) for v in (gain_one, shift_one, gain_two, shift_two)]
    clips = clip_starts.reshape(1, -1)
    weights, up, down, clips = setup(
        kernel_one.T, kernel_two.T, vectors, clips, features, cotangent, copies
    )
    ends = copies - 1
    up = lax.ppermute(up, AXES, [(i, i + 1) for i in range(ends)])
    down = lax.ppermute(down, AXES, [(i + 1, i) for i in range(ends)])
    weights = exchange(weights)
    pre_one, stats, taps_x, masks, k1, k2, vec = conv_one(
        features, up, down, clips, weights, row_count
    )
    stats = exchange(stats)
    pre_two, stats, taps_a, sums_one = conv_two(pre_one, stats, vec, masks, k2, count)
    stats = exchange(stats)
    block_out, lift, stats, sums_two = norm_two(pre_two, stats, vec, cotangent, up, down, count)
    stats = exchange(stats)
    lift, two, stats, back_two_sums = back_two(
        lift, pre_two, sums_two, stats, vec, masks, k2, pre_one, sums_one, taps_a, count
    )
    stats = exchange(stats)
    grad_features, blocks, back_one_sums = all_grads(
        lift, pre_one, sums_one, stats, vec, masks, k1, taps_x, two, share, count
    )
    own_one, own_two, ga, sa, gb, sb = finish(
        exchange(blocks), back_one_sums, back_two_sums, rows_one, rows_two
    )
    return (
        block_out,
        grad_features,
        own_one.T,
        own_two.T,
        ga.reshape(share),
        sa.reshape(share),
        gb.reshape(share),
        sb.reshape(share),
    )


def solution(mesh):
    placed = (
        P(AXES, None), P(), P("row", "grp"), P("row", "grp"),
        P("grp"), P("grp"), P("grp"), P("grp"), P(AXES, None),
    )
    return jax.shard_map(
        shards,
        mesh=mesh,
        in_specs=placed,
        out_specs=(
            P(AXES, None), P(AXES, None), P("row", "grp"), P("row", "grp"),
            P("grp"), P("grp"), P("grp"), P("grp"),
        ),
        check_vma=False,
    )
```

```python
import jax
import jax.numpy as jnp
from jax import lax
from jax.experimental import pallas as pl
from jax.experimental.pallas import tpu as pltpu
from jax.sharding import PartitionSpec as P

MEL = 32
C_IN = 64
C_MID = 128
EPS = 1e-05
AXES = ("grp", "row")
LANES = 128
TAIL = 16
WIDE = 4 * LANES
BOTH = 2 * C_MID
F32 = jnp.float32
BF16 = jnp.bfloat16
TILE = 16
MIB = 2**20

VMEM = pl.BlockSpec(memory_space=pltpu.VMEM)
ANY = pl.BlockSpec(memory_space=pl.ANY)
HBM = pl.BlockSpec(memory_space=pltpu.HBM)


def like(shape, dtype):
    return jax.ShapeDtypeStruct(shape, dtype)


def call(body, args, outs, scratch=(), limit=16, fuse=False, in_specs=None, out_specs=None, **more):
    return pl.pallas_call(
        body,
        in_specs=in_specs or [VMEM] * len(args),
        out_specs=out_specs or [VMEM] * len(outs),
        out_shape=outs,
        scratch_shapes=list(scratch),
        compiler_params=pltpu.CompilerParams(
            vmem_limit_bytes=limit * MIB, fuse_transposed_lhs_in_matmul=fuse
        ),
        **more,
    )(*args)


def padded(size):
    return -(-size // LANES) * LANES


def partial_sum(values):
    return jnp.sum(values.reshape(-1, 8, values.shape[-1]), axis=0)


def fold(values):
    total = jnp.sum(values, axis=0, keepdims=True)
    return total[:, :C_MID] + total[:, C_MID:]


def spread(first, second, out):
    sums = jnp.concatenate([first, second], axis=0)
    out[...] = jnp.broadcast_to(sums[None], out.shape)


def twice(row):
    return jnp.concatenate([row, row], axis=1)


def tiles(rows):
    return range(0, rows, TILE)


def emit_taps(taps, slot, masks, evens, odds, tile_of):
    rows = masks.shape[1]
    kept = taps.shape[1]
    for r in tiles(rows):
        even, odd = tile_of(r)
        evens[r : r + TILE] = even
        odds[8 + r : 8 + r + TILE] = odd
        if r == 0:
            evens[rows : rows + 1] = even[0:1]
        if r + TILE == rows:
            odds[7:8] = odd[TILE - 1 : TILE]
        if r < kept:
            taps[slot, r : r + TILE, 128:256] = even.astype(BF16)
            taps[slot, r : r + TILE, 256:384] = odd.astype(BF16)
    for r in tiles(kept):
        span = slice(r, r + TILE)
        before = odds[7 + r : 7 + r + TILE] * masks[0, span]
        after = evens[1 + r : 1 + r + TILE] * masks[1, span]
        taps[slot, span, 0:128] = before.astype(BF16)
        taps[slot, span, 384:512] = after.astype(BF16)


def halves_of(value):
    return value[:, :C_MID], value[:, C_MID:]


def add_sums(acc, first, second):
    acc[0] += first
    acc[1] += second


def side_scratch(rows):
    return [pltpu.VMEM((2, rows + 8, LANES), F32), pltpu.VMEM((2, rows + 8, LANES), F32)]


def stats_of(out, mels, rows, half, acc):
    first = jnp.zeros((8, BOTH), F32)
    second = jnp.zeros((8, BOTH), F32)
    for k in range(mels):
        for r in range(0, half, 8):
            value = out[k * rows + r : k * rows + r + 8]
            first += value
            second += value * value
    add_sums(acc, first, second)


def normed_sum(with_half_lifted, plain, gain, shift):
    return (2.0 * with_half_lifted - shift * plain) / gain


def stat_sums(stats):
    return jnp.sum(stats[...], axis=0)


def norm_terms(sums, count):
    mean = sums[0:1] / count
    rstd = lax.rsqrt(sums[1:2] / count - mean * mean + EPS)
    return mean, rstd


def dot_rows(first, second):
    return lax.dot_general(
        first, second, (((0,), (0,)), ((), ())), preferred_element_type=F32
    )


def ring_slot(taps, m):
    last = taps.shape[0] - 1
    return m % last if 0 <= m < MEL else last


def stack(taps, mels, rows, lanes=slice(None)):
    parts = [taps[ring_slot(taps, m), 0:rows, lanes] for m in mels]
    return jnp.concatenate(parts, axis=0)


def clear_ends(taps):
    blank = jnp.zeros(taps.shape[1:], BF16)
    taps[0] = blank
    taps[taps.shape[0] - 1] = blank


def setup_body(k1, k2, ga, sa, gb, sb, clips, x_head, x_tail, c_head, c_tail, w_out, up, down, clips_out):
    clips_out[...] = clips[...]
    share = k1.shape[0]
    copies = w_out.shape[0]
    w_out[...] = jnp.zeros(w_out.shape, BF16)
    first = lax.broadcasted_iota(jnp.int32, (share, share), 0)
    second = lax.broadcasted_iota(jnp.int32, (share, share), 1)
    columns = [k1[...].astype(F32), k2[...].astype(F32)]
    for vector in (ga, sa, gb, sb):
        wide = jnp.broadcast_to(vector[...].astype(F32), (share, share))
        columns.append(jnp.sum(jnp.where(first == second, wide, 0.0), axis=1, keepdims=True))
    chunk = jnp.concatenate(columns, axis=1).astype(BF16)
    for i in range(copies):
        w_out[i, :, 0 : chunk.shape[1]] = chunk
    row = lax.broadcasted_iota(jnp.int32, (8, x_head.shape[1]), 0)
    xt = x_tail[...].astype(F32)
    ct = c_tail[...].astype(F32)
    up[...] = jnp.where(
        row < 4, pltpu.roll(xt[8:16], 4, 0), jnp.where(row == 4, ct[15:16], 0.0)
    ).astype(BF16)
    xh = x_head[...].astype(F32)
    ch = c_head[...].astype(F32)
    down[...] = jnp.where(row < 4, xh[0:8], jnp.where(row == 4, ch[0:1], 0.0)).astype(BF16)


def setup(k1t, k2t, vectors, clips, features, cotangent, copies):
    frames, wide = features.shape
    halves = cotangent.shape[0]
    share = k1t.shape[0]
    w = (copies, share, padded(k1t.shape[1] + k2t.shape[1] + 4))
    whole = lambda shape: pl.BlockSpec(shape, lambda i: (0,) * len(shape))
    outs = [
        like(w, BF16), like((8, wide), BF16), like((8, wide), BF16), like(clips.shape, jnp.int32)
    ]
    return call(
        setup_body,
        (k1t, k2t, *vectors, clips, features, features, cotangent, cotangent),
        outs,
        limit=56,
        in_specs=[
            whole(k1t.shape),
            whole(k2t.shape),
            *[whole((1, share))] * 4,
            whole(clips.shape),
            pl.BlockSpec((16, wide), lambda i: (0, 0)),
            pl.BlockSpec((16, wide), lambda i: (frames // 16 - 1, 0)),
            pl.BlockSpec((16, wide), lambda i: (0, 0)),
            pl.BlockSpec((16, wide), lambda i: (halves // 16 - 1, 0)),
        ],
        out_specs=[whole(o.shape) for o in outs],
        grid=(1,),
    )


def emit_masks(copies, clips, masks):
    rows = masks.shape[1]
    half = rows - TAIL
    frames = 2 * half
    start = lax.axis_index(AXES) * frames
    place = lax.broadcasted_iota(jnp.int32, (rows, clips.shape[1]), 0)
    pair = jnp.where(place >= half + TAIL // 2, place - rows, place)
    frame = start + 2 * pair
    starts = jnp.broadcast_to(clips[...], (rows, clips.shape[1]))
    for slot, shift in ((0, 0), (1, 2)):
        hit = (frame + shift == starts) | (frame + shift >= frames * copies)
        begins = jnp.max(jnp.where(hit, 1.0, 0.0), axis=1, keepdims=True)
        masks[slot] = jnp.broadcast_to(1.0 - begins, (rows, LANES))


def split_bins(parts):
    low = lax.broadcasted_iota(jnp.int32, parts[0].shape, 1) < C_IN
    first, second = [], []
    for here, there in (parts[0:2], parts[2:4]):
        first.append(jnp.where(low, here, pltpu.roll(there, C_IN, 1)))
        second.append(jnp.where(low, pltpu.roll(here, C_IN, 1), there))
    return jnp.concatenate(first + second, axis=1)


def near_bins(taps, pairs, rows):
    left, mid, right = [
        jnp.concatenate([taps[1 + j + k, 0:rows] for j in pairs], axis=0) for k in (-1, 0, 1)
    ]
    first = jnp.concatenate([left[:, BOTH:], mid], axis=1)
    second = jnp.concatenate([mid, right[:, :BOTH]], axis=1)
    return jnp.concatenate([first, second], axis=0)


def emit_taps_one(fetch, x, up, down, masks, taps, frames):
    rows = masks.shape[1]
    half = rows - TAIL
    clear_ends(taps)
    row = lax.broadcasted_iota(jnp.int32, (8, LANES), 0)
    lead = 24
    own = 2 * half
    for b in range(2):
        frames[b, 0:16] = jnp.zeros((16, LANES), F32)
        frames[b, lead + own + 8 : lead + own + 24] = jnp.zeros((16, LANES), F32)

    def pair(j, b):
        lanes = pl.ds(pl.multiple_of(j * LANES, LANES), LANES)
        u = up[:, lanes].astype(F32)
        d = down[:, lanes].astype(F32)
        frames[b, lead - 8 : lead] = jnp.where(row >= 4, pltpu.roll(u, 4, 0), 0.0)
        frames[b, lead + own : lead + own + 8] = jnp.where(row < 4, d, 0.0)
        for r in tiles(own):
            frames[b, lead + r : lead + r + TILE] = x[r : r + TILE, lanes].astype(F32)

        def pick(first, count, shift):
            return frames[b, pl.ds(lead + 2 * first + shift, count, stride=2), :]

        for r in tiles(rows):
            parts = []
            for shift in (-1, 0, 1, 2):
                if r < half:
                    parts.append(pick(r, TILE, shift))
                else:
                    parts.append(
                        jnp.concatenate([pick(half, 8, shift), pick(-8, 8, shift)], axis=0)
                    )
            span = slice(r, r + TILE)
            parts[0] = parts[0] * masks[0, span]
            parts[3] = parts[3] * masks[1, span]
            taps[1 + j, span, :] = split_bins(parts).astype(BF16)

    def two_pairs(i, carry):
        pair(2 * i, 0)
        pair(2 * i + 1, 1)
        return carry

    each = MEL // 4 // len(fetch)
    for k, copy in enumerate(fetch):
        copy.wait()
        lax.fori_loop(k * each, (k + 1) * each, two_pairs, 0)


def conv_one_body(row_count, features, up_in, down_in, clips_in, wg,
                  pre, stats, taps, masks, k1_out, k2_out, vec_out,
                  kf, weight, acc, frames, x, up, down, clips, sems, side_sems):
    sides = [
        pltpu.make_async_copy(here, there, side_sems.at[k])
        for k, (here, there) in enumerate(((clips_in, clips), (up_in, up), (down_in, down)))
    ]
    for copy in sides:
        copy.start()
    wide = x.shape[1] // sems.shape[0]
    fetch = []
    for k in range(sems.shape[0]):
        lanes = pl.ds(k * wide, wide)
        fetch.append(pltpu.make_async_copy(features.at[:, lanes], x.at[:, lanes], sems.at[k]))
        fetch[k].start()
    for copy in sides:
        copy.wait()
    emit_masks(wg.shape[0], clips, masks)
    emit_taps_one(fetch, x, up, down, masks, taps, frames)
    rows = taps.shape[1]
    half = rows - TAIL
    pairs = 4
    rows_one = 9 * C_IN // row_count
    rows_two = 9 * C_MID // row_count
    grps = wg.shape[0] // row_count
    for r in range(row_count):
        shard = [wg[g * row_count + r] for g in range(grps)]
        shard = jnp.concatenate(shard, axis=0).astype(F32).T
        kf[rows_one * r : rows_one * (r + 1)] = shard[0:rows_one]
        at = 9 * C_IN + rows_two * r
        kf[at : at + rows_two] = shard[rows_one : rows_one + rows_two]
        if r == 0:
            vec_out[...] = shard[rows_one + rows_two : rows_one + rows_two + 4]
    k1_out[...] = kf[0 : 9 * C_IN].astype(BF16)
    k2_out[...] = kf[9 * C_IN :].astype(BF16)
    weight[...] = jnp.zeros(weight.shape, BF16)
    for d in range(3):
        for q in range(4):
            for p in range(2):
                t = q - p
                if 0 <= t < 3:
                    at = d * BOTH + q * C_IN
                    start = (3 * t + d) * C_IN
                    weight[at : at + C_IN, p * 128 : p * 128 + 128] = k1_out[start : start + C_IN]
    acc[...] = jnp.zeros(acc.shape, F32)
    for c in range(MEL // 2 // pairs):
        here = range(c * pairs, (c + 1) * pairs)
        out = jnp.dot(near_bins(taps, here, rows), weight[...], preferred_element_type=F32)
        for parity in range(2):
            for q in range(pairs):
                at = (parity * pairs + q) * rows
                pre[2 * (c * pairs + q) + parity] = out[at : at + rows]
        stats_of(out, 2 * pairs, rows, half, acc)
    spread(fold(acc[0]), fold(acc[1]), stats)


def conv_one(features, up, down, clips, wg, row_count):
    rows = features.shape[0] // 2 + TAIL
    copies = wg.shape[0]
    return call(
        lambda *refs: conv_one_body(row_count, *refs),
        (features, up, down, clips, wg),
        [
            like((MEL, rows, BOTH), F32),
            like((copies, 2, C_MID), F32),
            like((MEL // 2 + 2, rows, WIDE), BF16),
            like((2, rows, LANES), F32),
            like((9 * C_IN, C_MID), BF16),
            like((9 * C_MID, C_MID), BF16),
            like((4, C_MID), F32),
        ],
        [
            pltpu.VMEM((9 * (C_IN + C_MID), C_MID), F32),
            pltpu.VMEM((3 * BOTH, BOTH), BF16),
            pltpu.VMEM((2, 8, BOTH), F32),
            pltpu.VMEM((2, features.shape[0] + 48, LANES), F32),
            pltpu.VMEM(features.shape, BF16),
            pltpu.VMEM(up.shape, BF16),
            pltpu.VMEM(down.shape, BF16),
            pltpu.VMEM(clips.shape, jnp.int32),
            pltpu.SemaphoreType.DMA((4,)),
            pltpu.SemaphoreType.DMA((3,)),
        ],
        in_specs=[HBM, HBM, HBM, HBM, VMEM],
    )


def place_two(k2, weight):
    weight[...] = jnp.zeros(weight.shape, BF16)
    for d in range(3):
        for q in range(4):
            for p in range(2):
                t = q - p
                if 0 <= t < 3:
                    at = d * WIDE + q * 128
                    start = (3 * t + d) * C_MID
                    weight[at : at + 128, p * 128 : p * 128 + 128] = k2[start : start + C_MID]


def place_two_back(k2, weight):
    weight[...] = jnp.zeros(weight.shape, BF16)
    for t in range(3):
        for d in range(3):
            start = (3 * t + d) * C_MID
            turned = (0.5 * k2[start : start + C_MID].astype(F32).T).astype(BF16)
            for p in range(2):
                at = (2 - d) * WIDE + (2 - t + p) * 128
                weight[at : at + 128, p * 128 : p * 128 + 128] = turned


def place_one_back(k1, weight):
    weight[...] = jnp.zeros(weight.shape, BF16)
    for t in range(3):
        for d in range(3):
            start = (3 * t + d) * C_IN
            turned = k1[start : start + C_IN].astype(F32).T.astype(BF16)
            for mo in (1, 2):
                for p in range(2):
                    at = (mo - d + 1) * WIDE + (2 - t + p) * 128
                    to = p * 128 + (mo - 1) * 64
                    weight[at : at + 128, to : to + 64] = turned


def conv_two_body(count, pre_one, stats_one, vec, masks, k2, pre, stats, taps, sums_out,
                  acc, weight, evens, odds):
    place_two(k2, weight)
    rows = masks.shape[1]
    half = rows - TAIL
    mels = 2
    sums = stat_sums(stats_one)
    sums_out[...] = sums
    mean, rstd = norm_terms(sums, count)
    scale = 0.5 * vec[0:1] * rstd
    shift = twice(0.5 * vec[1:2] - mean * scale)
    scale = twice(scale)
    clear_ends(taps)
    acc[...] = jnp.zeros(acc.shape, F32)

    def activate(m):
        def tile(r):
            h = pre_one[m, r : r + TILE] * scale + shift
            return halves_of(h + h * jnp.tanh(h))

        emit_taps(taps, 1 + m, masks, evens.at[m % 2], odds.at[m % 2], tile)

    def convolve(c):
        lhs = [taps[c * mels + d : (c + 1) * mels + d].reshape(mels * rows, WIDE) for d in range(3)]
        out = jnp.dot(jnp.concatenate(lhs, axis=1), weight[...], preferred_element_type=F32)
        pre[c * mels : (c + 1) * mels] = out.reshape(mels, rows, BOTH)
        stats_of(out, mels, rows, half, acc)

    for m in range(MEL):
        activate(m)
        if m >= mels and m % mels == 0:
            convolve(m // mels - 1)
    convolve(MEL // mels - 1)
    spread(fold(acc[0]), fold(acc[1]), stats)


def conv_two(pre_one, stats_one, vec, masks, k2, count):
    copies = stats_one.shape[0]
    rows = masks.shape[1]
    return call(
        lambda *refs: conv_two_body(count, *refs),
        (pre_one, stats_one, vec, masks, k2),
        [
            like((MEL, rows, BOTH), F32),
            like((copies, 2, C_MID), F32),
            like((MEL + 2, rows, WIDE), BF16),
            like((2, C_MID), F32),
        ],
        [pltpu.VMEM((2, 8, BOTH), F32), pltpu.VMEM((3 * WIDE, BOTH), BF16), *side_scratch(rows)],
    )


def norm_two_body(count, pre, stats_two, vec, cot, up, down, pooled, lift, back_stats, sums_out, acc):
    half = cot.shape[0]
    sums = stat_sums(stats_two)
    sums_out[...] = sums
    mean, rstd = norm_terms(sums, count)
    scale = 0.5 * vec[2:3] * rstd
    shift = 0.5 * vec[3:4] - mean * scale
    acc[...] = jnp.zeros(acc.shape, F32)
    row = lax.broadcasted_iota(jnp.int32, (TAIL, LANES), 0)

    def pair(j, carry):
        lanes = pl.ds(pl.multiple_of(j * LANES, LANES), LANES)
        u = up[:, lanes].astype(F32)
        d = down[:, lanes].astype(F32)
        first = jnp.zeros((8, LANES), F32)
        second = jnp.zeros((8, LANES), F32)
        for r in tiles(half + TAIL):
            span = slice(r, r + TILE)
            if r < half:
                grad = cot[span, lanes].astype(F32) * 0.125
            else:
                grad = jnp.where(row == 0, d[4:5], jnp.where(row == TAIL - 1, u[4:5], 0.0)) * 0.125
            total = jnp.zeros((TILE, LANES), F32)
            for m in (2 * j, 2 * j + 1):
                for p in range(2):
                    side = slice(p * C_MID, (p + 1) * C_MID)
                    value = pre[m, span, side]
                    h = value * scale + shift
                    th = jnp.tanh(h)
                    one = 1.0 + th
                    silu = h * one
                    gl = grad * (one + (silu - silu * th))
                    lift[m, span, side] = gl
                    if r < half:
                        total += silu
                        first += partial_sum(gl)
                        second += partial_sum(gl * h)
            if r < half:
                pooled[span, lanes] = (total * 0.25).astype(BF16)
        add_sums(acc, first, second)
        return carry

    lax.fori_loop(0, MEL // 2, pair, 0)
    first, second = [jnp.sum(acc[k], axis=0, keepdims=True) for k in range(2)]
    spread(first, normed_sum(second, first, vec[2:3], vec[3:4]), back_stats)


def norm_two(pre, stats_two, vec, cot, up, down, count):
    copies = stats_two.shape[0]
    half, wide = cot.shape
    return call(
        lambda *refs: norm_two_body(count, *refs),
        (pre, stats_two, vec, cot, up, down),
        [
            like((half, wide), BF16),
            like((MEL, half + TAIL, BOTH), F32),
            like((copies, 2, C_MID), F32),
            like((2, C_MID), F32),
        ],
        [pltpu.VMEM((2, 8, LANES), F32)],
    )


def grad_terms(sums, back, gain, count):
    mean, rstd = norm_terms(sums, count)
    a = gain * rstd
    b = -a * rstd * (back[1:2] / count)
    c = -a * (back[0:1] / count) - b * mean
    return twice(a), twice(b), twice(c)


def back_two_body(count, lift, pre_two, sums_two, back_stats, vec, masks, k2, pre_one, sums_one,
                  taps_a, lift_one, two, back_out, sums_out, acc, acc_two, taps, weight, evens, odds):
    place_two_back(k2, weight)
    rows = masks.shape[1]
    half = rows - TAIL
    mels = 4
    back = stat_sums(back_stats)
    sums_out[...] = back
    a, b, c = grad_terms(sums_two[...], back, vec[2:3], count)
    mean, rstd = norm_terms(sums_one[...], count)
    scale = 0.5 * vec[0:1] * rstd
    shift = twice(0.5 * vec[1:2] - mean * scale)
    scale = twice(scale)
    taps[taps.shape[0] - 1] = jnp.zeros(taps.shape[1:], BF16)
    acc[...] = jnp.zeros(acc.shape, F32)

    def lower(m):
        def tile(r):
            span = slice(r, r + TILE)
            return halves_of(lift[m, span] * a + (pre_two[m, span] * b + c))

        emit_taps(taps, ring_slot(taps, m), masks, evens.at[m % 2], odds.at[m % 2], tile)

    def convolve(k):
        lhs = [stack(taps, range(k * mels + d - 1, (k + 1) * mels + d - 1), rows) for d in range(3)]
        out = jnp.dot(jnp.concatenate(lhs, axis=1), weight[...], preferred_element_type=F32)
        first = jnp.zeros((8, BOTH), F32)
        second = jnp.zeros((8, BOTH), F32)
        for i in range(mels):
            m = k * mels + i
            for r in range(0, rows, 8):
                span = slice(r, r + 8)
                h = pre_one[m, span] * scale + shift
                th = jnp.tanh(h)
                one = 1.0 + th
                silu = h * one
                gl = out[i * rows + r : i * rows + r + 8] * (one + (silu - silu * th))
                lift_one[m, span] = gl
                if r < half:
                    first += gl
                    second += gl * h
        add_sums(acc, first, second)

    def correlate(k):
        here = range(k * mels, (k + 1) * mels)
        near = [
            taps_a[k * mels + d : (k + 1) * mels + d, 0:half].reshape(mels * half, WIDE) for d in range(3)
        ]
        total = dot_rows(stack(taps, here, half, slice(128, 384)), jnp.concatenate(near, axis=1))
        if k == 0:
            acc_two[...] = total
        else:
            acc_two[...] += total

    for k in range(MEL // mels + 1):
        for m in range(k * mels, (k + 1) * mels):
            if m < MEL:
                lower(m)
        if k > 0:
            convolve(k - 1)
            correlate(k - 1)
    plain = fold(acc[0])
    spread(plain, normed_sum(fold(acc[1]), plain, vec[0:1], vec[1:2]), back_out)
    for t in range(3):
        for d in range(3):
            at = d * WIDE + t * 128
            to = (3 * t + d) * 128
            two[:, to : to + 128] = (
                acc_two[0:C_MID, at : at + 128] + acc_two[C_MID:BOTH, at + 128 : at + 256]
            )


def back_two(lift, pre_two, sums_two, back_stats, vec, masks, k2, pre_one, sums_one, taps_a, count):
    copies = back_stats.shape[0]
    rows = masks.shape[1]
    return call(
        lambda *refs: back_two_body(count, *refs),
        (lift, pre_two, sums_two, back_stats, vec, masks, k2, pre_one, sums_one, taps_a),
        [
            like((MEL, rows, BOTH), F32),
            like((C_MID, 9 * C_MID), F32),
            like((copies, 2, C_MID), F32),
            like((2, C_MID), F32),
        ],
        [
            pltpu.VMEM((2, 8, BOTH), F32),
            pltpu.VMEM((BOTH, 3 * WIDE), F32),
            pltpu.VMEM((17, rows, WIDE), BF16),
            pltpu.VMEM((3 * WIDE, BOTH), BF16),
            *side_scratch(rows),
        ],

        input_output_aliases={0: 0},
    )


def scatter_blocks(out, parts):
    copies, share, wide = out.shape
    grps = C_MID // share
    row_count = copies // grps
    turned = [part.T for part in parts]
    sizes = [part.shape[1] // row_count for part in parts]
    blank = jnp.zeros((wide - sum(sizes), C_MID), F32)
    for r in range(row_count):
        rows = [t[n * r : n * (r + 1)] for t, n in zip(turned, sizes)]
        back = jnp.concatenate([*rows, blank], axis=0).T.astype(BF16)
        for g in range(grps):
            out[g * row_count + r] = back[share * g : share * (g + 1)]


def kernel_one_step(taps_x, taps, acc, k, pairs):
    half = taps.shape[1]
    here = range(k * pairs, (k + 1) * pairs)
    mels = [2 * j + parity for parity in range(2) for j in here]
    total = dot_rows(stack(taps, mels, half, slice(128, 384)), near_bins(taps_x, here, half))
    if k == 0:
        acc[...] = total
    else:
        acc[...] += total


def kernel_one_sums(acc):
    pieces = []
    for t in range(3):
        for d in range(3):
            total = jnp.zeros((C_MID, C_IN), F32)
            for p in range(2):
                at = d * BOTH + (t + p) * C_IN
                total += acc[p * C_MID : (p + 1) * C_MID, at : at + C_IN]
            pieces.append(total)
    return jnp.concatenate(pieces, axis=1)


def features_step(taps, weight, out, woven, sems, k, pairs, copies):
    half = taps.shape[1]
    slots = woven.shape[0]
    near = [
        stack(taps, [2 * (k * pairs + q) + i - 1 for q in range(pairs)], half) for i in range(4)
    ]
    part = jnp.dot(jnp.concatenate(near, axis=1), weight[...], preferred_element_type=F32)
    for q in range(pairs):
        j = k * pairs + q
        b = j % slots
        rows = slice(q * half, (q + 1) * half)
        if j >= slots:
            copies[j - slots].wait()
        woven[b, pl.ds(0, half, stride=2), :] = part[rows, 0:128]
        woven[b, pl.ds(1, half, stride=2), :] = part[rows, 128:256]
        copy = pltpu.make_async_copy(woven.at[b], out.at[:, pl.ds(j * LANES, LANES)], sems.at[b])
        copy.start()
        copies.append(copy)


def grads_body(count, lift, pre_one, sums_one, back_stats, vec, masks, k1, taps_x, two,
               grad_x, blocks, sums_out, weight, taps, acc_one, evens, odds, woven, sems):
    place_one_back(k1, weight)
    back = stat_sums(back_stats)
    sums_out[...] = back
    a, b, c = grad_terms(sums_one[...], back, vec[0:1], count)
    taps[taps.shape[0] - 1] = jnp.zeros(taps.shape[1:], BF16)

    def lower(m):
        def tile(r):
            span = slice(r, r + TILE)
            return halves_of(lift[m, span] * a + (pre_one[m, span] * b + c))

        emit_taps(taps, ring_slot(taps, m), masks, evens.at[m % 2], odds.at[m % 2], tile)

    pairs = 4
    copies = []
    for k in range(MEL // 2 // pairs + 1):
        for m in range(2 * pairs * k, 2 * pairs * (k + 1)):
            if m < MEL:
                lower(m)
        if k > 0:
            kernel_one_step(taps_x, taps, acc_one, k - 1, pairs)
            features_step(taps, weight, grad_x, woven, sems, k - 1, pairs, copies)
    scatter_blocks(blocks, [kernel_one_sums(acc_one), two[...]])
    for copy in copies[-woven.shape[0] :]:
        copy.wait()


def all_grads(lift, pre_one, sums_one, back_stats, vec, masks, k1, taps_x, two, share, count):
    copies = back_stats.shape[0]
    half = masks.shape[1] - TAIL
    row_count = copies * share // C_MID
    wide = padded(9 * (C_IN + C_MID) // row_count)
    args = (lift, pre_one, sums_one, back_stats, vec, masks, k1, taps_x, two)
    return call(
        lambda *refs: grads_body(count, *refs),
        args,
        [
            like((2 * half, MEL * C_IN), F32),
            like((copies, share, wide), BF16),
            like((2, C_MID), F32),
        ],
        [
            pltpu.VMEM((4 * WIDE, BOTH), BF16),
            pltpu.VMEM((27, half, WIDE), BF16),
            pltpu.VMEM((BOTH, 3 * BOTH), F32),
            *side_scratch(half + TAIL),
            pltpu.VMEM((8, 2 * half, LANES), F32),
            pltpu.SemaphoreType.DMA((8,)),
        ],

        out_specs=[ANY, VMEM, VMEM],
    )


def finish_body(got, back_one_sums, back_two_sums, own_one, own_two, ga, sa, gb, sb):
    total = jnp.sum(got[...].astype(F32), axis=0)
    size = own_one.shape[1]
    own_one[...] = total[:, 0:size]
    own_two[...] = total[:, size : size + own_two.shape[1]]
    share = ga.shape[1]
    lane = lax.broadcasted_iota(jnp.int32, (share, C_MID), 1)
    row = lax.broadcasted_iota(jnp.int32, (share, C_MID), 0)
    chosen = lane == lax.axis_index("grp") * share + row
    first = lax.broadcasted_iota(jnp.int32, (share, share), 0)
    second = lax.broadcasted_iota(jnp.int32, (share, share), 1)
    for out, sums, k in (
        (ga, back_one_sums, 1), (sa, back_one_sums, 0), (gb, back_two_sums, 1), (sb, back_two_sums, 0)
    ):
        wide = jnp.broadcast_to(sums[k : k + 1], (share, C_MID))
        column = jnp.sum(jnp.where(chosen, wide, 0.0), axis=1, keepdims=True)
        wide = jnp.broadcast_to(column, (share, share))
        out[...] = jnp.sum(jnp.where(first == second, wide, 0.0), axis=0, keepdims=True)


def finish(got, back_one_sums, back_two_sums, rows_one, rows_two):
    share = got.shape[1]
    shapes = [(share, rows_one), (share, rows_two)] + [(1, share)] * 4
    return call(
        finish_body,
        (got, back_one_sums, back_two_sums),
        [like(s, F32) for s in shapes],
    )


def exchange(blocks):
    return lax.all_to_all(blocks, AXES, 0, 0, tiled=True)


def shards(
    features, clip_starts, kernel_one, kernel_two, gain_one, shift_one, gain_two, shift_two, cotangent
):
    frames = features.shape[0]
    copies = lax.axis_size(AXES)
    row_count = lax.axis_size("row")
    count = float(frames * MEL * copies)
    rows_one, rows_two = kernel_one.shape[0], kernel_two.shape[0]
    share = kernel_one.shape[1]
    vectors = [v.reshape(1, share) for v in (gain_one, shift_one, gain_two, shift_two)]
    clips = clip_starts.reshape(1, -1)
    weights, up, down, clips = setup(
        kernel_one.T, kernel_two.T, vectors, clips, features, cotangent, copies
    )
    ends = copies - 1
    up = lax.ppermute(up, AXES, [(i, i + 1) for i in range(ends)])
    down = lax.ppermute(down, AXES, [(i + 1, i) for i in range(ends)])
    weights = exchange(weights)
    pre_one, stats, taps_x, masks, k1, k2, vec = conv_one(
        features, up, down, clips, weights, row_count
    )
    stats = exchange(stats)
    pre_two, stats, taps_a, sums_one = conv_two(pre_one, stats, vec, masks, k2, count)
    stats = exchange(stats)
    block_out, lift, stats, sums_two = norm_two(pre_two, stats, vec, cotangent, up, down, count)
    stats = exchange(stats)
    lift, two, stats, back_two_sums = back_two(
        lift, pre_two, sums_two, stats, vec, masks, k2, pre_one, sums_one, taps_a, count
    )
    stats = exchange(stats)
    grad_features, blocks, back_one_sums = all_grads(
        lift, pre_one, sums_one, stats, vec, masks, k1, taps_x, two, share, count
    )
    own_one, own_two, ga, sa, gb, sb = finish(
        exchange(blocks), back_one_sums, back_two_sums, rows_one, rows_two
    )
    return (
        block_out,
        grad_features,
        own_one.T,
        own_two.T,
        ga.reshape(share),
        sa.reshape(share),
        gb.reshape(share),
        sb.reshape(share),
    )


def solution(mesh):
    placed = (
        P(AXES, None), P(), P("row", "grp"), P("row", "grp"),
        P("grp"), P("grp"), P("grp"), P("grp"), P(AXES, None),
    )
    return jax.shard_map(
        shards,
        mesh=mesh,
        in_specs=placed,
        out_specs=(
            P(AXES, None), P(AXES, None), P("row", "grp"), P("row", "grp"),
            P("grp"), P("grp"), P("grp"), P("grp"),
        ),
        check_vma=False,
    )
```

```python
import jax
import jax.numpy as jnp
from jax import lax
from jax.experimental import pallas as pl
from jax.experimental.pallas import tpu as pltpu
from jax.sharding import PartitionSpec as P

MEL = 32
C_IN = 64
C_MID = 128
EPS = 1e-05
AXES = ("grp", "row")
LANES = 128
TAIL = 16
WIDE = 4 * LANES
BOTH = 2 * C_MID
F32 = jnp.float32
BF16 = jnp.bfloat16
TILE = 16
MIB = 2**20

VMEM = pl.BlockSpec(memory_space=pltpu.VMEM)
ANY = pl.BlockSpec(memory_space=pl.ANY)
HBM = pl.BlockSpec(memory_space=pltpu.HBM)


def like(shape, dtype):
    return jax.ShapeDtypeStruct(shape, dtype)


def call(body, args, outs, scratch=(), limit=16, fuse=False, in_specs=None, out_specs=None, **more):
    return pl.pallas_call(
        body,
        in_specs=in_specs or [VMEM] * len(args),
        out_specs=out_specs or [VMEM] * len(outs),
        out_shape=outs,
        scratch_shapes=list(scratch),
        compiler_params=pltpu.CompilerParams(
            vmem_limit_bytes=limit * MIB, fuse_transposed_lhs_in_matmul=fuse
        ),
        **more,
    )(*args)


def padded(size):
    return -(-size // LANES) * LANES


def partial_sum(values):
    return jnp.sum(values.reshape(-1, 8, values.shape[-1]), axis=0)


def fold(values):
    total = jnp.sum(values, axis=0, keepdims=True)
    return total[:, :C_MID] + total[:, C_MID:]


def spread(first, second, out):
    sums = jnp.concatenate([first, second], axis=0)
    out[...] = jnp.broadcast_to(sums[None], out.shape)


def twice(row):
    return jnp.concatenate([row, row], axis=1)


def tiles(rows):
    return range(0, rows, TILE)


def emit_taps(taps, slot, masks, evens, odds, tile_of):
    rows = masks.shape[1]
    kept = taps.shape[1]
    for r in tiles(rows):
        even, odd = tile_of(r)
        evens[r : r + TILE] = even
        odds[8 + r : 8 + r + TILE] = odd
        if r == 0:
            evens[rows : rows + 1] = even[0:1]
        if r + TILE == rows:
            odds[7:8] = odd[TILE - 1 : TILE]
        if r < kept:
            taps[slot, r : r + TILE, 128:256] = even.astype(BF16)
            taps[slot, r : r + TILE, 256:384] = odd.astype(BF16)
    for r in tiles(kept):
        span = slice(r, r + TILE)
        before = odds[7 + r : 7 + r + TILE] * masks[0, span]
        after = evens[1 + r : 1 + r + TILE] * masks[1, span]
        taps[slot, span, 0:128] = before.astype(BF16)
        taps[slot, span, 384:512] = after.astype(BF16)


def halves_of(value):
    return value[:, :C_MID], value[:, C_MID:]


def add_sums(acc, first, second):
    acc[0] += first
    acc[1] += second


def side_scratch(rows):
    return [pltpu.VMEM((2, rows + 8, LANES), F32), pltpu.VMEM((2, rows + 8, LANES), F32)]


def stats_of(out, mels, rows, half, acc):
    first = jnp.zeros((8, BOTH), F32)
    second = jnp.zeros((8, BOTH), F32)
    for k in range(mels):
        for r in range(0, half, 8):
            value = out[k * rows + r : k * rows + r + 8]
            first += value
            second += value * value
    add_sums(acc, first, second)


def normed_sum(with_half_lifted, plain, gain, shift):
    return (2.0 * with_half_lifted - shift * plain) / gain


def stat_sums(stats):
    return jnp.sum(stats[...], axis=0)


def norm_terms(sums, count):
    mean = sums[0:1] / count
    rstd = lax.rsqrt(sums[1:2] / count - mean * mean + EPS)
    return mean, rstd


def dot_rows(first, second):
    return lax.dot_general(
        first, second, (((0,), (0,)), ((), ())), preferred_element_type=F32
    )


def ring_slot(taps, m):
    last = taps.shape[0] - 1
    return m % last if 0 <= m < MEL else last


def stack(taps, mels, rows, lanes=slice(None)):
    parts = [taps[ring_slot(taps, m), 0:rows, lanes] for m in mels]
    return jnp.concatenate(parts, axis=0)


def clear_ends(taps):
    blank = jnp.zeros(taps.shape[1:], BF16)
    taps[0] = blank
    taps[taps.shape[0] - 1] = blank


def setup_body(k1, k2, ga, sa, gb, sb, clips, x_head, x_tail, c_head, c_tail, w_out, up, down, clips_out):
    clips_out[...] = clips[...]
    share = k1.shape[0]
    copies = w_out.shape[0]
    w_out[...] = jnp.zeros(w_out.shape, BF16)
    first = lax.broadcasted_iota(jnp.int32, (share, share), 0)
    second = lax.broadcasted_iota(jnp.int32, (share, share), 1)
    columns = [k1[...].astype(F32), k2[...].astype(F32)]
    for vector in (ga, sa, gb, sb):
        wide = jnp.broadcast_to(vector[...].astype(F32), (share, share))
        columns.append(jnp.sum(jnp.where(first == second, wide, 0.0), axis=1, keepdims=True))
    chunk = jnp.concatenate(columns, axis=1).astype(BF16)
    for i in range(copies):
        w_out[i, :, 0 : chunk.shape[1]] = chunk
    row = lax.broadcasted_iota(jnp.int32, (8, x_head.shape[1]), 0)
    xt = x_tail[...].astype(F32)
    ct = c_tail[...].astype(F32)
    up[...] = jnp.where(
        row < 4, pltpu.roll(xt[8:16], 4, 0), jnp.where(row == 4, ct[15:16], 0.0)
    ).astype(BF16)
    xh = x_head[...].astype(F32)
    ch = c_head[...].astype(F32)
    down[...] = jnp.where(row < 4, xh[0:8], jnp.where(row == 4, ch[0:1], 0.0)).astype(BF16)


def setup(k1t, k2t, vectors, clips, features, cotangent, copies):
    frames, wide = features.shape
    halves = cotangent.shape[0]
    share = k1t.shape[0]
    w = (copies, share, padded(k1t.shape[1] + k2t.shape[1] + 4))
    whole = lambda shape: pl.BlockSpec(shape, lambda i: (0,) * len(shape))
    outs = [
        like(w, BF16), like((8, wide), BF16), like((8, wide), BF16), like(clips.shape, jnp.int32)
    ]
    return call(
        setup_body,
        (k1t, k2t, *vectors, clips, features, features, cotangent, cotangent),
        outs,
        limit=56,
        in_specs=[
            whole(k1t.shape),
            whole(k2t.shape),
            *[whole((1, share))] * 4,
            whole(clips.shape),
            pl.BlockSpec((16, wide), lambda i: (0, 0)),
            pl.BlockSpec((16, wide), lambda i: (frames // 16 - 1, 0)),
            pl.BlockSpec((16, wide), lambda i: (0, 0)),
            pl.BlockSpec((16, wide), lambda i: (halves // 16 - 1, 0)),
        ],
        out_specs=[whole(o.shape) for o in outs],
        grid=(1,),
    )


def emit_masks(copies, clips, masks):
    rows = masks.shape[1]
    half = rows - TAIL
    frames = 2 * half
    start = lax.axis_index(AXES) * frames
    place = lax.broadcasted_iota(jnp.int32, (rows, clips.shape[1]), 0)
    pair = jnp.where(place >= half + TAIL // 2, place - rows, place)
    frame = start + 2 * pair
    starts = jnp.broadcast_to(clips[...], (rows, clips.shape[1]))
    for slot, shift in ((0, 0), (1, 2)):
        hit = (frame + shift == starts) | (frame + shift >= frames * copies)
        begins = jnp.max(jnp.where(hit, 1.0, 0.0), axis=1, keepdims=True)
        masks[slot] = jnp.broadcast_to(1.0 - begins, (rows, LANES))


def split_bins(parts):
    parts = [part.astype(BF16) for part in parts]
    bins = [part[:, :C_IN] for part in parts] + [part[:, C_IN:] for part in parts]
    return jnp.concatenate(bins, axis=1)


def near_bins(taps, pairs, rows):
    left, mid, right = [
        jnp.concatenate([taps[1 + j + k, 0:rows] for j in pairs], axis=0) for k in (-1, 0, 1)
    ]
    first = jnp.concatenate([left[:, BOTH:], mid], axis=1)
    second = jnp.concatenate([mid, right[:, :BOTH]], axis=1)
    return jnp.concatenate([first, second], axis=0)


def emit_taps_one(fetch, x, up, down, masks, taps, frames):
    rows = masks.shape[1]
    half = rows - TAIL
    clear_ends(taps)
    row = lax.broadcasted_iota(jnp.int32, (8, LANES), 0)
    lead = 24
    own = 2 * half
    for b in range(2):
        frames[b, 0:16] = jnp.zeros((16, LANES), F32)
        frames[b, lead + own + 8 : lead + own + 24] = jnp.zeros((16, LANES), F32)

    def pair(j, b):
        lanes = pl.ds(pl.multiple_of(j * LANES, LANES), LANES)
        u = up[:, lanes].astype(F32)
        d = down[:, lanes].astype(F32)
        frames[b, lead - 8 : lead] = jnp.where(row >= 4, pltpu.roll(u, 4, 0), 0.0)
        frames[b, lead + own : lead + own + 8] = jnp.where(row < 4, d, 0.0)
        for r in tiles(own):
            frames[b, lead + r : lead + r + TILE] = x[r : r + TILE, lanes].astype(F32)

        def pick(first, count, shift):
            return frames[b, pl.ds(lead + 2 * first + shift, count, stride=2), :]

        for r in tiles(rows):
            parts = []
            for shift in (-1, 0, 1, 2):
                if r < half:
                    parts.append(pick(r, TILE, shift))
                else:
                    parts.append(
                        jnp.concatenate([pick(half, 8, shift), pick(-8, 8, shift)], axis=0)
                    )
            span = slice(r, r + TILE)
            parts[0] = parts[0] * masks[0, span]
            parts[3] = parts[3] * masks[1, span]
            taps[1 + j, span, :] = split_bins(parts)

    def two_pairs(i, carry):
        pair(2 * i, 0)
        pair(2 * i + 1, 1)
        return carry

    each = MEL // 4 // len(fetch)
    for k, copy in enumerate(fetch):
        copy.wait()
        lax.fori_loop(k * each, (k + 1) * each, two_pairs, 0)


def conv_one_body(row_count, features, up_in, down_in, clips_in, wg,
                  pre, stats, taps, masks, k1_out, k2_out, vec_out,
                  kf, weight, acc, frames, x, up, down, clips, sems, side_sems):
    sides = [
        pltpu.make_async_copy(here, there, side_sems.at[k])
        for k, (here, there) in enumerate(((clips_in, clips), (up_in, up), (down_in, down)))
    ]
    for copy in sides:
        copy.start()
    wide = x.shape[1] // sems.shape[0]
    fetch = []
    for k in range(sems.shape[0]):
        lanes = pl.ds(k * wide, wide)
        fetch.append(pltpu.make_async_copy(features.at[:, lanes], x.at[:, lanes], sems.at[k]))
        fetch[k].start()
    for copy in sides:
        copy.wait()
    emit_masks(wg.shape[0], clips, masks)
    emit_taps_one(fetch, x, up, down, masks, taps, frames)
    rows = taps.shape[1]
    half = rows - TAIL
    pairs = 4
    rows_one = 9 * C_IN // row_count
    rows_two = 9 * C_MID // row_count
    grps = wg.shape[0] // row_count
    for r in range(row_count):
        shard = [wg[g * row_count + r] for g in range(grps)]
        shard = jnp.concatenate(shard, axis=0).astype(F32).T
        kf[rows_one * r : rows_one * (r + 1)] = shard[0:rows_one]
        at = 9 * C_IN + rows_two * r
        kf[at : at + rows_two] = shard[rows_one : rows_one + rows_two]
        if r == 0:
            vec_out[...] = shard[rows_one + rows_two : rows_one + rows_two + 4]
    k1_out[...] = kf[0 : 9 * C_IN].astype(BF16)
    k2_out[...] = kf[9 * C_IN :].astype(BF16)
    weight[...] = jnp.zeros(weight.shape, BF16)
    for d in range(3):
        for q in range(4):
            for p in range(2):
                t = q - p
                if 0 <= t < 3:
                    at = d * BOTH + q * C_IN
                    start = (3 * t + d) * C_IN
                    weight[at : at + C_IN, p * 128 : p * 128 + 128] = k1_out[start : start + C_IN]
    acc[...] = jnp.zeros(acc.shape, F32)
    for c in range(MEL // 2 // pairs):
        here = range(c * pairs, (c + 1) * pairs)
        out = jnp.dot(near_bins(taps, here, rows), weight[...], preferred_element_type=F32)
        for parity in range(2):
            for q in range(pairs):
                at = (parity * pairs + q) * rows
                pre[2 * (c * pairs + q) + parity] = out[at : at + rows]
        stats_of(out, 2 * pairs, rows, half, acc)
    spread(fold(acc[0]), fold(acc[1]), stats)


def conv_one(features, up, down, clips, wg, row_count):
    rows = features.shape[0] // 2 + TAIL
    copies = wg.shape[0]
    return call(
        lambda *refs: conv_one_body(row_count, *refs),
        (features, up, down, clips, wg),
        [
            like((MEL, rows, BOTH), F32),
            like((copies, 2, C_MID), F32),
            like((MEL // 2 + 2, rows, WIDE), BF16),
            like((2, rows, LANES), F32),
            like((9 * C_IN, C_MID), BF16),
            like((9 * C_MID, C_MID), BF16),
            like((4, C_MID), F32),
        ],
        [
            pltpu.VMEM((9 * (C_IN + C_MID), C_MID), F32),
            pltpu.VMEM((3 * BOTH, BOTH), BF16),
            pltpu.VMEM((2, 8, BOTH), F32),
            pltpu.VMEM((2, features.shape[0] + 48, LANES), F32),
            pltpu.VMEM(features.shape, BF16),
            pltpu.VMEM(up.shape, BF16),
            pltpu.VMEM(down.shape, BF16),
            pltpu.VMEM(clips.shape, jnp.int32),
            pltpu.SemaphoreType.DMA((4,)),
            pltpu.SemaphoreType.DMA((3,)),
        ],
        in_specs=[HBM, HBM, HBM, HBM, VMEM],
    )


def place_two(k2, weight):
    weight[...] = jnp.zeros(weight.shape, BF16)
    for d in range(3):
        for q in range(4):
            for p in range(2):
                t = q - p
                if 0 <= t < 3:
                    at = d * WIDE + q * 128
                    start = (3 * t + d) * C_MID
                    weight[at : at + 128, p * 128 : p * 128 + 128] = k2[start : start + C_MID]


def place_two_back(k2, weight):
    weight[...] = jnp.zeros(weight.shape, BF16)
    for t in range(3):
        for d in range(3):
            start = (3 * t + d) * C_MID
            turned = (0.5 * k2[start : start + C_MID].astype(F32).T).astype(BF16)
            for p in range(2):
                at = (2 - d) * WIDE + (2 - t + p) * 128
                weight[at : at + 128, p * 128 : p * 128 + 128] = turned


def place_one_back(k1, weight):
    weight[...] = jnp.zeros(weight.shape, BF16)
    for t in range(3):
        for d in range(3):
            start = (3 * t + d) * C_IN
            turned = k1[start : start + C_IN].astype(F32).T.astype(BF16)
            for mo in (1, 2):
                for p in range(2):
                    at = (mo - d + 1) * WIDE + (2 - t + p) * 128
                    to = p * 128 + (mo - 1) * 64
                    weight[at : at + 128, to : to + 64] = turned


def conv_two_body(count, pre_one, stats_one, vec, masks, k2, pre, stats, taps, sums_out,
                  acc, weight, evens, odds):
    place_two(k2, weight)
    rows = masks.shape[1]
    half = rows - TAIL
    mels = 1
    sums = stat_sums(stats_one)
    sums_out[...] = sums
    mean, rstd = norm_terms(sums, count)
    scale = 0.5 * vec[0:1] * rstd
    shift = twice(0.5 * vec[1:2] - mean * scale)
    scale = twice(scale)
    clear_ends(taps)
    acc[...] = jnp.zeros(acc.shape, F32)

    def activate(m):
        def tile(r):
            h = pre_one[m, r : r + TILE] * scale + shift
            return halves_of(h + h * jnp.tanh(h))

        emit_taps(taps, 1 + m, masks, evens.at[m % 2], odds.at[m % 2], tile)

    def convolve(c):
        lhs = [taps[c * mels + d : (c + 1) * mels + d].reshape(mels * rows, WIDE) for d in range(3)]
        out = jnp.dot(jnp.concatenate(lhs, axis=1), weight[...], preferred_element_type=F32)
        pre[c * mels : (c + 1) * mels] = out.reshape(mels, rows, BOTH)
        stats_of(out, mels, rows, half, acc)

    for m in range(MEL):
        activate(m)
        if m >= mels and m % mels == 0:
            convolve(m // mels - 1)
    convolve(MEL // mels - 1)
    spread(fold(acc[0]), fold(acc[1]), stats)


def conv_two(pre_one, stats_one, vec, masks, k2, count):
    copies = stats_one.shape[0]
    rows = masks.shape[1]
    return call(
        lambda *refs: conv_two_body(count, *refs),
        (pre_one, stats_one, vec, masks, k2),
        [
            like((MEL, rows, BOTH), F32),
            like((copies, 2, C_MID), F32),
            like((MEL + 2, rows, WIDE), BF16),
            like((2, C_MID), F32),
        ],
        [pltpu.VMEM((2, 8, BOTH), F32), pltpu.VMEM((3 * WIDE, BOTH), BF16), *side_scratch(rows)],
    )


def norm_two_body(count, pre, stats_two, vec, cot, up, down, pooled, lift, back_stats, sums_out, acc):
    half = cot.shape[0]
    sums = stat_sums(stats_two)
    sums_out[...] = sums
    mean, rstd = norm_terms(sums, count)
    scale = 0.5 * vec[2:3] * rstd
    shift = 0.5 * vec[3:4] - mean * scale
    acc[...] = jnp.zeros(acc.shape, F32)
    row = lax.broadcasted_iota(jnp.int32, (TAIL, LANES), 0)

    def pair(j, carry):
        lanes = pl.ds(pl.multiple_of(j * LANES, LANES), LANES)
        u = up[:, lanes].astype(F32)
        d = down[:, lanes].astype(F32)
        first = jnp.zeros((8, LANES), F32)
        second = jnp.zeros((8, LANES), F32)
        for r in tiles(half + TAIL):
            span = slice(r, r + TILE)
            if r < half:
                grad = cot[span, lanes].astype(F32) * 0.125
            else:
                grad = jnp.where(row == 0, d[4:5], jnp.where(row == TAIL - 1, u[4:5], 0.0)) * 0.125
            total = jnp.zeros((TILE, LANES), F32)
            for m in (2 * j, 2 * j + 1):
                for p in range(2):
                    side = slice(p * C_MID, (p + 1) * C_MID)
                    value = pre[m, span, side]
                    h = value * scale + shift
                    th = jnp.tanh(h)
                    one = 1.0 + th
                    silu = h * one
                    gl = grad * (one + (silu - silu * th))
                    lift[m, span, side] = gl
                    if r < half:
                        total += silu
                        first += partial_sum(gl)
                        second += partial_sum(gl * h)
            if r < half:
                pooled[span, lanes] = (total * 0.25).astype(BF16)
        add_sums(acc, first, second)
        return carry

    lax.fori_loop(0, MEL // 2, pair, 0)
    first, second = [jnp.sum(acc[k], axis=0, keepdims=True) for k in range(2)]
    spread(first, normed_sum(second, first, vec[2:3], vec[3:4]), back_stats)


def norm_two(pre, stats_two, vec, cot, up, down, count):
    copies = stats_two.shape[0]
    half, wide = cot.shape
    return call(
        lambda *refs: norm_two_body(count, *refs),
        (pre, stats_two, vec, cot, up, down),
        [
            like((half, wide), BF16),
            like((MEL, half + TAIL, BOTH), F32),
            like((copies, 2, C_MID), F32),
            like((2, C_MID), F32),
        ],
        [pltpu.VMEM((2, 8, LANES), F32)],
    )


def grad_terms(sums, back, gain, count):
    mean, rstd = norm_terms(sums, count)
    a = gain * rstd
    b = -a * rstd * (back[1:2] / count)
    c = -a * (back[0:1] / count) - b * mean
    return twice(a), twice(b), twice(c)


def back_two_body(count, lift, pre_two, sums_two, back_stats, vec, masks, k2, pre_one, sums_one,
                  taps_a, lift_one, two, back_out, sums_out, acc, acc_two, taps, weight, evens, odds):
    place_two_back(k2, weight)
    rows = masks.shape[1]
    half = rows - TAIL
    mels = 2
    wide_mels = 4
    back = stat_sums(back_stats)
    sums_out[...] = back
    a, b, c = grad_terms(sums_two[...], back, vec[2:3], count)
    mean, rstd = norm_terms(sums_one[...], count)
    scale = 0.5 * vec[0:1] * rstd
    shift = twice(0.5 * vec[1:2] - mean * scale)
    scale = twice(scale)
    taps[taps.shape[0] - 1] = jnp.zeros(taps.shape[1:], BF16)
    acc[...] = jnp.zeros(acc.shape, F32)

    def lower(m):
        def tile(r):
            span = slice(r, r + TILE)
            return halves_of(lift[m, span] * a + (pre_two[m, span] * b + c))

        emit_taps(taps, ring_slot(taps, m), masks, evens.at[m % 2], odds.at[m % 2], tile)

    def convolve(k):
        lhs = [stack(taps, range(k * mels + d - 1, (k + 1) * mels + d - 1), rows) for d in range(3)]
        out = jnp.dot(jnp.concatenate(lhs, axis=1), weight[...], preferred_element_type=F32)
        first = jnp.zeros((8, BOTH), F32)
        second = jnp.zeros((8, BOTH), F32)
        for i in range(mels):
            m = k * mels + i
            for r in range(0, rows, 8):
                span = slice(r, r + 8)
                h = pre_one[m, span] * scale + shift
                th = jnp.tanh(h)
                one = 1.0 + th
                silu = h * one
                gl = out[i * rows + r : i * rows + r + 8] * (one + (silu - silu * th))
                lift_one[m, span] = gl
                if r < half:
                    first += gl
                    second += gl * h
        add_sums(acc, first, second)

    def correlate(k):
        here = range(k * wide_mels, (k + 1) * wide_mels)
        near = [
            taps_a[m + d : m + d + wide_mels, 0:half].reshape(wide_mels * half, WIDE)
            for m in here[:1]
            for d in range(3)
        ]
        total = dot_rows(stack(taps, here, half, slice(128, 384)), jnp.concatenate(near, axis=1))
        if k == 0:
            acc_two[...] = total
        else:
            acc_two[...] += total

    for m in range(MEL):
        lower(m)
        if m >= mels and m % mels == 0:
            convolve(m // mels - 1)
        if m >= wide_mels and m % wide_mels == 0:
            correlate(m // wide_mels - 1)
    convolve(MEL // mels - 1)
    correlate(MEL // wide_mels - 1)
    plain = fold(acc[0])
    spread(plain, normed_sum(fold(acc[1]), plain, vec[0:1], vec[1:2]), back_out)
    for t in range(3):
        for d in range(3):
            at = d * WIDE + t * 128
            to = (3 * t + d) * 128
            two[:, to : to + 128] = (
                acc_two[0:C_MID, at : at + 128] + acc_two[C_MID:BOTH, at + 128 : at + 256]
            )


def back_two(lift, pre_two, sums_two, back_stats, vec, masks, k2, pre_one, sums_one, taps_a, count):
    copies = back_stats.shape[0]
    rows = masks.shape[1]
    return call(
        lambda *refs: back_two_body(count, *refs),
        (lift, pre_two, sums_two, back_stats, vec, masks, k2, pre_one, sums_one, taps_a),
        [
            like((MEL, rows, BOTH), F32),
            like((C_MID, 9 * C_MID), F32),
            like((copies, 2, C_MID), F32),
            like((2, C_MID), F32),
        ],
        [
            pltpu.VMEM((2, 8, BOTH), F32),
            pltpu.VMEM((BOTH, 3 * WIDE), F32),
            pltpu.VMEM((17, rows, WIDE), BF16),
            pltpu.VMEM((3 * WIDE, BOTH), BF16),
            *side_scratch(rows),
        ],

        input_output_aliases={0: 0},
    )


def scatter_blocks(out, parts):
    copies, share, wide = out.shape
    grps = C_MID // share
    row_count = copies // grps
    turned = [part.T for part in parts]
    sizes = [part.shape[1] // row_count for part in parts]
    blank = jnp.zeros((wide - sum(sizes), C_MID), F32)
    for r in range(row_count):
        rows = [t[n * r : n * (r + 1)] for t, n in zip(turned, sizes)]
        back = jnp.concatenate([*rows, blank], axis=0).T.astype(BF16)
        for g in range(grps):
            out[g * row_count + r] = back[share * g : share * (g + 1)]


def kernel_one_step(taps_x, taps, acc, k, pairs):
    half = taps.shape[1]
    here = range(k * pairs, (k + 1) * pairs)
    mels = [2 * j + parity for parity in range(2) for j in here]
    total = dot_rows(stack(taps, mels, half, slice(128, 384)), near_bins(taps_x, here, half))
    if k == 0:
        acc[...] = total
    else:
        acc[...] += total


def kernel_one_sums(acc):
    pieces = []
    for t in range(3):
        for d in range(3):
            total = jnp.zeros((C_MID, C_IN), F32)
            for p in range(2):
                at = d * BOTH + (t + p) * C_IN
                total += acc[p * C_MID : (p + 1) * C_MID, at : at + C_IN]
            pieces.append(total)
    return jnp.concatenate(pieces, axis=1)


def features_step(taps, weight, out, woven, sems, k, pairs, copies):
    half = taps.shape[1]
    slots = woven.shape[0]
    near = [
        stack(taps, [2 * (k * pairs + q) + i - 1 for q in range(pairs)], half) for i in range(4)
    ]
    part = jnp.dot(jnp.concatenate(near, axis=1), weight[...], preferred_element_type=F32)
    for q in range(pairs):
        j = k * pairs + q
        b = j % slots
        rows = slice(q * half, (q + 1) * half)
        if j >= slots:
            copies[j - slots].wait()
        woven[b, pl.ds(0, half, stride=2), :] = part[rows, 0:128]
        woven[b, pl.ds(1, half, stride=2), :] = part[rows, 128:256]
        copy = pltpu.make_async_copy(woven.at[b], out.at[:, pl.ds(j * LANES, LANES)], sems.at[b])
        copy.start()
        copies.append(copy)


def grads_body(count, lift, pre_one, sums_one, back_stats, vec, masks, k1, taps_x, two,
               grad_x, blocks, sums_out, weight, taps, acc_one, evens, odds, woven, sems):
    place_one_back(k1, weight)
    back = stat_sums(back_stats)
    sums_out[...] = back
    a, b, c = grad_terms(sums_one[...], back, vec[0:1], count)
    taps[taps.shape[0] - 1] = jnp.zeros(taps.shape[1:], BF16)

    def lower(m):
        def tile(r):
            span = slice(r, r + TILE)
            return halves_of(lift[m, span] * a + (pre_one[m, span] * b + c))

        emit_taps(taps, ring_slot(taps, m), masks, evens.at[m % 2], odds.at[m % 2], tile)

    pairs = 4
    copies = []
    for k in range(MEL // 2 // pairs + 1):
        for m in range(2 * pairs * k, 2 * pairs * (k + 1)):
            if m < MEL:
                lower(m)
        if k > 0:
            kernel_one_step(taps_x, taps, acc_one, k - 1, pairs)
            features_step(taps, weight, grad_x, woven, sems, k - 1, pairs, copies)
    scatter_blocks(blocks, [kernel_one_sums(acc_one), two[...]])
    for copy in copies[-woven.shape[0] :]:
        copy.wait()


def all_grads(lift, pre_one, sums_one, back_stats, vec, masks, k1, taps_x, two, share, count):
    copies = back_stats.shape[0]
    half = masks.shape[1] - TAIL
    row_count = copies * share // C_MID
    wide = padded(9 * (C_IN + C_MID) // row_count)
    args = (lift, pre_one, sums_one, back_stats, vec, masks, k1, taps_x, two)
    return call(
        lambda *refs: grads_body(count, *refs),
        args,
        [
            like((2 * half, MEL * C_IN), F32),
            like((copies, share, wide), BF16),
            like((2, C_MID), F32),
        ],
        [
            pltpu.VMEM((4 * WIDE, BOTH), BF16),
            pltpu.VMEM((27, half, WIDE), BF16),
            pltpu.VMEM((BOTH, 3 * BOTH), F32),
            *side_scratch(half + TAIL),
            pltpu.VMEM((8, 2 * half, LANES), F32),
            pltpu.SemaphoreType.DMA((8,)),
        ],

        out_specs=[ANY, VMEM, VMEM],
        fuse=True,
    )


def finish_body(got, back_one_sums, back_two_sums, own_one, own_two, ga, sa, gb, sb):
    total = jnp.sum(got[...].astype(F32), axis=0)
    size = own_one.shape[1]
    own_one[...] = total[:, 0:size]
    own_two[...] = total[:, size : size + own_two.shape[1]]
    share = ga.shape[1]
    lane = lax.broadcasted_iota(jnp.int32, (share, C_MID), 1)
    row = lax.broadcasted_iota(jnp.int32, (share, C_MID), 0)
    chosen = lane == lax.axis_index("grp") * share + row
    first = lax.broadcasted_iota(jnp.int32, (share, share), 0)
    second = lax.broadcasted_iota(jnp.int32, (share, share), 1)
    for out, sums, k in (
        (ga, back_one_sums, 1), (sa, back_one_sums, 0), (gb, back_two_sums, 1), (sb, back_two_sums, 0)
    ):
        wide = jnp.broadcast_to(sums[k : k + 1], (share, C_MID))
        column = jnp.sum(jnp.where(chosen, wide, 0.0), axis=1, keepdims=True)
        wide = jnp.broadcast_to(column, (share, share))
        out[...] = jnp.sum(jnp.where(first == second, wide, 0.0), axis=0, keepdims=True)


def finish(got, back_one_sums, back_two_sums, rows_one, rows_two):
    share = got.shape[1]
    shapes = [(share, rows_one), (share, rows_two)] + [(1, share)] * 4
    return call(
        finish_body,
        (got, back_one_sums, back_two_sums),
        [like(s, F32) for s in shapes],
    )


def exchange(blocks):
    return lax.all_to_all(blocks, AXES, 0, 0, tiled=True)


def shards(
    features, clip_starts, kernel_one, kernel_two, gain_one, shift_one, gain_two, shift_two, cotangent
):
    frames = features.shape[0]
    copies = lax.axis_size(AXES)
    row_count = lax.axis_size("row")
    count = float(frames * MEL * copies)
    rows_one, rows_two = kernel_one.shape[0], kernel_two.shape[0]
    share = kernel_one.shape[1]
    vectors = [v.reshape(1, share) for v in (gain_one, shift_one, gain_two, shift_two)]
    clips = clip_starts.reshape(1, -1)
    weights, up, down, clips = setup(
        kernel_one.T, kernel_two.T, vectors, clips, features, cotangent, copies
    )
    ends = copies - 1
    up = lax.ppermute(up, AXES, [(i, i + 1) for i in range(ends)])
    down = lax.ppermute(down, AXES, [(i + 1, i) for i in range(ends)])
    weights = exchange(weights)
    pre_one, stats, taps_x, masks, k1, k2, vec = conv_one(
        features, up, down, clips, weights, row_count
    )
    stats = exchange(stats)
    pre_two, stats, taps_a, sums_one = conv_two(pre_one, stats, vec, masks, k2, count)
    stats = exchange(stats)
    block_out, lift, stats, sums_two = norm_two(pre_two, stats, vec, cotangent, up, down, count)
    stats = exchange(stats)
    lift, two, stats, back_two_sums = back_two(
        lift, pre_two, sums_two, stats, vec, masks, k2, pre_one, sums_one, taps_a, count
    )
    stats = exchange(stats)
    grad_features, blocks, back_one_sums = all_grads(
        lift, pre_one, sums_one, stats, vec, masks, k1, taps_x, two, share, count
    )
    own_one, own_two, ga, sa, gb, sb = finish(
        exchange(blocks), back_one_sums, back_two_sums, rows_one, rows_two
    )
    return (
        block_out,
        grad_features,
        own_one.T,
        own_two.T,
        ga.reshape(share),
        sa.reshape(share),
        gb.reshape(share),
        sb.reshape(share),
    )


def solution(mesh):
    placed = (
        P(AXES, None), P(), P("row", "grp"), P("row", "grp"),
        P("grp"), P("grp"), P("grp"), P("grp"), P(AXES, None),
    )
    return jax.shard_map(
        shards,
        mesh=mesh,
        in_specs=placed,
        out_specs=(
            P(AXES, None), P(AXES, None), P("row", "grp"), P("row", "grp"),
            P("grp"), P("grp"), P("grp"), P("grp"),
        ),
        check_vma=False,
    )
```

```python
import jax
import jax.numpy as jnp
from jax import lax
from jax.experimental import pallas as pl
from jax.experimental.pallas import tpu as pltpu
from jax.sharding import PartitionSpec as P

MEL = 32
C_IN = 64
C_MID = 128
EPS = 1e-05
AXES = ("grp", "row")
LANES = 128
TAIL = 16
WIDE = 4 * LANES
BOTH = 2 * C_MID
F32 = jnp.float32
BF16 = jnp.bfloat16
TILE = 16
SIDES = 4
MIB = 2**20

VMEM = pl.BlockSpec(memory_space=pltpu.VMEM)
ANY = pl.BlockSpec(memory_space=pl.ANY)
HBM = pl.BlockSpec(memory_space=pltpu.HBM)


def like(shape, dtype):
    return jax.ShapeDtypeStruct(shape, dtype)


def call(body, args, outs, scratch=(), limit=16, fuse=False, in_specs=None, out_specs=None, **more):
    return pl.pallas_call(
        body,
        in_specs=in_specs or [VMEM] * len(args),
        out_specs=out_specs or [VMEM] * len(outs),
        out_shape=outs,
        scratch_shapes=list(scratch),
        compiler_params=pltpu.CompilerParams(
            vmem_limit_bytes=limit * MIB, fuse_transposed_lhs_in_matmul=fuse
        ),
        **more,
    )(*args)


def padded(size):
    return -(-size // LANES) * LANES


def partial_sum(values):
    return jnp.sum(values.reshape(-1, 8, values.shape[-1]), axis=0)


def fold(values):
    total = jnp.sum(values, axis=0, keepdims=True)
    return total[:, :C_MID] + total[:, C_MID:]


def spread(first, second, out):
    sums = jnp.concatenate([first, second], axis=0)
    out[...] = jnp.broadcast_to(sums[None], out.shape)


def twice(row):
    return jnp.concatenate([row, row], axis=1)


def tiles(rows):
    return range(0, rows, TILE)


def emit_taps(taps, masks, evens, odds, tile_of):
    rows = masks.shape[1]
    kept = taps.shape[0]
    for r in tiles(rows):
        even, odd = tile_of(r)
        evens[r : r + TILE] = even
        odds[8 + r : 8 + r + TILE] = odd
        if r == 0:
            evens[rows : rows + 1] = even[0:1]
        if r + TILE == rows:
            odds[7:8] = odd[TILE - 1 : TILE]
        if r < kept:
            taps[r : r + TILE, 128:256] = even.astype(BF16)
            taps[r : r + TILE, 256:384] = odd.astype(BF16)
    for r in tiles(kept):
        span = slice(r, r + TILE)
        before = odds[7 + r : 7 + r + TILE] * masks[0, span]
        after = evens[1 + r : 1 + r + TILE] * masks[1, span]
        taps[span, 0:128] = before.astype(BF16)
        taps[span, 384:512] = after.astype(BF16)


def halves_of(value):
    return value[:, :C_MID], value[:, C_MID:]


def add_sums(acc, first, second):
    acc[0] += first
    acc[1] += second


def side_scratch(rows):
    return [pltpu.VMEM((rows + 8, LANES), F32)] * (2 * SIDES)


def stats_of(out, mels, rows, half, acc):
    first = jnp.zeros((8, BOTH), F32)
    second = jnp.zeros((8, BOTH), F32)
    for k in range(mels):
        for r in range(0, half, 8):
            value = out[k * rows + r : k * rows + r + 8]
            first += value
            second += value * value
    add_sums(acc, first, second)


def normed_sum(with_half_lifted, plain, gain, shift):
    return (2.0 * with_half_lifted - shift * plain) / gain


def stat_sums(stats):
    return jnp.sum(stats[...], axis=0)


def norm_terms(sums, count):
    mean = sums[0:1] / count
    rstd = lax.rsqrt(sums[1:2] / count - mean * mean + EPS)
    return mean, rstd


def dot_rows(first, second):
    return lax.dot_general(
        first, second, (((0,), (0,)), ((), ())), preferred_element_type=F32
    )


def ring_slot(ring, m):
    return ring[m % (len(ring) - 1)] if 0 <= m < MEL else ring[-1]


def stack(ring, mels, rows, lanes=slice(None)):
    return jnp.concatenate([ring_slot(ring, m)[0:rows, lanes] for m in mels], axis=0)


def ring_scratch(slots, rows):
    return [pltpu.VMEM((rows, WIDE), BF16)] * slots


def clear_ends(taps):
    blank = jnp.zeros(taps.shape[1:], BF16)
    taps[0] = blank
    taps[taps.shape[0] - 1] = blank


def setup_body(k1, k2, ga, sa, gb, sb, clips, x_head, x_tail, c_head, c_tail, w_out, up, down, clips_out):
    clips_out[...] = clips[...]
    share = k1.shape[0]
    copies = w_out.shape[0]
    w_out[...] = jnp.zeros(w_out.shape, BF16)
    first = lax.broadcasted_iota(jnp.int32, (share, share), 0)
    second = lax.broadcasted_iota(jnp.int32, (share, share), 1)
    columns = [k1[...].astype(F32), k2[...].astype(F32)]
    for vector in (ga, sa, gb, sb):
        wide = jnp.broadcast_to(vector[...].astype(F32), (share, share))
        columns.append(jnp.sum(jnp.where(first == second, wide, 0.0), axis=1, keepdims=True))
    chunk = jnp.concatenate(columns, axis=1).astype(BF16)
    for i in range(copies):
        w_out[i, :, 0 : chunk.shape[1]] = chunk
    row = lax.broadcasted_iota(jnp.int32, (8, x_head.shape[1]), 0)
    xt = x_tail[...].astype(F32)
    ct = c_tail[...].astype(F32)
    up[...] = jnp.where(
        row < 4, pltpu.roll(xt[8:16], 4, 0), jnp.where(row == 4, ct[15:16], 0.0)
    ).astype(BF16)
    xh = x_head[...].astype(F32)
    ch = c_head[...].astype(F32)
    down[...] = jnp.where(row < 4, xh[0:8], jnp.where(row == 4, ch[0:1], 0.0)).astype(BF16)


def setup(k1t, k2t, vectors, clips, features, cotangent, copies):
    frames, wide = features.shape
    halves = cotangent.shape[0]
    share = k1t.shape[0]
    w = (copies, share, padded(k1t.shape[1] + k2t.shape[1] + 4))
    whole = lambda shape: pl.BlockSpec(shape, lambda i: (0,) * len(shape))
    outs = [
        like(w, BF16), like((8, wide), BF16), like((8, wide), BF16), like(clips.shape, jnp.int32)
    ]
    return call(
        setup_body,
        (k1t, k2t, *vectors, clips, features, features, cotangent, cotangent),
        outs,
        limit=56,
        in_specs=[
            whole(k1t.shape),
            whole(k2t.shape),
            *[whole((1, share))] * 4,
            whole(clips.shape),
            pl.BlockSpec((16, wide), lambda i: (0, 0)),
            pl.BlockSpec((16, wide), lambda i: (frames // 16 - 1, 0)),
            pl.BlockSpec((16, wide), lambda i: (0, 0)),
            pl.BlockSpec((16, wide), lambda i: (halves // 16 - 1, 0)),
        ],
        out_specs=[whole(o.shape) for o in outs],
        grid=(1,),
    )


def emit_masks(copies, clips, masks):
    rows = masks.shape[1]
    half = rows - TAIL
    frames = 2 * half
    start = lax.axis_index(AXES) * frames
    place = lax.broadcasted_iota(jnp.int32, (rows, clips.shape[1]), 0)
    pair = jnp.where(place >= half + TAIL // 2, place - rows, place)
    frame = start + 2 * pair
    starts = jnp.broadcast_to(clips[...], (rows, clips.shape[1]))
    for slot, shift in ((0, 0), (1, 2)):
        hit = (frame + shift == starts) | (frame + shift >= frames * copies)
        begins = jnp.max(jnp.where(hit, 1.0, 0.0), axis=1, keepdims=True)
        masks[slot] = jnp.broadcast_to(1.0 - begins, (rows, LANES))


def split_bins(parts):
    low = lax.broadcasted_iota(jnp.int32, parts[0].shape, 1) < C_IN
    first, second = [], []
    for here, there in (parts[0:2], parts[2:4]):
        first.append(jnp.where(low, here, pltpu.roll(there, C_IN, 1)))
        second.append(jnp.where(low, pltpu.roll(here, C_IN, 1), there))
    return jnp.concatenate(first + second, axis=1)


def near_bins(taps, pairs, rows):
    left, mid, right = [
        jnp.concatenate([taps[1 + j + k, 0:rows] for j in pairs], axis=0) for k in (-1, 0, 1)
    ]
    first = jnp.concatenate([left[:, BOTH:], mid], axis=1)
    second = jnp.concatenate([mid, right[:, :BOTH]], axis=1)
    return jnp.concatenate([first, second], axis=0)


def emit_taps_one(fetch, x, up, down, masks, taps, frames):
    rows = masks.shape[1]
    half = rows - TAIL
    clear_ends(taps)
    row = lax.broadcasted_iota(jnp.int32, (8, LANES), 0)
    lead = 24
    own = 2 * half
    for b in range(2):
        frames[b, 0:16] = jnp.zeros((16, LANES), F32)
        frames[b, lead + own + 8 : lead + own + 24] = jnp.zeros((16, LANES), F32)

    def pair(j, b):
        lanes = pl.ds(pl.multiple_of(j * LANES, LANES), LANES)
        u = up[:, lanes].astype(F32)
        d = down[:, lanes].astype(F32)
        frames[b, lead - 8 : lead] = jnp.where(row >= 4, pltpu.roll(u, 4, 0), 0.0)
        frames[b, lead + own : lead + own + 8] = jnp.where(row < 4, d, 0.0)
        for r in tiles(own):
            frames[b, lead + r : lead + r + TILE] = x[r : r + TILE, lanes].astype(F32)

        def pick(first, count, shift):
            return frames[b, pl.ds(lead + 2 * first + shift, count, stride=2), :]

        for r in tiles(rows):
            parts = []
            for shift in (-1, 0, 1, 2):
                if r < half:
                    parts.append(pick(r, TILE, shift))
                else:
                    parts.append(
                        jnp.concatenate([pick(half, 8, shift), pick(-8, 8, shift)], axis=0)
                    )
            span = slice(r, r + TILE)
            parts[0] = parts[0] * masks[0, span]
            parts[3] = parts[3] * masks[1, span]
            taps[1 + j, span, :] = split_bins(parts).astype(BF16)

    def two_pairs(i, carry):
        pair(2 * i, 0)
        pair(2 * i + 1, 1)
        return carry

    each = MEL // 4 // len(fetch)
    for k, copy in enumerate(fetch):
        copy.wait()
        lax.fori_loop(k * each, (k + 1) * each, two_pairs, 0)


def conv_one_body(row_count, features, up_in, down_in, clips_in, wg,
                  pre, stats, taps, masks, k1_out, k2_out, vec_out,
                  kf, weight, acc, frames, x, up, down, clips, sems, side_sems):
    sides = [
        pltpu.make_async_copy(here, there, side_sems.at[k])
        for k, (here, there) in enumerate(((clips_in, clips), (up_in, up), (down_in, down)))
    ]
    for copy in sides:
        copy.start()
    wide = x.shape[1] // sems.shape[0]
    fetch = []
    for k in range(sems.shape[0]):
        lanes = pl.ds(k * wide, wide)
        fetch.append(pltpu.make_async_copy(features.at[:, lanes], x.at[:, lanes], sems.at[k]))
        fetch[k].start()
    for copy in sides:
        copy.wait()
    emit_masks(wg.shape[0], clips, masks)
    emit_taps_one(fetch, x, up, down, masks, taps, frames)
    rows = taps.shape[1]
    half = rows - TAIL
    pairs = 4
    rows_one = 9 * C_IN // row_count
    rows_two = 9 * C_MID // row_count
    grps = wg.shape[0] // row_count
    for r in range(row_count):
        shard = [wg[g * row_count + r] for g in range(grps)]
        shard = jnp.concatenate(shard, axis=0).astype(F32).T
        kf[rows_one * r : rows_one * (r + 1)] = shard[0:rows_one]
        at = 9 * C_IN + rows_two * r
        kf[at : at + rows_two] = shard[rows_one : rows_one + rows_two]
        if r == 0:
            vec_out[...] = shard[rows_one + rows_two : rows_one + rows_two + 4]
    k1_out[...] = kf[0 : 9 * C_IN].astype(BF16)
    k2_out[...] = kf[9 * C_IN :].astype(BF16)
    weight[...] = jnp.zeros(weight.shape, BF16)
    for d in range(3):
        for q in range(4):
            for p in range(2):
                t = q - p
                if 0 <= t < 3:
                    at = d * BOTH + q * C_IN
                    start = (3 * t + d) * C_IN
                    weight[at : at + C_IN, p * 128 : p * 128 + 128] = k1_out[start : start + C_IN]
    acc[...] = jnp.zeros(acc.shape, F32)
    for c in range(MEL // 2 // pairs):
        here = range(c * pairs, (c + 1) * pairs)
        out = jnp.dot(near_bins(taps, here, rows), weight[...], preferred_element_type=F32)
        for parity in range(2):
            for q in range(pairs):
                at = (parity * pairs + q) * rows
                pre[2 * (c * pairs + q) + parity] = out[at : at + rows]
        stats_of(out, 2 * pairs, rows, half, acc)
    spread(fold(acc[0]), fold(acc[1]), stats)


def conv_one(features, up, down, clips, wg, row_count):
    rows = features.shape[0] // 2 + TAIL
    copies = wg.shape[0]
    return call(
        lambda *refs: conv_one_body(row_count, *refs),
        (features, up, down, clips, wg),
        [
            like((MEL, rows, BOTH), F32),
            like((copies, 2, C_MID), F32),
            like((MEL // 2 + 2, rows, WIDE), BF16),
            like((2, rows, LANES), F32),
            like((9 * C_IN, C_MID), BF16),
            like((9 * C_MID, C_MID), BF16),
            like((4, C_MID), F32),
        ],
        [
            pltpu.VMEM((9 * (C_IN + C_MID), C_MID), F32),
            pltpu.VMEM((3 * BOTH, BOTH), BF16),
            pltpu.VMEM((2, 8, BOTH), F32),
            pltpu.VMEM((2, features.shape[0] + 48, LANES), F32),
            pltpu.VMEM(features.shape, BF16),
            pltpu.VMEM(up.shape, BF16),
            pltpu.VMEM(down.shape, BF16),
            pltpu.VMEM(clips.shape, jnp.int32),
            pltpu.SemaphoreType.DMA((4,)),
            pltpu.SemaphoreType.DMA((3,)),
        ],
        in_specs=[HBM, HBM, HBM, HBM, VMEM],
    )


def place_two(k2, weight):
    weight[...] = jnp.zeros(weight.shape, BF16)
    for d in range(3):
        for q in range(4):
            for p in range(2):
                t = q - p
                if 0 <= t < 3:
                    at = d * WIDE + q * 128
                    start = (3 * t + d) * C_MID
                    weight[at : at + 128, p * 128 : p * 128 + 128] = k2[start : start + C_MID]


def place_two_back(k2, weight):
    weight[...] = jnp.zeros(weight.shape, BF16)
    for t in range(3):
        for d in range(3):
            start = (3 * t + d) * C_MID
            turned = (0.5 * k2[start : start + C_MID].astype(F32).T).astype(BF16)
            for p in range(2):
                at = (2 - d) * WIDE + (2 - t + p) * 128
                weight[at : at + 128, p * 128 : p * 128 + 128] = turned


def place_one_back(k1, weight):
    weight[...] = jnp.zeros(weight.shape, BF16)
    for t in range(3):
        for d in range(3):
            start = (3 * t + d) * C_IN
            turned = k1[start : start + C_IN].astype(F32).T.astype(BF16)
            for mo in (1, 2):
                for p in range(2):
                    at = (mo - d + 1) * WIDE + (2 - t + p) * 128
                    to = p * 128 + (mo - 1) * 64
                    weight[at : at + 128, to : to + 64] = turned


def conv_two_body(count, pre_one, stats_one, vec, masks, k2, pre, stats, taps, sums_out,
                  acc, weight, *sides):
    place_two(k2, weight)
    rows = masks.shape[1]
    half = rows - TAIL
    mels = 2
    sums = stat_sums(stats_one)
    sums_out[...] = sums
    mean, rstd = norm_terms(sums, count)
    scale = 0.5 * vec[0:1] * rstd
    shift = twice(0.5 * vec[1:2] - mean * scale)
    scale = twice(scale)
    clear_ends(taps)
    acc[...] = jnp.zeros(acc.shape, F32)

    def activate(m):
        def tile(r):
            h = pre_one[m, r : r + TILE] * scale + shift
            return halves_of(h + h * jnp.tanh(h))

        emit_taps(taps.at[1 + m], masks, sides[m % SIDES], sides[SIDES + m % SIDES], tile)

    def convolve(c):
        lhs = [taps[c * mels + d : (c + 1) * mels + d].reshape(mels * rows, WIDE) for d in range(3)]
        out = jnp.dot(jnp.concatenate(lhs, axis=1), weight[...], preferred_element_type=F32)
        pre[c * mels : (c + 1) * mels] = out.reshape(mels, rows, BOTH)
        stats_of(out, mels, rows, half, acc)

    for m in range(MEL):
        activate(m)
        if m >= mels and m % mels == 0:
            convolve(m // mels - 1)
    convolve(MEL // mels - 1)
    spread(fold(acc[0]), fold(acc[1]), stats)


def conv_two(pre_one, stats_one, vec, masks, k2, count):
    copies = stats_one.shape[0]
    rows = masks.shape[1]
    return call(
        lambda *refs: conv_two_body(count, *refs),
        (pre_one, stats_one, vec, masks, k2),
        [
            like((MEL, rows, BOTH), F32),
            like((copies, 2, C_MID), F32),
            like((MEL + 2, rows, WIDE), BF16),
            like((2, C_MID), F32),
        ],
        [pltpu.VMEM((2, 8, BOTH), F32), pltpu.VMEM((3 * WIDE, BOTH), BF16), *side_scratch(rows)],
    )


def norm_two_body(count, pre, stats_two, vec, cot, up, down, pooled, lift, back_stats, sums_out, acc):
    half = cot.shape[0]
    sums = stat_sums(stats_two)
    sums_out[...] = sums
    mean, rstd = norm_terms(sums, count)
    scale = 0.5 * vec[2:3] * rstd
    shift = 0.5 * vec[3:4] - mean * scale
    acc[...] = jnp.zeros(acc.shape, F32)
    row = lax.broadcasted_iota(jnp.int32, (TAIL, LANES), 0)

    def pair(j, carry):
        lanes = pl.ds(pl.multiple_of(j * LANES, LANES), LANES)
        u = up[:, lanes].astype(F32)
        d = down[:, lanes].astype(F32)
        first = jnp.zeros((8, LANES), F32)
        second = jnp.zeros((8, LANES), F32)
        for r in tiles(half + TAIL):
            span = slice(r, r + TILE)
            if r < half:
                grad = cot[span, lanes].astype(F32) * 0.125
            else:
                grad = jnp.where(row == 0, d[4:5], jnp.where(row == TAIL - 1, u[4:5], 0.0)) * 0.125
            total = jnp.zeros((TILE, LANES), F32)
            for m in (2 * j, 2 * j + 1):
                for p in range(2):
                    side = slice(p * C_MID, (p + 1) * C_MID)
                    value = pre[m, span, side]
                    h = value * scale + shift
                    th = jnp.tanh(h)
                    one = 1.0 + th
                    silu = h * one
                    gl = grad * (one + (silu - silu * th))
                    lift[m, span, side] = gl
                    if r < half:
                        total += silu
                        first += partial_sum(gl)
                        second += partial_sum(gl * h)
            if r < half:
                pooled[span, lanes] = (total * 0.25).astype(BF16)
        add_sums(acc, first, second)
        return carry

    lax.fori_loop(0, MEL // 2, pair, 0)
    first, second = [jnp.sum(acc[k], axis=0, keepdims=True) for k in range(2)]
    spread(first, normed_sum(second, first, vec[2:3], vec[3:4]), back_stats)


def norm_two(pre, stats_two, vec, cot, up, down, count):
    copies = stats_two.shape[0]
    half, wide = cot.shape
    return call(
        lambda *refs: norm_two_body(count, *refs),
        (pre, stats_two, vec, cot, up, down),
        [
            like((half, wide), BF16),
            like((MEL, half + TAIL, BOTH), F32),
            like((copies, 2, C_MID), F32),
            like((2, C_MID), F32),
        ],
        [pltpu.VMEM((2, 8, LANES), F32)],
    )


def grad_terms(sums, back, gain, count):
    mean, rstd = norm_terms(sums, count)
    a = gain * rstd
    b = -a * rstd * (back[1:2] / count)
    c = -a * (back[0:1] / count) - b * mean
    return twice(a), twice(b), twice(c)


def back_two_body(count, lift, pre_two, sums_two, back_stats, vec, masks, k2, pre_one, sums_one,
                  taps_a, lift_one, two, back_out, sums_out, acc, acc_two, weight, *buffers):
    place_two_back(k2, weight)
    sides, taps = buffers[: 2 * SIDES], buffers[2 * SIDES :]
    rows = masks.shape[1]
    half = rows - TAIL
    mels = 4
    back = stat_sums(back_stats)
    sums_out[...] = back
    a, b, c = grad_terms(sums_two[...], back, vec[2:3], count)
    mean, rstd = norm_terms(sums_one[...], count)
    scale = 0.5 * vec[0:1] * rstd
    shift = twice(0.5 * vec[1:2] - mean * scale)
    scale = twice(scale)
    taps[-1][...] = jnp.zeros(taps[-1].shape, BF16)
    acc[...] = jnp.zeros(acc.shape, F32)

    def lower(m):
        def tile(r):
            span = slice(r, r + TILE)
            return halves_of(lift[m, span] * a + (pre_two[m, span] * b + c))

        emit_taps(ring_slot(taps, m), masks, sides[m % SIDES], sides[SIDES + m % SIDES], tile)

    def convolve(k):
        lhs = [stack(taps, range(k * mels + d - 1, (k + 1) * mels + d - 1), rows) for d in range(3)]
        out = jnp.dot(jnp.concatenate(lhs, axis=1), weight[...], preferred_element_type=F32)
        first = jnp.zeros((8, BOTH), F32)
        second = jnp.zeros((8, BOTH), F32)
        for i in range(mels):
            m = k * mels + i
            for r in range(0, rows, 8):
                span = slice(r, r + 8)
                h = pre_one[m, span] * scale + shift
                th = jnp.tanh(h)
                one = 1.0 + th
                silu = h * one
                gl = out[i * rows + r : i * rows + r + 8] * (one + (silu - silu * th))
                lift_one[m, span] = gl
                if r < half:
                    first += gl
                    second += gl * h
        add_sums(acc, first, second)

    def correlate(k):
        here = range(k * mels, (k + 1) * mels)
        near = [
            taps_a[k * mels + d : (k + 1) * mels + d, 0:half].reshape(mels * half, WIDE) for d in range(3)
        ]
        total = dot_rows(stack(taps, here, half, slice(128, 384)), jnp.concatenate(near, axis=1))
        if k == 0:
            acc_two[...] = total
        else:
            acc_two[...] += total

    for k in range(MEL // mels + 1):
        for m in range(k * mels, (k + 1) * mels):
            if m < MEL:
                lower(m)
        if k > 0:
            convolve(k - 1)
            correlate(k - 1)
    plain = fold(acc[0])
    spread(plain, normed_sum(fold(acc[1]), plain, vec[0:1], vec[1:2]), back_out)
    for t in range(3):
        for d in range(3):
            at = d * WIDE + t * 128
            to = (3 * t + d) * 128
            two[:, to : to + 128] = (
                acc_two[0:C_MID, at : at + 128] + acc_two[C_MID:BOTH, at + 128 : at + 256]
            )


def back_two(lift, pre_two, sums_two, back_stats, vec, masks, k2, pre_one, sums_one, taps_a, count):
    copies = back_stats.shape[0]
    rows = masks.shape[1]
    return call(
        lambda *refs: back_two_body(count, *refs),
        (lift, pre_two, sums_two, back_stats, vec, masks, k2, pre_one, sums_one, taps_a),
        [
            like((MEL, rows, BOTH), F32),
            like((C_MID, 9 * C_MID), F32),
            like((copies, 2, C_MID), F32),
            like((2, C_MID), F32),
        ],
        [
            pltpu.VMEM((2, 8, BOTH), F32),
            pltpu.VMEM((BOTH, 3 * WIDE), F32),
            pltpu.VMEM((3 * WIDE, BOTH), BF16),
            *side_scratch(rows),
            *ring_scratch(17, rows),
        ],

        input_output_aliases={0: 0},
    )


def scatter_blocks(out, parts):
    copies, share, wide = out.shape
    grps = C_MID // share
    row_count = copies // grps
    turned = [part.T for part in parts]
    sizes = [part.shape[1] // row_count for part in parts]
    blank = jnp.zeros((wide - sum(sizes), C_MID), F32)
    for r in range(row_count):
        rows = [t[n * r : n * (r + 1)] for t, n in zip(turned, sizes)]
        back = jnp.concatenate([*rows, blank], axis=0).T.astype(BF16)
        for g in range(grps):
            out[g * row_count + r] = back[share * g : share * (g + 1)]


def kernel_one_step(taps_x, taps, acc, k, pairs):
    half = taps[-1].shape[0]
    here = range(k * pairs, (k + 1) * pairs)
    mels = [2 * j + parity for parity in range(2) for j in here]
    total = dot_rows(stack(taps, mels, half, slice(128, 384)), near_bins(taps_x, here, half))
    if k == 0:
        acc[...] = total
    else:
        acc[...] += total


def kernel_one_sums(acc):
    pieces = []
    for t in range(3):
        for d in range(3):
            total = jnp.zeros((C_MID, C_IN), F32)
            for p in range(2):
                at = d * BOTH + (t + p) * C_IN
                total += acc[p * C_MID : (p + 1) * C_MID, at : at + C_IN]
            pieces.append(total)
    return jnp.concatenate(pieces, axis=1)


def features_step(taps, weight, out, woven, sems, k, pairs, copies):
    half = taps[-1].shape[0]
    slots = woven.shape[0]
    near = [
        stack(taps, [2 * (k * pairs + q) + i - 1 for q in range(pairs)], half) for i in range(4)
    ]
    part = jnp.dot(jnp.concatenate(near, axis=1), weight[...], preferred_element_type=F32)
    for q in range(pairs):
        j = k * pairs + q
        b = j % slots
        rows = slice(q * half, (q + 1) * half)
        if j >= slots:
            copies[j - slots].wait()
        woven[b, pl.ds(0, half, stride=2), :] = part[rows, 0:128]
        woven[b, pl.ds(1, half, stride=2), :] = part[rows, 128:256]
        copy = pltpu.make_async_copy(woven.at[b], out.at[:, pl.ds(j * LANES, LANES)], sems.at[b])
        copy.start()
        copies.append(copy)


def grads_body(count, lift, pre_one, sums_one, back_stats, vec, masks, k1, taps_x, two,
               grad_x, blocks, sums_out, weight, acc_one, woven, sems, *buffers):
    sides, taps = buffers[: 2 * SIDES], buffers[2 * SIDES :]
    place_one_back(k1, weight)
    back = stat_sums(back_stats)
    sums_out[...] = back
    a, b, c = grad_terms(sums_one[...], back, vec[0:1], count)
    taps[-1][...] = jnp.zeros(taps[-1].shape, BF16)

    def lower(m):
        def tile(r):
            span = slice(r, r + TILE)
            return halves_of(lift[m, span] * a + (pre_one[m, span] * b + c))

        emit_taps(ring_slot(taps, m), masks, sides[m % SIDES], sides[SIDES + m % SIDES], tile)

    pairs = 4
    copies = []
    for k in range(MEL // 2 // pairs + 1):
        for m in range(2 * pairs * k, 2 * pairs * (k + 1)):
            if m < MEL:
                lower(m)
        if k > 0:
            kernel_one_step(taps_x, taps, acc_one, k - 1, pairs)
            features_step(taps, weight, grad_x, woven, sems, k - 1, pairs, copies)
    scatter_blocks(blocks, [kernel_one_sums(acc_one), two[...]])
    for copy in copies[-woven.shape[0] :]:
        copy.wait()


def all_grads(lift, pre_one, sums_one, back_stats, vec, masks, k1, taps_x, two, share, count):
    copies = back_stats.shape[0]
    half = masks.shape[1] - TAIL
    row_count = copies * share // C_MID
    wide = padded(9 * (C_IN + C_MID) // row_count)
    args = (lift, pre_one, sums_one, back_stats, vec, masks, k1, taps_x, two)
    return call(
        lambda *refs: grads_body(count, *refs),
        args,
        [
            like((2 * half, MEL * C_IN), F32),
            like((copies, share, wide), BF16),
            like((2, C_MID), F32),
        ],
        [
            pltpu.VMEM((4 * WIDE, BOTH), BF16),
            pltpu.VMEM((BOTH, 3 * BOTH), F32),
            pltpu.VMEM((8, 2 * half, LANES), F32),
            pltpu.SemaphoreType.DMA((8,)),
            *side_scratch(half + TAIL),
            *ring_scratch(27, half),
        ],

        out_specs=[ANY, VMEM, VMEM],
    )


def finish_body(got, back_one_sums, back_two_sums, own_one, own_two, ga, sa, gb, sb):
    total = jnp.sum(got[...].astype(F32), axis=0)
    size = own_one.shape[1]
    own_one[...] = total[:, 0:size]
    own_two[...] = total[:, size : size + own_two.shape[1]]
    share = ga.shape[1]
    lane = lax.broadcasted_iota(jnp.int32, (share, C_MID), 1)
    row = lax.broadcasted_iota(jnp.int32, (share, C_MID), 0)
    chosen = lane == lax.axis_index("grp") * share + row
    first = lax.broadcasted_iota(jnp.int32, (share, share), 0)
    second = lax.broadcasted_iota(jnp.int32, (share, share), 1)
    for out, sums, k in (
        (ga, back_one_sums, 1), (sa, back_one_sums, 0), (gb, back_two_sums, 1), (sb, back_two_sums, 0)
    ):
        wide = jnp.broadcast_to(sums[k : k + 1], (share, C_MID))
        column = jnp.sum(jnp.where(chosen, wide, 0.0), axis=1, keepdims=True)
        wide = jnp.broadcast_to(column, (share, share))
        out[...] = jnp.sum(jnp.where(first == second, wide, 0.0), axis=0, keepdims=True)


def finish(got, back_one_sums, back_two_sums, rows_one, rows_two):
    share = got.shape[1]
    shapes = [(share, rows_one), (share, rows_two)] + [(1, share)] * 4
    return call(
        finish_body,
        (got, back_one_sums, back_two_sums),
        [like(s, F32) for s in shapes],
    )


def exchange(blocks):
    return lax.all_to_all(blocks, AXES, 0, 0, tiled=True)


def shards(
    features, clip_starts, kernel_one, kernel_two, gain_one, shift_one, gain_two, shift_two, cotangent
):
    frames = features.shape[0]
    copies = lax.axis_size(AXES)
    row_count = lax.axis_size("row")
    count = float(frames * MEL * copies)
    rows_one, rows_two = kernel_one.shape[0], kernel_two.shape[0]
    share = kernel_one.shape[1]
    vectors = [v.reshape(1, share) for v in (gain_one, shift_one, gain_two, shift_two)]
    clips = clip_starts.reshape(1, -1)
    weights, up, down, clips = setup(
        kernel_one.T, kernel_two.T, vectors, clips, features, cotangent, copies
    )
    ends = copies - 1
    up = lax.ppermute(up, AXES, [(i, i + 1) for i in range(ends)])
    down = lax.ppermute(down, AXES, [(i + 1, i) for i in range(ends)])
    weights = exchange(weights)
    pre_one, stats, taps_x, masks, k1, k2, vec = conv_one(
        features, up, down, clips, weights, row_count
    )
    stats = exchange(stats)
    pre_two, stats, taps_a, sums_one = conv_two(pre_one, stats, vec, masks, k2, count)
    stats = exchange(stats)
    block_out, lift, stats, sums_two = norm_two(pre_two, stats, vec, cotangent, up, down, count)
    stats = exchange(stats)
    lift, two, stats, back_two_sums = back_two(
        lift, pre_two, sums_two, stats, vec, masks, k2, pre_one, sums_one, taps_a, count
    )
    stats = exchange(stats)
    grad_features, blocks, back_one_sums = all_grads(
        lift, pre_one, sums_one, stats, vec, masks, k1, taps_x, two, share, count
    )
    own_one, own_two, ga, sa, gb, sb = finish(
        exchange(blocks), back_one_sums, back_two_sums, rows_one, rows_two
    )
    return (
        block_out,
        grad_features,
        own_one.T,
        own_two.T,
        ga.reshape(share),
        sa.reshape(share),
        gb.reshape(share),
        sb.reshape(share),
    )


def solution(mesh):
    placed = (
        P(AXES, None), P(), P("row", "grp"), P("row", "grp"),
        P("grp"), P("grp"), P("grp"), P("grp"), P(AXES, None),
    )
    return jax.shard_map(
        shards,
        mesh=mesh,
        in_specs=placed,
        out_specs=(
            P(AXES, None), P(AXES, None), P("row", "grp"), P("row", "grp"),
            P("grp"), P("grp"), P("grp"), P("grp"),
        ),
        check_vma=False,
    )
```

```python
import jax
import jax.numpy as jnp
from jax import lax
from jax.experimental import pallas as pl
from jax.experimental.pallas import tpu as pltpu
from jax.sharding import PartitionSpec as P

MEL = 32
C_IN = 64
C_MID = 128
EPS = 1e-05
AXES = ("grp", "row")
LANES = 128
TAIL = 16
WIDE = 4 * LANES
BOTH = 2 * C_MID
F32 = jnp.float32
BF16 = jnp.bfloat16
TILE = 16
SIDES = 4
MIB = 2**20

VMEM = pl.BlockSpec(memory_space=pltpu.VMEM)
ANY = pl.BlockSpec(memory_space=pl.ANY)
HBM = pl.BlockSpec(memory_space=pltpu.HBM)


def like(shape, dtype):
    return jax.ShapeDtypeStruct(shape, dtype)


def call(body, args, outs, scratch=(), limit=16, cost=None, in_specs=None, out_specs=None, **more):
    return pl.pallas_call(
        body,
        in_specs=in_specs or [VMEM] * len(args),
        out_specs=out_specs or [VMEM] * len(outs),
        out_shape=outs,
        scratch_shapes=list(scratch),
        compiler_params=pltpu.CompilerParams(vmem_limit_bytes=limit * MIB),
        cost_estimate=cost,
        **more,
    )(*args)


def padded(size):
    return -(-size // LANES) * LANES


def packed_rows(share, wide):
    rest = wide - LANES
    if rest > 0 and share == 32 and 3 * (LANES - rest) >= rest:
        return share + 24
    return share * (padded(wide) // LANES)


def pack(block, rows):
    share, wide = block.shape
    if rows % share == 0:
        block = jnp.concatenate([block, jnp.zeros((share, padded(wide) - wide), F32)], axis=1)
        return jnp.concatenate(
            [block[:, at : at + LANES] for at in range(0, block.shape[1], LANES)], axis=0
        )
    rest = block[:, LANES:]
    room = 2 * LANES - wide
    tail = jnp.concatenate(
        [rest[24:32], jnp.zeros((8, 3 * room - rest.shape[1]), F32)], axis=1
    )
    tail = jnp.concatenate([tail[:, k * room : (k + 1) * room] for k in range(3)], axis=0)
    return jnp.concatenate([block[:, :LANES], jnp.concatenate([rest[0:24], tail], axis=1)], axis=0)


def unpack(block, share, wide):
    rows = block.shape[0]
    if rows % share == 0:
        parts = [block[at : at + share] for at in range(0, rows, share)]
        return jnp.concatenate(parts, axis=1)[:, 0:wide]
    width = wide - LANES
    second = block[share:]
    tail = jnp.concatenate([second[8 * k : 8 * k + 8, width:] for k in range(3)], axis=1)
    rest = jnp.concatenate([second[:, :width], tail[:, :width]], axis=0)
    return jnp.concatenate([block[0:share], rest], axis=1)


def partial_sum(values):
    return jnp.sum(values.reshape(-1, 8, values.shape[-1]), axis=0)


def fold(values):
    total = jnp.sum(values, axis=0, keepdims=True)
    return total[:, :C_MID] + total[:, C_MID:]


def spread(first, second, out):
    sums = jnp.concatenate([first, second], axis=0)
    out[...] = jnp.broadcast_to(sums[None], out.shape)


def twice(row):
    return jnp.concatenate([row, row], axis=1)


def tiles(rows):
    return range(0, rows, TILE)


def emit_taps(taps, masks, evens, odds, tile_of):
    rows = masks.shape[1]
    kept = taps.shape[0]
    for r in tiles(rows):
        even, odd = tile_of(r)
        evens[r : r + TILE] = even
        odds[8 + r : 8 + r + TILE] = odd
        if r == 0:
            evens[rows : rows + 1] = even[0:1]
        if r + TILE == rows:
            odds[7:8] = odd[TILE - 1 : TILE]
        if r < kept:
            taps[r : r + TILE, 128:256] = even.astype(BF16)
            taps[r : r + TILE, 256:384] = odd.astype(BF16)
    for r in tiles(kept):
        span = slice(r, r + TILE)
        before = odds[7 + r : 7 + r + TILE] * masks[0, span]
        after = evens[1 + r : 1 + r + TILE] * masks[1, span]
        taps[span, 0:128] = before.astype(BF16)
        taps[span, 384:512] = after.astype(BF16)


def halves_of(value):
    return value[:, :C_MID], value[:, C_MID:]


def add_sums(acc, first, second):
    acc[0] += first
    acc[1] += second


def side_scratch(rows):
    return [pltpu.VMEM((rows + 8, LANES), F32)] * (2 * SIDES)


def stats_of(out, mels, rows, half, acc):
    first = jnp.zeros((8, BOTH), F32)
    second = jnp.zeros((8, BOTH), F32)
    for k in range(mels):
        for r in range(0, half, 8):
            value = out[k * rows + r : k * rows + r + 8]
            first += value
            second += value * value
    add_sums(acc, first, second)


def normed_sum(with_half_lifted, plain, gain, shift):
    return (2.0 * with_half_lifted - shift * plain) / gain


def stat_sums(stats):
    return jnp.sum(stats[...], axis=0)


def norm_terms(sums, count):
    mean = sums[0:1] / count
    rstd = lax.rsqrt(sums[1:2] / count - mean * mean + EPS)
    return mean, rstd


def dot_rows(first, second):
    return lax.dot_general(
        first, second, (((0,), (0,)), ((), ())), preferred_element_type=F32
    )


def ring_slot(ring, m):
    return ring[m % (len(ring) - 1)] if 0 <= m < MEL else ring[-1]


def stack(ring, mels, rows, lanes=slice(None)):
    return jnp.concatenate([ring_slot(ring, m)[0:rows, lanes] for m in mels], axis=0)


def ring_scratch(slots, rows):
    return [pltpu.VMEM((rows, WIDE), BF16)] * slots


def clear_ends(taps):
    blank = jnp.zeros(taps.shape[1:], BF16)
    taps[0] = blank
    taps[taps.shape[0] - 1] = blank


def emit_masks(copies, clips, masks):
    rows = masks.shape[0]
    half = rows - TAIL
    frames = 2 * half
    start = lax.axis_index(AXES) * frames
    place = lax.broadcasted_iota(jnp.int32, (rows, clips.shape[1]), 0)
    pair = jnp.where(place >= half + TAIL // 2, place - rows, place)
    frame = start + 2 * pair
    starts = jnp.broadcast_to(clips[...], (rows, clips.shape[1]))
    for slot, shift in ((0, 0), (1, 2)):
        hit = (frame + shift == starts) | (frame + shift >= frames * copies)
        begins = jnp.max(jnp.where(hit, 1.0, 0.0), axis=1, keepdims=True)
        keep = jnp.broadcast_to(1.0 - begins, (rows, LANES)).astype(BF16)
        masks[:, slot * LANES : (slot + 1) * LANES] = keep


HELD = 15360


def setup_body(k1, k2, ga, sa, gb, sb, clips, features, x_head, x_tail, c_head, c_tail,
               w_out, up, down, held, masks, sems):
    frames = features.shape[0]
    keep = pltpu.make_async_copy(features, held.at[pl.ds(0, frames)], sems.at[0])
    keep.start()
    emit_masks(w_out.shape[0], clips, masks)
    here = held.at[pl.ds(frames, masks.shape[0]), pl.ds(0, 2 * LANES)]
    keep_masks = pltpu.make_async_copy(masks, here, sems.at[1])
    keep_masks.start()
    share = k1.shape[0]
    copies = w_out.shape[0]
    first = lax.broadcasted_iota(jnp.int32, (share, share), 0)
    second = lax.broadcasted_iota(jnp.int32, (share, share), 1)
    columns = [k1[...].astype(F32), k2[...].astype(F32)]
    for vector in (ga, sa, gb, sb):
        wide = jnp.broadcast_to(vector[...].astype(F32), (share, share))
        columns.append(jnp.sum(jnp.where(first == second, wide, 0.0), axis=1, keepdims=True))
    chunk = pack(jnp.concatenate(columns, axis=1), w_out.shape[1]).astype(BF16)
    for i in range(copies):
        w_out[i] = chunk
    row = lax.broadcasted_iota(jnp.int32, (8, x_head.shape[1]), 0)
    xt = x_tail[...].astype(F32)
    ct = c_tail[...].astype(F32)
    up[...] = jnp.where(
        row < 4, pltpu.roll(xt[8:16], 4, 0), jnp.where(row == 4, ct[15:16], 0.0)
    ).astype(BF16)
    xh = x_head[...].astype(F32)
    ch = c_head[...].astype(F32)
    down[...] = jnp.where(row < 4, xh[0:8], jnp.where(row == 4, ch[0:1], 0.0)).astype(BF16)
    keep.wait()
    keep_masks.wait()


def setup(k1t, k2t, vectors, clips, features, cotangent, copies):
    frames, wide = features.shape
    halves = cotangent.shape[0]
    share = k1t.shape[0]
    w = (copies, packed_rows(share, k1t.shape[1] + k2t.shape[1] + 4), LANES)
    whole = lambda shape: pl.BlockSpec(shape, lambda i: (0,) * len(shape))
    side = (8, wide)
    outs = [like(w, BF16), like(side, BF16), like(side, BF16), like((HELD, wide), BF16)]
    return call(
        setup_body,
        (k1t, k2t, *vectors, clips, features, features, features, cotangent, cotangent),
        outs,
        limit=56,
        in_specs=[
            whole(k1t.shape),
            whole(k2t.shape),
            *[whole((1, share))] * 4,
            whole(clips.shape),
            HBM,
            pl.BlockSpec((16, wide), lambda i: (0, 0)),
            pl.BlockSpec((16, wide), lambda i: (frames // 16 - 1, 0)),
            pl.BlockSpec((16, wide), lambda i: (0, 0)),
            pl.BlockSpec((16, wide), lambda i: (halves // 16 - 1, 0)),
        ],
        out_specs=[whole(w), whole(side), whole(side), HBM],
        scratch=[pltpu.VMEM((frames // 2 + TAIL, 2 * LANES), BF16), pltpu.SemaphoreType.DMA((2,))],
        grid=(1,),
    )


def split_bins(parts):
    low = lax.broadcasted_iota(jnp.int32, parts[0].shape, 1) < C_IN
    first, second = [], []
    for here, there in (parts[0:2], parts[2:4]):
        first.append(jnp.where(low, here, pltpu.roll(there, C_IN, 1)))
        second.append(jnp.where(low, pltpu.roll(here, C_IN, 1), there))
    return jnp.concatenate(first + second, axis=1)


def near_bins(taps, pairs, rows):
    left, mid, right = [
        jnp.concatenate([taps[1 + j + k, 0:rows] for j in pairs], axis=0) for k in (-1, 0, 1)
    ]
    first = jnp.concatenate([left[:, BOTH:], mid], axis=1)
    second = jnp.concatenate([mid, right[:, :BOTH]], axis=1)
    return jnp.concatenate([first, second], axis=0)


def emit_taps_one(fetch, x, up, down, masks, taps, frames):
    rows = masks.shape[1]
    half = rows - TAIL
    clear_ends(taps)
    row = lax.broadcasted_iota(jnp.int32, (8, LANES), 0)
    lead = 24
    own = 2 * half
    for b in range(2):
        frames[b, 0:16] = jnp.zeros((16, LANES), F32)
        frames[b, lead + own + 8 : lead + own + 24] = jnp.zeros((16, LANES), F32)

    def pair(j, b):
        lanes = pl.ds(pl.multiple_of(j * LANES, LANES), LANES)
        u = up[:, lanes].astype(F32)
        d = down[:, lanes].astype(F32)
        frames[b, lead - 8 : lead] = jnp.where(row >= 4, pltpu.roll(u, 4, 0), 0.0)
        frames[b, lead + own : lead + own + 8] = jnp.where(row < 4, d, 0.0)
        for r in tiles(own):
            frames[b, lead + r : lead + r + TILE] = x[r : r + TILE, lanes].astype(F32)

        def pick(first, count, shift):
            return frames[b, pl.ds(lead + 2 * first + shift, count, stride=2), :]

        for r in tiles(rows):
            parts = []
            for shift in (-1, 0, 1, 2):
                if r < half:
                    parts.append(pick(r, TILE, shift))
                else:
                    parts.append(
                        jnp.concatenate([pick(half, 8, shift), pick(-8, 8, shift)], axis=0)
                    )
            span = slice(r, r + TILE)
            parts[0] = parts[0] * masks[0, span]
            parts[3] = parts[3] * masks[1, span]
            taps[1 + j, span, :] = split_bins(parts).astype(BF16)

    def two_pairs(i, carry):
        pair(2 * i, 0)
        pair(2 * i + 1, 1)
        return carry

    each = MEL // 4 // len(fetch)
    for k, copy in enumerate(fetch):
        copy.wait()
        lax.fori_loop(k * each, (k + 1) * each, two_pairs, 0)


def emit_weights_one(row_count, wg, k1_out, k2_out, vec_out, kf, weight):
    rows_one = 9 * C_IN // row_count
    rows_two = 9 * C_MID // row_count
    grps = wg.shape[0] // row_count
    share = C_MID // grps
    for r in range(row_count):
        shard = [
            unpack(wg[g * row_count + r].astype(F32), share, rows_one + rows_two + 4)
            for g in range(grps)
        ]
        shard = jnp.concatenate(shard, axis=0).T
        kf[rows_one * r : rows_one * (r + 1)] = shard[0:rows_one]
        at = 9 * C_IN + rows_two * r
        kf[at : at + rows_two] = shard[rows_one : rows_one + rows_two]
        if r == 0:
            vec_out[...] = shard[rows_one + rows_two : rows_one + rows_two + 4]
    k1_out[...] = kf[0 : 9 * C_IN].astype(BF16)
    k2_out[...] = kf[9 * C_IN :].astype(BF16)
    weight[...] = jnp.zeros(weight.shape, BF16)
    for d in range(3):
        for q in range(4):
            for p in range(2):
                t = q - p
                if 0 <= t < 3:
                    at = d * BOTH + q * C_IN
                    start = (3 * t + d) * C_IN
                    weight[at : at + C_IN, p * 128 : p * 128 + 128] = k1_out[start : start + C_IN]


def conv_one_body(row_count, held, up, down, wg,
                  pre, stats, taps, masks, k1_out, k2_out, vec_out,
                  kf, weight, acc, frames, x, both, sems, side_sem):
    own = x.shape[0]
    held_masks = held.at[pl.ds(own, both.shape[0]), pl.ds(0, 2 * LANES)]
    mask_copy = pltpu.make_async_copy(held_masks, both, side_sem)
    mask_copy.start()
    wide = x.shape[1] // sems.shape[0]
    fetch = []
    for k in range(sems.shape[0]):
        lanes = pl.ds(k * wide, wide)
        fetch.append(pltpu.make_async_copy(held.at[pl.ds(0, own), lanes], x.at[:, lanes], sems.at[k]))
        fetch[k].start()
    emit_weights_one(row_count, wg, k1_out, k2_out, vec_out, kf, weight)
    mask_copy.wait()
    for slot in range(2):
        masks[slot] = both[:, slot * LANES : (slot + 1) * LANES].astype(F32)
    emit_taps_one(fetch, x, up, down, masks, taps, frames)
    rows = taps.shape[1]
    half = rows - TAIL
    pairs = 4
    acc[...] = jnp.zeros(acc.shape, F32)
    for c in range(MEL // 2 // pairs):
        here = range(c * pairs, (c + 1) * pairs)
        out = jnp.dot(near_bins(taps, here, rows), weight[...], preferred_element_type=F32)
        for parity in range(2):
            for q in range(pairs):
                at = (parity * pairs + q) * rows
                pre[2 * (c * pairs + q) + parity] = out[at : at + rows]
        stats_of(out, 2 * pairs, rows, half, acc)
    spread(fold(acc[0]), fold(acc[1]), stats)


def conv_one(frames, held, up, down, wg, row_count):
    rows = frames // 2 + TAIL
    copies = wg.shape[0]
    return call(
        lambda *refs: conv_one_body(row_count, *refs),
        (held, up, down, wg),
        [
            like((MEL, rows, BOTH), F32),
            like((copies, 2, C_MID), F32),
            like((MEL // 2 + 2, rows, WIDE), BF16),
            like((2, rows, LANES), F32),
            like((9 * C_IN, C_MID), BF16),
            like((9 * C_MID, C_MID), BF16),
            like((4, C_MID), F32),
        ],
        [
            pltpu.VMEM((9 * (C_IN + C_MID), C_MID), F32),
            pltpu.VMEM((3 * BOTH, BOTH), BF16),
            pltpu.VMEM((2, 8, BOTH), F32),
            pltpu.VMEM((2, frames + 48, LANES), F32),
            pltpu.VMEM((frames, held.shape[1]), BF16),
            pltpu.VMEM((rows, 2 * LANES), BF16),
            pltpu.SemaphoreType.DMA((4,)),
            pltpu.SemaphoreType.DMA,
        ],
        in_specs=[HBM, VMEM, VMEM, VMEM],
    )


def place_two(k2, weight):
    weight[...] = jnp.zeros(weight.shape, BF16)
    for d in range(3):
        for q in range(4):
            for p in range(2):
                t = q - p
                if 0 <= t < 3:
                    at = d * WIDE + q * 128
                    start = (3 * t + d) * C_MID
                    weight[at : at + 128, p * 128 : p * 128 + 128] = k2[start : start + C_MID]


def place_two_back(k2, weight):
    weight[...] = jnp.zeros(weight.shape, BF16)
    for t in range(3):
        for d in range(3):
            start = (3 * t + d) * C_MID
            turned = (0.5 * k2[start : start + C_MID].astype(F32).T).astype(BF16)
            for p in range(2):
                at = (2 - d) * WIDE + (2 - t + p) * 128
                weight[at : at + 128, p * 128 : p * 128 + 128] = turned


def place_one_back(k1, weight):
    weight[...] = jnp.zeros(weight.shape, BF16)
    for t in range(3):
        for d in range(3):
            start = (3 * t + d) * C_IN
            turned = k1[start : start + C_IN].astype(F32).T.astype(BF16)
            for mo in (1, 2):
                for p in range(2):
                    at = (mo - d + 1) * WIDE + (2 - t + p) * 128
                    to = p * 128 + (mo - 1) * 64
                    weight[at : at + 128, to : to + 64] = turned


def conv_two_body(count, pre_one, stats_one, vec, masks, k2, pre, stats, taps, sums_out,
                  acc, weight, *sides):
    place_two(k2, weight)
    rows = masks.shape[1]
    half = rows - TAIL
    mels = 2
    sums = stat_sums(stats_one)
    sums_out[...] = sums
    mean, rstd = norm_terms(sums, count)
    scale = 0.5 * vec[0:1] * rstd
    shift = twice(0.5 * vec[1:2] - mean * scale)
    scale = twice(scale)
    clear_ends(taps)
    acc[...] = jnp.zeros(acc.shape, F32)

    def activate(m):
        def tile(r):
            h = pre_one[m, r : r + TILE] * scale + shift
            return halves_of(h + h * jnp.tanh(h))

        emit_taps(taps.at[1 + m], masks, sides[m % SIDES], sides[SIDES + m % SIDES], tile)

    def convolve(c):
        lhs = [taps[c * mels + d : (c + 1) * mels + d].reshape(mels * rows, WIDE) for d in range(3)]
        out = jnp.dot(jnp.concatenate(lhs, axis=1), weight[...], preferred_element_type=F32)
        pre[c * mels : (c + 1) * mels] = out.reshape(mels, rows, BOTH)
        stats_of(out, mels, rows, half, acc)

    for m in range(MEL):
        activate(m)
        if m >= mels and m % mels == 0:
            convolve(m // mels - 1)
    convolve(MEL // mels - 1)
    spread(fold(acc[0]), fold(acc[1]), stats)


def conv_two(pre_one, stats_one, vec, masks, k2, count):
    copies = stats_one.shape[0]
    rows = masks.shape[1]
    return call(
        lambda *refs: conv_two_body(count, *refs),
        (pre_one, stats_one, vec, masks, k2),
        [
            like((MEL, rows, BOTH), F32),
            like((copies, 2, C_MID), F32),
            like((MEL + 2, rows, WIDE), BF16),
            like((2, C_MID), F32),
        ],
        [pltpu.VMEM((2, 8, BOTH), F32), pltpu.VMEM((3 * WIDE, BOTH), BF16), *side_scratch(rows)],
        cost=pl.CostEstimate(flops=5 * 10**9, bytes_accessed=0, transcendentals=0),
    )


def norm_two_body(count, pre, stats_two, vec, cot, up, down, pooled, lift, back_stats, sums_out, acc):
    half = cot.shape[0]
    sums = stat_sums(stats_two)
    sums_out[...] = sums
    mean, rstd = norm_terms(sums, count)
    scale = 0.5 * vec[2:3] * rstd
    shift = 0.5 * vec[3:4] - mean * scale
    acc[...] = jnp.zeros(acc.shape, F32)
    row = lax.broadcasted_iota(jnp.int32, (TAIL, LANES), 0)

    def pair(j, carry):
        lanes = pl.ds(pl.multiple_of(j * LANES, LANES), LANES)
        u = up[:, lanes].astype(F32)
        d = down[:, lanes].astype(F32)
        first = jnp.zeros((8, LANES), F32)
        second = jnp.zeros((8, LANES), F32)
        for r in tiles(half + TAIL):
            span = slice(r, r + TILE)
            if r < half:
                grad = cot[span, lanes].astype(F32) * 0.125
            else:
                grad = jnp.where(row == 0, d[4:5], jnp.where(row == TAIL - 1, u[4:5], 0.0)) * 0.125
            total = jnp.zeros((TILE, LANES), F32)
            for m in (2 * j, 2 * j + 1):
                for p in range(2):
                    side = slice(p * C_MID, (p + 1) * C_MID)
                    value = pre[m, span, side]
                    h = value * scale + shift
                    th = jnp.tanh(h)
                    one = 1.0 + th
                    silu = h * one
                    gl = grad * (one + (silu - silu * th))
                    lift[m, span, side] = gl
                    if r < half:
                        total += silu
                        first += partial_sum(gl)
                        second += partial_sum(gl * h)
            if r < half:
                pooled[span, lanes] = (total * 0.25).astype(BF16)
        add_sums(acc, first, second)
        return carry

    lax.fori_loop(0, MEL // 2, pair, 0)
    first, second = [jnp.sum(acc[k], axis=0, keepdims=True) for k in range(2)]
    spread(first, normed_sum(second, first, vec[2:3], vec[3:4]), back_stats)


def norm_two(pre, stats_two, vec, cot, up, down, count):
    copies = stats_two.shape[0]
    half, wide = cot.shape
    return call(
        lambda *refs: norm_two_body(count, *refs),
        (pre, stats_two, vec, cot, up, down),
        [
            like((half, wide), BF16),
            like((MEL, half + TAIL, BOTH), F32),
            like((copies, 2, C_MID), F32),
            like((2, C_MID), F32),
        ],
        [pltpu.VMEM((2, 8, LANES), F32)],
    )


def grad_terms(sums, back, gain, count):
    mean, rstd = norm_terms(sums, count)
    a = gain * rstd
    b = -a * rstd * (back[1:2] / count)
    c = -a * (back[0:1] / count) - b * mean
    return twice(a), twice(b), twice(c)


def back_two_body(count, lift, pre_two, sums_two, back_stats, vec, masks, k2, pre_one, sums_one,
                  taps_a, lift_one, two, back_out, sums_out, acc, acc_two, weight, *buffers):
    place_two_back(k2, weight)
    sides, taps = buffers[: 2 * SIDES], buffers[2 * SIDES :]
    rows = masks.shape[1]
    half = rows - TAIL
    mels = 4
    back = stat_sums(back_stats)
    sums_out[...] = back
    a, b, c = grad_terms(sums_two[...], back, vec[2:3], count)
    mean, rstd = norm_terms(sums_one[...], count)
    scale = 0.5 * vec[0:1] * rstd
    shift = twice(0.5 * vec[1:2] - mean * scale)
    scale = twice(scale)
    taps[-1][...] = jnp.zeros(taps[-1].shape, BF16)
    acc[...] = jnp.zeros(acc.shape, F32)

    def lower(m):
        def tile(r):
            span = slice(r, r + TILE)
            return halves_of(lift[m, span] * a + (pre_two[m, span] * b + c))

        emit_taps(ring_slot(taps, m), masks, sides[m % SIDES], sides[SIDES + m % SIDES], tile)

    def convolve(k):
        lhs = [stack(taps, range(k * mels + d - 1, (k + 1) * mels + d - 1), rows) for d in range(3)]
        out = jnp.dot(jnp.concatenate(lhs, axis=1), weight[...], preferred_element_type=F32)
        first = jnp.zeros((8, BOTH), F32)
        second = jnp.zeros((8, BOTH), F32)
        for i in range(mels):
            m = k * mels + i
            for r in range(0, rows, 8):
                span = slice(r, r + 8)
                h = pre_one[m, span] * scale + shift
                th = jnp.tanh(h)
                one = 1.0 + th
                silu = h * one
                gl = out[i * rows + r : i * rows + r + 8] * (one + (silu - silu * th))
                lift_one[m, span] = gl
                if r < half:
                    first += gl
                    second += gl * h
        add_sums(acc, first, second)

    def correlate(k):
        here = range(k * mels, (k + 1) * mels)
        near = [
            taps_a[k * mels + d : (k + 1) * mels + d, 0:half].reshape(mels * half, WIDE) for d in range(3)
        ]
        total = dot_rows(stack(taps, here, half, slice(128, 384)), jnp.concatenate(near, axis=1))
        if k == 0:
            acc_two[...] = total
        else:
            acc_two[...] += total

    for k in range(MEL // mels + 1):
        for m in range(k * mels, (k + 1) * mels):
            if m < MEL:
                lower(m)
        if k > 0:
            convolve(k - 1)
            correlate(k - 1)
    plain = fold(acc[0])
    spread(plain, normed_sum(fold(acc[1]), plain, vec[0:1], vec[1:2]), back_out)
    for t in range(3):
        for d in range(3):
            at = d * WIDE + t * 128
            to = (3 * t + d) * 128
            two[:, to : to + 128] = (
                acc_two[0:C_MID, at : at + 128] + acc_two[C_MID:BOTH, at + 128 : at + 256]
            )


def back_two(lift, pre_two, sums_two, back_stats, vec, masks, k2, pre_one, sums_one, taps_a, count):
    copies = back_stats.shape[0]
    rows = masks.shape[1]
    return call(
        lambda *refs: back_two_body(count, *refs),
        (lift, pre_two, sums_two, back_stats, vec, masks, k2, pre_one, sums_one, taps_a),
        [
            like((MEL, rows, BOTH), F32),
            like((C_MID, 9 * C_MID), F32),
            like((copies, 2, C_MID), F32),
            like((2, C_MID), F32),
        ],
        [
            pltpu.VMEM((2, 8, BOTH), F32),
            pltpu.VMEM((BOTH, 3 * WIDE), F32),
            pltpu.VMEM((3 * WIDE, BOTH), BF16),
            *side_scratch(rows),
            *ring_scratch(17, rows),
        ],

        input_output_aliases={0: 0},
    )


def scatter_blocks(out, parts, row_count):
    copies = out.shape[0]
    grps = copies // row_count
    share = C_MID // grps
    turned = [part.T for part in parts]
    sizes = [part.shape[1] // row_count for part in parts]
    for r in range(row_count):
        rows = [t[n * r : n * (r + 1)] for t, n in zip(turned, sizes)]
        back = jnp.concatenate(rows, axis=0).T
        for g in range(grps):
            block = back[share * g : share * (g + 1)]
            out[g * row_count + r] = pack(block, out.shape[1]).astype(BF16)


def kernel_one_step(taps_x, taps, acc, k, pairs):
    half = taps[-1].shape[0]
    here = range(k * pairs, (k + 1) * pairs)
    mels = [2 * j + parity for parity in range(2) for j in here]
    chosen = jnp.concatenate([taps[m % len(taps)][:, 128:384] for m in mels], axis=0)
    total = dot_rows(chosen, near_bins(taps_x, here, half))
    if k == 0:
        acc[...] = total
    else:
        acc[...] += total


def kernel_one_sums(acc):
    pieces = []
    for t in range(3):
        for d in range(3):
            total = jnp.zeros((C_MID, C_IN), F32)
            for p in range(2):
                at = d * BOTH + (t + p) * C_IN
                total += acc[p * C_MID : (p + 1) * C_MID, at : at + C_IN]
            pieces.append(total)
    return jnp.concatenate(pieces, axis=1)


STORED = 320


def grads_body(count, row_count, lift, pre_one, sums_one, back_stats, vec, masks, taps_x, two,
               stored, blocks, sums_out, acc_one, sems, *buffers):
    sides, taps = buffers[: 2 * SIDES], buffers[2 * SIDES :]
    slots = len(taps)
    back = stat_sums(back_stats)
    sums_out[...] = back
    a, b, c = grad_terms(sums_one[...], back, vec[0:1], count)

    def lower(m):
        def tile(r):
            span = slice(r, r + TILE)
            return halves_of(lift[m, span] * a + (pre_one[m, span] * b + c))

        emit_taps(taps[m % slots], masks, sides[m % SIDES], sides[SIDES + m % SIDES], tile)

    pairs = 4
    copies = []
    for k in range(MEL // 2 // pairs + 1):
        for m in range(2 * pairs * k, 2 * pairs * (k + 1)):
            if m < MEL:
                if m >= slots:
                    copies[m - slots].wait()
                lower(m)
                copy = pltpu.make_async_copy(taps[m % slots], stored.at[m], sems.at[m % slots])
                copy.start()
                copies.append(copy)
        if k > 0:
            kernel_one_step(taps_x, taps, acc_one, k - 1, pairs)
    scatter_blocks(blocks, [kernel_one_sums(acc_one), two[...]], row_count)
    for copy in copies[-slots:]:
        copy.wait()


def kernel_grads(lift, pre_one, sums_one, back_stats, vec, masks, taps_x, two, row_count, count):
    copies = back_stats.shape[0]
    half = masks.shape[1] - TAIL
    share = C_MID * row_count // copies
    rows = packed_rows(share, 9 * (C_IN + C_MID) // row_count)
    slots = 24
    return call(
        lambda *refs: grads_body(count, row_count, *refs),
        (lift, pre_one, sums_one, back_stats, vec, masks, taps_x, two),
        [
            like((STORED, half, WIDE), BF16),
            like((copies, rows, LANES), BF16),
            like((2, C_MID), F32),
        ],
        [
            pltpu.VMEM((BOTH, 3 * BOTH), F32),
            pltpu.SemaphoreType.DMA((slots,)),
            *side_scratch(half + TAIL),
            *ring_scratch(slots, half),
        ],
        out_specs=[HBM, VMEM, VMEM],
    )


def features_body(stored, k1, out, taps, weight, woven, sems, out_sems):
    pairs = 4
    half = taps.shape[1]
    group = MEL // sems.shape[0]
    fetch = []
    for k in range(sems.shape[0]):
        here = pl.ds(k * group, group)
        fetch.append(
            pltpu.make_async_copy(
                stored.at[here], taps.at[pl.ds(1 + k * group, group)], sems.at[k]
            )
        )
        fetch[k].start()
    clear_ends(taps)
    place_one_back(k1, weight)
    fetched = 0
    copies = []
    slots = woven.shape[0]
    for k in range(MEL // 2 // pairs):
        while fetched * group < min(2 * pairs * (k + 1) + 1, MEL):
            fetch[fetched].wait()
            fetched += 1
        near = []
        for i in range(4):
            mels = [taps[2 * (k * pairs + q) + i] for q in range(pairs)]
            near.append(jnp.concatenate(mels, axis=0))
        part = jnp.dot(jnp.concatenate(near, axis=1), weight[...], preferred_element_type=F32)
        for q in range(pairs):
            j = k * pairs + q
            b = j % slots
            rows = slice(q * half, (q + 1) * half)
            if j >= slots:
                copies[j - slots].wait()
            woven[b, pl.ds(0, half, stride=2), :] = part[rows, 0:128]
            woven[b, pl.ds(1, half, stride=2), :] = part[rows, 128:256]
            copy = pltpu.make_async_copy(
                woven.at[b], out.at[:, pl.ds(j * LANES, LANES)], out_sems.at[b]
            )
            copy.start()
            copies.append(copy)
    for copy in copies[-slots:]:
        copy.wait()


def features_grad(stored, k1):
    half = stored.shape[1]
    return call(
        features_body,
        (stored, k1),
        [like((2 * half, MEL * C_IN), F32)],
        [
            pltpu.VMEM((MEL + 2, half, WIDE), BF16),
            pltpu.VMEM((4 * WIDE, BOTH), BF16),
            pltpu.VMEM((8, 2 * half, LANES), F32),
            pltpu.SemaphoreType.DMA((8,)),
            pltpu.SemaphoreType.DMA((8,)),
        ],
        in_specs=[HBM, VMEM],
        out_specs=[ANY],
    )[0]


def finish_body(got, back_one_sums, back_two_sums, own_one, own_two, ga, sa, gb, sb):
    size = own_one.shape[1]
    share = own_one.shape[0]
    total = jnp.sum(got[...].astype(F32), axis=0)
    total = unpack(total, share, size + own_two.shape[1])
    own_one[...] = total[:, 0:size]
    own_two[...] = total[:, size:]
    lane = lax.broadcasted_iota(jnp.int32, (share, C_MID), 1)
    row = lax.broadcasted_iota(jnp.int32, (share, C_MID), 0)
    chosen = lane == lax.axis_index("grp") * share + row
    first = lax.broadcasted_iota(jnp.int32, (share, share), 0)
    second = lax.broadcasted_iota(jnp.int32, (share, share), 1)
    for out, sums, k in (
        (ga, back_one_sums, 1), (sa, back_one_sums, 0), (gb, back_two_sums, 1), (sb, back_two_sums, 0)
    ):
        wide = jnp.broadcast_to(sums[k : k + 1], (share, C_MID))
        column = jnp.sum(jnp.where(chosen, wide, 0.0), axis=1, keepdims=True)
        wide = jnp.broadcast_to(column, (share, share))
        out[...] = jnp.sum(jnp.where(first == second, wide, 0.0), axis=0, keepdims=True)


def finish(got, back_one_sums, back_two_sums, share, rows_one, rows_two):
    shapes = [(share, rows_one), (share, rows_two)] + [(1, share)] * 4
    return call(
        finish_body,
        (got, back_one_sums, back_two_sums),
        [like(s, F32) for s in shapes],
    )


def exchange(blocks):
    return lax.all_to_all(blocks, AXES, 0, 0, tiled=True)


def shards(
    features, clip_starts, kernel_one, kernel_two, gain_one, shift_one, gain_two, shift_two, cotangent
):
    frames = features.shape[0]
    copies = lax.axis_size(AXES)
    row_count = lax.axis_size("row")
    count = float(frames * MEL * copies)
    rows_one, rows_two = kernel_one.shape[0], kernel_two.shape[0]
    share = kernel_one.shape[1]
    vectors = [v.reshape(1, share) for v in (gain_one, shift_one, gain_two, shift_two)]
    clips = clip_starts.reshape(1, -1)
    weights, up, down, held = setup(
        kernel_one.T, kernel_two.T, vectors, clips, features, cotangent, copies
    )
    ends = copies - 1
    up = lax.ppermute(up, AXES, [(i, i + 1) for i in range(ends)])
    down = lax.ppermute(down, AXES, [(i + 1, i) for i in range(ends)])
    weights = exchange(weights)
    pre_one, stats, taps_x, masks, k1, k2, vec = conv_one(
        frames, held, up, down, weights, row_count
    )
    stats = exchange(stats)
    pre_two, stats, taps_a, sums_one = conv_two(pre_one, stats, vec, masks, k2, count)
    stats = exchange(stats)
    block_out, lift, stats, sums_two = norm_two(pre_two, stats, vec, cotangent, up, down, count)
    stats = exchange(stats)
    lift, two, stats, back_two_sums = back_two(
        lift, pre_two, sums_two, stats, vec, masks, k2, pre_one, sums_one, taps_a, count
    )
    stats = exchange(stats)
    stored, blocks, back_one_sums = kernel_grads(
        lift, pre_one, sums_one, stats, vec, masks, taps_x, two, row_count, count
    )
    blocks = exchange(blocks)
    grad_features = features_grad(stored, k1)
    own_one, own_two, ga, sa, gb, sb = finish(
        blocks, back_one_sums, back_two_sums, share, rows_one, rows_two
    )
    return (
        block_out,
        grad_features,
        own_one.T,
        own_two.T,
        ga.reshape(share),
        sa.reshape(share),
        gb.reshape(share),
        sb.reshape(share),
    )


def solution(mesh):
    placed = (
        P(AXES, None), P(), P("row", "grp"), P("row", "grp"),
        P("grp"), P("grp"), P("grp"), P("grp"), P(AXES, None),
    )
    return jax.shard_map(
        shards,
        mesh=mesh,
        in_specs=placed,
        out_specs=(
            P(AXES, None), P(AXES, None), P("row", "grp"), P("row", "grp"),
            P("grp"), P("grp"), P("grp"), P("grp"),
        ),
        check_vma=False,
    )
```

```python
import jax
import jax.numpy as jnp
from jax import lax
from jax.experimental import pallas as pl
from jax.experimental.pallas import tpu as pltpu
from jax.sharding import PartitionSpec as P

MEL = 32
C_IN = 64
C_MID = 128
EPS = 1e-05
AXES = ("grp", "row")
LANES = 128
TAIL = 16
WIDE = 4 * LANES
BOTH = 2 * C_MID
F32 = jnp.float32
BF16 = jnp.bfloat16
TILE = 16
SIDES = 4
MIB = 2**20

VMEM = pl.BlockSpec(memory_space=pltpu.VMEM)
ANY = pl.BlockSpec(memory_space=pl.ANY)
HBM = pl.BlockSpec(memory_space=pltpu.HBM)


def like(shape, dtype):
    return jax.ShapeDtypeStruct(shape, dtype)


def call(body, args, outs, scratch=(), limit=16, cost=None, in_specs=None, out_specs=None, **more):
    return pl.pallas_call(
        body,
        in_specs=in_specs or [VMEM] * len(args),
        out_specs=out_specs or [VMEM] * len(outs),
        out_shape=outs,
        scratch_shapes=list(scratch),
        compiler_params=pltpu.CompilerParams(vmem_limit_bytes=limit * MIB),
        cost_estimate=cost,
        **more,
    )(*args)


def padded(size):
    return -(-size // LANES) * LANES


def packed_rows(share, wide):
    rest = wide - LANES
    if rest > 0 and share == 32 and 3 * (LANES - rest) >= rest:
        return share + 24
    return share * (padded(wide) // LANES)


def pack(block, rows):
    share, wide = block.shape
    if rows % share == 0:
        block = jnp.concatenate([block, jnp.zeros((share, padded(wide) - wide), F32)], axis=1)
        return jnp.concatenate(
            [block[:, at : at + LANES] for at in range(0, block.shape[1], LANES)], axis=0
        )
    rest = block[:, LANES:]
    room = 2 * LANES - wide
    tail = jnp.concatenate(
        [rest[24:32], jnp.zeros((8, 3 * room - rest.shape[1]), F32)], axis=1
    )
    tail = jnp.concatenate([tail[:, k * room : (k + 1) * room] for k in range(3)], axis=0)
    return jnp.concatenate([block[:, :LANES], jnp.concatenate([rest[0:24], tail], axis=1)], axis=0)


def unpack(block, share, wide):
    rows = block.shape[0]
    if rows % share == 0:
        parts = [block[at : at + share] for at in range(0, rows, share)]
        return jnp.concatenate(parts, axis=1)[:, 0:wide]
    width = wide - LANES
    second = block[share:]
    tail = jnp.concatenate([second[8 * k : 8 * k + 8, width:] for k in range(3)], axis=1)
    rest = jnp.concatenate([second[:, :width], tail[:, :width]], axis=0)
    return jnp.concatenate([block[0:share], rest], axis=1)


def partial_sum(values):
    return jnp.sum(values.reshape(-1, 8, values.shape[-1]), axis=0)


def fold(values):
    total = jnp.sum(values, axis=0, keepdims=True)
    return total[:, :C_MID] + total[:, C_MID:]


def spread(first, second, out):
    sums = jnp.concatenate([first, second], axis=0)
    out[...] = jnp.broadcast_to(sums[None], out.shape)


def twice(row):
    return jnp.concatenate([row, row], axis=1)


def tiles(rows):
    return range(0, rows, TILE)


def emit_taps(taps, masks, evens, odds, tile_of):
    rows = masks.shape[1]
    kept = taps.shape[0]
    for r in tiles(rows):
        even, odd = tile_of(r)
        evens[r : r + TILE] = even
        odds[8 + r : 8 + r + TILE] = odd
        if r == 0:
            evens[rows : rows + 1] = even[0:1]
        if r + TILE == rows:
            odds[7:8] = odd[TILE - 1 : TILE]
        if r < kept:
            taps[r : r + TILE, 128:256] = even.astype(BF16)
            taps[r : r + TILE, 256:384] = odd.astype(BF16)
    for r in tiles(kept):
        span = slice(r, r + TILE)
        before = odds[7 + r : 7 + r + TILE] * masks[0, span]
        after = evens[1 + r : 1 + r + TILE] * masks[1, span]
        taps[span, 0:128] = before.astype(BF16)
        taps[span, 384:512] = after.astype(BF16)


def halves_of(value):
    return value[:, :C_MID], value[:, C_MID:]


def add_sums(acc, first, second):
    acc[0] += first
    acc[1] += second


def side_scratch(rows):
    return [pltpu.VMEM((rows + 8, LANES), F32)] * (2 * SIDES)


def stats_of(out, mels, rows, half, acc):
    first = jnp.zeros((8, BOTH), F32)
    second = jnp.zeros((8, BOTH), F32)
    for k in range(mels):
        for r in range(0, half, 8):
            value = out[k * rows + r : k * rows + r + 8]
            first += value
            second += value * value
    add_sums(acc, first, second)


def normed_sum(with_half_lifted, plain, gain, shift):
    return (2.0 * with_half_lifted - shift * plain) / gain


def stat_sums(stats):
    return jnp.sum(stats[...], axis=0)


def norm_terms(sums, count):
    mean = sums[0:1] / count
    rstd = lax.rsqrt(sums[1:2] / count - mean * mean + EPS)
    return mean, rstd


def dot_rows(first, second):
    return lax.dot_general(
        first, second, (((0,), (0,)), ((), ())), preferred_element_type=F32
    )


def ring_slot(ring, m):
    return ring[m % (len(ring) - 1)] if 0 <= m < MEL else ring[-1]


def stack(ring, mels, rows, lanes=slice(None)):
    return jnp.concatenate([ring_slot(ring, m)[0:rows, lanes] for m in mels], axis=0)


def ring_scratch(slots, rows):
    return [pltpu.VMEM((rows, WIDE), BF16)] * slots


def clear_ends(taps):
    blank = jnp.zeros(taps.shape[1:], BF16)
    taps[0] = blank
    taps[taps.shape[0] - 1] = blank


def emit_masks(copies, clips, masks):
    rows = masks.shape[0]
    half = rows - TAIL
    frames = 2 * half
    start = lax.axis_index(AXES) * frames
    place = lax.broadcasted_iota(jnp.int32, (rows, clips.shape[1]), 0)
    pair = jnp.where(place >= half + TAIL // 2, place - rows, place)
    frame = start + 2 * pair
    starts = jnp.broadcast_to(clips[...], (rows, clips.shape[1]))
    for slot, shift in ((0, 0), (1, 2)):
        hit = (frame + shift == starts) | (frame + shift >= frames * copies)
        begins = jnp.max(jnp.where(hit, 1.0, 0.0), axis=1, keepdims=True)
        keep = jnp.broadcast_to(1.0 - begins, (rows, LANES)).astype(BF16)
        masks[:, slot * LANES : (slot + 1) * LANES] = keep


def setup_body(k1, k2, ga, sa, gb, sb, x_head, x_tail, c_head, c_tail, w_out, up, down):
    share = k1.shape[0]
    copies = w_out.shape[0]
    first = lax.broadcasted_iota(jnp.int32, (share, share), 0)
    second = lax.broadcasted_iota(jnp.int32, (share, share), 1)
    columns = [k1[...].astype(F32), k2[...].astype(F32)]
    for vector in (ga, sa, gb, sb):
        wide = jnp.broadcast_to(vector[...].astype(F32), (share, share))
        columns.append(jnp.sum(jnp.where(first == second, wide, 0.0), axis=1, keepdims=True))
    chunk = pack(jnp.concatenate(columns, axis=1), w_out.shape[1]).astype(BF16)
    for i in range(copies):
        w_out[i] = chunk
    row = lax.broadcasted_iota(jnp.int32, (8, x_head.shape[1]), 0)
    xt = x_tail[...].astype(F32)
    ct = c_tail[...].astype(F32)
    up[...] = jnp.where(
        row < 4, pltpu.roll(xt[8:16], 4, 0), jnp.where(row == 4, ct[15:16], 0.0)
    ).astype(BF16)
    xh = x_head[...].astype(F32)
    ch = c_head[...].astype(F32)
    down[...] = jnp.where(row < 4, xh[0:8], jnp.where(row == 4, ch[0:1], 0.0)).astype(BF16)


def setup(k1t, k2t, vectors, features, cotangent, copies):
    frames, wide = features.shape
    halves = cotangent.shape[0]
    share = k1t.shape[0]
    w = (copies, packed_rows(share, k1t.shape[1] + k2t.shape[1] + 4), LANES)
    whole = lambda shape: pl.BlockSpec(shape, lambda i: (0,) * len(shape))
    side = (8, wide)
    outs = [like(w, BF16), like(side, BF16), like(side, BF16)]
    return call(
        setup_body,
        (k1t, k2t, *vectors, features, features, cotangent, cotangent),
        outs,
        limit=56,
        in_specs=[
            whole(k1t.shape),
            whole(k2t.shape),
            *[whole((1, share))] * 4,
            pl.BlockSpec((16, wide), lambda i: (0, 0)),
            pl.BlockSpec((16, wide), lambda i: (frames // 16 - 1, 0)),
            pl.BlockSpec((16, wide), lambda i: (0, 0)),
            pl.BlockSpec((16, wide), lambda i: (halves // 16 - 1, 0)),
        ],
        out_specs=[whole(w), whole(side), whole(side)],
        grid=(1,),
    )


def split_bins(parts):
    low = lax.broadcasted_iota(jnp.int32, parts[0].shape, 1) < C_IN
    first, second = [], []
    for here, there in (parts[0:2], parts[2:4]):
        first.append(jnp.where(low, here, pltpu.roll(there, C_IN, 1)))
        second.append(jnp.where(low, pltpu.roll(here, C_IN, 1), there))
    return jnp.concatenate(first + second, axis=1)


def near_bins(taps, pairs, rows):
    left, mid, right = [
        jnp.concatenate([taps[1 + j + k, 0:rows] for j in pairs], axis=0) for k in (-1, 0, 1)
    ]
    first = jnp.concatenate([left[:, BOTH:], mid], axis=1)
    second = jnp.concatenate([mid, right[:, :BOTH]], axis=1)
    return jnp.concatenate([first, second], axis=0)


def emit_taps_one(x, up, down, masks, taps, frames, done):
    rows = masks.shape[1]
    half = rows - TAIL
    clear_ends(taps)
    row = lax.broadcasted_iota(jnp.int32, (8, LANES), 0)
    lead = 24
    own = 2 * half
    for b in range(2):
        frames[b, 0:16] = jnp.zeros((16, LANES), F32)
        frames[b, lead + own + 8 : lead + own + 24] = jnp.zeros((16, LANES), F32)

    def pair(j, b):
        lanes = pl.ds(pl.multiple_of(j * LANES, LANES), LANES)
        u = up[:, lanes].astype(F32)
        d = down[:, lanes].astype(F32)
        frames[b, lead - 8 : lead] = jnp.where(row >= 4, pltpu.roll(u, 4, 0), 0.0)
        frames[b, lead + own : lead + own + 8] = jnp.where(row < 4, d, 0.0)
        for r in tiles(own):
            frames[b, lead + r : lead + r + TILE] = x[r : r + TILE, lanes].astype(F32)

        def pick(first, count, shift):
            return frames[b, pl.ds(lead + 2 * first + shift, count, stride=2), :]

        for r in tiles(rows):
            parts = []
            for shift in (-1, 0, 1, 2):
                if r < half:
                    parts.append(pick(r, TILE, shift))
                else:
                    parts.append(
                        jnp.concatenate([pick(half, 8, shift), pick(-8, 8, shift)], axis=0)
                    )
            span = slice(r, r + TILE)
            parts[0] = parts[0] * masks[0, span]
            parts[3] = parts[3] * masks[1, span]
            taps[1 + j, span, :] = split_bins(parts).astype(BF16)

    def two_pairs(i, carry):
        pair(2 * i, 0)
        pair(2 * i + 1, 1)
        return carry

    for k in range(4):
        lax.fori_loop(k * MEL // 16, (k + 1) * MEL // 16, two_pairs, 0)
        done(k)


STORED = 320
MASKS_AT = MEL // 2 + 2
LAST_AT = MEL


def taps_one_body(copies, x, up, down, clips, stored, taps, both, masks, frames, sems):
    emit_masks(copies, clips, both)
    for slot in range(2):
        masks[slot] = both[:, slot * LANES : (slot + 1) * LANES].astype(F32)
    started = [pltpu.make_async_copy(both, stored.at[MASKS_AT, :, pl.ds(0, 2 * LANES)], sems.at[4])]
    started[0].start()

    def done(k):
        first, last = TAP_GROUPS[k]
        here = pl.ds(first, last - first)
        copy = pltpu.make_async_copy(taps.at[here], stored.at[here], sems.at[k])
        copy.start()
        started.append(copy)

    emit_taps_one(x, up, down, masks, taps, frames, done)
    for copy in started:
        copy.wait()


TAP_GROUPS = ((0, 5), (5, 9), (9, 13), (13, 18))


def taps_one(features, up, down, clips, copies):
    frames, wide = features.shape
    rows = frames // 2 + TAIL
    return call(
        lambda *refs: taps_one_body(copies, *refs),
        (features, up, down, clips),
        [like((STORED, rows, WIDE), BF16)],
        [
            pltpu.VMEM((MEL // 2 + 2, rows, WIDE), BF16),
            pltpu.VMEM((rows, 2 * LANES), BF16),
            pltpu.VMEM((2, rows, LANES), F32),
            pltpu.VMEM((2, frames + 48, LANES), F32),
            pltpu.SemaphoreType.DMA((5,)),
        ],
        out_specs=[HBM],
    )[0]


def fetch_taps_one(stored, taps, sems):
    fetch = []
    for k, (first, last) in enumerate(TAP_GROUPS):
        here = pl.ds(first, last - first)
        fetch.append(pltpu.make_async_copy(stored.at[here], taps.at[here], sems.at[k]))
        fetch[k].start()
    return fetch


def emit_weights_one(row_count, wg, k1_out, k2_out, vec_out, kf, weight):
    rows_one = 9 * C_IN // row_count
    rows_two = 9 * C_MID // row_count
    grps = wg.shape[0] // row_count
    share = C_MID // grps
    for r in range(row_count):
        shard = [
            unpack(wg[g * row_count + r].astype(F32), share, rows_one + rows_two + 4)
            for g in range(grps)
        ]
        shard = jnp.concatenate(shard, axis=0).T
        kf[rows_one * r : rows_one * (r + 1)] = shard[0:rows_one]
        at = 9 * C_IN + rows_two * r
        kf[at : at + rows_two] = shard[rows_one : rows_one + rows_two]
        if r == 0:
            vec_out[...] = shard[rows_one + rows_two : rows_one + rows_two + 4]
    k1_out[...] = kf[0 : 9 * C_IN].astype(BF16)
    k2_out[...] = kf[9 * C_IN :].astype(BF16)
    weight[...] = jnp.zeros(weight.shape, BF16)
    for d in range(3):
        for q in range(4):
            for p in range(2):
                t = q - p
                if 0 <= t < 3:
                    at = d * BOTH + q * C_IN
                    start = (3 * t + d) * C_IN
                    weight[at : at + C_IN, p * 128 : p * 128 + 128] = k1_out[start : start + C_IN]


def conv_one_body(row_count, stored, wg, pre, stats, masks, k1_out, k2_out, vec_out,
                  kf, weight, acc, taps, both, sems):
    held_masks = stored.at[MASKS_AT, :, pl.ds(0, 2 * LANES)]
    mask_copy = pltpu.make_async_copy(held_masks, both, sems.at[4])
    mask_copy.start()
    fetch = fetch_taps_one(stored, taps, sems)
    emit_weights_one(row_count, wg, k1_out, k2_out, vec_out, kf, weight)
    mask_copy.wait()
    for slot in range(2):
        masks[slot] = both[:, slot * LANES : (slot + 1) * LANES].astype(F32)
    rows = taps.shape[1]
    half = rows - TAIL
    pairs = 4
    acc[...] = jnp.zeros(acc.shape, F32)
    fetched = 0
    for c in range(MEL // 2 // pairs):
        here = range(c * pairs, (c + 1) * pairs)
        while fetched < len(fetch) and TAP_GROUPS[fetched][0] <= here[-1] + 2:
            fetch[fetched].wait()
            fetched += 1
        out = jnp.dot(near_bins(taps, here, rows), weight[...], preferred_element_type=F32)
        for parity in range(2):
            for q in range(pairs):
                at = (parity * pairs + q) * rows
                pre[2 * (c * pairs + q) + parity] = out[at : at + rows]
        stats_of(out, 2 * pairs, rows, half, acc)
    spread(fold(acc[0]), fold(acc[1]), stats)


def conv_one(stored, wg, row_count):
    rows = stored.shape[1]
    copies = wg.shape[0]
    return call(
        lambda *refs: conv_one_body(row_count, *refs),
        (stored, wg),
        [
            like((MEL, rows, BOTH), F32),
            like((copies, 2, C_MID), F32),
            like((2, rows, LANES), F32),
            like((9 * C_IN, C_MID), BF16),
            like((9 * C_MID, C_MID), BF16),
            like((4, C_MID), F32),
        ],
        [
            pltpu.VMEM((9 * (C_IN + C_MID), C_MID), F32),
            pltpu.VMEM((3 * BOTH, BOTH), BF16),
            pltpu.VMEM((2, 8, BOTH), F32),
            pltpu.VMEM((MEL // 2 + 2, rows, WIDE), BF16),
            pltpu.VMEM((rows, 2 * LANES), BF16),
            pltpu.SemaphoreType.DMA((5,)),
        ],
        in_specs=[HBM, VMEM],
    )


def place_two(k2, weight):
    weight[...] = jnp.zeros(weight.shape, BF16)
    for d in range(3):
        for q in range(4):
            for p in range(2):
                t = q - p
                if 0 <= t < 3:
                    at = d * WIDE + q * 128
                    start = (3 * t + d) * C_MID
                    weight[at : at + 128, p * 128 : p * 128 + 128] = k2[start : start + C_MID]


def place_two_back(k2, weight):
    weight[...] = jnp.zeros(weight.shape, BF16)
    for t in range(3):
        for d in range(3):
            start = (3 * t + d) * C_MID
            turned = (0.5 * k2[start : start + C_MID].astype(F32).T).astype(BF16)
            for p in range(2):
                at = (2 - d) * WIDE + (2 - t + p) * 128
                weight[at : at + 128, p * 128 : p * 128 + 128] = turned


def place_one_back(k1, weight):
    weight[...] = jnp.zeros(weight.shape, BF16)
    for t in range(3):
        for d in range(3):
            start = (3 * t + d) * C_IN
            turned = k1[start : start + C_IN].astype(F32).T.astype(BF16)
            for mo in (1, 2):
                for p in range(2):
                    at = (mo - d + 1) * WIDE + (2 - t + p) * 128
                    to = p * 128 + (mo - 1) * 64
                    weight[at : at + 128, to : to + 64] = turned


def conv_two_body(count, pre_one, stats_one, vec, masks, k2, pre, stats, taps, sums_out,
                  acc, weight, *sides):
    place_two(k2, weight)
    rows = masks.shape[1]
    half = rows - TAIL
    mels = 2
    sums = stat_sums(stats_one)
    sums_out[...] = sums
    mean, rstd = norm_terms(sums, count)
    scale = 0.5 * vec[0:1] * rstd
    shift = twice(0.5 * vec[1:2] - mean * scale)
    scale = twice(scale)
    clear_ends(taps)
    acc[...] = jnp.zeros(acc.shape, F32)

    def activate(m):
        def tile(r):
            h = pre_one[m, r : r + TILE] * scale + shift
            return halves_of(h + h * jnp.tanh(h))

        emit_taps(taps.at[1 + m], masks, sides[m % SIDES], sides[SIDES + m % SIDES], tile)

    def convolve(c):
        lhs = [taps[c * mels + d : (c + 1) * mels + d].reshape(mels * rows, WIDE) for d in range(3)]
        out = jnp.dot(jnp.concatenate(lhs, axis=1), weight[...], preferred_element_type=F32)
        pre[c * mels : (c + 1) * mels] = out.reshape(mels, rows, BOTH)
        stats_of(out, mels, rows, half, acc)

    for m in range(MEL):
        activate(m)
        if m >= mels and m % mels == 0:
            convolve(m // mels - 1)
    convolve(MEL // mels - 1)
    spread(fold(acc[0]), fold(acc[1]), stats)


def conv_two(pre_one, stats_one, vec, masks, k2, count):
    copies = stats_one.shape[0]
    rows = masks.shape[1]
    return call(
        lambda *refs: conv_two_body(count, *refs),
        (pre_one, stats_one, vec, masks, k2),
        [
            like((MEL, rows, BOTH), F32),
            like((copies, 2, C_MID), F32),
            like((MEL + 2, rows, WIDE), BF16),
            like((2, C_MID), F32),
        ],
        [pltpu.VMEM((2, 8, BOTH), F32), pltpu.VMEM((3 * WIDE, BOTH), BF16), *side_scratch(rows)],
        cost=pl.CostEstimate(flops=5 * 10**9, bytes_accessed=0, transcendentals=0),
    )


def norm_two_body(count, pre, stats_two, vec, cot, up, down, pooled, lift, back_stats, sums_out, acc):
    half = cot.shape[0]
    sums = stat_sums(stats_two)
    sums_out[...] = sums
    mean, rstd = norm_terms(sums, count)
    scale = 0.5 * vec[2:3] * rstd
    shift = 0.5 * vec[3:4] - mean * scale
    acc[...] = jnp.zeros(acc.shape, F32)
    row = lax.broadcasted_iota(jnp.int32, (TAIL, LANES), 0)

    def pair(j, carry):
        lanes = pl.ds(pl.multiple_of(j * LANES, LANES), LANES)
        u = up[:, lanes].astype(F32)
        d = down[:, lanes].astype(F32)
        first = jnp.zeros((8, LANES), F32)
        second = jnp.zeros((8, LANES), F32)
        for r in tiles(half + TAIL):
            span = slice(r, r + TILE)
            if r < half:
                grad = cot[span, lanes].astype(F32) * 0.125
            else:
                grad = jnp.where(row == 0, d[4:5], jnp.where(row == TAIL - 1, u[4:5], 0.0)) * 0.125
            total = jnp.zeros((TILE, LANES), F32)
            for m in (2 * j, 2 * j + 1):
                for p in range(2):
                    side = slice(p * C_MID, (p + 1) * C_MID)
                    value = pre[m, span, side]
                    h = value * scale + shift
                    th = jnp.tanh(h)
                    one = 1.0 + th
                    silu = h * one
                    gl = grad * (one + (silu - silu * th))
                    lift[m, span, side] = gl
                    if r < half:
                        total += silu
                        first += partial_sum(gl)
                        second += partial_sum(gl * h)
            if r < half:
                pooled[span, lanes] = (total * 0.25).astype(BF16)
        add_sums(acc, first, second)
        return carry

    lax.fori_loop(0, MEL // 2, pair, 0)
    first, second = [jnp.sum(acc[k], axis=0, keepdims=True) for k in range(2)]
    spread(first, normed_sum(second, first, vec[2:3], vec[3:4]), back_stats)


def norm_two(pre, stats_two, vec, cot, up, down, count):
    copies = stats_two.shape[0]
    half, wide = cot.shape
    return call(
        lambda *refs: norm_two_body(count, *refs),
        (pre, stats_two, vec, cot, up, down),
        [
            like((half, wide), BF16),
            like((MEL, half + TAIL, BOTH), F32),
            like((copies, 2, C_MID), F32),
            like((2, C_MID), F32),
        ],
        [pltpu.VMEM((2, 8, LANES), F32)],
    )


def grad_terms(sums, back, gain, count):
    mean, rstd = norm_terms(sums, count)
    a = gain * rstd
    b = -a * rstd * (back[1:2] / count)
    c = -a * (back[0:1] / count) - b * mean
    return twice(a), twice(b), twice(c)


def back_two_body(count, lift, pre_two, sums_two, back_stats, vec, masks, k2, pre_one, sums_one,
                  taps_a, lift_one, two, back_out, sums_out, acc, acc_two, weight, *buffers):
    place_two_back(k2, weight)
    sides, taps = buffers[: 2 * SIDES], buffers[2 * SIDES :]
    rows = masks.shape[1]
    half = rows - TAIL
    mels = 4
    back = stat_sums(back_stats)
    sums_out[...] = back
    a, b, c = grad_terms(sums_two[...], back, vec[2:3], count)
    mean, rstd = norm_terms(sums_one[...], count)
    scale = 0.5 * vec[0:1] * rstd
    shift = twice(0.5 * vec[1:2] - mean * scale)
    scale = twice(scale)
    taps[-1][...] = jnp.zeros(taps[-1].shape, BF16)
    acc[...] = jnp.zeros(acc.shape, F32)

    def lower(m):
        def tile(r):
            span = slice(r, r + TILE)
            return halves_of(lift[m, span] * a + (pre_two[m, span] * b + c))

        emit_taps(ring_slot(taps, m), masks, sides[m % SIDES], sides[SIDES + m % SIDES], tile)

    def convolve(k):
        lhs = [stack(taps, range(k * mels + d - 1, (k + 1) * mels + d - 1), rows) for d in range(3)]
        out = jnp.dot(jnp.concatenate(lhs, axis=1), weight[...], preferred_element_type=F32)
        first = jnp.zeros((8, BOTH), F32)
        second = jnp.zeros((8, BOTH), F32)
        for i in range(mels):
            m = k * mels + i
            for r in range(0, rows, 8):
                span = slice(r, r + 8)
                h = pre_one[m, span] * scale + shift
                th = jnp.tanh(h)
                one = 1.0 + th
                silu = h * one
                gl = out[i * rows + r : i * rows + r + 8] * (one + (silu - silu * th))
                lift_one[m, span] = gl
                if r < half:
                    first += gl
                    second += gl * h
        add_sums(acc, first, second)

    def correlate(k):
        here = range(k * mels, (k + 1) * mels)
        near = [
            taps_a[k * mels + d : (k + 1) * mels + d, 0:half].reshape(mels * half, WIDE) for d in range(3)
        ]
        total = dot_rows(stack(taps, here, half, slice(128, 384)), jnp.concatenate(near, axis=1))
        if k == 0:
            acc_two[...] = total
        else:
            acc_two[...] += total

    for k in range(MEL // mels + 1):
        for m in range(k * mels, (k + 1) * mels):
            if m < MEL:
                lower(m)
        if k > 0:
            convolve(k - 1)
            correlate(k - 1)
    plain = fold(acc[0])
    spread(plain, normed_sum(fold(acc[1]), plain, vec[0:1], vec[1:2]), back_out)
    for t in range(3):
        for d in range(3):
            at = d * WIDE + t * 128
            to = (3 * t + d) * 128
            two[:, to : to + 128] = (
                acc_two[0:C_MID, at : at + 128] + acc_two[C_MID:BOTH, at + 128 : at + 256]
            )


def back_two(lift, pre_two, sums_two, back_stats, vec, masks, k2, pre_one, sums_one, taps_a, count):
    copies = back_stats.shape[0]
    rows = masks.shape[1]
    return call(
        lambda *refs: back_two_body(count, *refs),
        (lift, pre_two, sums_two, back_stats, vec, masks, k2, pre_one, sums_one, taps_a),
        [
            like((MEL, rows, BOTH), F32),
            like((C_MID, 9 * C_MID), F32),
            like((copies, 2, C_MID), F32),
            like((2, C_MID), F32),
        ],
        [
            pltpu.VMEM((2, 8, BOTH), F32),
            pltpu.VMEM((BOTH, 3 * WIDE), F32),
            pltpu.VMEM((3 * WIDE, BOTH), BF16),
            *side_scratch(rows),
            *ring_scratch(17, rows),
        ],

        input_output_aliases={0: 0},
    )


def scatter_blocks(out, parts, row_count):
    copies = out.shape[0]
    grps = copies // row_count
    share = C_MID // grps
    turned = [part.T for part in parts]
    sizes = [part.shape[1] // row_count for part in parts]
    for r in range(row_count):
        rows = [t[n * r : n * (r + 1)] for t, n in zip(turned, sizes)]
        back = jnp.concatenate(rows, axis=0).T
        for g in range(grps):
            block = back[share * g : share * (g + 1)]
            out[g * row_count + r] = pack(block, out.shape[1]).astype(BF16)


def kernel_one_step(taps_x, taps, acc, k, pairs):
    half = taps[-1].shape[0]
    here = range(k * pairs, (k + 1) * pairs)
    mels = [2 * j + parity for parity in range(2) for j in here]
    chosen = jnp.concatenate([taps[m % len(taps)][:, 128:384] for m in mels], axis=0)
    total = dot_rows(chosen, near_bins(taps_x, here, half))
    if k == 0:
        acc[...] = total
    else:
        acc[...] += total


def kernel_one_sums(acc):
    pieces = []
    for t in range(3):
        for d in range(3):
            total = jnp.zeros((C_MID, C_IN), F32)
            for p in range(2):
                at = d * BOTH + (t + p) * C_IN
                total += acc[p * C_MID : (p + 1) * C_MID, at : at + C_IN]
            pieces.append(total)
    return jnp.concatenate(pieces, axis=1)


def grads_body(count, row_count, lift, pre_one, sums_one, back_stats, vec, masks, two, stored_in,
               stored, blocks, sums_out, acc_one, taps_x, sems, tap_sems, *buffers):
    fetch = fetch_taps_one(stored, taps_x, tap_sems)
    sides, taps = buffers[: 2 * SIDES], buffers[2 * SIDES :]
    slots = len(taps)
    back = stat_sums(back_stats)
    sums_out[...] = back
    a, b, c = grad_terms(sums_one[...], back, vec[0:1], count)

    def lower(m):
        def tile(r):
            span = slice(r, r + TILE)
            return halves_of(lift[m, span] * a + (pre_one[m, span] * b + c))

        emit_taps(taps[m % slots], masks, sides[m % SIDES], sides[SIDES + m % SIDES], tile)

    pairs = 4
    copies = []
    for k in range(MEL // 2 // pairs + 1):
        for m in range(2 * pairs * k, 2 * pairs * (k + 1)):
            if m < MEL:
                if m >= slots:
                    copies[m - slots].wait()
                lower(m)
                there = stored.at[LAST_AT + m, pl.ds(0, taps_x.shape[1] - TAIL)]
                copy = pltpu.make_async_copy(taps[m % slots], there, sems.at[m % slots])
                copy.start()
                copies.append(copy)
        if k == 1:
            for copy in fetch:
                copy.wait()
        if k > 0:
            kernel_one_step(taps_x, taps, acc_one, k - 1, pairs)
    scatter_blocks(blocks, [kernel_one_sums(acc_one), two[...]], row_count)
    for copy in copies[-slots:]:
        copy.wait()


def kernel_grads(lift, pre_one, sums_one, back_stats, vec, masks, two, stored, row_count, count):
    copies = back_stats.shape[0]
    half = masks.shape[1] - TAIL
    share = C_MID * row_count // copies
    rows = packed_rows(share, 9 * (C_IN + C_MID) // row_count)
    slots = 24
    return call(
        lambda *refs: grads_body(count, row_count, *refs),
        (lift, pre_one, sums_one, back_stats, vec, masks, two, stored),
        [
            like(stored.shape, BF16),
            like((copies, rows, LANES), BF16),
            like((2, C_MID), F32),
        ],
        [
            pltpu.VMEM((BOTH, 3 * BOTH), F32),
            pltpu.VMEM((MEL // 2 + 2, *stored.shape[1:]), BF16),
            pltpu.SemaphoreType.DMA((slots,)),
            pltpu.SemaphoreType.DMA((4,)),
            *side_scratch(half + TAIL),
            *ring_scratch(slots, half),
        ],
        in_specs=[VMEM] * 7 + [HBM],
        out_specs=[HBM, VMEM, VMEM],
        input_output_aliases={7: 0},
    )


def features_body(stored, k1, out, taps, weight, woven, sems, out_sems):
    pairs = 4
    half = taps.shape[1]
    group = MEL // sems.shape[0]
    fetch = []
    for k in range(sems.shape[0]):
        here = stored.at[pl.ds(LAST_AT + k * group, group), pl.ds(0, half)]
        there = taps.at[pl.ds(1 + k * group, group)]
        fetch.append(pltpu.make_async_copy(here, there, sems.at[k]))
        fetch[k].start()
    clear_ends(taps)
    place_one_back(k1, weight)
    fetched = 0
    copies = []
    slots = woven.shape[0]
    for k in range(MEL // 2 // pairs):
        while fetched * group < min(2 * pairs * (k + 1) + 1, MEL):
            fetch[fetched].wait()
            fetched += 1
        near = []
        for i in range(4):
            mels = [taps[2 * (k * pairs + q) + i] for q in range(pairs)]
            near.append(jnp.concatenate(mels, axis=0))
        part = jnp.dot(jnp.concatenate(near, axis=1), weight[...], preferred_element_type=F32)
        for q in range(pairs):
            j = k * pairs + q
            b = j % slots
            rows = slice(q * half, (q + 1) * half)
            if j >= slots:
                copies[j - slots].wait()
            woven[b, pl.ds(0, half, stride=2), :] = part[rows, 0:128]
            woven[b, pl.ds(1, half, stride=2), :] = part[rows, 128:256]
            copy = pltpu.make_async_copy(
                woven.at[b], out.at[:, pl.ds(j * LANES, LANES)], out_sems.at[b]
            )
            copy.start()
            copies.append(copy)
    for copy in copies[-slots:]:
        copy.wait()


def features_grad(stored, k1):
    half = stored.shape[1] - TAIL
    return call(
        features_body,
        (stored, k1),
        [like((2 * half, MEL * C_IN), F32)],
        [
            pltpu.VMEM((MEL + 2, half, WIDE), BF16),
            pltpu.VMEM((4 * WIDE, BOTH), BF16),
            pltpu.VMEM((8, 2 * half, LANES), F32),
            pltpu.SemaphoreType.DMA((8,)),
            pltpu.SemaphoreType.DMA((8,)),
        ],
        in_specs=[HBM, VMEM],
        out_specs=[ANY],
    )[0]


def finish_body(got, back_one_sums, back_two_sums, own_one, own_two, ga, sa, gb, sb):
    size = own_one.shape[1]
    share = own_one.shape[0]
    total = jnp.sum(got[...].astype(F32), axis=0)
    total = unpack(total, share, size + own_two.shape[1])
    own_one[...] = total[:, 0:size]
    own_two[...] = total[:, size:]
    lane = lax.broadcasted_iota(jnp.int32, (share, C_MID), 1)
    row = lax.broadcasted_iota(jnp.int32, (share, C_MID), 0)
    chosen = lane == lax.axis_index("grp") * share + row
    first = lax.broadcasted_iota(jnp.int32, (share, share), 0)
    second = lax.broadcasted_iota(jnp.int32, (share, share), 1)
    for out, sums, k in (
        (ga, back_one_sums, 1), (sa, back_one_sums, 0), (gb, back_two_sums, 1), (sb, back_two_sums, 0)
    ):
        wide = jnp.broadcast_to(sums[k : k + 1], (share, C_MID))
        column = jnp.sum(jnp.where(chosen, wide, 0.0), axis=1, keepdims=True)
        wide = jnp.broadcast_to(column, (share, share))
        out[...] = jnp.sum(jnp.where(first == second, wide, 0.0), axis=0, keepdims=True)


def finish(got, back_one_sums, back_two_sums, share, rows_one, rows_two):
    shapes = [(share, rows_one), (share, rows_two)] + [(1, share)] * 4
    return call(
        finish_body,
        (got, back_one_sums, back_two_sums),
        [like(s, F32) for s in shapes],
    )


def exchange(blocks):
    return lax.all_to_all(blocks, AXES, 0, 0, tiled=True)


def shards(
    features, clip_starts, kernel_one, kernel_two, gain_one, shift_one, gain_two, shift_two, cotangent
):
    frames = features.shape[0]
    copies = lax.axis_size(AXES)
    row_count = lax.axis_size("row")
    count = float(frames * MEL * copies)
    rows_one, rows_two = kernel_one.shape[0], kernel_two.shape[0]
    share = kernel_one.shape[1]
    vectors = [v.reshape(1, share) for v in (gain_one, shift_one, gain_two, shift_two)]
    weights, up, down = setup(
        kernel_one.T, kernel_two.T, vectors, features, cotangent, copies
    )
    ends = copies - 1
    up = lax.ppermute(up, AXES, [(i, i + 1) for i in range(ends)])
    down = lax.ppermute(down, AXES, [(i + 1, i) for i in range(ends)])
    weights = exchange(weights)
    stored = taps_one(features, up, down, clip_starts.reshape(1, -1), copies)
    pre_one, stats, masks, k1, k2, vec = conv_one(stored, weights, row_count)
    stats = exchange(stats)
    pre_two, stats, taps_a, sums_one = conv_two(pre_one, stats, vec, masks, k2, count)
    stats = exchange(stats)
    block_out, lift, stats, sums_two = norm_two(pre_two, stats, vec, cotangent, up, down, count)
    stats = exchange(stats)
    lift, two, stats, back_two_sums = back_two(
        lift, pre_two, sums_two, stats, vec, masks, k2, pre_one, sums_one, taps_a, count
    )
    stats = exchange(stats)
    stored, blocks, back_one_sums = kernel_grads(
        lift, pre_one, sums_one, stats, vec, masks, two, stored, row_count, count
    )
    blocks = exchange(blocks)
    grad_features = features_grad(stored, k1)
    own_one, own_two, ga, sa, gb, sb = finish(
        blocks, back_one_sums, back_two_sums, share, rows_one, rows_two
    )
    return (
        block_out,
        grad_features,
        own_one.T,
        own_two.T,
        ga.reshape(share),
        sa.reshape(share),
        gb.reshape(share),
        sb.reshape(share),
    )


def solution(mesh):
    placed = (
        P(AXES, None), P(), P("row", "grp"), P("row", "grp"),
        P("grp"), P("grp"), P("grp"), P("grp"), P(AXES, None),
    )
    return jax.shard_map(
        shards,
        mesh=mesh,
        in_specs=placed,
        out_specs=(
            P(AXES, None), P(AXES, None), P("row", "grp"), P("row", "grp"),
            P("grp"), P("grp"), P("grp"), P("grp"),
        ),
        check_vma=False,
    )
```

```python
import jax
import jax.numpy as jnp
from jax import lax
from jax.experimental import pallas as pl
from jax.experimental.pallas import tpu as pltpu
from jax.sharding import PartitionSpec as P

MEL = 32
C_IN = 64
C_MID = 128
EPS = 1e-05
AXES = ("grp", "row")
LANES = 128
TAIL = 16
WIDE = 4 * LANES
BOTH = 2 * C_MID
F32 = jnp.float32
BF16 = jnp.bfloat16
TILE = 16
SIDES = 4
MIB = 2**20

VMEM = pl.BlockSpec(memory_space=pltpu.VMEM)
ANY = pl.BlockSpec(memory_space=pl.ANY)
HBM = pl.BlockSpec(memory_space=pltpu.HBM)


def like(shape, dtype):
    return jax.ShapeDtypeStruct(shape, dtype)


def call(body, args, outs, scratch=(), limit=16, in_specs=None, out_specs=None, **more):
    return pl.pallas_call(
        body,
        in_specs=in_specs or [VMEM] * len(args),
        out_specs=out_specs or [VMEM] * len(outs),
        out_shape=outs,
        scratch_shapes=list(scratch),
        compiler_params=pltpu.CompilerParams(vmem_limit_bytes=limit * MIB),
        cost_estimate=pl.CostEstimate(flops=5 * 10**9, bytes_accessed=0, transcendentals=0),
        **more,
    )(*args)


def padded(size):
    return -(-size // LANES) * LANES


def packed_rows(share, wide):
    rest = wide - LANES
    if rest > 0 and share == 32 and 3 * (LANES - rest) >= rest:
        return share + 24
    return share * (padded(wide) // LANES)


def pack(block, rows):
    share, wide = block.shape
    if rows % share == 0:
        block = jnp.concatenate([block, jnp.zeros((share, padded(wide) - wide), F32)], axis=1)
        return jnp.concatenate(
            [block[:, at : at + LANES] for at in range(0, block.shape[1], LANES)], axis=0
        )
    rest = block[:, LANES:]
    room = 2 * LANES - wide
    tail = jnp.concatenate(
        [rest[24:32], jnp.zeros((8, 3 * room - rest.shape[1]), F32)], axis=1
    )
    tail = jnp.concatenate([tail[:, k * room : (k + 1) * room] for k in range(3)], axis=0)
    return jnp.concatenate([block[:, :LANES], jnp.concatenate([rest[0:24], tail], axis=1)], axis=0)


def unpack(block, share, wide):
    rows = block.shape[0]
    if rows % share == 0:
        parts = [block[at : at + share] for at in range(0, rows, share)]
        return jnp.concatenate(parts, axis=1)[:, 0:wide]
    width = wide - LANES
    second = block[share:]
    tail = jnp.concatenate([second[8 * k : 8 * k + 8, width:] for k in range(3)], axis=1)
    rest = jnp.concatenate([second[:, :width], tail[:, :width]], axis=0)
    return jnp.concatenate([block[0:share], rest], axis=1)


def partial_sum(values):
    return jnp.sum(values.reshape(-1, 8, values.shape[-1]), axis=0)


def fold(values):
    total = jnp.sum(values, axis=0, keepdims=True)
    return total[:, :C_MID] + total[:, C_MID:]


def spread(first, second, out):
    sums = jnp.concatenate([first, second], axis=0)
    out[...] = jnp.broadcast_to(sums[None], out.shape)


def twice(row):
    return jnp.concatenate([row, row], axis=1)


def tiles(rows):
    return range(0, rows, TILE)


def emit_taps(taps, masks, evens, odds, tile_of):
    rows = masks.shape[1]
    kept = taps.shape[0]
    for r in tiles(rows):
        even, odd = tile_of(r)
        evens[r : r + TILE] = even
        odds[8 + r : 8 + r + TILE] = odd
        if r == 0:
            evens[rows : rows + 1] = even[0:1]
        if r + TILE == rows:
            odds[7:8] = odd[TILE - 1 : TILE]
        if r < kept:
            taps[r : r + TILE, 128:256] = even.astype(BF16)
            taps[r : r + TILE, 256:384] = odd.astype(BF16)
    for r in tiles(kept):
        span = slice(r, r + TILE)
        before = odds[7 + r : 7 + r + TILE] * masks[0, span]
        after = evens[1 + r : 1 + r + TILE] * masks[1, span]
        taps[span, 0:128] = before.astype(BF16)
        taps[span, 384:512] = after.astype(BF16)


def halves_of(value):
    return value[:, :C_MID], value[:, C_MID:]


def add_sums(acc, first, second):
    acc[0] += first
    acc[1] += second


def side_scratch(rows):
    return [pltpu.VMEM((rows + 8, LANES), F32)] * (2 * SIDES)


def stats_of(out, mels, rows, half, acc):
    first = jnp.zeros((8, BOTH), F32)
    second = jnp.zeros((8, BOTH), F32)
    for k in range(mels):
        for r in range(0, half, 8):
            value = out[k * rows + r : k * rows + r + 8]
            first += value
            second += value * value
    add_sums(acc, first, second)


def normed_sum(with_half_lifted, plain, gain, shift):
    return (2.0 * with_half_lifted - shift * plain) / gain


def stat_sums(stats):
    return jnp.sum(stats[...], axis=0)


def norm_terms(sums, count):
    mean = sums[0:1] / count
    rstd = lax.rsqrt(sums[1:2] / count - mean * mean + EPS)
    return mean, rstd


def dot_rows(first, second):
    return lax.dot_general(
        first, second, (((0,), (0,)), ((), ())), preferred_element_type=F32
    )


def ring_slot(ring, m):
    return ring[m % (len(ring) - 1)] if 0 <= m < MEL else ring[-1]


def stack(ring, mels, rows, lanes=slice(None)):
    return jnp.concatenate([ring_slot(ring, m)[0:rows, lanes] for m in mels], axis=0)


def ring_scratch(slots, rows):
    return [pltpu.VMEM((rows, WIDE), BF16)] * slots


def clear_ends(taps):
    blank = jnp.zeros(taps.shape[1:], BF16)
    taps[0] = blank
    taps[taps.shape[0] - 1] = blank


def setup_body(k1, k2, ga, sa, gb, sb, clips, x_head, x_tail, c_head, c_tail, w_out, up, down, clips_out):
    clips_out[...] = clips[...]
    share = k1.shape[0]
    copies = w_out.shape[0]
    first = lax.broadcasted_iota(jnp.int32, (share, share), 0)
    second = lax.broadcasted_iota(jnp.int32, (share, share), 1)
    columns = [k1[...].astype(F32), k2[...].astype(F32)]
    for vector in (ga, sa, gb, sb):
        wide = jnp.broadcast_to(vector[...].astype(F32), (share, share))
        columns.append(jnp.sum(jnp.where(first == second, wide, 0.0), axis=1, keepdims=True))
    chunk = pack(jnp.concatenate(columns, axis=1), w_out.shape[1]).astype(BF16)
    for i in range(copies):
        w_out[i] = chunk
    row = lax.broadcasted_iota(jnp.int32, (8, x_head.shape[1]), 0)
    xt = x_tail[...].astype(F32)
    ct = c_tail[...].astype(F32)
    up[...] = jnp.where(
        row < 4, pltpu.roll(xt[8:16], 4, 0), jnp.where(row == 4, ct[15:16], 0.0)
    ).astype(BF16)
    xh = x_head[...].astype(F32)
    ch = c_head[...].astype(F32)
    down[...] = jnp.where(row < 4, xh[0:8], jnp.where(row == 4, ch[0:1], 0.0)).astype(BF16)


def setup(k1t, k2t, vectors, clips, features, cotangent, copies):
    frames, wide = features.shape
    halves = cotangent.shape[0]
    share = k1t.shape[0]
    w = (copies, packed_rows(share, k1t.shape[1] + k2t.shape[1] + 4), LANES)
    whole = lambda shape: pl.BlockSpec(shape, lambda i: (0,) * len(shape))
    outs = [
        like(w, BF16), like((8, wide), BF16), like((8, wide), BF16), like(clips.shape, jnp.int32)
    ]
    return call(
        setup_body,
        (k1t, k2t, *vectors, clips, features, features, cotangent, cotangent),
        outs,
        limit=56,
        in_specs=[
            whole(k1t.shape),
            whole(k2t.shape),
            *[whole((1, share))] * 4,
            whole(clips.shape),
            pl.BlockSpec((16, wide), lambda i: (0, 0)),
            pl.BlockSpec((16, wide), lambda i: (frames // 16 - 1, 0)),
            pl.BlockSpec((16, wide), lambda i: (0, 0)),
            pl.BlockSpec((16, wide), lambda i: (halves // 16 - 1, 0)),
        ],
        out_specs=[whole(o.shape) for o in outs],
        grid=(1,),
    )


def emit_masks(copies, clips, masks):
    rows = masks.shape[1]
    half = rows - TAIL
    frames = 2 * half
    start = lax.axis_index(AXES) * frames
    place = lax.broadcasted_iota(jnp.int32, (rows, clips.shape[1]), 0)
    pair = jnp.where(place >= half + TAIL // 2, place - rows, place)
    frame = start + 2 * pair
    starts = jnp.broadcast_to(clips[...], (rows, clips.shape[1]))
    for slot, shift in ((0, 0), (1, 2)):
        hit = (frame + shift == starts) | (frame + shift >= frames * copies)
        begins = jnp.max(jnp.where(hit, 1.0, 0.0), axis=1, keepdims=True)
        masks[slot] = jnp.broadcast_to(1.0 - begins, (rows, LANES))


def split_bins(parts):
    low = lax.broadcasted_iota(jnp.int32, parts[0].shape, 1) < C_IN
    first, second = [], []
    for here, there in (parts[0:2], parts[2:4]):
        first.append(jnp.where(low, here, pltpu.roll(there, C_IN, 1)))
        second.append(jnp.where(low, pltpu.roll(here, C_IN, 1), there))
    return jnp.concatenate(first + second, axis=1)


def near_bins(taps, pairs, rows):
    left, mid, right = [
        jnp.concatenate([taps[1 + j + k, 0:rows] for j in pairs], axis=0) for k in (-1, 0, 1)
    ]
    first = jnp.concatenate([left[:, BOTH:], mid], axis=1)
    second = jnp.concatenate([mid, right[:, :BOTH]], axis=1)
    return jnp.concatenate([first, second], axis=0)


def emit_taps_one(fetch, x, up, down, masks, taps, frames):
    rows = masks.shape[1]
    half = rows - TAIL
    clear_ends(taps)
    row = lax.broadcasted_iota(jnp.int32, (8, LANES), 0)
    lead = 24
    own = 2 * half
    for b in range(2):
        frames[b, 0:16] = jnp.zeros((16, LANES), F32)
        frames[b, lead + own + 8 : lead + own + 24] = jnp.zeros((16, LANES), F32)

    def pair(j, b):
        lanes = pl.ds(pl.multiple_of(j * LANES, LANES), LANES)
        u = up[:, lanes].astype(F32)
        d = down[:, lanes].astype(F32)
        frames[b, lead - 8 : lead] = jnp.where(row >= 4, pltpu.roll(u, 4, 0), 0.0)
        frames[b, lead + own : lead + own + 8] = jnp.where(row < 4, d, 0.0)
        for r in tiles(own):
            frames[b, lead + r : lead + r + TILE] = x[r : r + TILE, lanes].astype(F32)

        def pick(first, count, shift):
            return frames[b, pl.ds(lead + 2 * first + shift, count, stride=2), :]

        for r in tiles(rows):
            parts = []
            for shift in (-1, 0, 1, 2):
                if r < half:
                    parts.append(pick(r, TILE, shift))
                else:
                    parts.append(
                        jnp.concatenate([pick(half, 8, shift), pick(-8, 8, shift)], axis=0)
                    )
            span = slice(r, r + TILE)
            parts[0] = parts[0] * masks[0, span]
            parts[3] = parts[3] * masks[1, span]
            taps[1 + j, span, :] = split_bins(parts).astype(BF16)

    def two_pairs(i, carry):
        pair(2 * i, 0)
        pair(2 * i + 1, 1)
        return carry

    each = MEL // 4 // len(fetch)
    for k, copy in enumerate(fetch):
        copy.wait()
        lax.fori_loop(k * each, (k + 1) * each, two_pairs, 0)


def conv_one_body(row_count, features, up, down, clips_in, wg,
                  pre, stats, taps, masks, k1_out, k2_out, vec_out,
                  kf, weight, acc, frames, x, clips, sems, clip_sem):
    clip_copy = pltpu.make_async_copy(clips_in, clips, clip_sem)
    clip_copy.start()
    wide = x.shape[1] // sems.shape[0]
    fetch = []
    for k in range(sems.shape[0]):
        lanes = pl.ds(k * wide, wide)
        fetch.append(pltpu.make_async_copy(features.at[:, lanes], x.at[:, lanes], sems.at[k]))
        fetch[k].start()
    clip_copy.wait()
    emit_masks(wg.shape[0], clips, masks)
    emit_taps_one(fetch, x, up, down, masks, taps, frames)
    rows = taps.shape[1]
    half = rows - TAIL
    pairs = 4
    rows_one = 9 * C_IN // row_count
    rows_two = 9 * C_MID // row_count
    grps = wg.shape[0] // row_count
    share = C_MID // grps
    for r in range(row_count):
        shard = [
            unpack(wg[g * row_count + r].astype(F32), share, rows_one + rows_two + 4)
            for g in range(grps)
        ]
        shard = jnp.concatenate(shard, axis=0).T
        kf[rows_one * r : rows_one * (r + 1)] = shard[0:rows_one]
        at = 9 * C_IN + rows_two * r
        kf[at : at + rows_two] = shard[rows_one : rows_one + rows_two]
        if r == 0:
            vec_out[...] = shard[rows_one + rows_two : rows_one + rows_two + 4]
    k1_out[...] = kf[0 : 9 * C_IN].astype(BF16)
    k2_out[...] = kf[9 * C_IN :].astype(BF16)
    weight[...] = jnp.zeros(weight.shape, BF16)
    for d in range(3):
        for q in range(4):
            for p in range(2):
                t = q - p
                if 0 <= t < 3:
                    at = d * BOTH + q * C_IN
                    start = (3 * t + d) * C_IN
                    weight[at : at + C_IN, p * 128 : p * 128 + 128] = k1_out[start : start + C_IN]
    acc[...] = jnp.zeros(acc.shape, F32)
    for c in range(MEL // 2 // pairs):
        here = range(c * pairs, (c + 1) * pairs)
        out = jnp.dot(near_bins(taps, here, rows), weight[...], preferred_element_type=F32)
        for parity in range(2):
            for q in range(pairs):
                at = (parity * pairs + q) * rows
                pre[2 * (c * pairs + q) + parity] = out[at : at + rows]
        stats_of(out, 2 * pairs, rows, half, acc)
    spread(fold(acc[0]), fold(acc[1]), stats)


def conv_one(features, up, down, clips, wg, row_count):
    rows = features.shape[0] // 2 + TAIL
    copies = wg.shape[0]
    return call(
        lambda *refs: conv_one_body(row_count, *refs),
        (features, up, down, clips, wg),
        [
            like((MEL, rows, BOTH), F32),
            like((copies, 2, C_MID), F32),
            like((MEL // 2 + 2, rows, WIDE), BF16),
            like((2, rows, LANES), F32),
            like((9 * C_IN, C_MID), BF16),
            like((9 * C_MID, C_MID), BF16),
            like((4, C_MID), F32),
        ],
        [
            pltpu.VMEM((9 * (C_IN + C_MID), C_MID), F32),
            pltpu.VMEM((3 * BOTH, BOTH), BF16),
            pltpu.VMEM((2, 8, BOTH), F32),
            pltpu.VMEM((2, features.shape[0] + 48, LANES), F32),
            pltpu.VMEM(features.shape, BF16),
            pltpu.VMEM(clips.shape, jnp.int32),
            pltpu.SemaphoreType.DMA((4,)),
            pltpu.SemaphoreType.DMA,
        ],
        in_specs=[HBM, VMEM, VMEM, HBM, VMEM],
    )


def place_two(k2, weight):
    weight[...] = jnp.zeros(weight.shape, BF16)
    for d in range(3):
        for q in range(4):
            for p in range(2):
                t = q - p
                if 0 <= t < 3:
                    at = d * WIDE + q * 128
                    start = (3 * t + d) * C_MID
                    weight[at : at + 128, p * 128 : p * 128 + 128] = k2[start : start + C_MID]


def place_two_back(k2, weight):
    weight[...] = jnp.zeros(weight.shape, BF16)
    for t in range(3):
        for d in range(3):
            start = (3 * t + d) * C_MID
            turned = (0.5 * k2[start : start + C_MID].astype(F32).T).astype(BF16)
            for p in range(2):
                at = (2 - d) * WIDE + (2 - t + p) * 128
                weight[at : at + 128, p * 128 : p * 128 + 128] = turned


def place_one_back(k1, weight):
    weight[...] = jnp.zeros(weight.shape, BF16)
    for t in range(3):
        for d in range(3):
            start = (3 * t + d) * C_IN
            turned = k1[start : start + C_IN].astype(F32).T.astype(BF16)
            for mo in (1, 2):
                for p in range(2):
                    at = (mo - d + 1) * WIDE + (2 - t + p) * 128
                    to = p * 128 + (mo - 1) * 64
                    weight[at : at + 128, to : to + 64] = turned


def conv_two_body(count, pre_one, stats_one, vec, masks, k2, pre, stats, taps, sums_out,
                  acc, weight, *sides):
    place_two(k2, weight)
    rows = masks.shape[1]
    half = rows - TAIL
    mels = 2
    sums = stat_sums(stats_one)
    sums_out[...] = sums
    mean, rstd = norm_terms(sums, count)
    scale = 0.5 * vec[0:1] * rstd
    shift = twice(0.5 * vec[1:2] - mean * scale)
    scale = twice(scale)
    clear_ends(taps)
    acc[...] = jnp.zeros(acc.shape, F32)

    def activate(m):
        def tile(r):
            h = pre_one[m, r : r + TILE] * scale + shift
            return halves_of(h + h * jnp.tanh(h))

        emit_taps(taps.at[1 + m], masks, sides[m % SIDES], sides[SIDES + m % SIDES], tile)

    def convolve(c):
        lhs = [taps[c * mels + d : (c + 1) * mels + d].reshape(mels * rows, WIDE) for d in range(3)]
        out = jnp.dot(jnp.concatenate(lhs, axis=1), weight[...], preferred_element_type=F32)
        pre[c * mels : (c + 1) * mels] = out.reshape(mels, rows, BOTH)
        stats_of(out, mels, rows, half, acc)

    for m in range(MEL):
        activate(m)
        if m >= mels and m % mels == 0:
            convolve(m // mels - 1)
    convolve(MEL // mels - 1)
    spread(fold(acc[0]), fold(acc[1]), stats)


def conv_two(pre_one, stats_one, vec, masks, k2, count):
    copies = stats_one.shape[0]
    rows = masks.shape[1]
    return call(
        lambda *refs: conv_two_body(count, *refs),
        (pre_one, stats_one, vec, masks, k2),
        [
            like((MEL, rows, BOTH), F32),
            like((copies, 2, C_MID), F32),
            like((MEL + 2, rows, WIDE), BF16),
            like((2, C_MID), F32),
        ],
        [pltpu.VMEM((2, 8, BOTH), F32), pltpu.VMEM((3 * WIDE, BOTH), BF16), *side_scratch(rows)],
    )


def norm_two_body(count, pre, stats_two, vec, cot, up, down, pooled, lift, back_stats, sums_out, acc):
    half = cot.shape[0]
    sums = stat_sums(stats_two)
    sums_out[...] = sums
    mean, rstd = norm_terms(sums, count)
    scale = 0.5 * vec[2:3] * rstd
    shift = 0.5 * vec[3:4] - mean * scale
    acc[...] = jnp.zeros(acc.shape, F32)
    row = lax.broadcasted_iota(jnp.int32, (TAIL, LANES), 0)

    def pair(j, carry):
        lanes = pl.ds(pl.multiple_of(j * LANES, LANES), LANES)
        u = up[:, lanes].astype(F32)
        d = down[:, lanes].astype(F32)
        first = jnp.zeros((8, LANES), F32)
        second = jnp.zeros((8, LANES), F32)
        for r in tiles(half + TAIL):
            span = slice(r, r + TILE)
            if r < half:
                grad = cot[span, lanes].astype(F32) * 0.125
            else:
                grad = jnp.where(row == 0, d[4:5], jnp.where(row == TAIL - 1, u[4:5], 0.0)) * 0.125
            total = jnp.zeros((TILE, LANES), F32)
            for m in (2 * j, 2 * j + 1):
                for p in range(2):
                    side = slice(p * C_MID, (p + 1) * C_MID)
                    value = pre[m, span, side]
                    h = value * scale + shift
                    th = jnp.tanh(h)
                    one = 1.0 + th
                    silu = h * one
                    gl = grad * (one + (silu - silu * th))
                    lift[m, span, side] = gl
                    if r < half:
                        total += silu
                        first += partial_sum(gl)
                        second += partial_sum(gl * h)
            if r < half:
                pooled[span, lanes] = (total * 0.25).astype(BF16)
        add_sums(acc, first, second)
        return carry

    lax.fori_loop(0, MEL // 2, pair, 0)
    first, second = [jnp.sum(acc[k], axis=0, keepdims=True) for k in range(2)]
    spread(first, normed_sum(second, first, vec[2:3], vec[3:4]), back_stats)


def norm_two(pre, stats_two, vec, cot, up, down, count):
    copies = stats_two.shape[0]
    half, wide = cot.shape
    return call(
        lambda *refs: norm_two_body(count, *refs),
        (pre, stats_two, vec, cot, up, down),
        [
            like((half, wide), BF16),
            like((MEL, half + TAIL, BOTH), F32),
            like((copies, 2, C_MID), F32),
            like((2, C_MID), F32),
        ],
        [pltpu.VMEM((2, 8, LANES), F32)],
    )


def grad_terms(sums, back, gain, count):
    mean, rstd = norm_terms(sums, count)
    a = gain * rstd
    b = -a * rstd * (back[1:2] / count)
    c = -a * (back[0:1] / count) - b * mean
    return twice(a), twice(b), twice(c)


def back_two_body(count, lift, pre_two, sums_two, back_stats, vec, masks, k2, pre_one, sums_one,
                  taps_a, lift_one, two, back_out, sums_out, acc, acc_two, weight, *buffers):
    place_two_back(k2, weight)
    sides, taps = buffers[: 2 * SIDES], buffers[2 * SIDES :]
    rows = masks.shape[1]
    half = rows - TAIL
    mels = 4
    wide_mels = 8
    back = stat_sums(back_stats)
    sums_out[...] = back
    a, b, c = grad_terms(sums_two[...], back, vec[2:3], count)
    mean, rstd = norm_terms(sums_one[...], count)
    scale = 0.5 * vec[0:1] * rstd
    shift = twice(0.5 * vec[1:2] - mean * scale)
    scale = twice(scale)
    taps[-1][...] = jnp.zeros(taps[-1].shape, BF16)
    acc[...] = jnp.zeros(acc.shape, F32)

    def lower(m):
        def tile(r):
            span = slice(r, r + TILE)
            return halves_of(lift[m, span] * a + (pre_two[m, span] * b + c))

        emit_taps(ring_slot(taps, m), masks, sides[m % SIDES], sides[SIDES + m % SIDES], tile)

    def convolve(k):
        lhs = [stack(taps, range(k * mels + d - 1, (k + 1) * mels + d - 1), rows) for d in range(3)]
        out = jnp.dot(jnp.concatenate(lhs, axis=1), weight[...], preferred_element_type=F32)
        first = jnp.zeros((8, BOTH), F32)
        second = jnp.zeros((8, BOTH), F32)
        for i in range(mels):
            m = k * mels + i
            for r in range(0, rows, 8):
                span = slice(r, r + 8)
                h = pre_one[m, span] * scale + shift
                th = jnp.tanh(h)
                one = 1.0 + th
                silu = h * one
                gl = out[i * rows + r : i * rows + r + 8] * (one + (silu - silu * th))
                lift_one[m, span] = gl
                if r < half:
                    first += gl
                    second += gl * h
        add_sums(acc, first, second)

    def correlate(k):
        here = range(k * wide_mels, (k + 1) * wide_mels)
        first = here[0]
        near = [
            taps_a[first + d : first + d + wide_mels, 0:half].reshape(wide_mels * half, WIDE)
            for d in range(3)
        ]
        total = dot_rows(stack(taps, here, half, slice(128, 384)), jnp.concatenate(near, axis=1))
        if k == 0:
            acc_two[...] = total
        else:
            acc_two[...] += total

    for k in range(MEL // mels + 1):
        for m in range(k * mels, (k + 1) * mels):
            if m < MEL:
                lower(m)
        if k > 0:
            convolve(k - 1)
            if k * mels % wide_mels == 0:
                correlate(k * mels // wide_mels - 1)
    plain = fold(acc[0])
    spread(plain, normed_sum(fold(acc[1]), plain, vec[0:1], vec[1:2]), back_out)
    for t in range(3):
        for d in range(3):
            at = d * WIDE + t * 128
            to = (3 * t + d) * 128
            two[:, to : to + 128] = (
                acc_two[0:C_MID, at : at + 128] + acc_two[C_MID:BOTH, at + 128 : at + 256]
            )


def back_two(lift, pre_two, sums_two, back_stats, vec, masks, k2, pre_one, sums_one, taps_a, count):
    copies = back_stats.shape[0]
    rows = masks.shape[1]
    return call(
        lambda *refs: back_two_body(count, *refs),
        (lift, pre_two, sums_two, back_stats, vec, masks, k2, pre_one, sums_one, taps_a),
        [
            like((MEL, rows, BOTH), F32),
            like((C_MID, 9 * C_MID), F32),
            like((copies, 2, C_MID), F32),
            like((2, C_MID), F32),
        ],
        [
            pltpu.VMEM((2, 8, BOTH), F32),
            pltpu.VMEM((BOTH, 3 * WIDE), F32),
            pltpu.VMEM((3 * WIDE, BOTH), BF16),
            *side_scratch(rows),
            *ring_scratch(17, rows),
        ],

        input_output_aliases={0: 0},
    )


def scatter_blocks(out, parts, row_count):
    copies = out.shape[0]
    grps = copies // row_count
    share = C_MID // grps
    turned = [part.T for part in parts]
    sizes = [part.shape[1] // row_count for part in parts]
    for r in range(row_count):
        rows = [t[n * r : n * (r + 1)] for t, n in zip(turned, sizes)]
        back = jnp.concatenate(rows, axis=0).T
        for g in range(grps):
            block = back[share * g : share * (g + 1)]
            out[g * row_count + r] = pack(block, out.shape[1]).astype(BF16)


def kernel_one_step(taps_x, taps, acc, k, pairs):
    half = taps[-1].shape[0]
    here = range(k * pairs, (k + 1) * pairs)
    mels = [2 * j + parity for parity in range(2) for j in here]
    chosen = jnp.concatenate([taps[m % len(taps)][:, 128:384] for m in mels], axis=0)
    total = dot_rows(chosen, near_bins(taps_x, here, half))
    if k == 0:
        acc[...] = total
    else:
        acc[...] += total


def kernel_one_sums(acc):
    pieces = []
    for t in range(3):
        for d in range(3):
            total = jnp.zeros((C_MID, C_IN), F32)
            for p in range(2):
                at = d * BOTH + (t + p) * C_IN
                total += acc[p * C_MID : (p + 1) * C_MID, at : at + C_IN]
            pieces.append(total)
    return jnp.concatenate(pieces, axis=1)


STORED = 320


def grads_body(count, row_count, lift, pre_one, sums_one, back_stats, vec, masks, taps_x, two,
               stored, blocks, sums_out, acc_one, sems, *buffers):
    sides, taps = buffers[: 2 * SIDES], buffers[2 * SIDES :]
    slots = len(taps)
    back = stat_sums(back_stats)
    sums_out[...] = back
    a, b, c = grad_terms(sums_one[...], back, vec[0:1], count)

    def lower(m):
        def tile(r):
            span = slice(r, r + TILE)
            return halves_of(lift[m, span] * a + (pre_one[m, span] * b + c))

        emit_taps(taps[m % slots], masks, sides[m % SIDES], sides[SIDES + m % SIDES], tile)

    pairs = 4
    copies = []
    for k in range(MEL // 2 // pairs + 1):
        for m in range(2 * pairs * k, 2 * pairs * (k + 1)):
            if m < MEL:
                if m >= slots:
                    copies[m - slots].wait()
                lower(m)
                copy = pltpu.make_async_copy(taps[m % slots], stored.at[m], sems.at[m % slots])
                copy.start()
                copies.append(copy)
        if k > 0:
            kernel_one_step(taps_x, taps, acc_one, k - 1, pairs)
    scatter_blocks(blocks, [kernel_one_sums(acc_one), two[...]], row_count)
    for copy in copies[-slots:]:
        copy.wait()


def kernel_grads(lift, pre_one, sums_one, back_stats, vec, masks, taps_x, two, row_count, count):
    copies = back_stats.shape[0]
    half = masks.shape[1] - TAIL
    share = C_MID * row_count // copies
    rows = packed_rows(share, 9 * (C_IN + C_MID) // row_count)
    slots = 24
    return call(
        lambda *refs: grads_body(count, row_count, *refs),
        (lift, pre_one, sums_one, back_stats, vec, masks, taps_x, two),
        [
            like((STORED, half, WIDE), BF16),
            like((copies, rows, LANES), BF16),
            like((2, C_MID), F32),
        ],
        [
            pltpu.VMEM((BOTH, 3 * BOTH), F32),
            pltpu.SemaphoreType.DMA((slots,)),
            *side_scratch(half + TAIL),
            *ring_scratch(slots, half),
        ],
        out_specs=[HBM, VMEM, VMEM],
    )


def features_body(stored, k1, out, taps, weight, woven, sems, out_sems):
    pairs = 4
    half = taps.shape[1]
    group = MEL // sems.shape[0]
    fetch = []
    for k in range(sems.shape[0]):
        here = pl.ds(k * group, group)
        fetch.append(
            pltpu.make_async_copy(
                stored.at[here], taps.at[pl.ds(1 + k * group, group)], sems.at[k]
            )
        )
        fetch[k].start()
    clear_ends(taps)
    place_one_back(k1, weight)
    fetched = 0
    copies = []
    slots = woven.shape[0]
    for k in range(MEL // 2 // pairs):
        while fetched * group < min(2 * pairs * (k + 1) + 1, MEL):
            fetch[fetched].wait()
            fetched += 1
        near = []
        for i in range(4):
            mels = [taps[2 * (k * pairs + q) + i] for q in range(pairs)]
            near.append(jnp.concatenate(mels, axis=0))
        part = jnp.dot(jnp.concatenate(near, axis=1), weight[...], preferred_element_type=F32)
        for q in range(pairs):
            j = k * pairs + q
            b = j % slots
            rows = slice(q * half, (q + 1) * half)
            if j >= slots:
                copies[j - slots].wait()
            woven[b, pl.ds(0, half, stride=2), :] = part[rows, 0:128]
            woven[b, pl.ds(1, half, stride=2), :] = part[rows, 128:256]
            copy = pltpu.make_async_copy(
                woven.at[b], out.at[:, pl.ds(j * LANES, LANES)], out_sems.at[b]
            )
            copy.start()
            copies.append(copy)
    for copy in copies[-slots:]:
        copy.wait()


def features_grad(stored, k1):
    half = stored.shape[1]
    return call(
        features_body,
        (stored, k1),
        [like((2 * half, MEL * C_IN), F32)],
        [
            pltpu.VMEM((MEL + 2, half, WIDE), BF16),
            pltpu.VMEM((4 * WIDE, BOTH), BF16),
            pltpu.VMEM((8, 2 * half, LANES), F32),
            pltpu.SemaphoreType.DMA((8,)),
            pltpu.SemaphoreType.DMA((8,)),
        ],
        in_specs=[HBM, VMEM],
        out_specs=[ANY],
    )[0]


def finish_body(got, back_one_sums, back_two_sums, own_one, own_two, ga, sa, gb, sb):
    size = own_one.shape[1]
    share = own_one.shape[0]
    total = jnp.sum(got[...].astype(F32), axis=0)
    total = unpack(total, share, size + own_two.shape[1])
    own_one[...] = total[:, 0:size]
    own_two[...] = total[:, size:]
    lane = lax.broadcasted_iota(jnp.int32, (share, C_MID), 1)
    row = lax.broadcasted_iota(jnp.int32, (share, C_MID), 0)
    chosen = lane == lax.axis_index("grp") * share + row
    first = lax.broadcasted_iota(jnp.int32, (share, share), 0)
    second = lax.broadcasted_iota(jnp.int32, (share, share), 1)
    for out, sums, k in (
        (ga, back_one_sums, 1), (sa, back_one_sums, 0), (gb, back_two_sums, 1), (sb, back_two_sums, 0)
    ):
        wide = jnp.broadcast_to(sums[k : k + 1], (share, C_MID))
        column = jnp.sum(jnp.where(chosen, wide, 0.0), axis=1, keepdims=True)
        wide = jnp.broadcast_to(column, (share, share))
        out[...] = jnp.sum(jnp.where(first == second, wide, 0.0), axis=0, keepdims=True)


def finish(got, back_one_sums, back_two_sums, share, rows_one, rows_two):
    shapes = [(share, rows_one), (share, rows_two)] + [(1, share)] * 4
    return call(
        finish_body,
        (got, back_one_sums, back_two_sums),
        [like(s, F32) for s in shapes],
    )


def exchange(blocks):
    return lax.all_to_all(blocks, AXES, 0, 0, tiled=True)


def shards(
    features, clip_starts, kernel_one, kernel_two, gain_one, shift_one, gain_two, shift_two, cotangent
):
    frames = features.shape[0]
    copies = lax.axis_size(AXES)
    row_count = lax.axis_size("row")
    count = float(frames * MEL * copies)
    rows_one, rows_two = kernel_one.shape[0], kernel_two.shape[0]
    share = kernel_one.shape[1]
    vectors = [v.reshape(1, share) for v in (gain_one, shift_one, gain_two, shift_two)]
    clips = clip_starts.reshape(1, -1)
    weights, up, down, clips = setup(
        kernel_one.T, kernel_two.T, vectors, clips, features, cotangent, copies
    )
    ends = copies - 1
    up = lax.ppermute(up, AXES, [(i, i + 1) for i in range(ends)])
    down = lax.ppermute(down, AXES, [(i + 1, i) for i in range(ends)])
    weights = exchange(weights)
    pre_one, stats, taps_x, masks, k1, k2, vec = conv_one(
        features, up, down, clips, weights, row_count
    )
    stats = exchange(stats)
    pre_two, stats, taps_a, sums_one = conv_two(pre_one, stats, vec, masks, k2, count)
    stats = exchange(stats)
    block_out, lift, stats, sums_two = norm_two(pre_two, stats, vec, cotangent, up, down, count)
    stats = exchange(stats)
    lift, two, stats, back_two_sums = back_two(
        lift, pre_two, sums_two, stats, vec, masks, k2, pre_one, sums_one, taps_a, count
    )
    stats = exchange(stats)
    stored, blocks, back_one_sums = kernel_grads(
        lift, pre_one, sums_one, stats, vec, masks, taps_x, two, row_count, count
    )
    blocks = exchange(blocks)
    grad_features = features_grad(stored, k1)
    own_one, own_two, ga, sa, gb, sb = finish(
        blocks, back_one_sums, back_two_sums, share, rows_one, rows_two
    )
    return (
        block_out,
        grad_features,
        own_one.T,
        own_two.T,
        ga.reshape(share),
        sa.reshape(share),
        gb.reshape(share),
        sb.reshape(share),
    )


def solution(mesh):
    placed = (
        P(AXES, None), P(), P("row", "grp"), P("row", "grp"),
        P("grp"), P("grp"), P("grp"), P("grp"), P(AXES, None),
    )
    return jax.shard_map(
        shards,
        mesh=mesh,
        in_specs=placed,
        out_specs=(
            P(AXES, None), P(AXES, None), P("row", "grp"), P("row", "grp"),
            P("grp"), P("grp"), P("grp"), P("grp"),
        ),
        check_vma=False,
    )
```

```python
import jax
import jax.numpy as jnp
from jax import lax
from jax.experimental import pallas as pl
from jax.experimental.pallas import tpu as pltpu
from jax.sharding import PartitionSpec as P

MEL = 32
C_IN = 64
C_MID = 128
EPS = 1e-05
AXES = ("grp", "row")
LANES = 128
TAIL = 16
WIDE = 4 * LANES
BOTH = 2 * C_MID
F32 = jnp.float32
BF16 = jnp.bfloat16
TILE = 16
SIDES = 4
MIB = 2**20

VMEM = pl.BlockSpec(memory_space=pltpu.VMEM)
ANY = pl.BlockSpec(memory_space=pl.ANY)
HBM = pl.BlockSpec(memory_space=pltpu.HBM)


def like(shape, dtype):
    return jax.ShapeDtypeStruct(shape, dtype)


def call(body, args, outs, scratch=(), limit=16, in_specs=None, out_specs=None, **more):
    return pl.pallas_call(
        body,
        in_specs=in_specs or [VMEM] * len(args),
        out_specs=out_specs or [VMEM] * len(outs),
        out_shape=outs,
        scratch_shapes=list(scratch),
        compiler_params=pltpu.CompilerParams(vmem_limit_bytes=limit * MIB),
        cost_estimate=pl.CostEstimate(flops=5 * 10**9, bytes_accessed=0, transcendentals=0),
        **more,
    )(*args)


def padded(size):
    return -(-size // LANES) * LANES


def packed_rows(share, wide):
    rest = wide - LANES
    if rest > 0 and share == 32 and 3 * (LANES - rest) >= rest:
        return share + 24
    return share * (padded(wide) // LANES)


def pack(block, rows):
    share, wide = block.shape
    if rows % share == 0:
        block = jnp.concatenate([block, jnp.zeros((share, padded(wide) - wide), F32)], axis=1)
        return jnp.concatenate(
            [block[:, at : at + LANES] for at in range(0, block.shape[1], LANES)], axis=0
        )
    rest = block[:, LANES:]
    room = 2 * LANES - wide
    tail = jnp.concatenate(
        [rest[24:32], jnp.zeros((8, 3 * room - rest.shape[1]), F32)], axis=1
    )
    tail = jnp.concatenate([tail[:, k * room : (k + 1) * room] for k in range(3)], axis=0)
    return jnp.concatenate([block[:, :LANES], jnp.concatenate([rest[0:24], tail], axis=1)], axis=0)


def unpack(block, share, wide):
    rows = block.shape[0]
    if rows % share == 0:
        parts = [block[at : at + share] for at in range(0, rows, share)]
        return jnp.concatenate(parts, axis=1)[:, 0:wide]
    width = wide - LANES
    second = block[share:]
    tail = jnp.concatenate([second[8 * k : 8 * k + 8, width:] for k in range(3)], axis=1)
    rest = jnp.concatenate([second[:, :width], tail[:, :width]], axis=0)
    return jnp.concatenate([block[0:share], rest], axis=1)


def partial_sum(values):
    return jnp.sum(values.reshape(-1, 8, values.shape[-1]), axis=0)


def fold(values):
    total = jnp.sum(values, axis=0, keepdims=True)
    return total[:, :C_MID] + total[:, C_MID:]


def spread(first, second, out):
    sums = jnp.concatenate([first, second], axis=0)
    out[...] = jnp.broadcast_to(sums[None], out.shape)


def twice(row):
    return jnp.concatenate([row, row], axis=1)


def tiles(rows):
    return range(0, rows, TILE)


def emit_taps(taps, masks, evens, odds, tile_of):
    rows = masks.shape[1]
    kept = taps.shape[0]
    for r in tiles(rows):
        even, odd = tile_of(r)
        evens[r : r + TILE] = even
        odds[8 + r : 8 + r + TILE] = odd
        if r == 0:
            evens[rows : rows + 1] = even[0:1]
        if r + TILE == rows:
            odds[7:8] = odd[TILE - 1 : TILE]
        if r < kept:
            taps[r : r + TILE, 128:256] = even.astype(BF16)
            taps[r : r + TILE, 256:384] = odd.astype(BF16)
    for r in tiles(kept):
        span = slice(r, r + TILE)
        before = odds[7 + r : 7 + r + TILE] * masks[0, span]
        after = evens[1 + r : 1 + r + TILE] * masks[1, span]
        taps[span, 0:128] = before.astype(BF16)
        taps[span, 384:512] = after.astype(BF16)


def halves_of(value):
    return value[:, :C_MID], value[:, C_MID:]


def add_sums(acc, first, second):
    acc[0] += first
    acc[1] += second


def side_scratch(rows):
    return [pltpu.VMEM((rows + 8, LANES), F32)] * (2 * SIDES)


def stats_of(out, mels, rows, half, acc):
    first = jnp.zeros((8, BOTH), F32)
    second = jnp.zeros((8, BOTH), F32)
    for k in range(mels):
        for r in range(0, half, 8):
            value = out[k * rows + r : k * rows + r + 8]
            first += value
            second += value * value
    add_sums(acc, first, second)


def normed_sum(with_half_lifted, plain, gain, shift):
    return (2.0 * with_half_lifted - shift * plain) / gain


def stat_sums(stats):
    return jnp.sum(stats[...], axis=0)


def norm_terms(sums, count):
    mean = sums[0:1] / count
    rstd = lax.rsqrt(sums[1:2] / count - mean * mean + EPS)
    return mean, rstd


def dot_rows(first, second):
    return lax.dot_general(
        first, second, (((0,), (0,)), ((), ())), preferred_element_type=F32
    )


def ring_slot(ring, m):
    return ring[m % (len(ring) - 1)] if 0 <= m < MEL else ring[-1]


def stack(ring, mels, rows, lanes=slice(None)):
    return jnp.concatenate([ring_slot(ring, m)[0:rows, lanes] for m in mels], axis=0)


def ring_scratch(slots, rows):
    return [pltpu.VMEM((rows, WIDE), BF16)] * slots


def clear_ends(taps):
    blank = jnp.zeros(taps.shape[1:], BF16)
    taps[0] = blank
    taps[taps.shape[0] - 1] = blank


def setup_body(k1, k2, ga, sa, gb, sb, x_head, x_tail, c_head, c_tail, w_out, up, down):
    share = k1.shape[0]
    copies = w_out.shape[0]
    first = lax.broadcasted_iota(jnp.int32, (share, share), 0)
    second = lax.broadcasted_iota(jnp.int32, (share, share), 1)
    columns = [k1[...].astype(F32), k2[...].astype(F32)]
    for vector in (ga, sa, gb, sb):
        wide = jnp.broadcast_to(vector[...].astype(F32), (share, share))
        columns.append(jnp.sum(jnp.where(first == second, wide, 0.0), axis=1, keepdims=True))
    chunk = pack(jnp.concatenate(columns, axis=1), w_out.shape[1]).astype(BF16)
    for i in range(copies):
        w_out[i] = chunk
    row = lax.broadcasted_iota(jnp.int32, (8, x_head.shape[1]), 0)
    xt = x_tail[...].astype(F32)
    ct = c_tail[...].astype(F32)
    up[...] = jnp.where(
        row < 4, pltpu.roll(xt[8:16], 4, 0), jnp.where(row == 4, ct[15:16], 0.0)
    ).astype(BF16)
    xh = x_head[...].astype(F32)
    ch = c_head[...].astype(F32)
    down[...] = jnp.where(row < 4, xh[0:8], jnp.where(row == 4, ch[0:1], 0.0)).astype(BF16)


def setup(k1t, k2t, vectors, features, cotangent, copies):
    frames, wide = features.shape
    halves = cotangent.shape[0]
    share = k1t.shape[0]
    w = (copies, packed_rows(share, k1t.shape[1] + k2t.shape[1] + 4), LANES)
    whole = lambda shape: pl.BlockSpec(shape, lambda i: (0,) * len(shape))
    outs = [like(w, BF16), like((8, wide), BF16), like((8, wide), BF16)]
    return call(
        setup_body,
        (k1t, k2t, *vectors, features, features, cotangent, cotangent),
        outs,
        limit=56,
        in_specs=[
            whole(k1t.shape),
            whole(k2t.shape),
            *[whole((1, share))] * 4,
            pl.BlockSpec((16, wide), lambda i: (0, 0)),
            pl.BlockSpec((16, wide), lambda i: (frames // 16 - 1, 0)),
            pl.BlockSpec((16, wide), lambda i: (0, 0)),
            pl.BlockSpec((16, wide), lambda i: (halves // 16 - 1, 0)),
        ],
        out_specs=[whole(o.shape) for o in outs],
        grid=(1,),
    )


def emit_masks(copies, clips, masks):
    rows = masks.shape[1]
    half = rows - TAIL
    frames = 2 * half
    start = lax.axis_index(AXES) * frames
    place = lax.broadcasted_iota(jnp.int32, (rows, clips.shape[1]), 0)
    pair = jnp.where(place >= half + TAIL // 2, place - rows, place)
    frame = start + 2 * pair
    starts = jnp.broadcast_to(clips[...], (rows, clips.shape[1]))
    for slot, shift in ((0, 0), (1, 2)):
        hit = (frame + shift == starts) | (frame + shift >= frames * copies)
        begins = jnp.max(jnp.where(hit, 1.0, 0.0), axis=1, keepdims=True)
        masks[slot] = jnp.broadcast_to(1.0 - begins, (rows, LANES))


def split_bins(parts):
    low = lax.broadcasted_iota(jnp.int32, parts[0].shape, 1) < C_IN
    first, second = [], []
    for here, there in (parts[0:2], parts[2:4]):
        first.append(jnp.where(low, here, pltpu.roll(there, C_IN, 1)))
        second.append(jnp.where(low, pltpu.roll(here, C_IN, 1), there))
    return jnp.concatenate(first + second, axis=1)


def near_bins(taps, pairs, rows):
    left, mid, right = [
        jnp.concatenate([taps[1 + j + k, 0:rows] for j in pairs], axis=0) for k in (-1, 0, 1)
    ]
    first = jnp.concatenate([left[:, BOTH:], mid], axis=1)
    second = jnp.concatenate([mid, right[:, :BOTH]], axis=1)
    return jnp.concatenate([first, second], axis=0)


def taps_one_emitter(x, up, down, masks, taps, frames):
    rows = masks.shape[1]
    half = rows - TAIL
    clear_ends(taps)
    row = lax.broadcasted_iota(jnp.int32, (8, LANES), 0)
    lead = 24
    own = 2 * half
    for held in frames:
        held[0:16] = jnp.zeros((16, LANES), F32)
        held[lead + own + 8 : lead + own + 24] = jnp.zeros((16, LANES), F32)

    def pair(j):
        held = frames[j % len(frames)]
        lanes = slice(j * LANES, (j + 1) * LANES)
        u = up[:, lanes].astype(F32)
        d = down[:, lanes].astype(F32)
        held[lead - 8 : lead] = jnp.where(row >= 4, pltpu.roll(u, 4, 0), 0.0)
        held[lead + own : lead + own + 8] = jnp.where(row < 4, d, 0.0)
        for r in tiles(own):
            held[lead + r : lead + r + TILE] = x[r : r + TILE, lanes].astype(F32)

        def pick(first, count, shift):
            return held[pl.ds(lead + 2 * first + shift, count, stride=2), :]

        for r in tiles(rows):
            parts = []
            for shift in (-1, 0, 1, 2):
                if r < half:
                    parts.append(pick(r, TILE, shift))
                else:
                    parts.append(
                        jnp.concatenate([pick(half, 8, shift), pick(-8, 8, shift)], axis=0)
                    )
            span = slice(r, r + TILE)
            parts[0] = parts[0] * masks[0, span]
            parts[3] = parts[3] * masks[1, span]
            taps[1 + j, span, :] = split_bins(parts).astype(BF16)

    return pair


def conv_one_body(row_count, features, up, down, clips_in, wg,
                  pre, stats, taps, masks, k1_out, k2_out, vec_out,
                  kf, weight, acc, x, clips, sems, clip_sem, *frames):
    clip_copy = pltpu.make_async_copy(clips_in, clips, clip_sem)
    clip_copy.start()
    wide = x.shape[1] // sems.shape[0]
    fetch = []
    for k in range(sems.shape[0]):
        lanes = pl.ds(k * wide, wide)
        fetch.append(pltpu.make_async_copy(features.at[:, lanes], x.at[:, lanes], sems.at[k]))
        fetch[k].start()
    clip_copy.wait()
    emit_masks(wg.shape[0], clips, masks)
    emit_pair = taps_one_emitter(x, up, down, masks, taps, frames)
    rows = taps.shape[1]
    half = rows - TAIL
    pairs = 2
    rows_one = 9 * C_IN // row_count
    rows_two = 9 * C_MID // row_count
    grps = wg.shape[0] // row_count
    share = C_MID // grps
    for r in range(row_count):
        shard = [
            unpack(wg[g * row_count + r].astype(F32), share, rows_one + rows_two + 4)
            for g in range(grps)
        ]
        shard = jnp.concatenate(shard, axis=0).T
        kf[rows_one * r : rows_one * (r + 1)] = shard[0:rows_one]
        at = 9 * C_IN + rows_two * r
        kf[at : at + rows_two] = shard[rows_one : rows_one + rows_two]
        if r == 0:
            vec_out[...] = shard[rows_one + rows_two : rows_one + rows_two + 4]
    k1_out[...] = kf[0 : 9 * C_IN].astype(BF16)
    k2_out[...] = kf[9 * C_IN :].astype(BF16)
    weight[...] = jnp.zeros(weight.shape, BF16)
    for d in range(3):
        for q in range(4):
            for p in range(2):
                t = q - p
                if 0 <= t < 3:
                    at = d * BOTH + q * C_IN
                    start = (3 * t + d) * C_IN
                    weight[at : at + C_IN, p * 128 : p * 128 + 128] = k1_out[start : start + C_IN]
    acc[...] = jnp.zeros(acc.shape, F32)

    def convolve(c):
        here = range(c * pairs, (c + 1) * pairs)
        out = jnp.dot(near_bins(taps, here, rows), weight[...], preferred_element_type=F32)
        for parity in range(2):
            for q in range(pairs):
                at = (parity * pairs + q) * rows
                pre[2 * (c * pairs + q) + parity] = out[at : at + rows]
        stats_of(out, 2 * pairs, rows, half, acc)

    total = MEL // 2
    for j in range(total):
        if j % (total // len(fetch)) == 0:
            fetch[j // (total // len(fetch))].wait()
        emit_pair(j)
        if j >= pairs and j % pairs == 0:
            convolve(j // pairs - 1)
    convolve(total // pairs - 1)
    spread(fold(acc[0]), fold(acc[1]), stats)


def conv_one(features, up, down, clips, wg, row_count):
    rows = features.shape[0] // 2 + TAIL
    copies = wg.shape[0]
    return call(
        lambda *refs: conv_one_body(row_count, *refs),
        (features, up, down, clips, wg),
        [
            like((MEL, rows, BOTH), F32),
            like((copies, 2, C_MID), F32),
            like((MEL // 2 + 2, rows, WIDE), BF16),
            like((2, rows, LANES), F32),
            like((9 * C_IN, C_MID), BF16),
            like((9 * C_MID, C_MID), BF16),
            like((4, C_MID), F32),
        ],
        [
            pltpu.VMEM((9 * (C_IN + C_MID), C_MID), F32),
            pltpu.VMEM((3 * BOTH, BOTH), BF16),
            pltpu.VMEM((2, 8, BOTH), F32),
            pltpu.VMEM(features.shape, BF16),
            pltpu.VMEM(clips.shape, jnp.int32),
            pltpu.SemaphoreType.DMA((4,)),
            pltpu.SemaphoreType.DMA,
            *[pltpu.VMEM((features.shape[0] + 48, LANES), F32)] * 4,
        ],
        in_specs=[HBM, VMEM, VMEM, HBM, VMEM],
    )


def place_two(k2, weight):
    weight[...] = jnp.zeros(weight.shape, BF16)
    for d in range(3):
        for q in range(4):
            for p in range(2):
                t = q - p
                if 0 <= t < 3:
                    at = d * WIDE + q * 128
                    start = (3 * t + d) * C_MID
                    weight[at : at + 128, p * 128 : p * 128 + 128] = k2[start : start + C_MID]


def place_two_back(k2, weight):
    weight[...] = jnp.zeros(weight.shape, BF16)
    for t in range(3):
        for d in range(3):
            start = (3 * t + d) * C_MID
            turned = (0.5 * k2[start : start + C_MID].astype(F32).T).astype(BF16)
            for p in range(2):
                at = (2 - d) * WIDE + (2 - t + p) * 128
                weight[at : at + 128, p * 128 : p * 128 + 128] = turned


def place_one_back(k1, weight):
    weight[...] = jnp.zeros(weight.shape, BF16)
    for t in range(3):
        for d in range(3):
            start = (3 * t + d) * C_IN
            turned = k1[start : start + C_IN].astype(F32).T.astype(BF16)
            for mo in (1, 2):
                for p in range(2):
                    at = (mo - d + 1) * WIDE + (2 - t + p) * 128
                    to = p * 128 + (mo - 1) * 64
                    weight[at : at + 128, to : to + 64] = turned


def conv_two_body(count, pre_one, stats_one, vec, masks, k2, pre, stats, taps, sums_out,
                  acc, weight, *sides):
    place_two(k2, weight)
    rows = masks.shape[1]
    half = rows - TAIL
    mels = 2
    sums = stat_sums(stats_one)
    sums_out[...] = sums
    mean, rstd = norm_terms(sums, count)
    scale = 0.5 * vec[0:1] * rstd
    shift = twice(0.5 * vec[1:2] - mean * scale)
    scale = twice(scale)
    clear_ends(taps)
    acc[...] = jnp.zeros(acc.shape, F32)

    def activate(m):
        def tile(r):
            h = pre_one[m, r : r + TILE] * scale + shift
            return halves_of(h + h * jnp.tanh(h))

        emit_taps(taps.at[1 + m], masks, sides[m % SIDES], sides[SIDES + m % SIDES], tile)

    def convolve(c):
        lhs = [taps[c * mels + d : (c + 1) * mels + d].reshape(mels * rows, WIDE) for d in range(3)]
        out = jnp.dot(jnp.concatenate(lhs, axis=1), weight[...], preferred_element_type=F32)
        pre[c * mels : (c + 1) * mels] = out.reshape(mels, rows, BOTH)
        stats_of(out, mels, rows, half, acc)

    for m in range(MEL):
        activate(m)
        if m >= mels and m % mels == 0:
            convolve(m // mels - 1)
    convolve(MEL // mels - 1)
    spread(fold(acc[0]), fold(acc[1]), stats)


def conv_two(pre_one, stats_one, vec, masks, k2, count):
    copies = stats_one.shape[0]
    rows = masks.shape[1]
    return call(
        lambda *refs: conv_two_body(count, *refs),
        (pre_one, stats_one, vec, masks, k2),
        [
            like((MEL, rows, BOTH), F32),
            like((copies, 2, C_MID), F32),
            like((MEL + 2, rows, WIDE), BF16),
            like((2, C_MID), F32),
        ],
        [pltpu.VMEM((2, 8, BOTH), F32), pltpu.VMEM((3 * WIDE, BOTH), BF16), *side_scratch(rows)],
    )


def norm_two_body(count, pre, stats_two, vec, cot, up, down, pooled, lift, back_stats, sums_out, acc):
    half = cot.shape[0]
    sums = stat_sums(stats_two)
    sums_out[...] = sums
    mean, rstd = norm_terms(sums, count)
    scale = 0.5 * vec[2:3] * rstd
    shift = 0.5 * vec[3:4] - mean * scale
    acc[...] = jnp.zeros(acc.shape, F32)
    row = lax.broadcasted_iota(jnp.int32, (TAIL, LANES), 0)

    def pair(j, carry):
        lanes = pl.ds(pl.multiple_of(j * LANES, LANES), LANES)
        u = up[:, lanes].astype(F32)
        d = down[:, lanes].astype(F32)
        first = jnp.zeros((8, LANES), F32)
        second = jnp.zeros((8, LANES), F32)
        for r in tiles(half + TAIL):
            span = slice(r, r + TILE)
            if r < half:
                grad = cot[span, lanes].astype(F32) * 0.125
            else:
                grad = jnp.where(row == 0, d[4:5], jnp.where(row == TAIL - 1, u[4:5], 0.0)) * 0.125
            total = jnp.zeros((TILE, LANES), F32)
            for m in (2 * j, 2 * j + 1):
                for p in range(2):
                    side = slice(p * C_MID, (p + 1) * C_MID)
                    value = pre[m, span, side]
                    h = value * scale + shift
                    th = jnp.tanh(h)
                    one = 1.0 + th
                    silu = h * one
                    gl = grad * (one + (silu - silu * th))
                    lift[m, span, side] = gl
                    if r < half:
                        total += silu
                        first += partial_sum(gl)
                        second += partial_sum(gl * h)
            if r < half:
                pooled[span, lanes] = (total * 0.25).astype(BF16)
        add_sums(acc, first, second)
        return carry

    lax.fori_loop(0, MEL // 2, pair, 0)
    first, second = [jnp.sum(acc[k], axis=0, keepdims=True) for k in range(2)]
    spread(first, normed_sum(second, first, vec[2:3], vec[3:4]), back_stats)


def norm_two(pre, stats_two, vec, cot, up, down, count):
    copies = stats_two.shape[0]
    half, wide = cot.shape
    return call(
        lambda *refs: norm_two_body(count, *refs),
        (pre, stats_two, vec, cot, up, down),
        [
            like((half, wide), BF16),
            like((MEL, half + TAIL, BOTH), F32),
            like((copies, 2, C_MID), F32),
            like((2, C_MID), F32),
        ],
        [pltpu.VMEM((2, 8, LANES), F32)],
    )


def grad_terms(sums, back, gain, count):
    mean, rstd = norm_terms(sums, count)
    a = gain * rstd
    b = -a * rstd * (back[1:2] / count)
    c = -a * (back[0:1] / count) - b * mean
    return twice(a), twice(b), twice(c)


def back_two_body(count, lift, pre_two, sums_two, back_stats, vec, masks, k2, pre_one, sums_one,
                  taps_a, lift_one, two, back_out, sums_out, acc, acc_two, weight, *buffers):
    place_two_back(k2, weight)
    sides, taps = buffers[: 2 * SIDES], buffers[2 * SIDES :]
    rows = masks.shape[1]
    half = rows - TAIL
    mels = 4
    wide_mels = 4
    back = stat_sums(back_stats)
    sums_out[...] = back
    a, b, c = grad_terms(sums_two[...], back, vec[2:3], count)
    mean, rstd = norm_terms(sums_one[...], count)
    scale = 0.5 * vec[0:1] * rstd
    shift = twice(0.5 * vec[1:2] - mean * scale)
    scale = twice(scale)
    taps[-1][...] = jnp.zeros(taps[-1].shape, BF16)
    acc[...] = jnp.zeros(acc.shape, F32)

    def lower(m):
        def tile(r):
            span = slice(r, r + TILE)
            return halves_of(lift[m, span] * a + (pre_two[m, span] * b + c))

        emit_taps(ring_slot(taps, m), masks, sides[m % SIDES], sides[SIDES + m % SIDES], tile)

    def convolve(k):
        lhs = [stack(taps, range(k * mels + d - 1, (k + 1) * mels + d - 1), rows) for d in range(3)]
        out = jnp.dot(jnp.concatenate(lhs, axis=1), weight[...], preferred_element_type=F32)
        first = jnp.zeros((8, BOTH), F32)
        second = jnp.zeros((8, BOTH), F32)
        for i in range(mels):
            m = k * mels + i
            for r in range(0, rows, 8):
                span = slice(r, r + 8)
                h = pre_one[m, span] * scale + shift
                th = jnp.tanh(h)
                one = 1.0 + th
                silu = h * one
                gl = out[i * rows + r : i * rows + r + 8] * (one + (silu - silu * th))
                lift_one[m, span] = gl
                if r < half:
                    first += gl
                    second += gl * h
        add_sums(acc, first, second)

    def correlate(k):
        here = range(k * wide_mels, (k + 1) * wide_mels)
        first = here[0]
        near = [
            taps_a[first + d : first + d + wide_mels, 0:half].reshape(wide_mels * half, WIDE)
            for d in range(3)
        ]
        total = dot_rows(stack(taps, here, half, slice(128, 384)), jnp.concatenate(near, axis=1))
        if k == 0:
            acc_two[...] = total
        else:
            acc_two[...] += total

    for k in range(MEL // mels + 1):
        for m in range(k * mels, (k + 1) * mels):
            if m < MEL:
                lower(m)
        if k > 0:
            convolve(k - 1)
            if k * mels % wide_mels == 0:
                correlate(k * mels // wide_mels - 1)
    plain = fold(acc[0])
    spread(plain, normed_sum(fold(acc[1]), plain, vec[0:1], vec[1:2]), back_out)
    for t in range(3):
        for d in range(3):
            at = d * WIDE + t * 128
            to = (3 * t + d) * 128
            two[:, to : to + 128] = (
                acc_two[0:C_MID, at : at + 128] + acc_two[C_MID:BOTH, at + 128 : at + 256]
            )


def back_two(lift, pre_two, sums_two, back_stats, vec, masks, k2, pre_one, sums_one, taps_a, count):
    copies = back_stats.shape[0]
    rows = masks.shape[1]
    return call(
        lambda *refs: back_two_body(count, *refs),
        (lift, pre_two, sums_two, back_stats, vec, masks, k2, pre_one, sums_one, taps_a),
        [
            like((MEL, rows, BOTH), F32),
            like((C_MID, 9 * C_MID), F32),
            like((copies, 2, C_MID), F32),
            like((2, C_MID), F32),
        ],
        [
            pltpu.VMEM((2, 8, BOTH), F32),
            pltpu.VMEM((BOTH, 3 * WIDE), F32),
            pltpu.VMEM((3 * WIDE, BOTH), BF16),
            *side_scratch(rows),
            *ring_scratch(17, rows),
        ],

        input_output_aliases={0: 0},
    )


def scatter_blocks(out, parts, row_count):
    copies = out.shape[0]
    grps = copies // row_count
    share = C_MID // grps
    turned = [part.T for part in parts]
    sizes = [part.shape[1] // row_count for part in parts]
    for r in range(row_count):
        rows = [t[n * r : n * (r + 1)] for t, n in zip(turned, sizes)]
        back = jnp.concatenate(rows, axis=0).T
        for g in range(grps):
            block = back[share * g : share * (g + 1)]
            out[g * row_count + r] = pack(block, out.shape[1]).astype(BF16)


def kernel_one_step(taps_x, taps, acc, k, pairs):
    half = taps[-1].shape[0]
    here = range(k * pairs, (k + 1) * pairs)
    mels = [2 * j + parity for parity in range(2) for j in here]
    chosen = jnp.concatenate([taps[m % len(taps)][:, 128:384] for m in mels], axis=0)
    total = dot_rows(chosen, near_bins(taps_x, here, half))
    if k == 0:
        acc[...] = total
    else:
        acc[...] += total


def kernel_one_sums(acc):
    pieces = []
    for t in range(3):
        for d in range(3):
            total = jnp.zeros((C_MID, C_IN), F32)
            for p in range(2):
                at = d * BOTH + (t + p) * C_IN
                total += acc[p * C_MID : (p + 1) * C_MID, at : at + C_IN]
            pieces.append(total)
    return jnp.concatenate(pieces, axis=1)


STORED = 320


def grads_body(count, row_count, lift, pre_one, sums_one, back_stats, vec, masks, taps_x, two,
               stored, blocks, sums_out, acc_one, sems, *buffers):
    sides, taps = buffers[: 2 * SIDES], buffers[2 * SIDES :]
    slots = len(taps)
    back = stat_sums(back_stats)
    sums_out[...] = back
    a, b, c = grad_terms(sums_one[...], back, vec[0:1], count)

    def lower(m):
        def tile(r):
            span = slice(r, r + TILE)
            return halves_of(lift[m, span] * a + (pre_one[m, span] * b + c))

        emit_taps(taps[m % slots], masks, sides[m % SIDES], sides[SIDES + m % SIDES], tile)

    pairs = 2
    copies = []
    for k in range(MEL // 2 // pairs + 1):
        for m in range(2 * pairs * k, 2 * pairs * (k + 1)):
            if m < MEL:
                if m >= slots:
                    copies[m - slots].wait()
                lower(m)
                copy = pltpu.make_async_copy(taps[m % slots], stored.at[m], sems.at[m % slots])
                copy.start()
                copies.append(copy)
        if k > 0:
            kernel_one_step(taps_x, taps, acc_one, k - 1, pairs)
    scatter_blocks(blocks, [kernel_one_sums(acc_one), two[...]], row_count)
    for copy in copies[-slots:]:
        copy.wait()


def kernel_grads(lift, pre_one, sums_one, back_stats, vec, masks, taps_x, two, row_count, count):
    copies = back_stats.shape[0]
    half = masks.shape[1] - TAIL
    share = C_MID * row_count // copies
    rows = packed_rows(share, 9 * (C_IN + C_MID) // row_count)
    slots = 24
    return call(
        lambda *refs: grads_body(count, row_count, *refs),
        (lift, pre_one, sums_one, back_stats, vec, masks, taps_x, two),
        [
            like((STORED, half, WIDE), BF16),
            like((copies, rows, LANES), BF16),
            like((2, C_MID), F32),
        ],
        [
            pltpu.VMEM((BOTH, 3 * BOTH), F32),
            pltpu.SemaphoreType.DMA((slots,)),
            *side_scratch(half + TAIL),
            *ring_scratch(slots, half),
        ],
        out_specs=[HBM, VMEM, VMEM],
    )


def features_body(stored, k1, out, taps, weight, woven, sems, out_sems):
    pairs = 4
    half = taps.shape[1]
    group = MEL // sems.shape[0]
    fetch = []
    for k in range(sems.shape[0]):
        here = pl.ds(k * group, group)
        fetch.append(
            pltpu.make_async_copy(
                stored.at[here], taps.at[pl.ds(1 + k * group, group)], sems.at[k]
            )
        )
        fetch[k].start()
    clear_ends(taps)
    place_one_back(k1, weight)
    fetched = 0
    copies = []
    slots = woven.shape[0]
    for k in range(MEL // 2 // pairs):
        while fetched * group < min(2 * pairs * (k + 1) + 1, MEL):
            fetch[fetched].wait()
            fetched += 1
        near = []
        for i in range(4):
            mels = [taps[2 * (k * pairs + q) + i] for q in range(pairs)]
            near.append(jnp.concatenate(mels, axis=0))
        part = jnp.dot(jnp.concatenate(near, axis=1), weight[...], preferred_element_type=F32)
        for q in range(pairs):
            j = k * pairs + q
            b = j % slots
            rows = slice(q * half, (q + 1) * half)
            if j >= slots:
                copies[j - slots].wait()
            woven[b, pl.ds(0, half, stride=2), :] = part[rows, 0:128]
            woven[b, pl.ds(1, half, stride=2), :] = part[rows, 128:256]
            copy = pltpu.make_async_copy(
                woven.at[b], out.at[:, pl.ds(j * LANES, LANES)], out_sems.at[b]
            )
            copy.start()
            copies.append(copy)
    for copy in copies[-slots:]:
        copy.wait()


def features_grad(stored, k1):
    half = stored.shape[1]
    return call(
        features_body,
        (stored, k1),
        [like((2 * half, MEL * C_IN), F32)],
        [
            pltpu.VMEM((MEL + 2, half, WIDE), BF16),
            pltpu.VMEM((4 * WIDE, BOTH), BF16),
            pltpu.VMEM((8, 2 * half, LANES), F32),
            pltpu.SemaphoreType.DMA((8,)),
            pltpu.SemaphoreType.DMA((8,)),
        ],
        in_specs=[HBM, VMEM],
        out_specs=[ANY],
    )[0]


def finish_body(got, back_one_sums, back_two_sums, own_one, own_two, ga, sa, gb, sb):
    size = own_one.shape[1]
    share = own_one.shape[0]
    total = jnp.sum(got[...].astype(F32), axis=0)
    total = unpack(total, share, size + own_two.shape[1])
    own_one[...] = total[:, 0:size]
    own_two[...] = total[:, size:]
    lane = lax.broadcasted_iota(jnp.int32, (share, C_MID), 1)
    row = lax.broadcasted_iota(jnp.int32, (share, C_MID), 0)
    chosen = lane == lax.axis_index("grp") * share + row
    first = lax.broadcasted_iota(jnp.int32, (share, share), 0)
    second = lax.broadcasted_iota(jnp.int32, (share, share), 1)
    for out, sums, k in (
        (ga, back_one_sums, 1), (sa, back_one_sums, 0), (gb, back_two_sums, 1), (sb, back_two_sums, 0)
    ):
        wide = jnp.broadcast_to(sums[k : k + 1], (share, C_MID))
        column = jnp.sum(jnp.where(chosen, wide, 0.0), axis=1, keepdims=True)
        wide = jnp.broadcast_to(column, (share, share))
        out[...] = jnp.sum(jnp.where(first == second, wide, 0.0), axis=0, keepdims=True)


def finish(got, back_one_sums, back_two_sums, share, rows_one, rows_two):
    shapes = [(share, rows_one), (share, rows_two)] + [(1, share)] * 4
    return call(
        finish_body,
        (got, back_one_sums, back_two_sums),
        [like(s, F32) for s in shapes],
    )


def exchange(blocks):
    return lax.all_to_all(blocks, AXES, 0, 0, tiled=True)


def shards(
    features, clip_starts, kernel_one, kernel_two, gain_one, shift_one, gain_two, shift_two, cotangent
):
    frames = features.shape[0]
    copies = lax.axis_size(AXES)
    row_count = lax.axis_size("row")
    count = float(frames * MEL * copies)
    rows_one, rows_two = kernel_one.shape[0], kernel_two.shape[0]
    share = kernel_one.shape[1]
    vectors = [v.reshape(1, share) for v in (gain_one, shift_one, gain_two, shift_two)]
    clips = clip_starts.reshape(1, -1)
    weights, up, down = setup(kernel_one.T, kernel_two.T, vectors, features, cotangent, copies)
    ends = copies - 1
    up = lax.ppermute(up, AXES, [(i, i + 1) for i in range(ends)])
    down = lax.ppermute(down, AXES, [(i + 1, i) for i in range(ends)])
    weights = exchange(weights)
    pre_one, stats, taps_x, masks, k1, k2, vec = conv_one(
        features, up, down, clips, weights, row_count
    )
    stats = exchange(stats)
    pre_two, stats, taps_a, sums_one = conv_two(pre_one, stats, vec, masks, k2, count)
    stats = exchange(stats)
    block_out, lift, stats, sums_two = norm_two(pre_two, stats, vec, cotangent, up, down, count)
    stats = exchange(stats)
    lift, two, stats, back_two_sums = back_two(
        lift, pre_two, sums_two, stats, vec, masks, k2, pre_one, sums_one, taps_a, count
    )
    stats = exchange(stats)
    stored, blocks, back_one_sums = kernel_grads(
        lift, pre_one, sums_one, stats, vec, masks, taps_x, two, row_count, count
    )
    blocks = exchange(blocks)
    grad_features = features_grad(stored, k1)
    own_one, own_two, ga, sa, gb, sb = finish(
        blocks, back_one_sums, back_two_sums, share, rows_one, rows_two
    )
    return (
        block_out,
        grad_features,
        own_one.T,
        own_two.T,
        ga.reshape(share),
        sa.reshape(share),
        gb.reshape(share),
        sb.reshape(share),
    )


def solution(mesh):
    placed = (
        P(AXES, None), P(), P("row", "grp"), P("row", "grp"),
        P("grp"), P("grp"), P("grp"), P("grp"), P(AXES, None),
    )
    return jax.shard_map(
        shards,
        mesh=mesh,
        in_specs=placed,
        out_specs=(
            P(AXES, None), P(AXES, None), P("row", "grp"), P("row", "grp"),
            P("grp"), P("grp"), P("grp"), P("grp"),
        ),
        check_vma=False,
    )
```

```python
import jax
import jax.numpy as jnp
from jax import lax
from jax.experimental import pallas as pl
from jax.experimental.pallas import tpu as pltpu
from jax.sharding import PartitionSpec as P

MEL = 32
C_IN = 64
C_MID = 128
EPS = 1e-05
AXES = ("grp", "row")
LANES = 128
TAIL = 16
WIDE = 4 * LANES
BOTH = 2 * C_MID
F32 = jnp.float32
BF16 = jnp.bfloat16
TILE = 16
SIDES = 4
MIB = 2**20

VMEM = pl.BlockSpec(memory_space=pltpu.VMEM)
ANY = pl.BlockSpec(memory_space=pl.ANY)
HBM = pl.BlockSpec(memory_space=pltpu.HBM)


def like(shape, dtype):
    return jax.ShapeDtypeStruct(shape, dtype)


def call(body, args, outs, scratch=(), limit=14, in_specs=None, out_specs=None, **more):
    return pl.pallas_call(
        body,
        in_specs=in_specs or [VMEM] * len(args),
        out_specs=out_specs or [VMEM] * len(outs),
        out_shape=outs,
        scratch_shapes=list(scratch),
        compiler_params=pltpu.CompilerParams(vmem_limit_bytes=limit * MIB),
        cost_estimate=pl.CostEstimate(flops=5 * 10**9, bytes_accessed=0, transcendentals=0),
        **more,
    )(*args)


def padded(size):
    return -(-size // LANES) * LANES


def packed_rows(share, wide):
    rest = wide - LANES
    if rest > 0 and share == 32 and 3 * (LANES - rest) >= rest:
        return share + 24
    return share * (padded(wide) // LANES)


def pack(block, rows):
    share, wide = block.shape
    if rows % share == 0:
        block = jnp.concatenate([block, jnp.zeros((share, padded(wide) - wide), F32)], axis=1)
        return jnp.concatenate(
            [block[:, at : at + LANES] for at in range(0, block.shape[1], LANES)], axis=0
        )
    rest = block[:, LANES:]
    room = 2 * LANES - wide
    tail = jnp.concatenate(
        [rest[24:32], jnp.zeros((8, 3 * room - rest.shape[1]), F32)], axis=1
    )
    tail = jnp.concatenate([tail[:, k * room : (k + 1) * room] for k in range(3)], axis=0)
    return jnp.concatenate([block[:, :LANES], jnp.concatenate([rest[0:24], tail], axis=1)], axis=0)


def unpack(block, share, wide):
    rows = block.shape[0]
    if rows % share == 0:
        parts = [block[at : at + share] for at in range(0, rows, share)]
        return jnp.concatenate(parts, axis=1)[:, 0:wide]
    width = wide - LANES
    second = block[share:]
    tail = jnp.concatenate([second[8 * k : 8 * k + 8, width:] for k in range(3)], axis=1)
    rest = jnp.concatenate([second[:, :width], tail[:, :width]], axis=0)
    return jnp.concatenate([block[0:share], rest], axis=1)


def partial_sum(values):
    return jnp.sum(values.reshape(-1, 8, values.shape[-1]), axis=0)


def fold(values):
    total = jnp.sum(values, axis=0, keepdims=True)
    return total[:, :C_MID] + total[:, C_MID:]


def spread(first, second, out):
    sums = jnp.concatenate([first, second], axis=0)
    out[...] = jnp.broadcast_to(sums[None], out.shape)


def twice(row):
    return jnp.concatenate([row, row], axis=1)


def tiles(rows):
    return range(0, rows, TILE)


def emit_taps(taps, masks, evens, odds, tile_of):
    rows = masks.shape[1]
    kept = taps.shape[0]
    for r in tiles(rows):
        even, odd = tile_of(r)
        evens[r : r + TILE] = even
        odds[8 + r : 8 + r + TILE] = odd
        if r == 0:
            evens[rows : rows + 1] = even[0:1]
        if r + TILE == rows:
            odds[7:8] = odd[TILE - 1 : TILE]
        if r < kept:
            taps[r : r + TILE, 128:256] = even.astype(BF16)
            taps[r : r + TILE, 256:384] = odd.astype(BF16)
    for r in tiles(kept):
        span = slice(r, r + TILE)
        before = odds[7 + r : 7 + r + TILE] * masks[0, span]
        after = evens[1 + r : 1 + r + TILE] * masks[1, span]
        taps[span, 0:128] = before.astype(BF16)
        taps[span, 384:512] = after.astype(BF16)


def halves_of(value):
    return value[:, :C_MID], value[:, C_MID:]


def add_sums(acc, first, second):
    acc[0] += first
    acc[1] += second


def side_scratch(rows):
    return [pltpu.VMEM((rows + 8, LANES), F32)] * (2 * SIDES)


def stats_of(out, mels, rows, half, acc):
    first = jnp.zeros((8, BOTH), F32)
    second = jnp.zeros((8, BOTH), F32)
    for k in range(mels):
        for r in range(0, half, 8):
            value = out[k * rows + r : k * rows + r + 8]
            first += value
            second += value * value
    add_sums(acc, first, second)


def normed_sum(with_half_lifted, plain, gain, shift):
    return (2.0 * with_half_lifted - shift * plain) / gain


def stat_sums(stats):
    return jnp.sum(stats[...], axis=0)


def norm_terms(sums, count):
    mean = sums[0:1] / count
    rstd = lax.rsqrt(sums[1:2] / count - mean * mean + EPS)
    return mean, rstd


def dot_rows(first, second):
    return lax.dot_general(
        first, second, (((0,), (0,)), ((), ())), preferred_element_type=F32
    )


def ring_slot(ring, m):
    return ring[m % (len(ring) - 1)] if 0 <= m < MEL else ring[-1]


def stack(ring, mels, rows, lanes=slice(None)):
    return jnp.concatenate([ring_slot(ring, m)[0:rows, lanes] for m in mels], axis=0)


def ring_scratch(slots, rows):
    return [pltpu.VMEM((rows, WIDE), BF16)] * slots


def clear_ends(taps):
    blank = jnp.zeros(taps.shape[1:], BF16)
    taps[0] = blank
    taps[taps.shape[0] - 1] = blank


def setup_body(k1, k2, ga, sa, gb, sb, x_head, x_tail, c_head, c_tail, w_out, up, down):
    share = k1.shape[0]
    copies = w_out.shape[0]
    first = lax.broadcasted_iota(jnp.int32, (share, share), 0)
    second = lax.broadcasted_iota(jnp.int32, (share, share), 1)
    columns = [k1[...].astype(F32), k2[...].astype(F32)]
    for vector in (ga, sa, gb, sb):
        wide = jnp.broadcast_to(vector[...].astype(F32), (share, share))
        columns.append(jnp.sum(jnp.where(first == second, wide, 0.0), axis=1, keepdims=True))
    chunk = pack(jnp.concatenate(columns, axis=1), w_out.shape[1]).astype(BF16)
    for i in range(copies):
        w_out[i] = chunk
    row = lax.broadcasted_iota(jnp.int32, (8, x_head.shape[1]), 0)
    xt = x_tail[...].astype(F32)
    ct = c_tail[...].astype(F32)
    up[...] = jnp.where(
        row < 4, pltpu.roll(xt[8:16], 4, 0), jnp.where(row == 4, ct[15:16], 0.0)
    ).astype(BF16)
    xh = x_head[...].astype(F32)
    ch = c_head[...].astype(F32)
    down[...] = jnp.where(row < 4, xh[0:8], jnp.where(row == 4, ch[0:1], 0.0)).astype(BF16)


def setup(k1t, k2t, vectors, features, cotangent, copies):
    frames, wide = features.shape
    halves = cotangent.shape[0]
    share = k1t.shape[0]
    w = (copies, packed_rows(share, k1t.shape[1] + k2t.shape[1] + 4), LANES)
    whole = lambda shape: pl.BlockSpec(shape, lambda i: (0,) * len(shape))
    outs = [like(w, BF16), like((8, wide), BF16), like((8, wide), BF16)]
    return call(
        setup_body,
        (k1t, k2t, *vectors, features, features, cotangent, cotangent),
        outs,
        limit=56,
        in_specs=[
            whole(k1t.shape),
            whole(k2t.shape),
            *[whole((1, share))] * 4,
            pl.BlockSpec((16, wide), lambda i: (0, 0)),
            pl.BlockSpec((16, wide), lambda i: (frames // 16 - 1, 0)),
            pl.BlockSpec((16, wide), lambda i: (0, 0)),
            pl.BlockSpec((16, wide), lambda i: (halves // 16 - 1, 0)),
        ],
        out_specs=[whole(o.shape) for o in outs],
        grid=(1,),
    )


def emit_masks(copies, clips, masks):
    rows = masks.shape[1]
    half = rows - TAIL
    frames = 2 * half
    start = lax.axis_index(AXES) * frames
    place = lax.broadcasted_iota(jnp.int32, (rows, clips.shape[1]), 0)
    pair = jnp.where(place >= half + TAIL // 2, place - rows, place)
    frame = start + 2 * pair
    starts = jnp.broadcast_to(clips[...], (rows, clips.shape[1]))
    for slot, shift in ((0, 0), (1, 2)):
        hit = (frame + shift == starts) | (frame + shift >= frames * copies)
        begins = jnp.max(jnp.where(hit, 1.0, 0.0), axis=1, keepdims=True)
        masks[slot] = jnp.broadcast_to(1.0 - begins, (rows, LANES))


def split_bins(parts):
    low = lax.broadcasted_iota(jnp.int32, parts[0].shape, 1) < C_IN
    first, second = [], []
    for here, there in (parts[0:2], parts[2:4]):
        first.append(jnp.where(low, here, pltpu.roll(there, C_IN, 1)))
        second.append(jnp.where(low, pltpu.roll(here, C_IN, 1), there))
    return jnp.concatenate(first + second, axis=1)


def near_bins(taps, pairs, rows):
    left, mid, right = [
        jnp.concatenate([taps[1 + j + k, 0:rows] for j in pairs], axis=0) for k in (-1, 0, 1)
    ]
    first = jnp.concatenate([left[:, BOTH:], mid], axis=1)
    second = jnp.concatenate([mid, right[:, :BOTH]], axis=1)
    return jnp.concatenate([first, second], axis=0)


def taps_one_emitter(x, up, down, masks, taps, frames):
    rows = masks.shape[1]
    half = rows - TAIL
    clear_ends(taps)
    row = lax.broadcasted_iota(jnp.int32, (8, LANES), 0)
    lead = 24
    own = 2 * half
    for held in frames:
        held[0:16] = jnp.zeros((16, LANES), F32)
        held[lead + own + 8 : lead + own + 24] = jnp.zeros((16, LANES), F32)

    def pair(j):
        held = frames[j % len(frames)]
        lanes = slice(j * LANES, (j + 1) * LANES)
        u = up[:, lanes].astype(F32)
        d = down[:, lanes].astype(F32)
        held[lead - 8 : lead] = jnp.where(row >= 4, pltpu.roll(u, 4, 0), 0.0)
        held[lead + own : lead + own + 8] = jnp.where(row < 4, d, 0.0)
        for r in tiles(own):
            held[lead + r : lead + r + TILE] = x[r : r + TILE, lanes].astype(F32)

        def pick(first, count, shift):
            return held[pl.ds(lead + 2 * first + shift, count, stride=2), :]

        for r in tiles(rows):
            parts = []
            for shift in (-1, 0, 1, 2):
                if r < half:
                    parts.append(pick(r, TILE, shift))
                else:
                    parts.append(
                        jnp.concatenate([pick(half, 8, shift), pick(-8, 8, shift)], axis=0)
                    )
            span = slice(r, r + TILE)
            parts[0] = parts[0] * masks[0, span]
            parts[3] = parts[3] * masks[1, span]
            taps[1 + j, span, :] = split_bins(parts).astype(BF16)

    return pair


def conv_one_body(row_count, features, up, down, clips_in, wg,
                  pre, stats, taps, masks, k1_out, k2_out, vec_out, weight_two,
                  kf, weight, acc, x, clips, sems, clip_sem, *frames):
    clip_copy = pltpu.make_async_copy(clips_in, clips, clip_sem)
    clip_copy.start()
    wide = x.shape[1] // sems.shape[0]
    fetch = []
    for k in range(sems.shape[0]):
        lanes = pl.ds(k * wide, wide)
        fetch.append(pltpu.make_async_copy(features.at[:, lanes], x.at[:, lanes], sems.at[k]))
        fetch[k].start()
    clip_copy.wait()
    emit_masks(wg.shape[0], clips, masks)
    emit_pair = taps_one_emitter(x, up, down, masks, taps, frames)
    rows = taps.shape[1]
    half = rows - TAIL
    pairs = 2
    rows_one = 9 * C_IN // row_count
    rows_two = 9 * C_MID // row_count
    grps = wg.shape[0] // row_count
    share = C_MID // grps
    for r in range(row_count):
        shard = [
            unpack(wg[g * row_count + r].astype(F32), share, rows_one + rows_two + 4)
            for g in range(grps)
        ]
        shard = jnp.concatenate(shard, axis=0).T
        kf[rows_one * r : rows_one * (r + 1)] = shard[0:rows_one]
        at = 9 * C_IN + rows_two * r
        kf[at : at + rows_two] = shard[rows_one : rows_one + rows_two]
        if r == 0:
            vec_out[...] = shard[rows_one + rows_two : rows_one + rows_two + 4]
    k1_out[...] = kf[0 : 9 * C_IN].astype(BF16)
    k2_out[...] = kf[9 * C_IN :].astype(BF16)
    weight[...] = jnp.zeros(weight.shape, BF16)
    for d in range(3):
        for q in range(4):
            for p in range(2):
                t = q - p
                if 0 <= t < 3:
                    at = d * BOTH + q * C_IN
                    start = (3 * t + d) * C_IN
                    weight[at : at + C_IN, p * 128 : p * 128 + 128] = k1_out[start : start + C_IN]
    acc[...] = jnp.zeros(acc.shape, F32)

    def convolve(c):
        here = range(c * pairs, (c + 1) * pairs)
        out = jnp.dot(near_bins(taps, here, rows), weight[...], preferred_element_type=F32)
        for parity in range(2):
            for q in range(pairs):
                at = (parity * pairs + q) * rows
                pre[2 * (c * pairs + q) + parity] = out[at : at + rows]
        stats_of(out, 2 * pairs, rows, half, acc)

    total = MEL // 2
    for j in range(total):
        if j % (total // len(fetch)) == 0:
            fetch[j // (total // len(fetch))].wait()
        emit_pair(j)
        if j >= pairs and j % pairs == 0:
            convolve(j // pairs - 1)
        if j == 4:
            place_two(k2_out, weight_two)
    convolve(total // pairs - 1)
    spread(fold(acc[0]), fold(acc[1]), stats)


def conv_one(features, up, down, clips, wg, row_count):
    rows = features.shape[0] // 2 + TAIL
    copies = wg.shape[0]
    return call(
        lambda *refs: conv_one_body(row_count, *refs),
        (features, up, down, clips, wg),
        [
            like((MEL, rows, BOTH), F32),
            like((copies, 2, C_MID), F32),
            like((MEL // 2 + 2, rows, WIDE), BF16),
            like((2, rows, LANES), F32),
            like((9 * C_IN, C_MID), BF16),
            like((9 * C_MID, C_MID), BF16),
            like((4, C_MID), F32),
            like((3 * WIDE, BOTH), BF16),
        ],
        [
            pltpu.VMEM((9 * (C_IN + C_MID), C_MID), F32),
            pltpu.VMEM((3 * BOTH, BOTH), BF16),
            pltpu.VMEM((2, 8, BOTH), F32),
            pltpu.VMEM(features.shape, BF16),
            pltpu.VMEM(clips.shape, jnp.int32),
            pltpu.SemaphoreType.DMA((4,)),
            pltpu.SemaphoreType.DMA,
            *[pltpu.VMEM((features.shape[0] + 48, LANES), F32)] * 4,
        ],
        in_specs=[HBM, VMEM, VMEM, HBM, VMEM],
    )


def place_two(k2, weight):
    weight[...] = jnp.zeros(weight.shape, BF16)
    for d in range(3):
        for q in range(4):
            for p in range(2):
                t = q - p
                if 0 <= t < 3:
                    at = d * WIDE + q * 128
                    start = (3 * t + d) * C_MID
                    weight[at : at + 128, p * 128 : p * 128 + 128] = k2[start : start + C_MID]


def place_two_back(k2, weight):
    weight[...] = jnp.zeros(weight.shape, BF16)
    for t in range(3):
        for d in range(3):
            start = (3 * t + d) * C_MID
            turned = (0.5 * k2[start : start + C_MID].astype(F32).T).astype(BF16)
            for p in range(2):
                at = (2 - d) * WIDE + (2 - t + p) * 128
                weight[at : at + 128, p * 128 : p * 128 + 128] = turned


def place_one_back(k1, weight):
    weight[...] = jnp.zeros(weight.shape, BF16)
    for t in range(3):
        for d in range(3):
            start = (3 * t + d) * C_IN
            turned = k1[start : start + C_IN].astype(F32).T.astype(BF16)
            for mo in (1, 2):
                for p in range(2):
                    at = (mo - d + 1) * WIDE + (2 - t + p) * 128
                    to = p * 128 + (mo - 1) * 64
                    weight[at : at + 128, to : to + 64] = turned


def conv_two_body(count, pre_one, stats_one, vec, masks, k2, weight,
                  pre, stats, taps, sums_out, weight_back, acc, *sides):
    rows = masks.shape[1]
    half = rows - TAIL
    mels = 2
    sums = stat_sums(stats_one)
    sums_out[...] = sums
    mean, rstd = norm_terms(sums, count)
    scale = 0.5 * vec[0:1] * rstd
    shift = twice(0.5 * vec[1:2] - mean * scale)
    scale = twice(scale)
    clear_ends(taps)
    acc[...] = jnp.zeros(acc.shape, F32)

    def activate(m):
        def tile(r):
            h = pre_one[m, r : r + TILE] * scale + shift
            return halves_of(h + h * jnp.tanh(h))

        emit_taps(taps.at[1 + m], masks, sides[m % SIDES], sides[SIDES + m % SIDES], tile)

    def convolve(c):
        lhs = [taps[c * mels + d : (c + 1) * mels + d].reshape(mels * rows, WIDE) for d in range(3)]
        out = jnp.dot(jnp.concatenate(lhs, axis=1), weight[...], preferred_element_type=F32)
        pre[c * mels : (c + 1) * mels] = out.reshape(mels, rows, BOTH)
        stats_of(out, mels, rows, half, acc)

    for m in range(MEL):
        activate(m)
        if m >= mels and m % mels == 0:
            convolve(m // mels - 1)
        if m == 8:
            place_two_back(k2, weight_back)
    convolve(MEL // mels - 1)
    spread(fold(acc[0]), fold(acc[1]), stats)


def conv_two(pre_one, stats_one, vec, masks, k2, weight, count):
    copies = stats_one.shape[0]
    rows = masks.shape[1]
    return call(
        lambda *refs: conv_two_body(count, *refs),
        (pre_one, stats_one, vec, masks, k2, weight),
        [
            like((MEL, rows, BOTH), F32),
            like((copies, 2, C_MID), F32),
            like((MEL + 2, rows, WIDE), BF16),
            like((2, C_MID), F32),
            like((3 * WIDE, BOTH), BF16),
        ],
        [pltpu.VMEM((2, 8, BOTH), F32), *side_scratch(rows)],
    )


def norm_two_body(count, pre, stats_two, vec, cot, up, down, pooled, lift, back_stats, sums_out, acc):
    half = cot.shape[0]
    sums = stat_sums(stats_two)
    sums_out[...] = sums
    mean, rstd = norm_terms(sums, count)
    scale = 0.5 * vec[2:3] * rstd
    shift = 0.5 * vec[3:4] - mean * scale
    acc[...] = jnp.zeros(acc.shape, F32)
    row = lax.broadcasted_iota(jnp.int32, (TAIL, LANES), 0)

    factor = 0.125 * vec[2:3] * rstd

    def pair(j):
        lanes = pl.ds(pl.multiple_of(j * LANES, LANES), LANES)
        u = up[:, lanes].astype(F32)
        d = down[:, lanes].astype(F32)
        first = jnp.zeros((8, LANES), F32)
        second = jnp.zeros((8, LANES), F32)
        for r in tiles(half + TAIL):
            span = slice(r, r + TILE)
            if r < half:
                grad = cot[span, lanes].astype(F32) * factor
            else:
                grad = jnp.where(row == 0, d[4:5], jnp.where(row == TAIL - 1, u[4:5], 0.0)) * factor
            total = jnp.zeros((TILE, LANES), F32)
            for m in (2 * j, 2 * j + 1):
                for p in range(2):
                    side = slice(p * C_MID, (p + 1) * C_MID)
                    value = pre[m, span, side]
                    h = value * scale + shift
                    th = jnp.tanh(h)
                    one = 1.0 + th
                    silu = h * one
                    gl = grad * (one + (silu - silu * th))
                    lift[m, span, side] = gl
                    if r < half:
                        total += silu
                        first += partial_sum(gl)
                        second += partial_sum(gl * h)
            if r < half:
                pooled[span, lanes] = (total * 0.25).astype(BF16)
        add_sums(acc, first, second)

    def four_pairs(i, carry):
        for k in range(4):
            pair(4 * i + k)
        return carry

    lax.fori_loop(0, MEL // 8, four_pairs, 0)
    first, second = [jnp.sum(acc[k], axis=0, keepdims=True) for k in range(2)]
    scaled = vec[2:3] * rstd
    first = first / scaled
    spread(first, normed_sum(second / scaled, first, vec[2:3], vec[3:4]), back_stats)


def norm_two(pre, stats_two, vec, cot, up, down, count):
    copies = stats_two.shape[0]
    half, wide = cot.shape
    return call(
        lambda *refs: norm_two_body(count, *refs),
        (pre, stats_two, vec, cot, up, down),
        [
            like((half, wide), BF16),
            like((MEL, half + TAIL, BOTH), F32),
            like((copies, 2, C_MID), F32),
            like((2, C_MID), F32),
        ],
        [pltpu.VMEM((2, 8, LANES), F32)],
    )


def grad_terms(sums, back, gain, count):
    mean, rstd = norm_terms(sums, count)
    a = gain * rstd
    b = -a * rstd * (back[1:2] / count)
    c = -a * (back[0:1] / count) - b * mean
    return twice(a), twice(b), twice(c)


def back_two_body(count, lift, pre_two, sums_two, back_stats, vec, masks, weight, pre_one, sums_one,
                  taps_a, lift_one, two, back_out, sums_out, acc, acc_two, turned, *buffers):
    sides, taps = buffers[: 2 * SIDES], buffers[2 * SIDES :]
    rows = masks.shape[1]
    half = rows - TAIL
    mels = 1
    wide_mels = 4
    back = stat_sums(back_stats)
    sums_out[...] = back
    _, b, c = grad_terms(sums_two[...], back, vec[2:3], count)
    mean, rstd = norm_terms(sums_one[...], count)
    scale = 0.5 * vec[0:1] * rstd
    shift = twice(0.5 * vec[1:2] - mean * scale)
    scale = twice(scale)
    taps[-1][...] = jnp.zeros(taps[-1].shape, BF16)
    acc[...] = jnp.zeros(acc.shape, F32)

    def lower(m):
        def tile(r):
            span = slice(r, r + TILE)
            return halves_of(lift[m, span] + (pre_two[m, span] * b + c))

        emit_taps(ring_slot(taps, m), masks, sides[m % SIDES], sides[SIDES + m % SIDES], tile)

    def convolve(k):
        lhs = [ring_slot(taps, k + d - 1)[...] for d in range(3)]
        out = jnp.dot(jnp.concatenate(lhs, axis=1), weight[...], preferred_element_type=F32)
        first = jnp.zeros((8, BOTH), F32)
        second = jnp.zeros((8, BOTH), F32)
        for i in range(mels):
            m = k * mels + i
            for r in range(0, rows, 8):
                span = slice(r, r + 8)
                h = pre_one[m, span] * scale + shift
                th = jnp.tanh(h)
                one = 1.0 + th
                silu = h * one
                gl = out[i * rows + r : i * rows + r + 8] * (one + (silu - silu * th))
                lift_one[m, span] = gl
                if r < half:
                    first += gl
                    second += gl * h
        add_sums(acc, first, second)

    def correlate(k):
        here = range(k * wide_mels, (k + 1) * wide_mels)
        turned[...] = stack(taps, here, half, slice(128, 384)).T
        for d in range(3):
            first = here[0] + d
            near = taps_a[first : first + wide_mels, 0:half].reshape(wide_mels * half, WIDE)
            total = jnp.dot(turned[...], near, preferred_element_type=F32)
            lanes = slice(d * WIDE, (d + 1) * WIDE)
            if k == 0:
                acc_two[:, lanes] = total
            else:
                acc_two[:, lanes] += total

    for k in range(MEL // mels + 1):
        for m in range(k * mels, (k + 1) * mels):
            if m < MEL:
                lower(m)
        if k > 0:
            convolve(k - 1)
            if k * mels % wide_mels == 0:
                correlate(k * mels // wide_mels - 1)
    plain = fold(acc[0])
    spread(plain, normed_sum(fold(acc[1]), plain, vec[0:1], vec[1:2]), back_out)
    for t in range(3):
        for d in range(3):
            at = d * WIDE + t * 128
            to = (3 * t + d) * 128
            two[:, to : to + 128] = (
                acc_two[0:C_MID, at : at + 128] + acc_two[C_MID:BOTH, at + 128 : at + 256]
            )


def back_two(lift, pre_two, sums_two, back_stats, vec, masks, weight, pre_one, sums_one, taps_a, count):
    copies = back_stats.shape[0]
    rows = masks.shape[1]
    return call(
        lambda *refs: back_two_body(count, *refs),
        (lift, pre_two, sums_two, back_stats, vec, masks, weight, pre_one, sums_one, taps_a),
        [
            like((MEL, rows, BOTH), F32),
            like((C_MID, 9 * C_MID), F32),
            like((copies, 2, C_MID), F32),
            like((2, C_MID), F32),
        ],
        [
            pltpu.VMEM((2, 8, BOTH), F32),
            pltpu.VMEM((BOTH, 3 * WIDE), F32),
            pltpu.VMEM((BOTH, 4 * (rows - TAIL)), BF16),
            *side_scratch(rows),
            *ring_scratch(17, rows),
        ],

        input_output_aliases={0: 0},
    )


def scatter_blocks(out, parts, row_count):
    copies = out.shape[0]
    grps = copies // row_count
    share = C_MID // grps
    turned = [part.T for part in parts]
    sizes = [part.shape[1] // row_count for part in parts]
    for r in range(row_count):
        rows = [t[n * r : n * (r + 1)] for t, n in zip(turned, sizes)]
        back = jnp.concatenate(rows, axis=0).T
        for g in range(grps):
            block = back[share * g : share * (g + 1)]
            out[g * row_count + r] = pack(block, out.shape[1]).astype(BF16)


def kernel_one_step(taps_x, taps, acc, k, pairs):
    half = taps[-1].shape[0]
    here = range(k * pairs, (k + 1) * pairs)
    mels = [2 * j + parity for parity in range(2) for j in here]
    chosen = jnp.concatenate([taps[m % len(taps)][:, 128:384] for m in mels], axis=0)
    total = dot_rows(chosen, near_bins(taps_x, here, half))
    if k == 0:
        acc[...] = total
    else:
        acc[...] += total


def kernel_one_sums(acc):
    pieces = []
    for t in range(3):
        for d in range(3):
            total = jnp.zeros((C_MID, C_IN), F32)
            for p in range(2):
                at = d * BOTH + (t + p) * C_IN
                total += acc[p * C_MID : (p + 1) * C_MID, at : at + C_IN]
            pieces.append(total)
    return jnp.concatenate(pieces, axis=1)


STORED = 320


def grads_body(count, row_count, lift, pre_one, sums_one, back_stats, vec, masks, taps_x, two,
               stored, blocks, sums_out, acc_one, sems, *buffers):
    sides, taps = buffers[: 2 * SIDES], buffers[2 * SIDES :]
    slots = len(taps)
    back = stat_sums(back_stats)
    sums_out[...] = back
    a, b, c = grad_terms(sums_one[...], back, vec[0:1], count)

    def lower(m):
        def tile(r):
            span = slice(r, r + TILE)
            return halves_of(lift[m, span] * a + (pre_one[m, span] * b + c))

        emit_taps(taps[m % slots], masks, sides[m % SIDES], sides[SIDES + m % SIDES], tile)

    pairs = 2
    copies = []
    for k in range(MEL // 2 // pairs + 1):
        for m in range(2 * pairs * k, 2 * pairs * (k + 1)):
            if m < MEL:
                if m >= slots:
                    copies[m - slots].wait()
                lower(m)
                copy = pltpu.make_async_copy(taps[m % slots], stored.at[m], sems.at[m % slots])
                copy.start()
                copies.append(copy)
        if k > 0:
            kernel_one_step(taps_x, taps, acc_one, k - 1, pairs)
    scatter_blocks(blocks, [kernel_one_sums(acc_one), two[...]], row_count)
    for copy in copies[-slots:]:
        copy.wait()


def kernel_grads(lift, pre_one, sums_one, back_stats, vec, masks, taps_x, two, row_count, count):
    copies = back_stats.shape[0]
    half = masks.shape[1] - TAIL
    share = C_MID * row_count // copies
    rows = packed_rows(share, 9 * (C_IN + C_MID) // row_count)
    slots = 24
    return call(
        lambda *refs: grads_body(count, row_count, *refs),
        (lift, pre_one, sums_one, back_stats, vec, masks, taps_x, two),
        [
            like((STORED, half, WIDE), BF16),
            like((copies, rows, LANES), BF16),
            like((2, C_MID), F32),
        ],
        [
            pltpu.VMEM((BOTH, 3 * BOTH), F32),
            pltpu.SemaphoreType.DMA((slots,)),
            *side_scratch(half + TAIL),
            *ring_scratch(slots, half),
        ],
        out_specs=[HBM, VMEM, VMEM],
    )


def features_body(stored, k1, out, taps, weight, woven, sems, out_sems):
    pairs = 4
    half = taps.shape[1]
    group = MEL // sems.shape[0]
    fetch = []
    for k in range(sems.shape[0]):
        here = pl.ds(k * group, group)
        fetch.append(
            pltpu.make_async_copy(
                stored.at[here], taps.at[pl.ds(1 + k * group, group)], sems.at[k]
            )
        )
        fetch[k].start()
    clear_ends(taps)
    place_one_back(k1, weight)
    fetched = 0
    copies = []
    slots = woven.shape[0]
    for k in range(MEL // 2 // pairs):
        while fetched * group < min(2 * pairs * (k + 1) + 1, MEL):
            fetch[fetched].wait()
            fetched += 1
        near = []
        for i in range(4):
            mels = [taps[2 * (k * pairs + q) + i] for q in range(pairs)]
            near.append(jnp.concatenate(mels, axis=0))
        part = jnp.dot(jnp.concatenate(near, axis=1), weight[...], preferred_element_type=F32)
        for q in range(pairs):
            j = k * pairs + q
            b = j % slots
            rows = slice(q * half, (q + 1) * half)
            if j >= slots:
                copies[j - slots].wait()
            woven[b, pl.ds(0, half, stride=2), :] = part[rows, 0:128]
            woven[b, pl.ds(1, half, stride=2), :] = part[rows, 128:256]
            copy = pltpu.make_async_copy(
                woven.at[b], out.at[:, pl.ds(j * LANES, LANES)], out_sems.at[b]
            )
            copy.start()
            copies.append(copy)
    for copy in copies[-slots:]:
        copy.wait()


def features_grad(stored, k1):
    half = stored.shape[1]
    return call(
        features_body,
        (stored, k1),
        [like((2 * half, MEL * C_IN), F32)],
        [
            pltpu.VMEM((MEL + 2, half, WIDE), BF16),
            pltpu.VMEM((4 * WIDE, BOTH), BF16),
            pltpu.VMEM((8, 2 * half, LANES), F32),
            pltpu.SemaphoreType.DMA((8,)),
            pltpu.SemaphoreType.DMA((8,)),
        ],
        in_specs=[HBM, VMEM],
        out_specs=[ANY],
    )[0]


def finish_body(got, back_one_sums, back_two_sums, own_one, own_two, ga, sa, gb, sb):
    size = own_one.shape[1]
    share = own_one.shape[0]
    total = jnp.sum(got[...].astype(F32), axis=0)
    total = unpack(total, share, size + own_two.shape[1])
    own_one[...] = total[:, 0:size]
    own_two[...] = total[:, size:]
    lane = lax.broadcasted_iota(jnp.int32, (share, C_MID), 1)
    row = lax.broadcasted_iota(jnp.int32, (share, C_MID), 0)
    chosen = lane == lax.axis_index("grp") * share + row
    first = lax.broadcasted_iota(jnp.int32, (share, share), 0)
    second = lax.broadcasted_iota(jnp.int32, (share, share), 1)
    for out, sums, k in (
        (ga, back_one_sums, 1), (sa, back_one_sums, 0), (gb, back_two_sums, 1), (sb, back_two_sums, 0)
    ):
        wide = jnp.broadcast_to(sums[k : k + 1], (share, C_MID))
        column = jnp.sum(jnp.where(chosen, wide, 0.0), axis=1, keepdims=True)
        wide = jnp.broadcast_to(column, (share, share))
        out[...] = jnp.sum(jnp.where(first == second, wide, 0.0), axis=0, keepdims=True)


def finish(got, back_one_sums, back_two_sums, share, rows_one, rows_two):
    shapes = [(share, rows_one), (share, rows_two)] + [(1, share)] * 4
    return call(
        finish_body,
        (got, back_one_sums, back_two_sums),
        [like(s, F32) for s in shapes],
    )


def exchange(blocks):
    return lax.all_to_all(blocks, AXES, 0, 0, tiled=True)


def shards(
    features, clip_starts, kernel_one, kernel_two, gain_one, shift_one, gain_two, shift_two, cotangent
):
    frames = features.shape[0]
    copies = lax.axis_size(AXES)
    row_count = lax.axis_size("row")
    count = float(frames * MEL * copies)
    rows_one, rows_two = kernel_one.shape[0], kernel_two.shape[0]
    share = kernel_one.shape[1]
    vectors = [v.reshape(1, share) for v in (gain_one, shift_one, gain_two, shift_two)]
    clips = clip_starts.reshape(1, -1)
    weights, up, down = setup(kernel_one.T, kernel_two.T, vectors, features, cotangent, copies)
    ends = copies - 1
    up = lax.ppermute(up, AXES, [(i, i + 1) for i in range(ends)])
    down = lax.ppermute(down, AXES, [(i + 1, i) for i in range(ends)])
    weights = exchange(weights)
    pre_one, stats, taps_x, masks, k1, k2, vec, weight = conv_one(
        features, up, down, clips, weights, row_count
    )
    stats = exchange(stats)
    pre_two, stats, taps_a, sums_one, weight_back = conv_two(
        pre_one, stats, vec, masks, k2, weight, count
    )
    stats = exchange(stats)
    block_out, lift, stats, sums_two = norm_two(pre_two, stats, vec, cotangent, up, down, count)
    stats = exchange(stats)
    lift, two, stats, back_two_sums = back_two(
        lift, pre_two, sums_two, stats, vec, masks, weight_back, pre_one, sums_one, taps_a, count
    )
    stats = exchange(stats)
    stored, blocks, back_one_sums = kernel_grads(
        lift, pre_one, sums_one, stats, vec, masks, taps_x, two, row_count, count
    )
    blocks = exchange(blocks)
    grad_features = features_grad(stored, k1)
    own_one, own_two, ga, sa, gb, sb = finish(
        blocks, back_one_sums, back_two_sums, share, rows_one, rows_two
    )
    return (
        block_out,
        grad_features,
        own_one.T,
        own_two.T,
        ga.reshape(share),
        sa.reshape(share),
        gb.reshape(share),
        sb.reshape(share),
    )


def solution(mesh):
    placed = (
        P(AXES, None), P(), P("row", "grp"), P("row", "grp"),
        P("grp"), P("grp"), P("grp"), P("grp"), P(AXES, None),
    )
    return jax.shard_map(
        shards,
        mesh=mesh,
        in_specs=placed,
        out_specs=(
            P(AXES, None), P(AXES, None), P("row", "grp"), P("row", "grp"),
            P("grp"), P("grp"), P("grp"), P("grp"),
        ),
        check_vma=False,
    )
```

```python
import jax
import jax.numpy as jnp
from jax import lax
from jax.experimental import pallas as pl
from jax.experimental.pallas import tpu as pltpu
from jax.sharding import PartitionSpec as P

MEL = 32
C_IN = 64
C_MID = 128
EPS = 1e-05
AXES = ("grp", "row")
LANES = 128
TAIL = 16
WIDE = 4 * LANES
BOTH = 2 * C_MID
F32 = jnp.float32
BF16 = jnp.bfloat16
TILE = 16
SIDES = 4
MIB = 2**20

VMEM = pl.BlockSpec(memory_space=pltpu.VMEM)
ANY = pl.BlockSpec(memory_space=pl.ANY)
HBM = pl.BlockSpec(memory_space=pltpu.HBM)


def like(shape, dtype):
    return jax.ShapeDtypeStruct(shape, dtype)


def call(body, args, outs, scratch=(), limit=14, in_specs=None, out_specs=None, **more):
    return pl.pallas_call(
        body,
        in_specs=in_specs or [VMEM] * len(args),
        out_specs=out_specs or [VMEM] * len(outs),
        out_shape=outs,
        scratch_shapes=list(scratch),
        compiler_params=pltpu.CompilerParams(vmem_limit_bytes=limit * MIB),
        cost_estimate=pl.CostEstimate(flops=5 * 10**9, bytes_accessed=0, transcendentals=0),
        **more,
    )(*args)


def padded(size):
    return -(-size // LANES) * LANES


def packed_rows(share, wide):
    rest = wide - LANES
    if rest > 0 and share == 32 and 3 * (LANES - rest) >= rest:
        return share + 24
    return share * (padded(wide) // LANES)


def pack(block, rows):
    share, wide = block.shape
    if rows % share == 0:
        block = jnp.concatenate([block, jnp.zeros((share, padded(wide) - wide), F32)], axis=1)
        return jnp.concatenate(
            [block[:, at : at + LANES] for at in range(0, block.shape[1], LANES)], axis=0
        )
    rest = block[:, LANES:]
    room = 2 * LANES - wide
    tail = jnp.concatenate(
        [rest[24:32], jnp.zeros((8, 3 * room - rest.shape[1]), F32)], axis=1
    )
    tail = jnp.concatenate([tail[:, k * room : (k + 1) * room] for k in range(3)], axis=0)
    return jnp.concatenate([block[:, :LANES], jnp.concatenate([rest[0:24], tail], axis=1)], axis=0)


def unpack(block, share, wide):
    rows = block.shape[0]
    if rows % share == 0:
        parts = [block[at : at + share] for at in range(0, rows, share)]
        return jnp.concatenate(parts, axis=1)[:, 0:wide]
    width = wide - LANES
    second = block[share:]
    tail = jnp.concatenate([second[8 * k : 8 * k + 8, width:] for k in range(3)], axis=1)
    rest = jnp.concatenate([second[:, :width], tail[:, :width]], axis=0)
    return jnp.concatenate([block[0:share], rest], axis=1)


def partial_sum(values):
    return jnp.sum(values.reshape(-1, 8, values.shape[-1]), axis=0)


def fold(values):
    total = jnp.sum(values, axis=0, keepdims=True)
    return total[:, :C_MID] + total[:, C_MID:]


def spread(first, second, out):
    sums = jnp.concatenate([first, second], axis=0)
    out[...] = jnp.broadcast_to(sums[None], out.shape)


def twice(row):
    return jnp.concatenate([row, row], axis=1)


def tiles(rows):
    return range(0, rows, TILE)


def emit_taps(taps, masks, evens, odds, tile_of):
    rows = masks.shape[1]
    kept = taps.shape[0]
    for r in tiles(rows):
        even, odd = tile_of(r)
        evens[r : r + TILE] = even
        odds[8 + r : 8 + r + TILE] = odd
        if r == 0:
            evens[rows : rows + 1] = even[0:1]
        if r + TILE == rows:
            odds[7:8] = odd[TILE - 1 : TILE]
        if r < kept:
            taps[r : r + TILE, 128:256] = even.astype(BF16)
            taps[r : r + TILE, 256:384] = odd.astype(BF16)
    for r in tiles(kept):
        span = slice(r, r + TILE)
        before = odds[7 + r : 7 + r + TILE] * masks[0, span]
        after = evens[1 + r : 1 + r + TILE] * masks[1, span]
        taps[span, 0:128] = before.astype(BF16)
        taps[span, 384:512] = after.astype(BF16)


def halves_of(value):
    return value[:, :C_MID], value[:, C_MID:]


def add_sums(acc, first, second):
    acc[0] += first
    acc[1] += second


def side_scratch(rows):
    return [pltpu.VMEM((rows + 8, LANES), F32)] * (2 * SIDES)


def stats_of(out, mels, rows, half, acc):
    first = jnp.zeros((8, BOTH), F32)
    second = jnp.zeros((8, BOTH), F32)
    for k in range(mels):
        for r in range(0, half, 8):
            value = out[k * rows + r : k * rows + r + 8]
            first += value
            second += value * value
    add_sums(acc, first, second)


def normed_sum(with_half_lifted, plain, gain, shift):
    return (2.0 * with_half_lifted - shift * plain) / gain


def stat_sums(stats):
    return jnp.sum(stats[...], axis=0)


def norm_terms(sums, count):
    mean = sums[0:1] / count
    rstd = lax.rsqrt(sums[1:2] / count - mean * mean + EPS)
    return mean, rstd


def dot_rows(first, second):
    return lax.dot_general(
        first, second, (((0,), (0,)), ((), ())), preferred_element_type=F32
    )


def ring_slot(ring, m):
    return ring[m % (len(ring) - 1)] if 0 <= m < MEL else ring[-1]


def stack(ring, mels, rows, lanes=slice(None)):
    return jnp.concatenate([ring_slot(ring, m)[0:rows, lanes] for m in mels], axis=0)


def ring_scratch(slots, rows):
    return [pltpu.VMEM((rows, WIDE), BF16)] * slots


def clear_ends(taps):
    blank = jnp.zeros(taps.shape[1:], BF16)
    taps[0] = blank
    taps[taps.shape[0] - 1] = blank


def setup_body(k1, k2, ga, sa, gb, sb, x_head, x_tail, c_head, c_tail, w_out, up, down):
    share = k1.shape[0]
    copies = w_out.shape[0]
    first = lax.broadcasted_iota(jnp.int32, (share, share), 0)
    second = lax.broadcasted_iota(jnp.int32, (share, share), 1)
    columns = [k1[...].astype(F32), k2[...].astype(F32)]
    for vector in (ga, sa, gb, sb):
        wide = jnp.broadcast_to(vector[...].astype(F32), (share, share))
        columns.append(jnp.sum(jnp.where(first == second, wide, 0.0), axis=1, keepdims=True))
    chunk = pack(jnp.concatenate(columns, axis=1), w_out.shape[1]).astype(BF16)
    for i in range(copies):
        w_out[i] = chunk
    row = lax.broadcasted_iota(jnp.int32, (8, x_head.shape[1]), 0)
    xt = x_tail[...].astype(F32)
    ct = c_tail[...].astype(F32)
    up[...] = jnp.where(
        row < 4, pltpu.roll(xt[8:16], 4, 0), jnp.where(row == 4, ct[15:16], 0.0)
    ).astype(BF16)
    xh = x_head[...].astype(F32)
    ch = c_head[...].astype(F32)
    down[...] = jnp.where(row < 4, xh[0:8], jnp.where(row == 4, ch[0:1], 0.0)).astype(BF16)


def setup(k1t, k2t, vectors, features, cotangent, copies):
    frames, wide = features.shape
    halves = cotangent.shape[0]
    share = k1t.shape[0]
    w = (copies, packed_rows(share, k1t.shape[1] + k2t.shape[1] + 4), LANES)
    whole = lambda shape: pl.BlockSpec(shape, lambda i: (0,) * len(shape))
    outs = [like(w, BF16), like((8, wide), BF16), like((8, wide), BF16)]
    return call(
        setup_body,
        (k1t, k2t, *vectors, features, features, cotangent, cotangent),
        outs,
        limit=56,
        in_specs=[
            whole(k1t.shape),
            whole(k2t.shape),
            *[whole((1, share))] * 4,
            pl.BlockSpec((16, wide), lambda i: (0, 0)),
            pl.BlockSpec((16, wide), lambda i: (frames // 16 - 1, 0)),
            pl.BlockSpec((16, wide), lambda i: (0, 0)),
            pl.BlockSpec((16, wide), lambda i: (halves // 16 - 1, 0)),
        ],
        out_specs=[whole(o.shape) for o in outs],
        grid=(1,),
    )


def emit_masks(copies, clips, masks):
    rows = masks.shape[1]
    half = rows - TAIL
    frames = 2 * half
    start = lax.axis_index(AXES) * frames
    place = lax.broadcasted_iota(jnp.int32, (rows, clips.shape[1]), 0)
    pair = jnp.where(place >= half + TAIL // 2, place - rows, place)
    frame = start + 2 * pair
    starts = jnp.broadcast_to(clips[...], (rows, clips.shape[1]))
    for slot, shift in ((0, 0), (1, 2)):
        hit = (frame + shift == starts) | (frame + shift >= frames * copies)
        begins = jnp.max(jnp.where(hit, 1.0, 0.0), axis=1, keepdims=True)
        masks[slot] = jnp.broadcast_to(1.0 - begins, (rows, LANES))


def split_bins(parts):
    low = lax.broadcasted_iota(jnp.int32, parts[0].shape, 1) < C_IN
    first, second = [], []
    for here, there in (parts[0:2], parts[2:4]):
        first.append(jnp.where(low, here, pltpu.roll(there, C_IN, 1)))
        second.append(jnp.where(low, pltpu.roll(here, C_IN, 1), there))
    return jnp.concatenate(first + second, axis=1)


def near_bins(taps, pairs, rows):
    left, mid, right = [
        jnp.concatenate([taps[1 + j + k, 0:rows] for j in pairs], axis=0) for k in (-1, 0, 1)
    ]
    first = jnp.concatenate([left[:, BOTH:], mid], axis=1)
    second = jnp.concatenate([mid, right[:, :BOTH]], axis=1)
    return jnp.concatenate([first, second], axis=0)


def taps_one_emitter(x, up, down, masks, taps, frames):
    rows = masks.shape[1]
    half = rows - TAIL
    clear_ends(taps)
    row = lax.broadcasted_iota(jnp.int32, (8, LANES), 0)
    lead = 24
    own = 2 * half
    for held in frames:
        held[0:16] = jnp.zeros((16, LANES), F32)
        held[lead + own + 8 : lead + own + 24] = jnp.zeros((16, LANES), F32)

    def pair(j):
        held = frames[j % len(frames)]
        lanes = slice(j * LANES, (j + 1) * LANES)
        u = up[:, lanes].astype(F32)
        d = down[:, lanes].astype(F32)
        held[lead - 8 : lead] = jnp.where(row >= 4, pltpu.roll(u, 4, 0), 0.0)
        held[lead + own : lead + own + 8] = jnp.where(row < 4, d, 0.0)
        for r in tiles(own):
            held[lead + r : lead + r + TILE] = x[r : r + TILE, lanes].astype(F32)

        def pick(first, count, shift):
            return held[pl.ds(lead + 2 * first + shift, count, stride=2), :]

        for r in tiles(rows):
            parts = []
            for shift in (-1, 0, 1, 2):
                if r < half:
                    parts.append(pick(r, TILE, shift))
                else:
                    parts.append(
                        jnp.concatenate([pick(half, 8, shift), pick(-8, 8, shift)], axis=0)
                    )
            span = slice(r, r + TILE)
            parts[0] = parts[0] * masks[0, span]
            parts[3] = parts[3] * masks[1, span]
            taps[1 + j, span, :] = split_bins(parts).astype(BF16)

    return pair


def conv_one_body(row_count, features, up, down, clips_in, wg,
                  pre, stats, taps, masks, k1_out, k2_out, vec_out, weight_two,
                  kf, weight, acc, x, clips, sems, clip_sem, *frames):
    clip_copy = pltpu.make_async_copy(clips_in, clips, clip_sem)
    clip_copy.start()
    wide = x.shape[1] // sems.shape[0]
    fetch = []
    for k in range(sems.shape[0]):
        lanes = pl.ds(k * wide, wide)
        fetch.append(pltpu.make_async_copy(features.at[:, lanes], x.at[:, lanes], sems.at[k]))
        fetch[k].start()
    clip_copy.wait()
    emit_masks(wg.shape[0], clips, masks)
    emit_pair = taps_one_emitter(x, up, down, masks, taps, frames)
    rows = taps.shape[1]
    half = rows - TAIL
    pairs = 2
    rows_one = 9 * C_IN // row_count
    rows_two = 9 * C_MID // row_count
    grps = wg.shape[0] // row_count
    share = C_MID // grps
    for r in range(row_count):
        shard = [
            unpack(wg[g * row_count + r].astype(F32), share, rows_one + rows_two + 4)
            for g in range(grps)
        ]
        shard = jnp.concatenate(shard, axis=0).T
        kf[rows_one * r : rows_one * (r + 1)] = shard[0:rows_one]
        at = 9 * C_IN + rows_two * r
        kf[at : at + rows_two] = shard[rows_one : rows_one + rows_two]
        if r == 0:
            vec_out[...] = shard[rows_one + rows_two : rows_one + rows_two + 4]
    k1_out[...] = kf[0 : 9 * C_IN].astype(BF16)
    k2_out[...] = kf[9 * C_IN :].astype(BF16)
    weight[...] = jnp.zeros(weight.shape, BF16)
    for d in range(3):
        for q in range(4):
            for p in range(2):
                t = q - p
                if 0 <= t < 3:
                    at = d * BOTH + q * C_IN
                    start = (3 * t + d) * C_IN
                    weight[at : at + C_IN, p * 128 : p * 128 + 128] = k1_out[start : start + C_IN]
    acc[...] = jnp.zeros(acc.shape, F32)

    def convolve(c):
        here = range(c * pairs, (c + 1) * pairs)
        out = jnp.dot(near_bins(taps, here, rows), weight[...], preferred_element_type=F32)
        for parity in range(2):
            for q in range(pairs):
                at = (parity * pairs + q) * rows
                pre[2 * (c * pairs + q) + parity] = out[at : at + rows]
        stats_of(out, 2 * pairs, rows, half, acc)

    total = MEL // 2
    for j in range(total):
        if j % (total // len(fetch)) == 0:
            fetch[j // (total // len(fetch))].wait()
        emit_pair(j)
        if j >= pairs and j % pairs == 0:
            convolve(j // pairs - 1)
        if j == 4:
            place_two(k2_out, weight_two)
    convolve(total // pairs - 1)
    spread(fold(acc[0]), fold(acc[1]), stats)


def conv_one(features, up, down, clips, wg, row_count):
    rows = features.shape[0] // 2 + TAIL
    copies = wg.shape[0]
    return call(
        lambda *refs: conv_one_body(row_count, *refs),
        (features, up, down, clips, wg),
        [
            like((MEL, rows, BOTH), F32),
            like((copies, 2, C_MID), F32),
            like((MEL // 2 + 2, rows, WIDE), BF16),
            like((2, rows, LANES), F32),
            like((9 * C_IN, C_MID), BF16),
            like((9 * C_MID, C_MID), BF16),
            like((4, C_MID), F32),
            like((3 * WIDE, BOTH), BF16),
        ],
        [
            pltpu.VMEM((9 * (C_IN + C_MID), C_MID), F32),
            pltpu.VMEM((3 * BOTH, BOTH), BF16),
            pltpu.VMEM((2, 8, BOTH), F32),
            pltpu.VMEM(features.shape, BF16),
            pltpu.VMEM(clips.shape, jnp.int32),
            pltpu.SemaphoreType.DMA((4,)),
            pltpu.SemaphoreType.DMA,
            *[pltpu.VMEM((features.shape[0] + 48, LANES), F32)] * 4,
        ],
        in_specs=[HBM, VMEM, VMEM, HBM, VMEM],
    )


def place_two(k2, weight):
    weight[...] = jnp.zeros(weight.shape, BF16)
    for d in range(3):
        for q in range(4):
            for p in range(2):
                t = q - p
                if 0 <= t < 3:
                    at = d * WIDE + q * 128
                    start = (3 * t + d) * C_MID
                    weight[at : at + 128, p * 128 : p * 128 + 128] = k2[start : start + C_MID]


def place_two_back(k2, weight):
    weight[...] = jnp.zeros(weight.shape, BF16)
    for t in range(3):
        for d in range(3):
            start = (3 * t + d) * C_MID
            turned = (0.5 * k2[start : start + C_MID].astype(F32).T).astype(BF16)
            for p in range(2):
                at = (2 - d) * WIDE + (2 - t + p) * 128
                weight[at : at + 128, p * 128 : p * 128 + 128] = turned


def place_one_back(k1, weight):
    weight[...] = jnp.zeros(weight.shape, BF16)
    for t in range(3):
        for d in range(3):
            start = (3 * t + d) * C_IN
            turned = k1[start : start + C_IN].astype(F32).T.astype(BF16)
            for mo in (1, 2):
                for p in range(2):
                    at = (mo - d + 1) * WIDE + (2 - t + p) * 128
                    to = p * 128 + (mo - 1) * 64
                    weight[at : at + 128, to : to + 64] = turned


def conv_two_body(count, pre_one, stats_one, vec, masks, k2, weight,
                  pre, stats, taps, sums_out, weight_back, acc, *sides):
    rows = masks.shape[1]
    half = rows - TAIL
    mels = 2
    sums = stat_sums(stats_one)
    sums_out[...] = sums
    mean, rstd = norm_terms(sums, count)
    scale = 0.5 * vec[0:1] * rstd
    shift = twice(0.5 * vec[1:2] - mean * scale)
    scale = twice(scale)
    clear_ends(taps)
    acc[...] = jnp.zeros(acc.shape, F32)

    def activate(m):
        def tile(r):
            h = pre_one[m, r : r + TILE] * scale + shift
            return halves_of(h + h * jnp.tanh(h))

        emit_taps(taps.at[1 + m], masks, sides[m % SIDES], sides[SIDES + m % SIDES], tile)

    def convolve(c):
        lhs = [taps[c * mels + d : (c + 1) * mels + d].reshape(mels * rows, WIDE) for d in range(3)]
        out = jnp.dot(jnp.concatenate(lhs, axis=1), weight[...], preferred_element_type=F32)
        pre[c * mels : (c + 1) * mels] = out.reshape(mels, rows, BOTH)
        stats_of(out, mels, rows, half, acc)

    for m in range(MEL):
        activate(m)
        if m >= mels and m % mels == 0:
            convolve(m // mels - 1)
        if m == 8:
            place_two_back(k2, weight_back)
    convolve(MEL // mels - 1)
    spread(fold(acc[0]), fold(acc[1]), stats)


def conv_two(pre_one, stats_one, vec, masks, k2, weight, count):
    copies = stats_one.shape[0]
    rows = masks.shape[1]
    return call(
        lambda *refs: conv_two_body(count, *refs),
        (pre_one, stats_one, vec, masks, k2, weight),
        [
            like((MEL, rows, BOTH), F32),
            like((copies, 2, C_MID), F32),
            like((MEL + 2, rows, WIDE), BF16),
            like((2, C_MID), F32),
            like((3 * WIDE, BOTH), BF16),
        ],
        [pltpu.VMEM((2, 8, BOTH), F32), *side_scratch(rows)],
    )


def norm_two_body(count, pre, stats_two, vec, cot, up, down, pooled, lift, back_stats, sums_out, acc):
    half = cot.shape[0]
    sums = stat_sums(stats_two)
    sums_out[...] = sums
    mean, rstd = norm_terms(sums, count)
    scale = 0.5 * vec[2:3] * rstd
    shift = 0.5 * vec[3:4] - mean * scale
    acc[...] = jnp.zeros(acc.shape, F32)
    row = lax.broadcasted_iota(jnp.int32, (TAIL, LANES), 0)

    factor = 0.125 * vec[2:3] * rstd

    def pair(j):
        lanes = pl.ds(pl.multiple_of(j * LANES, LANES), LANES)
        u = up[:, lanes].astype(F32)
        d = down[:, lanes].astype(F32)
        first = jnp.zeros((8, LANES), F32)
        second = jnp.zeros((8, LANES), F32)
        for r in tiles(half + TAIL):
            span = slice(r, r + TILE)
            if r < half:
                grad = cot[span, lanes].astype(F32) * factor
            else:
                grad = jnp.where(row == 0, d[4:5], jnp.where(row == TAIL - 1, u[4:5], 0.0)) * factor
            total = jnp.zeros((TILE, LANES), F32)
            for m in (2 * j, 2 * j + 1):
                for p in range(2):
                    side = slice(p * C_MID, (p + 1) * C_MID)
                    value = pre[m, span, side]
                    h = value * scale + shift
                    th = jnp.tanh(h)
                    one = 1.0 + th
                    silu = h * one
                    gl = grad * (one + (silu - silu * th))
                    lift[m, span, side] = gl
                    if r < half:
                        total += silu
                        first += partial_sum(gl)
                        second += partial_sum(gl * h)
            if r < half:
                pooled[span, lanes] = (total * 0.25).astype(BF16)
        add_sums(acc, first, second)

    def four_pairs(i, carry):
        for k in range(4):
            pair(4 * i + k)
        return carry

    lax.fori_loop(0, MEL // 8, four_pairs, 0)
    first, second = [jnp.sum(acc[k], axis=0, keepdims=True) for k in range(2)]
    scaled = vec[2:3] * rstd
    first = first / scaled
    spread(first, normed_sum(second / scaled, first, vec[2:3], vec[3:4]), back_stats)


def norm_two(pre, stats_two, vec, cot, up, down, count):
    copies = stats_two.shape[0]
    half, wide = cot.shape
    return call(
        lambda *refs: norm_two_body(count, *refs),
        (pre, stats_two, vec, cot, up, down),
        [
            like((half, wide), BF16),
            like((MEL, half + TAIL, BOTH), F32),
            like((copies, 2, C_MID), F32),
            like((2, C_MID), F32),
        ],
        [pltpu.VMEM((2, 8, LANES), F32)],
    )


def grad_terms(sums, back, gain, count):
    mean, rstd = norm_terms(sums, count)
    a = gain * rstd
    b = -a * rstd * (back[1:2] / count)
    c = -a * (back[0:1] / count) - b * mean
    return twice(a), twice(b), twice(c)


def back_two_body(count, lift, pre_two, sums_two, back_stats, vec, masks, weight, pre_one, sums_one,
                  taps_a, lift_one, two, back_out, sums_out, acc, acc_two, turned, *buffers):
    sides, taps = buffers[: 2 * SIDES], buffers[2 * SIDES :]
    rows = masks.shape[1]
    half = rows - TAIL
    mels = 1
    wide_mels = 4
    back = stat_sums(back_stats)
    sums_out[...] = back
    _, b, c = grad_terms(sums_two[...], back, vec[2:3], count)
    mean, rstd = norm_terms(sums_one[...], count)
    scale = 0.5 * vec[0:1] * rstd
    shift = twice(0.5 * vec[1:2] - mean * scale)
    scale = twice(scale)
    taps[-1][...] = jnp.zeros(taps[-1].shape, BF16)
    acc[...] = jnp.zeros(acc.shape, F32)

    def lower(m):
        def tile(r):
            span = slice(r, r + TILE)
            return halves_of(lift[m, span] + (pre_two[m, span] * b + c))

        emit_taps(ring_slot(taps, m), masks, sides[m % SIDES], sides[SIDES + m % SIDES], tile)

    def convolve(k):
        lhs = [ring_slot(taps, k + d - 1)[...] for d in range(3)]
        out = jnp.dot(jnp.concatenate(lhs, axis=1), weight[...], preferred_element_type=F32)
        first = jnp.zeros((8, BOTH), F32)
        second = jnp.zeros((8, BOTH), F32)
        for i in range(mels):
            m = k * mels + i
            for r in range(0, rows, 8):
                span = slice(r, r + 8)
                h = pre_one[m, span] * scale + shift
                th = jnp.tanh(h)
                one = 1.0 + th
                silu = h * one
                gl = out[i * rows + r : i * rows + r + 8] * (one + (silu - silu * th))
                lift_one[m, span] = gl
                if r < half:
                    first += gl
                    second += gl * h
        add_sums(acc, first, second)

    def correlate(k):
        here = range(k * wide_mels, (k + 1) * wide_mels)
        turned[...] = stack(taps, here, half, slice(128, 384)).T
        for d in range(3):
            first = here[0] + d
            near = taps_a[first : first + wide_mels, 0:half].reshape(wide_mels * half, WIDE)
            total = jnp.dot(turned[...], near, preferred_element_type=F32)
            lanes = slice(d * WIDE, (d + 1) * WIDE)
            if k == 0:
                acc_two[:, lanes] = total
            else:
                acc_two[:, lanes] += total

    for k in range(MEL // mels + 1):
        for m in range(k * mels, (k + 1) * mels):
            if m < MEL:
                lower(m)
        if k > 0:
            convolve(k - 1)
            if k * mels % wide_mels == 0:
                correlate(k * mels // wide_mels - 1)
    plain = fold(acc[0])
    spread(plain, normed_sum(fold(acc[1]), plain, vec[0:1], vec[1:2]), back_out)
    for t in range(3):
        for d in range(3):
            at = d * WIDE + t * 128
            to = (3 * t + d) * 128
            two[:, to : to + 128] = (
                acc_two[0:C_MID, at : at + 128] + acc_two[C_MID:BOTH, at + 128 : at + 256]
            )


def back_two(lift, pre_two, sums_two, back_stats, vec, masks, weight, pre_one, sums_one, taps_a, count):
    copies = back_stats.shape[0]
    rows = masks.shape[1]
    return call(
        lambda *refs: back_two_body(count, *refs),
        (lift, pre_two, sums_two, back_stats, vec, masks, weight, pre_one, sums_one, taps_a),
        [
            like((MEL, rows, BOTH), F32),
            like((C_MID, 9 * C_MID), F32),
            like((copies, 2, C_MID), F32),
            like((2, C_MID), F32),
        ],
        [
            pltpu.VMEM((2, 8, BOTH), F32),
            pltpu.VMEM((BOTH, 3 * WIDE), F32),
            pltpu.VMEM((BOTH, 4 * (rows - TAIL)), BF16),
            *side_scratch(rows),
            *ring_scratch(17, rows),
        ],

        input_output_aliases={0: 0},
    )


def scatter_blocks(out, parts, row_count):
    copies = out.shape[0]
    grps = copies // row_count
    share = C_MID // grps
    turned = [part.T for part in parts]
    sizes = [part.shape[1] // row_count for part in parts]
    for r in range(row_count):
        rows = [t[n * r : n * (r + 1)] for t, n in zip(turned, sizes)]
        back = jnp.concatenate(rows, axis=0).T
        for g in range(grps):
            block = back[share * g : share * (g + 1)]
            out[g * row_count + r] = pack(block, out.shape[1]).astype(BF16)


def kernel_one_step(taps_x, grads, acc, k, pairs):
    half = grads.shape[1] - TAIL
    here = range(k * pairs, (k + 1) * pairs)
    mels = [2 * j + parity for parity in range(2) for j in here]
    chosen = jnp.concatenate([grads[m, 0:half] for m in mels], axis=0)
    total = dot_rows(chosen, near_bins(taps_x, here, half))
    if k == 0:
        acc[...] = total
    else:
        acc[...] += total


def kernel_one_sums(acc):
    pieces = []
    for t in range(3):
        for d in range(3):
            total = jnp.zeros((C_MID, C_IN), F32)
            for p in range(2):
                at = d * BOTH + (t + p) * C_IN
                total += acc[p * C_MID : (p + 1) * C_MID, at : at + C_IN]
            pieces.append(total)
    return jnp.concatenate(pieces, axis=1)


STORED = 640


def grads_body(count, row_count, lift, pre_one, sums_one, back_stats, vec, masks, taps_x, two,
               stored, blocks, sums_out, acc_one, grads, low_masks, sems):
    back = stat_sums(back_stats)
    sums_out[...] = back
    a, b, c = grad_terms(sums_one[...], back, vec[0:1], count)
    rows = masks.shape[1]
    for slot in range(2):
        low_masks[:, slot * LANES : (slot + 1) * LANES] = masks[slot].astype(BF16)
    copies = [pltpu.make_async_copy(low_masks, stored.at[MEL], sems.at[sems.shape[0] - 1])]
    copies[0].start()

    def lower(m):
        for r in tiles(rows):
            span = slice(r, r + TILE)
            grads[m, span] = (lift[m, span] * a + (pre_one[m, span] * b + c)).astype(BF16)

    pairs = 2
    mels = 2 * pairs
    steps = MEL // mels
    for k in range(steps + 1):
        if k < steps:
            for m in range(mels * k, mels * (k + 1)):
                lower(m)
            here = pl.ds(mels * k, mels)
            copies.append(pltpu.make_async_copy(grads.at[here], stored.at[here], sems.at[k]))
            copies[-1].start()
        if k > 0:
            kernel_one_step(taps_x, grads, acc_one, k - 1, pairs)
    scatter_blocks(blocks, [kernel_one_sums(acc_one), two[...]], row_count)
    for copy in copies:
        copy.wait()


def kernel_grads(lift, pre_one, sums_one, back_stats, vec, masks, taps_x, two, row_count, count):
    copies = back_stats.shape[0]
    rows = masks.shape[1]
    share = C_MID * row_count // copies
    block_rows = packed_rows(share, 9 * (C_IN + C_MID) // row_count)
    return call(
        lambda *refs: grads_body(count, row_count, *refs),
        (lift, pre_one, sums_one, back_stats, vec, masks, taps_x, two),
        [
            like((STORED, rows, BOTH), BF16),
            like((copies, block_rows, LANES), BF16),
            like((2, C_MID), F32),
        ],
        [
            pltpu.VMEM((BOTH, 3 * BOTH), F32),
            pltpu.VMEM((MEL, rows, BOTH), BF16),
            pltpu.VMEM((rows, BOTH), BF16),
            pltpu.SemaphoreType.DMA((9,)),
        ],
        out_specs=[HBM, VMEM, VMEM],
    )


def features_body(stored, k1, out, grads, low_masks, masks, weight, woven, sems, out_sems, *buffers):
    sides, taps = buffers[: 2 * SIDES], buffers[2 * SIDES :]
    pairs = 4
    rows = grads.shape[1]
    half = rows - TAIL
    groups = sems.shape[0] - 1
    group = MEL // groups
    mask_copy = pltpu.make_async_copy(stored.at[MEL], low_masks, sems.at[groups])
    mask_copy.start()
    fetch = []
    for k in range(groups):
        here = pl.ds(k * group, group)
        fetch.append(pltpu.make_async_copy(stored.at[here], grads.at[here], sems.at[k]))
        fetch[k].start()
    taps[-1][...] = jnp.zeros(taps[-1].shape, BF16)
    place_one_back(k1, weight)
    mask_copy.wait()
    for slot in range(2):
        masks[slot] = low_masks[:, slot * LANES : (slot + 1) * LANES].astype(F32)

    def emit(m):
        def tile(r):
            return halves_of(grads[m, r : r + TILE].astype(F32))

        emit_taps(ring_slot(taps, m), masks, sides[m % SIDES], sides[SIDES + m % SIDES], tile)

    copies = []
    slots = woven.shape[0]

    def convolve(k):
        near = [
            stack(taps, [2 * (k * pairs + q) + i - 1 for q in range(pairs)], half) for i in range(4)
        ]
        part = jnp.dot(jnp.concatenate(near, axis=1), weight[...], preferred_element_type=F32)
        for q in range(pairs):
            j = k * pairs + q
            b = j % slots
            here = slice(q * half, (q + 1) * half)
            if j >= slots:
                copies[j - slots].wait()
            woven[b, pl.ds(0, half, stride=2), :] = part[here, 0:128]
            woven[b, pl.ds(1, half, stride=2), :] = part[here, 128:256]
            copy = pltpu.make_async_copy(
                woven.at[b], out.at[:, pl.ds(j * LANES, LANES)], out_sems.at[b]
            )
            copy.start()
            copies.append(copy)

    for m in range(MEL):
        if m % group == 0:
            fetch[m // group].wait()
        emit(m)
        if m > 0 and m % (2 * pairs) == 0:
            convolve(m // (2 * pairs) - 1)
    convolve(MEL // (2 * pairs) - 1)
    for copy in copies[-slots:]:
        copy.wait()


def features_grad(stored, k1):
    rows = stored.shape[1]
    half = rows - TAIL
    return call(
        features_body,
        (stored, k1),
        [like((2 * half, MEL * C_IN), F32)],
        [
            pltpu.VMEM((MEL, rows, BOTH), BF16),
            pltpu.VMEM((rows, BOTH), BF16),
            pltpu.VMEM((2, rows, LANES), F32),
            pltpu.VMEM((4 * WIDE, BOTH), BF16),
            pltpu.VMEM((8, 2 * half, LANES), F32),
            pltpu.SemaphoreType.DMA((9,)),
            pltpu.SemaphoreType.DMA((8,)),
            *side_scratch(rows),
            *ring_scratch(27, half),
        ],
        limit=24,
        in_specs=[HBM, VMEM],
        out_specs=[ANY],
    )[0]


def finish_body(got, back_one_sums, back_two_sums, own_one, own_two, ga, sa, gb, sb):
    size = own_one.shape[1]
    share = own_one.shape[0]
    total = jnp.sum(got[...].astype(F32), axis=0)
    total = unpack(total, share, size + own_two.shape[1])
    own_one[...] = total[:, 0:size]
    own_two[...] = total[:, size:]
    lane = lax.broadcasted_iota(jnp.int32, (share, C_MID), 1)
    row = lax.broadcasted_iota(jnp.int32, (share, C_MID), 0)
    chosen = lane == lax.axis_index("grp") * share + row
    first = lax.broadcasted_iota(jnp.int32, (share, share), 0)
    second = lax.broadcasted_iota(jnp.int32, (share, share), 1)
    for out, sums, k in (
        (ga, back_one_sums, 1), (sa, back_one_sums, 0), (gb, back_two_sums, 1), (sb, back_two_sums, 0)
    ):
        wide = jnp.broadcast_to(sums[k : k + 1], (share, C_MID))
        column = jnp.sum(jnp.where(chosen, wide, 0.0), axis=1, keepdims=True)
        wide = jnp.broadcast_to(column, (share, share))
        out[...] = jnp.sum(jnp.where(first == second, wide, 0.0), axis=0, keepdims=True)


def finish(got, back_one_sums, back_two_sums, share, rows_one, rows_two):
    shapes = [(share, rows_one), (share, rows_two)] + [(1, share)] * 4
    return call(
        finish_body,
        (got, back_one_sums, back_two_sums),
        [like(s, F32) for s in shapes],
    )


def exchange(blocks):
    return lax.all_to_all(blocks, AXES, 0, 0, tiled=True)


def shards(
    features, clip_starts, kernel_one, kernel_two, gain_one, shift_one, gain_two, shift_two, cotangent
):
    frames = features.shape[0]
    copies = lax.axis_size(AXES)
    row_count = lax.axis_size("row")
    count = float(frames * MEL * copies)
    rows_one, rows_two = kernel_one.shape[0], kernel_two.shape[0]
    share = kernel_one.shape[1]
    vectors = [v.reshape(1, share) for v in (gain_one, shift_one, gain_two, shift_two)]
    clips = clip_starts.reshape(1, -1)
    weights, up, down = setup(kernel_one.T, kernel_two.T, vectors, features, cotangent, copies)
    ends = copies - 1
    up = lax.ppermute(up, AXES, [(i, i + 1) for i in range(ends)])
    down = lax.ppermute(down, AXES, [(i + 1, i) for i in range(ends)])
    weights = exchange(weights)
    pre_one, stats, taps_x, masks, k1, k2, vec, weight = conv_one(
        features, up, down, clips, weights, row_count
    )
    stats = exchange(stats)
    pre_two, stats, taps_a, sums_one, weight_back = conv_two(
        pre_one, stats, vec, masks, k2, weight, count
    )
    stats = exchange(stats)
    block_out, lift, stats, sums_two = norm_two(pre_two, stats, vec, cotangent, up, down, count)
    stats = exchange(stats)
    lift, two, stats, back_two_sums = back_two(
        lift, pre_two, sums_two, stats, vec, masks, weight_back, pre_one, sums_one, taps_a, count
    )
    stats = exchange(stats)
    stored, blocks, back_one_sums = kernel_grads(
        lift, pre_one, sums_one, stats, vec, masks, taps_x, two, row_count, count
    )
    blocks = exchange(blocks)
    grad_features = features_grad(stored, k1)
    own_one, own_two, ga, sa, gb, sb = finish(
        blocks, back_one_sums, back_two_sums, share, rows_one, rows_two
    )
    return (
        block_out,
        grad_features,
        own_one.T,
        own_two.T,
        ga.reshape(share),
        sa.reshape(share),
        gb.reshape(share),
        sb.reshape(share),
    )


def solution(mesh):
    placed = (
        P(AXES, None), P(), P("row", "grp"), P("row", "grp"),
        P("grp"), P("grp"), P("grp"), P("grp"), P(AXES, None),
    )
    return jax.shard_map(
        shards,
        mesh=mesh,
        in_specs=placed,
        out_specs=(
            P(AXES, None), P(AXES, None), P("row", "grp"), P("row", "grp"),
            P("grp"), P("grp"), P("grp"), P("grp"),
        ),
        check_vma=False,
    )
```

```python
import jax
import jax.numpy as jnp
from jax import lax
from jax.experimental import pallas as pl
from jax.experimental.pallas import tpu as pltpu
from jax.sharding import PartitionSpec as P

MEL = 32
C_IN = 64
C_MID = 128
EPS = 1e-05
AXES = ("grp", "row")
LANES = 128
TAIL = 16
WIDE = 4 * LANES
BOTH = 2 * C_MID
F32 = jnp.float32
BF16 = jnp.bfloat16
TILE = 16
SIDES = 4
MIB = 2**20

VMEM = pl.BlockSpec(memory_space=pltpu.VMEM)
ANY = pl.BlockSpec(memory_space=pl.ANY)
HBM = pl.BlockSpec(memory_space=pltpu.HBM)


def like(shape, dtype):
    return jax.ShapeDtypeStruct(shape, dtype)


def call(body, args, outs, scratch=(), limit=14, in_specs=None, out_specs=None, **more):
    return pl.pallas_call(
        body,
        in_specs=in_specs or [VMEM] * len(args),
        out_specs=out_specs or [VMEM] * len(outs),
        out_shape=outs,
        scratch_shapes=list(scratch),
        compiler_params=pltpu.CompilerParams(vmem_limit_bytes=limit * MIB),
        cost_estimate=pl.CostEstimate(flops=5 * 10**9, bytes_accessed=0, transcendentals=0),
        **more,
    )(*args)


def padded(size):
    return -(-size // LANES) * LANES


def packed_rows(share, wide):
    rest = wide - LANES
    if rest > 0 and share == 32 and 3 * (LANES - rest) >= rest:
        return share + 24
    return share * (padded(wide) // LANES)


def pack(block, rows):
    share, wide = block.shape
    if rows % share == 0:
        block = jnp.concatenate([block, jnp.zeros((share, padded(wide) - wide), F32)], axis=1)
        return jnp.concatenate(
            [block[:, at : at + LANES] for at in range(0, block.shape[1], LANES)], axis=0
        )
    return jnp.concatenate([block[:, :LANES], pack_rest(block[:, LANES:])], axis=0)


def pack_rest(rest):
    room = LANES - rest.shape[1]
    tail = jnp.concatenate(
        [rest[24:32], jnp.zeros((8, 3 * room - rest.shape[1]), F32)], axis=1
    )
    tail = jnp.concatenate([tail[:, k * room : (k + 1) * room] for k in range(3)], axis=0)
    return jnp.concatenate([rest[0:24], tail], axis=1)


def unpack(block, share, wide):
    rows = block.shape[0]
    if rows % share == 0:
        parts = [block[at : at + share] for at in range(0, rows, share)]
        return jnp.concatenate(parts, axis=1)[:, 0:wide]
    width = wide - LANES
    second = block[share:]
    tail = jnp.concatenate([second[8 * k : 8 * k + 8, width:] for k in range(3)], axis=1)
    rest = jnp.concatenate([second[:, :width], tail[:, :width]], axis=0)
    return jnp.concatenate([block[0:share], rest], axis=1)


def partial_sum(values):
    return jnp.sum(values.reshape(-1, 8, values.shape[-1]), axis=0)


def fold(values):
    total = jnp.sum(values, axis=0, keepdims=True)
    return total[:, :C_MID] + total[:, C_MID:]


def spread(first, second, out):
    sums = jnp.concatenate([first, second], axis=0)
    out[...] = jnp.broadcast_to(sums[None], out.shape)


def twice(row):
    return jnp.concatenate([row, row], axis=1)


def tiles(rows):
    return range(0, rows, TILE)


def emit_taps(taps, masks, evens, odds, tile_of):
    rows = masks.shape[1]
    kept = taps.shape[0]
    for r in tiles(rows):
        even, odd = tile_of(r)
        evens[r : r + TILE] = even
        odds[8 + r : 8 + r + TILE] = odd
        if r == 0:
            evens[rows : rows + 1] = even[0:1]
        if r + TILE == rows:
            odds[7:8] = odd[TILE - 1 : TILE]
        if r < kept:
            taps[r : r + TILE, 128:256] = even.astype(BF16)
            taps[r : r + TILE, 256:384] = odd.astype(BF16)
    for r in tiles(kept):
        span = slice(r, r + TILE)
        before = odds[7 + r : 7 + r + TILE] * masks[0, span]
        after = evens[1 + r : 1 + r + TILE] * masks[1, span]
        taps[span, 0:128] = before.astype(BF16)
        taps[span, 384:512] = after.astype(BF16)


def halves_of(value):
    return value[:, :C_MID], value[:, C_MID:]


def add_sums(acc, first, second):
    acc[0] += first
    acc[1] += second


def side_scratch(rows):
    return [pltpu.VMEM((rows + 8, LANES), F32)] * (2 * SIDES)


def stats_of(out, mels, rows, half, acc):
    first = jnp.zeros((8, BOTH), F32)
    second = jnp.zeros((8, BOTH), F32)
    for k in range(mels):
        for r in range(0, half, 8):
            value = out[k * rows + r : k * rows + r + 8]
            first += value
            second += value * value
    add_sums(acc, first, second)


def normed_sum(with_half_lifted, plain, gain, shift):
    return (2.0 * with_half_lifted - shift * plain) / gain


def stat_sums(stats):
    return jnp.sum(stats[...], axis=0)


def norm_terms(sums, count):
    mean = sums[0:1] / count
    rstd = lax.rsqrt(sums[1:2] / count - mean * mean + EPS)
    return mean, rstd


def dot_rows(first, second):
    return lax.dot_general(
        first, second, (((0,), (0,)), ((), ())), preferred_element_type=F32
    )


def ring_slot(ring, m):
    return ring[m % (len(ring) - 1)] if 0 <= m < MEL else ring[-1]


def stack(ring, mels, rows, lanes=slice(None)):
    return jnp.concatenate([ring_slot(ring, m)[0:rows, lanes] for m in mels], axis=0)


def ring_scratch(slots, rows):
    return [pltpu.VMEM((rows, WIDE), BF16)] * slots


def clear_ends(taps):
    blank = jnp.zeros(taps.shape[1:], BF16)
    taps[0] = blank
    taps[taps.shape[0] - 1] = blank


def setup_body(k1, k2, ga, sa, gb, sb, x_head, x_tail, c_head, c_tail, w_out, up, down):
    share = k1.shape[0]
    copies = w_out.shape[0]
    first = lax.broadcasted_iota(jnp.int32, (share, share), 0)
    second = lax.broadcasted_iota(jnp.int32, (share, share), 1)
    columns = [k1[...].astype(F32), k2[...].astype(F32)]
    for vector in (ga, sa, gb, sb):
        wide = jnp.broadcast_to(vector[...].astype(F32), (share, share))
        columns.append(jnp.sum(jnp.where(first == second, wide, 0.0), axis=1, keepdims=True))
    chunk = pack(jnp.concatenate(columns, axis=1), w_out.shape[1]).astype(BF16)
    for i in range(copies):
        w_out[i] = chunk
    row = lax.broadcasted_iota(jnp.int32, (8, x_head.shape[1]), 0)
    xt = x_tail[...].astype(F32)
    ct = c_tail[...].astype(F32)
    up[...] = jnp.where(
        row < 4, pltpu.roll(xt[8:16], 4, 0), jnp.where(row == 4, ct[15:16], 0.0)
    ).astype(BF16)
    xh = x_head[...].astype(F32)
    ch = c_head[...].astype(F32)
    down[...] = jnp.where(row < 4, xh[0:8], jnp.where(row == 4, ch[0:1], 0.0)).astype(BF16)


def setup(k1t, k2t, vectors, features, cotangent, copies):
    frames, wide = features.shape
    halves = cotangent.shape[0]
    share = k1t.shape[0]
    w = (copies, packed_rows(share, k1t.shape[1] + k2t.shape[1] + 4), LANES)
    whole = lambda shape: pl.BlockSpec(shape, lambda i: (0,) * len(shape))
    outs = [like(w, BF16), like((8, wide), BF16), like((8, wide), BF16)]
    return call(
        setup_body,
        (k1t, k2t, *vectors, features, features, cotangent, cotangent),
        outs,
        limit=56,
        in_specs=[
            whole(k1t.shape),
            whole(k2t.shape),
            *[whole((1, share))] * 4,
            pl.BlockSpec((16, wide), lambda i: (0, 0)),
            pl.BlockSpec((16, wide), lambda i: (frames // 16 - 1, 0)),
            pl.BlockSpec((16, wide), lambda i: (0, 0)),
            pl.BlockSpec((16, wide), lambda i: (halves // 16 - 1, 0)),
        ],
        out_specs=[whole(o.shape) for o in outs],
        grid=(1,),
    )


def emit_masks(copies, clips, masks):
    rows = masks.shape[1]
    half = rows - TAIL
    frames = 2 * half
    start = lax.axis_index(AXES) * frames
    place = lax.broadcasted_iota(jnp.int32, (rows, clips.shape[1]), 0)
    pair = jnp.where(place >= half + TAIL // 2, place - rows, place)
    frame = start + 2 * pair
    starts = jnp.broadcast_to(clips[...], (rows, clips.shape[1]))
    for slot, shift in ((0, 0), (1, 2)):
        hit = (frame + shift == starts) | (frame + shift >= frames * copies)
        begins = jnp.max(jnp.where(hit, 1.0, 0.0), axis=1, keepdims=True)
        masks[slot] = jnp.broadcast_to(1.0 - begins, (rows, LANES))


def split_bins(parts):
    low = lax.broadcasted_iota(jnp.int32, parts[0].shape, 1) < C_IN
    first, second = [], []
    for here, there in (parts[0:2], parts[2:4]):
        first.append(jnp.where(low, here, pltpu.roll(there, C_IN, 1)))
        second.append(jnp.where(low, pltpu.roll(here, C_IN, 1), there))
    return jnp.concatenate(first + second, axis=1)


def near_bins(taps, pairs, rows):
    left, mid, right = [
        jnp.concatenate([taps[1 + j + k, 0:rows] for j in pairs], axis=0) for k in (-1, 0, 1)
    ]
    first = jnp.concatenate([left[:, BOTH:], mid], axis=1)
    second = jnp.concatenate([mid, right[:, :BOTH]], axis=1)
    return jnp.concatenate([first, second], axis=0)


def taps_one_emitter(x, up, down, masks, taps, frames):
    rows = masks.shape[1]
    half = rows - TAIL
    clear_ends(taps)
    row = lax.broadcasted_iota(jnp.int32, (8, LANES), 0)
    lead = 24
    own = 2 * half
    for held in frames:
        held[0:16] = jnp.zeros((16, LANES), F32)
        held[lead + own + 8 : lead + own + 24] = jnp.zeros((16, LANES), F32)

    def pair(j):
        held = frames[j % len(frames)]
        lanes = slice(j * LANES, (j + 1) * LANES)
        u = up[:, lanes].astype(F32)
        d = down[:, lanes].astype(F32)
        held[lead - 8 : lead] = jnp.where(row >= 4, pltpu.roll(u, 4, 0), 0.0)
        held[lead + own : lead + own + 8] = jnp.where(row < 4, d, 0.0)
        for r in tiles(own):
            held[lead + r : lead + r + TILE] = x[r : r + TILE, lanes].astype(F32)

        def pick(first, count, shift):
            return held[pl.ds(lead + 2 * first + shift, count, stride=2), :]

        for r in tiles(rows):
            parts = []
            for shift in (-1, 0, 1, 2):
                if r < half:
                    parts.append(pick(r, TILE, shift))
                else:
                    parts.append(
                        jnp.concatenate([pick(half, 8, shift), pick(-8, 8, shift)], axis=0)
                    )
            span = slice(r, r + TILE)
            parts[0] = parts[0] * masks[0, span]
            parts[3] = parts[3] * masks[1, span]
            taps[1 + j, span, :] = split_bins(parts).astype(BF16)

    return pair


def conv_one_body(row_count, features, up, down, clips_in, wg,
                  pre, stats, taps, masks, k1_out, k2_out, vec_out, weight_two,
                  kf, weight, acc, x, clips, sems, clip_sem, *frames):
    clip_copy = pltpu.make_async_copy(clips_in, clips, clip_sem)
    clip_copy.start()
    wide = x.shape[1] // sems.shape[0]
    fetch = []
    for k in range(sems.shape[0]):
        lanes = pl.ds(k * wide, wide)
        fetch.append(pltpu.make_async_copy(features.at[:, lanes], x.at[:, lanes], sems.at[k]))
        fetch[k].start()
    clip_copy.wait()
    emit_masks(wg.shape[0], clips, masks)
    emit_pair = taps_one_emitter(x, up, down, masks, taps, frames)
    rows = taps.shape[1]
    half = rows - TAIL
    pairs = 2
    rows_one = 9 * C_IN // row_count
    rows_two = 9 * C_MID // row_count
    grps = wg.shape[0] // row_count
    share = C_MID // grps
    for r in range(row_count):
        shard = [
            unpack(wg[g * row_count + r].astype(F32), share, rows_one + rows_two + 4)
            for g in range(grps)
        ]
        shard = jnp.concatenate(shard, axis=0).T
        kf[rows_one * r : rows_one * (r + 1)] = shard[0:rows_one]
        at = 9 * C_IN + rows_two * r
        kf[at : at + rows_two] = shard[rows_one : rows_one + rows_two]
        if r == 0:
            vec_out[...] = shard[rows_one + rows_two : rows_one + rows_two + 4]
    k1_out[...] = kf[0 : 9 * C_IN].astype(BF16)
    k2_out[...] = kf[9 * C_IN :].astype(BF16)
    weight[...] = jnp.zeros(weight.shape, BF16)
    for d in range(3):
        for q in range(4):
            for p in range(2):
                t = q - p
                if 0 <= t < 3:
                    at = d * BOTH + q * C_IN
                    start = (3 * t + d) * C_IN
                    weight[at : at + C_IN, p * 128 : p * 128 + 128] = k1_out[start : start + C_IN]
    acc[...] = jnp.zeros(acc.shape, F32)

    def convolve(c):
        here = range(c * pairs, (c + 1) * pairs)
        out = jnp.dot(near_bins(taps, here, rows), weight[...], preferred_element_type=F32)
        for parity in range(2):
            for q in range(pairs):
                at = (parity * pairs + q) * rows
                pre[2 * (c * pairs + q) + parity] = out[at : at + rows]
        stats_of(out, 2 * pairs, rows, half, acc)

    total = MEL // 2
    for j in range(total):
        if j % (total // len(fetch)) == 0:
            fetch[j // (total // len(fetch))].wait()
        emit_pair(j)
        if j >= pairs and j % pairs == 0:
            convolve(j // pairs - 1)
        if j == 4:
            place_two(k2_out, weight_two)
    convolve(total // pairs - 1)
    spread(fold(acc[0]), fold(acc[1]), stats)


def conv_one(features, up, down, clips, wg, row_count):
    rows = features.shape[0] // 2 + TAIL
    copies = wg.shape[0]
    return call(
        lambda *refs: conv_one_body(row_count, *refs),
        (features, up, down, clips, wg),
        [
            like((MEL, rows, BOTH), F32),
            like((copies, 2, C_MID), F32),
            like((MEL // 2 + 2, rows, WIDE), BF16),
            like((2, rows, LANES), F32),
            like((9 * C_IN, C_MID), BF16),
            like((9 * C_MID, C_MID), BF16),
            like((4, C_MID), F32),
            like((3 * WIDE, BOTH), BF16),
        ],
        [
            pltpu.VMEM((9 * (C_IN + C_MID), C_MID), F32),
            pltpu.VMEM((3 * BOTH, BOTH), BF16),
            pltpu.VMEM((2, 8, BOTH), F32),
            pltpu.VMEM(features.shape, BF16),
            pltpu.VMEM(clips.shape, jnp.int32),
            pltpu.SemaphoreType.DMA((4,)),
            pltpu.SemaphoreType.DMA,
            *[pltpu.VMEM((features.shape[0] + 48, LANES), F32)] * 4,
        ],
        in_specs=[HBM, VMEM, VMEM, HBM, VMEM],
    )


def place_two(k2, weight):
    weight[...] = jnp.zeros(weight.shape, BF16)
    for d in range(3):
        for q in range(4):
            for p in range(2):
                t = q - p
                if 0 <= t < 3:
                    at = d * WIDE + q * 128
                    start = (3 * t + d) * C_MID
                    weight[at : at + 128, p * 128 : p * 128 + 128] = k2[start : start + C_MID]


def place_two_back(k2, weight):
    weight[...] = jnp.zeros(weight.shape, BF16)
    for t in range(3):
        for d in range(3):
            start = (3 * t + d) * C_MID
            turned = (0.5 * k2[start : start + C_MID].astype(F32).T).astype(BF16)
            for p in range(2):
                at = (2 - d) * WIDE + (2 - t + p) * 128
                weight[at : at + 128, p * 128 : p * 128 + 128] = turned


def place_one_back(k1, weight):
    weight[...] = jnp.zeros(weight.shape, BF16)
    for t in range(3):
        for d in range(3):
            start = (3 * t + d) * C_IN
            turned = k1[start : start + C_IN].astype(F32).T.astype(BF16)
            for mo in (1, 2):
                for p in range(2):
                    at = (mo - d + 1) * WIDE + (2 - t + p) * 128
                    to = p * 128 + (mo - 1) * 64
                    weight[at : at + 128, to : to + 64] = turned


def conv_two_body(count, pre_one, stats_one, vec, masks, k2, weight,
                  pre, stats, taps, sums_out, weight_back, acc, *sides):
    rows = masks.shape[1]
    half = rows - TAIL
    mels = 2
    sums = stat_sums(stats_one)
    sums_out[...] = sums
    mean, rstd = norm_terms(sums, count)
    scale = 0.5 * vec[0:1] * rstd
    shift = twice(0.5 * vec[1:2] - mean * scale)
    scale = twice(scale)
    clear_ends(taps)
    acc[...] = jnp.zeros(acc.shape, F32)

    def activate(m):
        def tile(r):
            h = pre_one[m, r : r + TILE] * scale + shift
            return halves_of(h + h * jnp.tanh(h))

        emit_taps(taps.at[1 + m], masks, sides[m % SIDES], sides[SIDES + m % SIDES], tile)

    def convolve(c):
        lhs = [taps[c * mels + d : (c + 1) * mels + d].reshape(mels * rows, WIDE) for d in range(3)]
        out = jnp.dot(jnp.concatenate(lhs, axis=1), weight[...], preferred_element_type=F32)
        pre[c * mels : (c + 1) * mels] = out.reshape(mels, rows, BOTH)
        stats_of(out, mels, rows, half, acc)

    for m in range(MEL):
        activate(m)
        if m >= mels and m % mels == 0:
            convolve(m // mels - 1)
        if m == 8:
            place_two_back(k2, weight_back)
    convolve(MEL // mels - 1)
    spread(fold(acc[0]), fold(acc[1]), stats)


def conv_two(pre_one, stats_one, vec, masks, k2, weight, count):
    copies = stats_one.shape[0]
    rows = masks.shape[1]
    return call(
        lambda *refs: conv_two_body(count, *refs),
        (pre_one, stats_one, vec, masks, k2, weight),
        [
            like((MEL, rows, BOTH), F32),
            like((copies, 2, C_MID), F32),
            like((MEL + 2, rows, WIDE), BF16),
            like((2, C_MID), F32),
            like((3 * WIDE, BOTH), BF16),
        ],
        [pltpu.VMEM((2, 8, BOTH), F32), *side_scratch(rows)],
    )


def norm_two_body(count, pre, stats_two, vec, cot, up, down, pooled, lift, back_stats, sums_out, acc):
    half = cot.shape[0]
    sums = stat_sums(stats_two)
    sums_out[...] = sums
    mean, rstd = norm_terms(sums, count)
    scale = 0.5 * vec[2:3] * rstd
    shift = 0.5 * vec[3:4] - mean * scale
    acc[...] = jnp.zeros(acc.shape, F32)
    row = lax.broadcasted_iota(jnp.int32, (TAIL, LANES), 0)

    factor = 0.125 * vec[2:3] * rstd

    def pair(j):
        lanes = pl.ds(pl.multiple_of(j * LANES, LANES), LANES)
        u = up[:, lanes].astype(F32)
        d = down[:, lanes].astype(F32)
        first = jnp.zeros((8, LANES), F32)
        second = jnp.zeros((8, LANES), F32)
        for r in tiles(half + TAIL):
            span = slice(r, r + TILE)
            if r < half:
                grad = cot[span, lanes].astype(F32) * factor
            else:
                grad = jnp.where(row == 0, d[4:5], jnp.where(row == TAIL - 1, u[4:5], 0.0)) * factor
            total = jnp.zeros((TILE, LANES), F32)
            for m in (2 * j, 2 * j + 1):
                for p in range(2):
                    side = slice(p * C_MID, (p + 1) * C_MID)
                    value = pre[m, span, side]
                    h = value * scale + shift
                    th = jnp.tanh(h)
                    one = 1.0 + th
                    silu = h * one
                    gl = grad * (one + (silu - silu * th))
                    lift[m, span, side] = gl
                    if r < half:
                        total += silu
                        first += partial_sum(gl)
                        second += partial_sum(gl * h)
            if r < half:
                pooled[span, lanes] = (total * 0.25).astype(BF16)
        add_sums(acc, first, second)

    def four_pairs(i, carry):
        for k in range(4):
            pair(4 * i + k)
        return carry

    lax.fori_loop(0, MEL // 8, four_pairs, 0)
    first, second = [jnp.sum(acc[k], axis=0, keepdims=True) for k in range(2)]
    scaled = vec[2:3] * rstd
    first = first / scaled
    spread(first, normed_sum(second / scaled, first, vec[2:3], vec[3:4]), back_stats)


def norm_two(pre, stats_two, vec, cot, up, down, count):
    copies = stats_two.shape[0]
    half, wide = cot.shape
    return call(
        lambda *refs: norm_two_body(count, *refs),
        (pre, stats_two, vec, cot, up, down),
        [
            like((half, wide), BF16),
            like((MEL, half + TAIL, BOTH), F32),
            like((copies, 2, C_MID), F32),
            like((2, C_MID), F32),
        ],
        [pltpu.VMEM((2, 8, LANES), F32)],
    )


def grad_terms(sums, back, gain, count):
    mean, rstd = norm_terms(sums, count)
    a = gain * rstd
    b = -a * rstd * (back[1:2] / count)
    c = -a * (back[0:1] / count) - b * mean
    return twice(a), twice(b), twice(c)


def back_two_body(count, lift, pre_two, sums_two, back_stats, vec, masks, weight, pre_one, sums_one,
                  taps_a, lift_one, two, back_out, sums_out, acc, acc_two, turned, *buffers):
    sides, taps = buffers[: 2 * SIDES], buffers[2 * SIDES :]
    rows = masks.shape[1]
    half = rows - TAIL
    mels = 1
    wide_mels = 4
    back = stat_sums(back_stats)
    sums_out[...] = back
    _, b, c = grad_terms(sums_two[...], back, vec[2:3], count)
    mean, rstd = norm_terms(sums_one[...], count)
    scale = 0.5 * vec[0:1] * rstd
    shift = twice(0.5 * vec[1:2] - mean * scale)
    scale = twice(scale)
    taps[-1][...] = jnp.zeros(taps[-1].shape, BF16)
    acc[...] = jnp.zeros(acc.shape, F32)

    def lower(m):
        def tile(r):
            span = slice(r, r + TILE)
            return halves_of(lift[m, span] + (pre_two[m, span] * b + c))

        emit_taps(ring_slot(taps, m), masks, sides[m % SIDES], sides[SIDES + m % SIDES], tile)

    def convolve(k):
        lhs = [ring_slot(taps, k + d - 1)[...] for d in range(3)]
        out = jnp.dot(jnp.concatenate(lhs, axis=1), weight[...], preferred_element_type=F32)
        first = jnp.zeros((8, BOTH), F32)
        second = jnp.zeros((8, BOTH), F32)
        for i in range(mels):
            m = k * mels + i
            for r in range(0, rows, 8):
                span = slice(r, r + 8)
                h = pre_one[m, span] * scale + shift
                th = jnp.tanh(h)
                one = 1.0 + th
                silu = h * one
                gl = out[i * rows + r : i * rows + r + 8] * (one + (silu - silu * th))
                lift_one[m, span] = gl
                if r < half:
                    first += gl
                    second += gl * h
        add_sums(acc, first, second)

    def correlate(k):
        here = range(k * wide_mels, (k + 1) * wide_mels)
        flat = wide_mels * half
        chosen = stack(taps, here, half, slice(128, 384)).T
        for p in range(2):
            turned[:, p * flat : (p + 1) * flat] = chosen[p * C_MID : (p + 1) * C_MID]
        for p in range(2):
            near = []
            for d in range(3):
                first = here[0] + d
                lanes = slice(p * LANES, p * LANES + 3 * LANES)
                near.append(taps_a[first : first + wide_mels, 0:half, lanes].reshape(flat, 3 * LANES))
            total = jnp.dot(
                turned[:, p * flat : (p + 1) * flat],
                jnp.concatenate(near, axis=1),
                preferred_element_type=F32,
            )
            if k == 0 and p == 0:
                acc_two[...] = total
            else:
                acc_two[...] += total

    for k in range(MEL // mels + 1):
        for m in range(k * mels, (k + 1) * mels):
            if m < MEL:
                lower(m)
        if k > 0:
            convolve(k - 1)
            if k * mels % wide_mels == 0:
                correlate(k * mels // wide_mels - 1)
    plain = fold(acc[0])
    spread(plain, normed_sum(fold(acc[1]), plain, vec[0:1], vec[1:2]), back_out)
    for t in range(3):
        for d in range(3):
            at = (3 * d + t) * 128
            to = (3 * t + d) * 128
            two[:, to : to + 128] = acc_two[:, at : at + 128]


def back_two(lift, pre_two, sums_two, back_stats, vec, masks, weight, pre_one, sums_one, taps_a, count):
    copies = back_stats.shape[0]
    rows = masks.shape[1]
    return call(
        lambda *refs: back_two_body(count, *refs),
        (lift, pre_two, sums_two, back_stats, vec, masks, weight, pre_one, sums_one, taps_a),
        [
            like((MEL, rows, BOTH), F32),
            like((C_MID, 9 * C_MID), F32),
            like((copies, 2, C_MID), F32),
            like((2, C_MID), F32),
        ],
        [
            pltpu.VMEM((2, 8, BOTH), F32),
            pltpu.VMEM((C_MID, 9 * C_MID), F32),
            pltpu.VMEM((C_MID, 8 * (rows - TAIL)), BF16),
            *side_scratch(rows),
            *ring_scratch(17, rows),
        ],

        input_output_aliases={0: 0},
    )


def scatter_blocks(out, tops, two, one, row_count):
    copies, block_rows = out.shape[0:2]
    grps = copies // row_count
    share = C_MID // grps
    size_two = 9 * C_MID // row_count
    size_one = 9 * C_IN // row_count
    ahead = LANES if block_rows == share + 24 and size_two >= LANES else 0

    def first():
        turned = two[...].T
        for r in range(row_count if ahead else 0):
            tops[r] = turned[size_two * r : size_two * r + ahead].T

    def second():
        turned = two[...].T
        turned_one = one().T
        for r in range(row_count):
            rows = [
                turned[size_two * r + ahead : size_two * (r + 1)],
                turned_one[size_one * r : size_one * (r + 1)],
            ]
            back = jnp.concatenate(rows, axis=0).T
            for g in range(grps):
                here = slice(share * g, share * (g + 1))
                if ahead:
                    block = jnp.concatenate([tops[r, here], pack_rest(back[here])], axis=0)
                else:
                    block = pack(back[here], block_rows)
                out[g * row_count + r] = block.astype(BF16)

    return first, second


def kernel_one_step(taps_x, grads, acc, k, pairs):
    half = grads.shape[1] - TAIL
    here = range(k * pairs, (k + 1) * pairs)
    mels = [2 * j + parity for parity in range(2) for j in here]
    chosen = jnp.concatenate([grads[m, 0:half] for m in mels], axis=0)
    total = dot_rows(chosen, near_bins(taps_x, here, half))
    if k == 0:
        acc[...] = total
    else:
        acc[...] += total


def kernel_one_sums(acc):
    pieces = []
    for t in range(3):
        for d in range(3):
            total = jnp.zeros((C_MID, C_IN), F32)
            for p in range(2):
                at = d * BOTH + (t + p) * C_IN
                total += acc[p * C_MID : (p + 1) * C_MID, at : at + C_IN]
            pieces.append(total)
    return jnp.concatenate(pieces, axis=1)


STORED = 640


def grads_body(count, row_count, lift, pre_one, sums_one, back_stats, vec, masks, taps_x, two,
               stored, blocks, sums_out, acc_one, grads, low_masks, tops, sems):
    back = stat_sums(back_stats)
    sums_out[...] = back
    a, b, c = grad_terms(sums_one[...], back, vec[0:1], count)
    rows = masks.shape[1]
    for slot in range(2):
        low_masks[:, slot * LANES : (slot + 1) * LANES] = masks[slot].astype(BF16)
    copies = [pltpu.make_async_copy(low_masks, stored.at[MEL], sems.at[sems.shape[0] - 1])]
    copies[0].start()

    def lower(m):
        for r in tiles(rows):
            span = slice(r, r + TILE)
            grads[m, span] = (lift[m, span] * a + (pre_one[m, span] * b + c)).astype(BF16)

    scatter_ahead, scatter_rest = scatter_blocks(
        blocks, tops, two, lambda: kernel_one_sums(acc_one), row_count
    )
    pairs = 2
    mels = 2 * pairs
    steps = MEL // mels
    for k in range(steps + 1):
        if k == 2:
            scatter_ahead()
        if k < steps:
            for m in range(mels * k, mels * (k + 1)):
                lower(m)
            here = pl.ds(mels * k, mels)
            copies.append(pltpu.make_async_copy(grads.at[here], stored.at[here], sems.at[k]))
            copies[-1].start()
        if k > 0:
            kernel_one_step(taps_x, grads, acc_one, k - 1, pairs)
    scatter_rest()
    for copy in copies:
        copy.wait()


def kernel_grads(lift, pre_one, sums_one, back_stats, vec, masks, taps_x, two, row_count, count):
    copies = back_stats.shape[0]
    rows = masks.shape[1]
    share = C_MID * row_count // copies
    block_rows = packed_rows(share, 9 * (C_IN + C_MID) // row_count)
    return call(
        lambda *refs: grads_body(count, row_count, *refs),
        (lift, pre_one, sums_one, back_stats, vec, masks, taps_x, two),
        [
            like((STORED, rows, BOTH), BF16),
            like((copies, block_rows, LANES), BF16),
            like((2, C_MID), F32),
        ],
        [
            pltpu.VMEM((BOTH, 3 * BOTH), F32),
            pltpu.VMEM((MEL, rows, BOTH), BF16),
            pltpu.VMEM((rows, BOTH), BF16),
            pltpu.VMEM((row_count, C_MID, LANES), F32),
            pltpu.SemaphoreType.DMA((9,)),
        ],
        out_specs=[HBM, VMEM, VMEM],
    )


def features_body(stored, k1, out, grads, low_masks, masks, weight, woven, sems, out_sems, *buffers):
    sides, taps = buffers[: 2 * SIDES], buffers[2 * SIDES :]
    pairs = 4
    rows = grads.shape[1]
    half = rows - TAIL
    groups = sems.shape[0] - 1
    group = MEL // groups
    mask_copy = pltpu.make_async_copy(stored.at[MEL], low_masks, sems.at[groups])
    mask_copy.start()
    fetch = []
    for k in range(groups):
        here = pl.ds(k * group, group)
        fetch.append(pltpu.make_async_copy(stored.at[here], grads.at[here], sems.at[k]))
        fetch[k].start()
    taps[-1][...] = jnp.zeros(taps[-1].shape, BF16)
    place_one_back(k1, weight)
    mask_copy.wait()
    for slot in range(2):
        masks[slot] = low_masks[:, slot * LANES : (slot + 1) * LANES].astype(F32)

    def emit(m):
        def tile(r):
            return halves_of(grads[m, r : r + TILE].astype(F32))

        emit_taps(ring_slot(taps, m), masks, sides[m % SIDES], sides[SIDES + m % SIDES], tile)

    copies = []
    slots = woven.shape[0]

    def convolve(k):
        near = [
            stack(taps, [2 * (k * pairs + q) + i - 1 for q in range(pairs)], half) for i in range(4)
        ]
        part = jnp.dot(jnp.concatenate(near, axis=1), weight[...], preferred_element_type=F32)
        for q in range(pairs):
            j = k * pairs + q
            b = j % slots
            here = slice(q * half, (q + 1) * half)
            if j >= slots:
                copies[j - slots].wait()
            woven[b, pl.ds(0, half, stride=2), :] = part[here, 0:128]
            woven[b, pl.ds(1, half, stride=2), :] = part[here, 128:256]
            copy = pltpu.make_async_copy(
                woven.at[b], out.at[:, pl.ds(j * LANES, LANES)], out_sems.at[b]
            )
            copy.start()
            copies.append(copy)

    for m in range(MEL):
        if m % group == 0:
            fetch[m // group].wait()
        emit(m)
        if m > 0 and m % (2 * pairs) == 0:
            convolve(m // (2 * pairs) - 1)
    convolve(MEL // (2 * pairs) - 1)
    for copy in copies[-slots:]:
        copy.wait()


def features_grad(stored, k1):
    rows = stored.shape[1]
    half = rows - TAIL
    return call(
        features_body,
        (stored, k1),
        [like((2 * half, MEL * C_IN), F32)],
        [
            pltpu.VMEM((MEL, rows, BOTH), BF16),
            pltpu.VMEM((rows, BOTH), BF16),
            pltpu.VMEM((2, rows, LANES), F32),
            pltpu.VMEM((4 * WIDE, BOTH), BF16),
            pltpu.VMEM((8, 2 * half, LANES), F32),
            pltpu.SemaphoreType.DMA((9,)),
            pltpu.SemaphoreType.DMA((8,)),
            *side_scratch(rows),
            *ring_scratch(27, half),
        ],
        limit=24,
        in_specs=[HBM, VMEM],
        out_specs=[ANY],
    )[0]


def finish_body(got, back_one_sums, back_two_sums, own_one, own_two, ga, sa, gb, sb):
    size = own_two.shape[1]
    share = own_two.shape[0]
    total = jnp.sum(got[...].astype(F32), axis=0)
    total = unpack(total, share, size + own_one.shape[1])
    own_two[...] = total[:, 0:size]
    own_one[...] = total[:, size:]
    lane = lax.broadcasted_iota(jnp.int32, (share, C_MID), 1)
    row = lax.broadcasted_iota(jnp.int32, (share, C_MID), 0)
    chosen = lane == lax.axis_index("grp") * share + row
    first = lax.broadcasted_iota(jnp.int32, (share, share), 0)
    second = lax.broadcasted_iota(jnp.int32, (share, share), 1)
    for out, sums, k in (
        (ga, back_one_sums, 1), (sa, back_one_sums, 0), (gb, back_two_sums, 1), (sb, back_two_sums, 0)
    ):
        wide = jnp.broadcast_to(sums[k : k + 1], (share, C_MID))
        column = jnp.sum(jnp.where(chosen, wide, 0.0), axis=1, keepdims=True)
        wide = jnp.broadcast_to(column, (share, share))
        out[...] = jnp.sum(jnp.where(first == second, wide, 0.0), axis=0, keepdims=True)


def finish(got, back_one_sums, back_two_sums, share, rows_one, rows_two):
    shapes = [(share, rows_one), (share, rows_two)] + [(1, share)] * 4
    return call(
        finish_body,
        (got, back_one_sums, back_two_sums),
        [like(s, F32) for s in shapes],
    )


def exchange(blocks):
    return lax.all_to_all(blocks, AXES, 0, 0, tiled=True)


def shards(
    features, clip_starts, kernel_one, kernel_two, gain_one, shift_one, gain_two, shift_two, cotangent
):
    frames = features.shape[0]
    copies = lax.axis_size(AXES)
    row_count = lax.axis_size("row")
    count = float(frames * MEL * copies)
    rows_one, rows_two = kernel_one.shape[0], kernel_two.shape[0]
    share = kernel_one.shape[1]
    vectors = [v.reshape(1, share) for v in (gain_one, shift_one, gain_two, shift_two)]
    clips = clip_starts.reshape(1, -1)
    weights, up, down = setup(kernel_one.T, kernel_two.T, vectors, features, cotangent, copies)
    ends = copies - 1
    up = lax.ppermute(up, AXES, [(i, i + 1) for i in range(ends)])
    down = lax.ppermute(down, AXES, [(i + 1, i) for i in range(ends)])
    weights = exchange(weights)
    pre_one, stats, taps_x, masks, k1, k2, vec, weight = conv_one(
        features, up, down, clips, weights, row_count
    )
    stats = exchange(stats)
    pre_two, stats, taps_a, sums_one, weight_back = conv_two(
        pre_one, stats, vec, masks, k2, weight, count
    )
    stats = exchange(stats)
    block_out, lift, stats, sums_two = norm_two(pre_two, stats, vec, cotangent, up, down, count)
    stats = exchange(stats)
    lift, two, stats, back_two_sums = back_two(
        lift, pre_two, sums_two, stats, vec, masks, weight_back, pre_one, sums_one, taps_a, count
    )
    stats = exchange(stats)
    stored, blocks, back_one_sums = kernel_grads(
        lift, pre_one, sums_one, stats, vec, masks, taps_x, two, row_count, count
    )
    blocks = exchange(blocks)
    grad_features = features_grad(stored, k1)
    own_one, own_two, ga, sa, gb, sb = finish(
        blocks, back_one_sums, back_two_sums, share, rows_one, rows_two
    )
    return (
        block_out,
        grad_features,
        own_one.T,
        own_two.T,
        ga.reshape(share),
        sa.reshape(share),
        gb.reshape(share),
        sb.reshape(share),
    )


def solution(mesh):
    placed = (
        P(AXES, None), P(), P("row", "grp"), P("row", "grp"),
        P("grp"), P("grp"), P("grp"), P("grp"), P(AXES, None),
    )
    return jax.shard_map(
        shards,
        mesh=mesh,
        in_specs=placed,
        out_specs=(
            P(AXES, None), P(AXES, None), P("row", "grp"), P("row", "grp"),
            P("grp"), P("grp"), P("grp"), P("grp"),
        ),
        check_vma=False,
    )
```

```python
import jax
import jax.numpy as jnp
from jax import lax
from jax.experimental import pallas as pl
from jax.experimental.pallas import tpu as pltpu
from jax.sharding import PartitionSpec as P

MEL = 32
C_IN = 64
C_MID = 128
EPS = 1e-05
AXES = ("grp", "row")
LANES = 128
TAIL = 16
WIDE = 4 * LANES
BOTH = 2 * C_MID
F32 = jnp.float32
BF16 = jnp.bfloat16
TILE = 16
SIDES = 4
MIB = 2**20

VMEM = pl.BlockSpec(memory_space=pltpu.VMEM)
ANY = pl.BlockSpec(memory_space=pl.ANY)
HBM = pl.BlockSpec(memory_space=pltpu.HBM)


def like(shape, dtype):
    return jax.ShapeDtypeStruct(shape, dtype)


def call(body, args, outs, scratch=(), limit=9, in_specs=None, out_specs=None, **more):
    return pl.pallas_call(
        body,
        in_specs=in_specs or [VMEM] * len(args),
        out_specs=out_specs or [VMEM] * len(outs),
        out_shape=outs,
        scratch_shapes=list(scratch),
        compiler_params=pltpu.CompilerParams(vmem_limit_bytes=limit * MIB),
        cost_estimate=pl.CostEstimate(flops=5 * 10**9, bytes_accessed=0, transcendentals=0),
        **more,
    )(*args)


def padded(size):
    return -(-size // LANES) * LANES


def packed_rows(share, wide):
    rest = wide - LANES
    if rest > 0 and share == 32 and 3 * (LANES - rest) >= rest:
        return share + 24
    return share * (padded(wide) // LANES)


def pack(block, rows):
    share, wide = block.shape
    if rows % share == 0:
        block = jnp.concatenate([block, jnp.zeros((share, padded(wide) - wide), F32)], axis=1)
        return jnp.concatenate(
            [block[:, at : at + LANES] for at in range(0, block.shape[1], LANES)], axis=0
        )
    return jnp.concatenate([block[:, :LANES], pack_rest(block[:, LANES:])], axis=0)


def pack_rest(rest):
    room = LANES - rest.shape[1]
    tail = jnp.concatenate(
        [rest[24:32], jnp.zeros((8, 3 * room - rest.shape[1]), F32)], axis=1
    )
    tail = jnp.concatenate([tail[:, k * room : (k + 1) * room] for k in range(3)], axis=0)
    return jnp.concatenate([rest[0:24], tail], axis=1)


def unpack(block, share, wide):
    rows = block.shape[0]
    if rows % share == 0:
        parts = [block[at : at + share] for at in range(0, rows, share)]
        return jnp.concatenate(parts, axis=1)[:, 0:wide]
    width = wide - LANES
    second = block[share:]
    tail = jnp.concatenate([second[8 * k : 8 * k + 8, width:] for k in range(3)], axis=1)
    rest = jnp.concatenate([second[:, :width], tail[:, :width]], axis=0)
    return jnp.concatenate([block[0:share], rest], axis=1)


def partial_sum(values):
    return jnp.sum(values.reshape(-1, 8, values.shape[-1]), axis=0)


def fold(values):
    total = jnp.sum(values, axis=0, keepdims=True)
    return total[:, :C_MID] + total[:, C_MID:]


def spread(first, second, out):
    sums = jnp.concatenate([first, second], axis=0)
    out[...] = jnp.broadcast_to(sums[None], out.shape)


def twice(row):
    return jnp.concatenate([row, row], axis=1)


def tiles(rows):
    return range(0, rows, TILE)


def emit_taps(taps, masks, evens, odds, tile_of, pair=None):
    rows = masks.shape[1]
    kept = taps.shape[0]
    for r in tiles(rows):
        even, odd = tile_of(r)
        evens[r : r + TILE] = even
        odds[8 + r : 8 + r + TILE] = odd
        if r == 0:
            evens[rows : rows + 1] = even[0:1]
        if r + TILE == rows:
            odds[7:8] = odd[TILE - 1 : TILE]
        if r < kept:
            taps[r : r + TILE, 128:256] = even.astype(BF16)
            taps[r : r + TILE, 256:384] = odd.astype(BF16)
        if pair is not None and r < pair.shape[0]:
            pair[r : r + TILE] = jnp.concatenate([even, odd], axis=1).astype(BF16)
    for r in tiles(kept):
        span = slice(r, r + TILE)
        before = odds[7 + r : 7 + r + TILE] * masks[0, span]
        after = evens[1 + r : 1 + r + TILE] * masks[1, span]
        taps[span, 0:128] = before.astype(BF16)
        taps[span, 384:512] = after.astype(BF16)


def halves_of(value):
    return value[:, :C_MID], value[:, C_MID:]


def add_sums(acc, first, second):
    acc[0] += first
    acc[1] += second


def side_scratch(rows):
    return [pltpu.VMEM((rows + 8, LANES), F32)] * (2 * SIDES)


def stats_of(out, mels, rows, half, acc):
    first = jnp.zeros((8, BOTH), F32)
    second = jnp.zeros((8, BOTH), F32)
    for k in range(mels):
        for r in range(0, half, 8):
            value = out[k * rows + r : k * rows + r + 8]
            first += value
            second += value * value
    add_sums(acc, first, second)


def normed_sum(with_half_lifted, plain, gain, shift):
    return (2.0 * with_half_lifted - shift * plain) / gain


def stat_sums(stats):
    return jnp.sum(stats[...], axis=0)


def norm_terms(sums, count):
    mean = sums[0:1] / count
    rstd = lax.rsqrt(sums[1:2] / count - mean * mean + EPS)
    return mean, rstd


def dot_rows(first, second):
    return lax.dot_general(
        first, second, (((0,), (0,)), ((), ())), preferred_element_type=F32
    )


def ring_slot(ring, m):
    return ring[m % (len(ring) - 1)] if 0 <= m < MEL else ring[-1]


def stack(ring, mels, rows, lanes=slice(None)):
    return jnp.concatenate([ring_slot(ring, m)[0:rows, lanes] for m in mels], axis=0)


def ring_scratch(slots, rows):
    return [pltpu.VMEM((rows, WIDE), BF16)] * slots


def clear_ends(taps):
    blank = jnp.zeros(taps.shape[1:], BF16)
    taps[0] = blank
    taps[taps.shape[0] - 1] = blank


def setup_body(k1, k2, ga, sa, gb, sb, x_head, x_tail, c_head, c_tail, w_out, up, down):
    share = k1.shape[0]
    copies = w_out.shape[0]
    first = lax.broadcasted_iota(jnp.int32, (share, share), 0)
    second = lax.broadcasted_iota(jnp.int32, (share, share), 1)
    columns = [k1[...].astype(F32), k2[...].astype(F32)]
    for vector in (ga, sa, gb, sb):
        wide = jnp.broadcast_to(vector[...].astype(F32), (share, share))
        columns.append(jnp.sum(jnp.where(first == second, wide, 0.0), axis=1, keepdims=True))
    chunk = pack(jnp.concatenate(columns, axis=1), w_out.shape[1]).astype(BF16)
    for i in range(copies):
        w_out[i] = chunk
    row = lax.broadcasted_iota(jnp.int32, (8, x_head.shape[1]), 0)
    xt = x_tail[...].astype(F32)
    ct = c_tail[...].astype(F32)
    up[...] = jnp.where(
        row < 4, pltpu.roll(xt[8:16], 4, 0), jnp.where(row == 4, ct[15:16], 0.0)
    ).astype(BF16)
    xh = x_head[...].astype(F32)
    ch = c_head[...].astype(F32)
    down[...] = jnp.where(row < 4, xh[0:8], jnp.where(row == 4, ch[0:1], 0.0)).astype(BF16)


def setup(k1t, k2t, vectors, features, cotangent, copies):
    frames, wide = features.shape
    halves = cotangent.shape[0]
    share = k1t.shape[0]
    w = (copies, packed_rows(share, k1t.shape[1] + k2t.shape[1] + 4), LANES)
    whole = lambda shape: pl.BlockSpec(shape, lambda i: (0,) * len(shape))
    outs = [like(w, BF16), like((8, wide), BF16), like((8, wide), BF16)]
    return call(
        setup_body,
        (k1t, k2t, *vectors, features, features, cotangent, cotangent),
        outs,
        limit=56,
        in_specs=[
            whole(k1t.shape),
            whole(k2t.shape),
            *[whole((1, share))] * 4,
            pl.BlockSpec((16, wide), lambda i: (0, 0)),
            pl.BlockSpec((16, wide), lambda i: (frames // 16 - 1, 0)),
            pl.BlockSpec((16, wide), lambda i: (0, 0)),
            pl.BlockSpec((16, wide), lambda i: (halves // 16 - 1, 0)),
        ],
        out_specs=[whole(o.shape) for o in outs],
        grid=(1,),
    )


def emit_masks(copies, clips, masks):
    rows = masks.shape[1]
    half = rows - TAIL
    frames = 2 * half
    start = lax.axis_index(AXES) * frames
    place = lax.broadcasted_iota(jnp.int32, (rows, clips.shape[1]), 0)
    pair = jnp.where(place >= half + TAIL // 2, place - rows, place)
    frame = start + 2 * pair
    starts = jnp.broadcast_to(clips[...], (rows, clips.shape[1]))
    for slot, shift in ((0, 0), (1, 2)):
        hit = (frame + shift == starts) | (frame + shift >= frames * copies)
        begins = jnp.max(jnp.where(hit, 1.0, 0.0), axis=1, keepdims=True)
        masks[slot] = jnp.broadcast_to(1.0 - begins, (rows, LANES))


def split_bins(parts):
    low = lax.broadcasted_iota(jnp.int32, parts[0].shape, 1) < C_IN
    first, second = [], []
    for here, there in (parts[0:2], parts[2:4]):
        first.append(jnp.where(low, here, pltpu.roll(there, C_IN, 1)))
        second.append(jnp.where(low, pltpu.roll(here, C_IN, 1), there))
    return jnp.concatenate(first + second, axis=1)


def near_bins(taps, pairs, rows):
    left, mid, right = [
        jnp.concatenate([taps[1 + j + k, 0:rows] for j in pairs], axis=0) for k in (-1, 0, 1)
    ]
    first = jnp.concatenate([left[:, BOTH:], mid], axis=1)
    second = jnp.concatenate([mid, right[:, :BOTH]], axis=1)
    return jnp.concatenate([first, second], axis=0)


def taps_one_emitter(x, up, down, masks, taps, frames):
    rows = masks.shape[1]
    half = rows - TAIL
    clear_ends(taps)
    row = lax.broadcasted_iota(jnp.int32, (8, LANES), 0)
    lead = 24
    own = 2 * half
    for held in frames:
        held[0:16] = jnp.zeros((16, LANES), F32)
        held[lead + own + 8 : lead + own + 24] = jnp.zeros((16, LANES), F32)

    def pair(j):
        held = frames[j % len(frames)]
        lanes = slice(j * LANES, (j + 1) * LANES)
        u = up[:, lanes].astype(F32)
        d = down[:, lanes].astype(F32)
        held[lead - 8 : lead] = jnp.where(row >= 4, pltpu.roll(u, 4, 0), 0.0)
        held[lead + own : lead + own + 8] = jnp.where(row < 4, d, 0.0)
        for r in tiles(own):
            held[lead + r : lead + r + TILE] = x[r : r + TILE, lanes].astype(F32)

        def pick(first, count, shift):
            return held[pl.ds(lead + 2 * first + shift, count, stride=2), :]

        for r in tiles(rows):
            parts = []
            for shift in (-1, 0, 1, 2):
                if r < half:
                    parts.append(pick(r, TILE, shift))
                else:
                    parts.append(
                        jnp.concatenate([pick(half, 8, shift), pick(-8, 8, shift)], axis=0)
                    )
            span = slice(r, r + TILE)
            parts[0] = parts[0] * masks[0, span]
            parts[3] = parts[3] * masks[1, span]
            taps[1 + j, span, :] = split_bins(parts).astype(BF16)

    return pair


def conv_one_body(row_count, features, up, down, clips_in, wg,
                  pre, stats, taps, masks, k1_out, k2_out, vec_out, weight_two,
                  kf, weight, acc, x, clips, sems, clip_sem, *frames):
    clip_copy = pltpu.make_async_copy(clips_in, clips, clip_sem)
    clip_copy.start()
    wide = x.shape[1] // sems.shape[0]
    fetch = []
    for k in range(sems.shape[0]):
        lanes = pl.ds(k * wide, wide)
        fetch.append(pltpu.make_async_copy(features.at[:, lanes], x.at[:, lanes], sems.at[k]))
        fetch[k].start()
    clip_copy.wait()
    emit_masks(wg.shape[0], clips, masks)
    emit_pair = taps_one_emitter(x, up, down, masks, taps, frames)
    rows = taps.shape[1]
    half = rows - TAIL
    pairs = 2
    rows_one = 9 * C_IN // row_count
    rows_two = 9 * C_MID // row_count
    grps = wg.shape[0] // row_count
    share = C_MID // grps
    for r in range(row_count):
        shard = [
            unpack(wg[g * row_count + r].astype(F32), share, rows_one + rows_two + 4)
            for g in range(grps)
        ]
        shard = jnp.concatenate(shard, axis=0).T
        kf[rows_one * r : rows_one * (r + 1)] = shard[0:rows_one]
        at = 9 * C_IN + rows_two * r
        kf[at : at + rows_two] = shard[rows_one : rows_one + rows_two]
        if r == 0:
            vec_out[...] = shard[rows_one + rows_two : rows_one + rows_two + 4]
    k1_out[...] = kf[0 : 9 * C_IN].astype(BF16)
    k2_out[...] = kf[9 * C_IN :].astype(BF16)
    weight[...] = jnp.zeros(weight.shape, BF16)
    for d in range(3):
        for q in range(4):
            for p in range(2):
                t = q - p
                if 0 <= t < 3:
                    at = d * BOTH + q * C_IN
                    start = (3 * t + d) * C_IN
                    weight[at : at + C_IN, p * 128 : p * 128 + 128] = k1_out[start : start + C_IN]
    acc[...] = jnp.zeros(acc.shape, F32)

    def convolve(c):
        here = range(c * pairs, (c + 1) * pairs)
        out = jnp.dot(near_bins(taps, here, rows), weight[...], preferred_element_type=F32)
        for parity in range(2):
            for q in range(pairs):
                at = (parity * pairs + q) * rows
                pre[2 * (c * pairs + q) + parity] = out[at : at + rows]
        stats_of(out, 2 * pairs, rows, half, acc)

    total = MEL // 2
    for j in range(total):
        if j % (total // len(fetch)) == 0:
            fetch[j // (total // len(fetch))].wait()
        emit_pair(j)
        if j >= pairs and j % pairs == 0:
            convolve(j // pairs - 1)
        if j == 4:
            place_two(k2_out, weight_two)
    convolve(total // pairs - 1)
    spread(fold(acc[0]), fold(acc[1]), stats)


def conv_one(features, up, down, clips, wg, row_count):
    rows = features.shape[0] // 2 + TAIL
    copies = wg.shape[0]
    return call(
        lambda *refs: conv_one_body(row_count, *refs),
        (features, up, down, clips, wg),
        [
            like((MEL, rows, BOTH), F32),
            like((copies, 2, C_MID), F32),
            like((MEL // 2 + 2, rows, WIDE), BF16),
            like((2, rows, LANES), F32),
            like((9 * C_IN, C_MID), BF16),
            like((9 * C_MID, C_MID), BF16),
            like((4, C_MID), F32),
            like((3 * WIDE, BOTH), BF16),
        ],
        [
            pltpu.VMEM((9 * (C_IN + C_MID), C_MID), F32),
            pltpu.VMEM((3 * BOTH, BOTH), BF16),
            pltpu.VMEM((2, 8, BOTH), F32),
            pltpu.VMEM(features.shape, BF16),
            pltpu.VMEM(clips.shape, jnp.int32),
            pltpu.SemaphoreType.DMA((4,)),
            pltpu.SemaphoreType.DMA,
            *[pltpu.VMEM((features.shape[0] + 48, LANES), F32)] * 4,
        ],
        in_specs=[HBM, VMEM, VMEM, HBM, VMEM],
    )


def place_two(k2, weight):
    weight[...] = jnp.zeros(weight.shape, BF16)
    for d in range(3):
        for q in range(4):
            for p in range(2):
                t = q - p
                if 0 <= t < 3:
                    at = d * WIDE + q * 128
                    start = (3 * t + d) * C_MID
                    weight[at : at + 128, p * 128 : p * 128 + 128] = k2[start : start + C_MID]


def place_two_back(k2, weight):
    weight[...] = jnp.zeros(weight.shape, BF16)
    for t in range(3):
        for d in range(3):
            start = (3 * t + d) * C_MID
            turned = (0.5 * k2[start : start + C_MID].astype(F32).T).astype(BF16)
            for p in range(2):
                at = (2 - d) * WIDE + (2 - t + p) * 128
                weight[at : at + 128, p * 128 : p * 128 + 128] = turned


def place_one_back(k1, weight):
    weight[...] = jnp.zeros(weight.shape, BF16)
    for t in range(3):
        for d in range(3):
            start = (3 * t + d) * C_IN
            turned = k1[start : start + C_IN].astype(F32).T.astype(BF16)
            for mo in (1, 2):
                for p in range(2):
                    at = (mo - d + 1) * WIDE + (2 - t + p) * 128
                    to = p * 128 + (mo - 1) * 64
                    weight[at : at + 128, to : to + 64] = turned


def conv_two_body(count, pre_one, stats_one, vec, masks, k2, weight,
                  pre, stats, taps, sums_out, weight_back, acc, *sides):
    rows = masks.shape[1]
    half = rows - TAIL
    mels = 2
    sums = stat_sums(stats_one)
    sums_out[...] = sums
    mean, rstd = norm_terms(sums, count)
    scale = 0.5 * vec[0:1] * rstd
    shift = twice(0.5 * vec[1:2] - mean * scale)
    scale = twice(scale)
    clear_ends(taps)
    acc[...] = jnp.zeros(acc.shape, F32)

    def activate(m):
        def tile(r):
            h = pre_one[m, r : r + TILE] * scale + shift
            return halves_of(h + h * jnp.tanh(h))

        emit_taps(taps.at[1 + m], masks, sides[m % SIDES], sides[SIDES + m % SIDES], tile)

    def convolve(c):
        lhs = [taps[c * mels + d : (c + 1) * mels + d].reshape(mels * rows, WIDE) for d in range(3)]
        out = jnp.dot(jnp.concatenate(lhs, axis=1), weight[...], preferred_element_type=F32)
        pre[c * mels : (c + 1) * mels] = out.reshape(mels, rows, BOTH)
        stats_of(out, mels, rows, half, acc)

    for m in range(MEL):
        activate(m)
        if m >= mels and m % mels == 0:
            convolve(m // mels - 1)
        if m == 8:
            place_two_back(k2, weight_back)
    convolve(MEL // mels - 1)
    spread(fold(acc[0]), fold(acc[1]), stats)


def conv_two(pre_one, stats_one, vec, masks, k2, weight, count):
    copies = stats_one.shape[0]
    rows = masks.shape[1]
    return call(
        lambda *refs: conv_two_body(count, *refs),
        (pre_one, stats_one, vec, masks, k2, weight),
        [
            like((MEL, rows, BOTH), F32),
            like((copies, 2, C_MID), F32),
            like((MEL + 2, rows, WIDE), BF16),
            like((2, C_MID), F32),
            like((3 * WIDE, BOTH), BF16),
        ],
        [pltpu.VMEM((2, 8, BOTH), F32), *side_scratch(rows)],
    )


def norm_two_body(count, pre, stats_two, vec, cot, up, down, pooled, lift, back_stats, sums_out, acc):
    half = cot.shape[0]
    sums = stat_sums(stats_two)
    sums_out[...] = sums
    mean, rstd = norm_terms(sums, count)
    scale = 0.5 * vec[2:3] * rstd
    shift = 0.5 * vec[3:4] - mean * scale
    acc[...] = jnp.zeros(acc.shape, F32)
    row = lax.broadcasted_iota(jnp.int32, (TAIL, LANES), 0)

    factor = 0.125 * vec[2:3] * rstd

    def pair(j):
        lanes = pl.ds(pl.multiple_of(j * LANES, LANES), LANES)
        u = up[:, lanes].astype(F32)
        d = down[:, lanes].astype(F32)
        first = jnp.zeros((8, LANES), F32)
        second = jnp.zeros((8, LANES), F32)
        for r in tiles(half + TAIL):
            span = slice(r, r + TILE)
            if r < half:
                grad = cot[span, lanes].astype(F32) * factor
            else:
                grad = jnp.where(row == 0, d[4:5], jnp.where(row == TAIL - 1, u[4:5], 0.0)) * factor
            total = jnp.zeros((TILE, LANES), F32)
            for m in (2 * j, 2 * j + 1):
                for p in range(2):
                    side = slice(p * C_MID, (p + 1) * C_MID)
                    value = pre[m, span, side]
                    h = value * scale + shift
                    th = jnp.tanh(h)
                    one = 1.0 + th
                    silu = h * one
                    gl = grad * (one + (silu - silu * th))
                    lift[m, span, side] = gl
                    if r < half:
                        total += silu
                        first += partial_sum(gl)
                        second += partial_sum(gl * h)
            if r < half:
                pooled[span, lanes] = (total * 0.25).astype(BF16)
        add_sums(acc, first, second)

    def four_pairs(i, carry):
        for k in range(4):
            pair(4 * i + k)
        return carry

    lax.fori_loop(0, MEL // 8, four_pairs, 0)
    first, second = [jnp.sum(acc[k], axis=0, keepdims=True) for k in range(2)]
    scaled = vec[2:3] * rstd
    first = first / scaled
    spread(first, normed_sum(second / scaled, first, vec[2:3], vec[3:4]), back_stats)


def norm_two(pre, stats_two, vec, cot, up, down, count):
    copies = stats_two.shape[0]
    half, wide = cot.shape
    return call(
        lambda *refs: norm_two_body(count, *refs),
        (pre, stats_two, vec, cot, up, down),
        [
            like((half, wide), BF16),
            like((MEL, half + TAIL, BOTH), F32),
            like((copies, 2, C_MID), F32),
            like((2, C_MID), F32),
        ],
        [pltpu.VMEM((2, 8, LANES), F32)],
    )


def grad_terms(sums, back, gain, count):
    mean, rstd = norm_terms(sums, count)
    a = gain * rstd
    b = -a * rstd * (back[1:2] / count)
    c = -a * (back[0:1] / count) - b * mean
    return twice(a), twice(b), twice(c)


def back_two_body(count, lift, pre_two, sums_two, back_stats, vec, masks, weight, pre_one, sums_one,
                  lift_one, grads, back_out, sums_out, acc, *buffers):
    sides, taps = buffers[: 2 * SIDES], buffers[2 * SIDES :]
    rows = masks.shape[1]
    half = rows - TAIL
    mels = 1
    back = stat_sums(back_stats)
    sums_out[...] = back
    _, b, c = grad_terms(sums_two[...], back, vec[2:3], count)
    mean, rstd = norm_terms(sums_one[...], count)
    scale = 0.5 * vec[0:1] * rstd
    shift = twice(0.5 * vec[1:2] - mean * scale)
    scale = twice(scale)
    taps[-1][...] = jnp.zeros(taps[-1].shape, BF16)
    acc[...] = jnp.zeros(acc.shape, F32)

    def lower(m):
        def tile(r):
            span = slice(r, r + TILE)
            return halves_of(lift[m, span] + (pre_two[m, span] * b + c))

        evens, odds = sides[m % SIDES], sides[SIDES + m % SIDES]
        emit_taps(ring_slot(taps, m), masks, evens, odds, tile, grads.at[m])

    def convolve(k):
        lhs = [ring_slot(taps, k + d - 1)[...] for d in range(3)]
        out = jnp.dot(jnp.concatenate(lhs, axis=1), weight[...], preferred_element_type=F32)
        first = jnp.zeros((8, BOTH), F32)
        second = jnp.zeros((8, BOTH), F32)
        for i in range(mels):
            m = k * mels + i
            for r in range(0, rows, 8):
                span = slice(r, r + 8)
                h = pre_one[m, span] * scale + shift
                th = jnp.tanh(h)
                one = 1.0 + th
                silu = h * one
                gl = out[i * rows + r : i * rows + r + 8] * (one + (silu - silu * th))
                lift_one[m, span] = gl
                if r < half:
                    first += gl
                    second += gl * h
        add_sums(acc, first, second)

    for k in range(MEL // mels + 1):
        for m in range(k * mels, (k + 1) * mels):
            if m < MEL:
                lower(m)
        if k > 0:
            convolve(k - 1)
    plain = fold(acc[0])
    spread(plain, normed_sum(fold(acc[1]), plain, vec[0:1], vec[1:2]), back_out)


def back_two(lift, pre_two, sums_two, back_stats, vec, masks, weight, pre_one, sums_one, count):
    copies = back_stats.shape[0]
    rows = masks.shape[1]
    return call(
        lambda *refs: back_two_body(count, *refs),
        (lift, pre_two, sums_two, back_stats, vec, masks, weight, pre_one, sums_one),
        [
            like((MEL, rows, BOTH), F32),
            like((MEL, rows - TAIL, BOTH), BF16),
            like((copies, 2, C_MID), F32),
            like((2, C_MID), F32),
        ],
        [
            pltpu.VMEM((2, 8, BOTH), F32),
            *side_scratch(rows),
            *ring_scratch(17, rows),
        ],

        input_output_aliases={0: 0},
    )


def scatter_blocks(out, tops, two, one, row_count):
    copies, block_rows = out.shape[0:2]
    grps = copies // row_count
    share = C_MID // grps
    size_two = 9 * C_MID // row_count
    size_one = 9 * C_IN // row_count
    ahead = LANES if block_rows == share + 24 and size_two >= LANES else 0

    def first():
        turned = two[...].T
        for r in range(row_count if ahead else 0):
            tops[r] = turned[size_two * r : size_two * r + ahead].T

    def second():
        turned = two[...].T
        turned_one = one().T
        for r in range(row_count):
            rows = [
                turned[size_two * r + ahead : size_two * (r + 1)],
                turned_one[size_one * r : size_one * (r + 1)],
            ]
            back = jnp.concatenate(rows, axis=0).T
            for g in range(grps):
                here = slice(share * g, share * (g + 1))
                if ahead:
                    block = jnp.concatenate([tops[r, here], pack_rest(back[here])], axis=0)
                else:
                    block = pack(back[here], block_rows)
                out[g * row_count + r] = block.astype(BF16)

    return first, second


def kernel_one_step(taps_x, grads, acc, k, pairs):
    half = grads.shape[1] - TAIL
    here = range(k * pairs, (k + 1) * pairs)
    mels = [2 * j + parity for parity in range(2) for j in here]
    chosen = jnp.concatenate([grads[m, 0:half] for m in mels], axis=0)
    total = dot_rows(chosen, near_bins(taps_x, here, half))
    if k == 0:
        acc[...] = total
    else:
        acc[...] += total


def kernel_one_sums(acc):
    pieces = []
    for t in range(3):
        for d in range(3):
            total = jnp.zeros((C_MID, C_IN), F32)
            for p in range(2):
                at = d * BOTH + (t + p) * C_IN
                total += acc[p * C_MID : (p + 1) * C_MID, at : at + C_IN]
            pieces.append(total)
    return jnp.concatenate(pieces, axis=1)


STORED = 640


def grads_body(count, row_count, lift, pre_one, sums_one, back_stats, vec, masks, taps_x, taps_a, grads_two,
               stored, blocks, sums_out, acc_one, grads, low_masks, tops, acc_two, turned, two, sems):
    back = stat_sums(back_stats)
    sums_out[...] = back
    a, b, c = grad_terms(sums_one[...], back, vec[0:1], count)
    rows = masks.shape[1]
    half = rows - TAIL
    wide_mels = 4
    for slot in range(2):
        low_masks[:, slot * LANES : (slot + 1) * LANES] = masks[slot].astype(BF16)
    copies = [pltpu.make_async_copy(low_masks, stored.at[MEL], sems.at[sems.shape[0] - 1])]
    copies[0].start()

    def lower(m):
        for r in tiles(rows):
            span = slice(r, r + TILE)
            grads[m, span] = (lift[m, span] * a + (pre_one[m, span] * b + c)).astype(BF16)

    scatter_ahead, scatter_rest = scatter_blocks(
        blocks, tops, two, lambda: kernel_one_sums(acc_one), row_count
    )
    def correlate(k):
        here = range(k * wide_mels, (k + 1) * wide_mels)
        flat = wide_mels * half
        chosen = grads_two[here[0] : here[0] + wide_mels].reshape(flat, BOTH).T
        for p in range(2):
            turned[:, p * flat : (p + 1) * flat] = chosen[p * C_MID : (p + 1) * C_MID]
        for p in range(2):
            near = []
            for d in range(3):
                first = here[0] + d
                lanes = slice(p * LANES, p * LANES + 3 * LANES)
                near.append(taps_a[first : first + wide_mels, 0:half, lanes].reshape(flat, 3 * LANES))
            total = jnp.dot(
                turned[:, p * flat : (p + 1) * flat],
                jnp.concatenate(near, axis=1),
                preferred_element_type=F32,
            )
            if k == 0 and p == 0:
                acc_two[...] = total
            else:
                acc_two[...] += total

    pairs = 2
    mels = 2 * pairs
    steps = MEL // mels
    for k in range(steps):
        for m in range(mels * k, mels * (k + 1)):
            lower(m)
        here = pl.ds(mels * k, mels)
        copies.append(pltpu.make_async_copy(grads.at[here], stored.at[here], sems.at[k]))
        copies[-1].start()
        correlate(k)
    for t in range(3):
        for d in range(3):
            at = (3 * d + t) * 128
            to = (3 * t + d) * 128
            two[:, to : to + 128] = acc_two[:, at : at + 128]
    for k in range(steps):
        if k == 2:
            scatter_ahead()
        kernel_one_step(taps_x, grads, acc_one, k, pairs)
    scatter_rest()
    for copy in copies:
        copy.wait()


def kernel_grads(lift, pre_one, sums_one, back_stats, vec, masks, taps_x, taps_a, grads_two,
                 row_count, count):
    copies = back_stats.shape[0]
    rows = masks.shape[1]
    share = C_MID * row_count // copies
    block_rows = packed_rows(share, 9 * (C_IN + C_MID) // row_count)
    return call(
        lambda *refs: grads_body(count, row_count, *refs),
        (lift, pre_one, sums_one, back_stats, vec, masks, taps_x, taps_a, grads_two),
        [
            like((STORED, rows, BOTH), BF16),
            like((copies, block_rows, LANES), BF16),
            like((2, C_MID), F32),
        ],
        [
            pltpu.VMEM((BOTH, 3 * BOTH), F32),
            pltpu.VMEM((MEL, rows, BOTH), BF16),
            pltpu.VMEM((rows, BOTH), BF16),
            pltpu.VMEM((row_count, C_MID, LANES), F32),
            pltpu.VMEM((C_MID, 9 * C_MID), F32),
            pltpu.VMEM((C_MID, 8 * (rows - TAIL)), BF16),
            pltpu.VMEM((C_MID, 9 * C_MID), F32),
            pltpu.SemaphoreType.DMA((9,)),
        ],
        out_specs=[HBM, VMEM, VMEM],
    )


def features_body(stored, k1, out, grads, low_masks, masks, weight, woven, sems, out_sems, *buffers):
    sides, taps = buffers[: 2 * SIDES], buffers[2 * SIDES :]
    pairs = 4
    rows = grads.shape[1]
    half = rows - TAIL
    groups = sems.shape[0] - 1
    group = MEL // groups
    mask_copy = pltpu.make_async_copy(stored.at[MEL], low_masks, sems.at[groups])
    mask_copy.start()
    fetch = []
    for k in range(groups):
        here = pl.ds(k * group, group)
        fetch.append(pltpu.make_async_copy(stored.at[here], grads.at[here], sems.at[k]))
        fetch[k].start()
    taps[-1][...] = jnp.zeros(taps[-1].shape, BF16)
    place_one_back(k1, weight)
    mask_copy.wait()
    for slot in range(2):
        masks[slot] = low_masks[:, slot * LANES : (slot + 1) * LANES].astype(F32)

    def emit(m):
        def tile(r):
            return halves_of(grads[m, r : r + TILE].astype(F32))

        emit_taps(ring_slot(taps, m), masks, sides[m % SIDES], sides[SIDES + m % SIDES], tile)

    copies = []
    slots = woven.shape[0]

    def convolve(k):
        near = [
            stack(taps, [2 * (k * pairs + q) + i - 1 for q in range(pairs)], half) for i in range(4)
        ]
        part = jnp.dot(jnp.concatenate(near, axis=1), weight[...], preferred_element_type=F32)
        for q in range(pairs):
            j = k * pairs + q
            b = j % slots
            here = slice(q * half, (q + 1) * half)
            if j >= slots:
                copies[j - slots].wait()
            woven[b, pl.ds(0, half, stride=2), :] = part[here, 0:128]
            woven[b, pl.ds(1, half, stride=2), :] = part[here, 128:256]
            copy = pltpu.make_async_copy(
                woven.at[b], out.at[:, pl.ds(j * LANES, LANES)], out_sems.at[b]
            )
            copy.start()
            copies.append(copy)

    for m in range(MEL):
        if m % group == 0:
            fetch[m // group].wait()
        emit(m)
        if m > 0 and m % (2 * pairs) == 0:
            convolve(m // (2 * pairs) - 1)
    convolve(MEL // (2 * pairs) - 1)
    for copy in copies[-slots:]:
        copy.wait()


def features_grad(stored, k1):
    rows = stored.shape[1]
    half = rows - TAIL
    return call(
        features_body,
        (stored, k1),
        [like((2 * half, MEL * C_IN), F32)],
        [
            pltpu.VMEM((MEL, rows, BOTH), BF16),
            pltpu.VMEM((rows, BOTH), BF16),
            pltpu.VMEM((2, rows, LANES), F32),
            pltpu.VMEM((4 * WIDE, BOTH), BF16),
            pltpu.VMEM((8, 2 * half, LANES), F32),
            pltpu.SemaphoreType.DMA((9,)),
            pltpu.SemaphoreType.DMA((8,)),
            *side_scratch(rows),
            *ring_scratch(27, half),
        ],
        limit=24,
        in_specs=[HBM, VMEM],
        out_specs=[ANY],
    )[0]


def finish_body(got, back_one_sums, back_two_sums, own_one, own_two, ga, sa, gb, sb):
    size = own_two.shape[1]
    share = own_two.shape[0]
    total = jnp.sum(got[...].astype(F32), axis=0)
    total = unpack(total, share, size + own_one.shape[1])
    own_two[...] = total[:, 0:size]
    own_one[...] = total[:, size:]
    lane = lax.broadcasted_iota(jnp.int32, (share, C_MID), 1)
    row = lax.broadcasted_iota(jnp.int32, (share, C_MID), 0)
    chosen = lane == lax.axis_index("grp") * share + row
    first = lax.broadcasted_iota(jnp.int32, (share, share), 0)
    second = lax.broadcasted_iota(jnp.int32, (share, share), 1)
    for out, sums, k in (
        (ga, back_one_sums, 1), (sa, back_one_sums, 0), (gb, back_two_sums, 1), (sb, back_two_sums, 0)
    ):
        wide = jnp.broadcast_to(sums[k : k + 1], (share, C_MID))
        column = jnp.sum(jnp.where(chosen, wide, 0.0), axis=1, keepdims=True)
        wide = jnp.broadcast_to(column, (share, share))
        out[...] = jnp.sum(jnp.where(first == second, wide, 0.0), axis=0, keepdims=True)


def finish(got, back_one_sums, back_two_sums, share, rows_one, rows_two):
    shapes = [(share, rows_one), (share, rows_two)] + [(1, share)] * 4
    return call(
        finish_body,
        (got, back_one_sums, back_two_sums),
        [like(s, F32) for s in shapes],
    )


def exchange(blocks):
    return lax.all_to_all(blocks, AXES, 0, 0, tiled=True)


def shards(
    features, clip_starts, kernel_one, kernel_two, gain_one, shift_one, gain_two, shift_two, cotangent
):
    frames = features.shape[0]
    copies = lax.axis_size(AXES)
    row_count = lax.axis_size("row")
    count = float(frames * MEL * copies)
    rows_one, rows_two = kernel_one.shape[0], kernel_two.shape[0]
    share = kernel_one.shape[1]
    vectors = [v.reshape(1, share) for v in (gain_one, shift_one, gain_two, shift_two)]
    clips = clip_starts.reshape(1, -1)
    weights, up, down = setup(kernel_one.T, kernel_two.T, vectors, features, cotangent, copies)
    ends = copies - 1
    up = lax.ppermute(up, AXES, [(i, i + 1) for i in range(ends)])
    down = lax.ppermute(down, AXES, [(i + 1, i) for i in range(ends)])
    weights = exchange(weights)
    pre_one, stats, taps_x, masks, k1, k2, vec, weight = conv_one(
        features, up, down, clips, weights, row_count
    )
    stats = exchange(stats)
    pre_two, stats, taps_a, sums_one, weight_back = conv_two(
        pre_one, stats, vec, masks, k2, weight, count
    )
    stats = exchange(stats)
    block_out, lift, stats, sums_two = norm_two(pre_two, stats, vec, cotangent, up, down, count)
    stats = exchange(stats)
    lift, grads_two, stats, back_two_sums = back_two(
        lift, pre_two, sums_two, stats, vec, masks, weight_back, pre_one, sums_one, count
    )
    stats = exchange(stats)
    stored, blocks, back_one_sums = kernel_grads(
        lift, pre_one, sums_one, stats, vec, masks, taps_x, taps_a, grads_two, row_count, count
    )
    blocks = exchange(blocks)
    grad_features = features_grad(stored, k1)
    own_one, own_two, ga, sa, gb, sb = finish(
        blocks, back_one_sums, back_two_sums, share, rows_one, rows_two
    )
    return (
        block_out,
        grad_features,
        own_one.T,
        own_two.T,
        ga.reshape(share),
        sa.reshape(share),
        gb.reshape(share),
        sb.reshape(share),
    )


def solution(mesh):
    placed = (
        P(AXES, None), P(), P("row", "grp"), P("row", "grp"),
        P("grp"), P("grp"), P("grp"), P("grp"), P(AXES, None),
    )
    return jax.shard_map(
        shards,
        mesh=mesh,
        in_specs=placed,
        out_specs=(
            P(AXES, None), P(AXES, None), P("row", "grp"), P("row", "grp"),
            P("grp"), P("grp"), P("grp"), P("grp"),
        ),
        check_vma=False,
    )
```

```python
import jax
import jax.numpy as jnp
from jax import lax
from jax.experimental import pallas as pl
from jax.experimental.pallas import tpu as pltpu
from jax.sharding import PartitionSpec as P

MEL = 32
C_IN = 64
C_MID = 128
EPS = 1e-05
AXES = ("grp", "row")
LANES = 128
TAIL = 16
WIDE = 4 * LANES
BOTH = 2 * C_MID
F32 = jnp.float32
BF16 = jnp.bfloat16
TILE = 16
SIDES = 4
MIB = 2**20

VMEM = pl.BlockSpec(memory_space=pltpu.VMEM)
ANY = pl.BlockSpec(memory_space=pl.ANY)
HBM = pl.BlockSpec(memory_space=pltpu.HBM)


def like(shape, dtype):
    return jax.ShapeDtypeStruct(shape, dtype)


def call(body, args, outs, scratch=(), limit=14, in_specs=None, out_specs=None, **more):
    return pl.pallas_call(
        body,
        in_specs=in_specs or [VMEM] * len(args),
        out_specs=out_specs or [VMEM] * len(outs),
        out_shape=outs,
        scratch_shapes=list(scratch),
        compiler_params=pltpu.CompilerParams(vmem_limit_bytes=limit * MIB),
        cost_estimate=pl.CostEstimate(flops=5 * 10**9, bytes_accessed=0, transcendentals=0),
        **more,
    )(*args)


def padded(size):
    return -(-size // LANES) * LANES


def packed_rows(share, wide):
    rest = wide - LANES
    if rest > 0 and share == 32 and 3 * (LANES - rest) >= rest:
        return share + 24
    return share * (padded(wide) // LANES)


def pack(block, rows):
    share, wide = block.shape
    if rows % share == 0:
        block = jnp.concatenate([block, jnp.zeros((share, padded(wide) - wide), F32)], axis=1)
        return jnp.concatenate(
            [block[:, at : at + LANES] for at in range(0, block.shape[1], LANES)], axis=0
        )
    return jnp.concatenate([block[:, :LANES], pack_rest(block[:, LANES:])], axis=0)


def pack_rest(rest):
    room = LANES - rest.shape[1]
    tail = jnp.concatenate(
        [rest[24:32], jnp.zeros((8, 3 * room - rest.shape[1]), F32)], axis=1
    )
    tail = jnp.concatenate([tail[:, k * room : (k + 1) * room] for k in range(3)], axis=0)
    return jnp.concatenate([rest[0:24], tail], axis=1)


def unpack(block, share, wide):
    rows = block.shape[0]
    if rows % share == 0:
        parts = [block[at : at + share] for at in range(0, rows, share)]
        return jnp.concatenate(parts, axis=1)[:, 0:wide]
    width = wide - LANES
    second = block[share:]
    tail = jnp.concatenate([second[8 * k : 8 * k + 8, width:] for k in range(3)], axis=1)
    rest = jnp.concatenate([second[:, :width], tail[:, :width]], axis=0)
    return jnp.concatenate([block[0:share], rest], axis=1)


def partial_sum(values):
    return jnp.sum(values.reshape(-1, 8, values.shape[-1]), axis=0)


def fold(values):
    total = jnp.sum(values, axis=0, keepdims=True)
    return total[:, :C_MID] + total[:, C_MID:]


def spread(first, second, out):
    sums = jnp.concatenate([first, second], axis=0)
    out[...] = jnp.broadcast_to(sums[None], out.shape)


def twice(row):
    return jnp.concatenate([row, row], axis=1)


def tiles(rows):
    return range(0, rows, TILE)


def emit_taps(taps, masks, evens, odds, tile_of):
    rows = masks.shape[1]
    kept = taps.shape[0]
    for r in tiles(rows):
        even, odd = tile_of(r)
        evens[r : r + TILE] = even
        odds[8 + r : 8 + r + TILE] = odd
        if r == 0:
            evens[rows : rows + 1] = even[0:1]
        if r + TILE == rows:
            odds[7:8] = odd[TILE - 1 : TILE]
        if r < kept:
            taps[r : r + TILE, 128:256] = even.astype(BF16)
            taps[r : r + TILE, 256:384] = odd.astype(BF16)
    for r in tiles(kept):
        span = slice(r, r + TILE)
        before = odds[7 + r : 7 + r + TILE] * masks[0, span]
        after = evens[1 + r : 1 + r + TILE] * masks[1, span]
        taps[span, 0:128] = before.astype(BF16)
        taps[span, 384:512] = after.astype(BF16)


def halves_of(value):
    return value[:, :C_MID], value[:, C_MID:]


def add_sums(acc, first, second):
    acc[0] += first
    acc[1] += second


def side_scratch(rows):
    return [pltpu.VMEM((rows + 8, LANES), F32)] * (2 * SIDES)


def stats_of(out, mels, rows, half, acc):
    first = jnp.zeros((8, BOTH), F32)
    second = jnp.zeros((8, BOTH), F32)
    for k in range(mels):
        for r in range(0, half, 8):
            value = out[k * rows + r : k * rows + r + 8]
            first += value
            second += value * value
    add_sums(acc, first, second)


def normed_sum(with_half_lifted, plain, gain, shift):
    return (2.0 * with_half_lifted - shift * plain) / gain


def stat_sums(stats):
    return jnp.sum(stats[...], axis=0)


def norm_terms(sums, count):
    mean = sums[0:1] / count
    rstd = lax.rsqrt(sums[1:2] / count - mean * mean + EPS)
    return mean, rstd


def dot_rows(first, second):
    return lax.dot_general(
        first, second, (((0,), (0,)), ((), ())), preferred_element_type=F32
    )


def ring_slot(ring, m):
    return ring[m % (len(ring) - 1)] if 0 <= m < MEL else ring[-1]


def stack(ring, mels, rows, lanes=slice(None)):
    return jnp.concatenate([ring_slot(ring, m)[0:rows, lanes] for m in mels], axis=0)


def ring_scratch(slots, rows):
    return [pltpu.VMEM((rows, WIDE), BF16)] * slots


def clear_ends(taps):
    blank = jnp.zeros(taps.shape[1:], BF16)
    taps[0] = blank
    taps[taps.shape[0] - 1] = blank


def setup_body(k1, k2, ga, sa, gb, sb, x_head, x_tail, c_head, c_tail, w_out, up, down):
    share = k1.shape[0]
    copies = w_out.shape[0]
    first = lax.broadcasted_iota(jnp.int32, (share, share), 0)
    second = lax.broadcasted_iota(jnp.int32, (share, share), 1)
    columns = [k1[...].astype(F32), k2[...].astype(F32)]
    for vector in (ga, sa, gb, sb):
        wide = jnp.broadcast_to(vector[...].astype(F32), (share, share))
        columns.append(jnp.sum(jnp.where(first == second, wide, 0.0), axis=1, keepdims=True))
    chunk = pack(jnp.concatenate(columns, axis=1), w_out.shape[1]).astype(BF16)
    for i in range(copies):
        w_out[i] = chunk
    row = lax.broadcasted_iota(jnp.int32, (8, x_head.shape[1]), 0)
    xt = x_tail[...].astype(F32)
    ct = c_tail[...].astype(F32)
    up[...] = jnp.where(
        row < 4, pltpu.roll(xt[8:16], 4, 0), jnp.where(row == 4, ct[15:16], 0.0)
    ).astype(BF16)
    xh = x_head[...].astype(F32)
    ch = c_head[...].astype(F32)
    down[...] = jnp.where(row < 4, xh[0:8], jnp.where(row == 4, ch[0:1], 0.0)).astype(BF16)


def setup(k1t, k2t, vectors, features, cotangent, copies):
    frames, wide = features.shape
    halves = cotangent.shape[0]
    share = k1t.shape[0]
    w = (copies, packed_rows(share, k1t.shape[1] + k2t.shape[1] + 4), LANES)
    whole = lambda shape: pl.BlockSpec(shape, lambda i: (0,) * len(shape))
    outs = [like(w, BF16), like((8, wide), BF16), like((8, wide), BF16)]
    return call(
        setup_body,
        (k1t, k2t, *vectors, features, features, cotangent, cotangent),
        outs,
        limit=56,
        in_specs=[
            whole(k1t.shape),
            whole(k2t.shape),
            *[whole((1, share))] * 4,
            pl.BlockSpec((16, wide), lambda i: (0, 0)),
            pl.BlockSpec((16, wide), lambda i: (frames // 16 - 1, 0)),
            pl.BlockSpec((16, wide), lambda i: (0, 0)),
            pl.BlockSpec((16, wide), lambda i: (halves // 16 - 1, 0)),
        ],
        out_specs=[whole(o.shape) for o in outs],
        grid=(1,),
    )


def emit_masks(copies, clips, masks):
    rows = masks.shape[1]
    half = rows - TAIL
    frames = 2 * half
    start = lax.axis_index(AXES) * frames
    place = lax.broadcasted_iota(jnp.int32, (rows, clips.shape[1]), 0)
    pair = jnp.where(place >= half + TAIL // 2, place - rows, place)
    frame = start + 2 * pair
    starts = jnp.broadcast_to(clips[...], (rows, clips.shape[1]))
    for slot, shift in ((0, 0), (1, 2)):
        hit = (frame + shift == starts) | (frame + shift >= frames * copies)
        begins = jnp.max(jnp.where(hit, 1.0, 0.0), axis=1, keepdims=True)
        masks[slot] = jnp.broadcast_to(1.0 - begins, (rows, LANES))


def split_bins(parts):
    low = lax.broadcasted_iota(jnp.int32, parts[0].shape, 1) < C_IN
    first, second = [], []
    for here, there in (parts[0:2], parts[2:4]):
        first.append(jnp.where(low, here, pltpu.roll(there, C_IN, 1)))
        second.append(jnp.where(low, pltpu.roll(here, C_IN, 1), there))
    return jnp.concatenate(first + second, axis=1)


def near_bins(taps, pairs, rows):
    left, mid, right = [
        jnp.concatenate([taps[1 + j + k, 0:rows] for j in pairs], axis=0) for k in (-1, 0, 1)
    ]
    first = jnp.concatenate([left[:, BOTH:], mid], axis=1)
    second = jnp.concatenate([mid, right[:, :BOTH]], axis=1)
    return jnp.concatenate([first, second], axis=0)


def taps_one_emitter(x, up, down, masks, taps, frames):
    rows = masks.shape[1]
    half = rows - TAIL
    clear_ends(taps)
    row = lax.broadcasted_iota(jnp.int32, (8, LANES), 0)
    lead = 24
    own = 2 * half
    for held in frames:
        held[0:16] = jnp.zeros((16, LANES), F32)
        held[lead + own + 8 : lead + own + 24] = jnp.zeros((16, LANES), F32)

    def pair(j):
        held = frames[j % len(frames)]
        lanes = slice(j * LANES, (j + 1) * LANES)
        u = up[:, lanes].astype(F32)
        d = down[:, lanes].astype(F32)
        held[lead - 8 : lead] = jnp.where(row >= 4, pltpu.roll(u, 4, 0), 0.0)
        held[lead + own : lead + own + 8] = jnp.where(row < 4, d, 0.0)
        for r in tiles(own):
            held[lead + r : lead + r + TILE] = x[r : r + TILE, lanes].astype(F32)

        def pick(first, count, shift):
            return held[pl.ds(lead + 2 * first + shift, count, stride=2), :]

        for r in tiles(rows):
            parts = []
            for shift in (-1, 0, 1, 2):
                if r < half:
                    parts.append(pick(r, TILE, shift))
                else:
                    parts.append(
                        jnp.concatenate([pick(half, 8, shift), pick(-8, 8, shift)], axis=0)
                    )
            span = slice(r, r + TILE)
            parts[0] = parts[0] * masks[0, span]
            parts[3] = parts[3] * masks[1, span]
            taps[1 + j, span, :] = split_bins(parts).astype(BF16)

    return pair


def conv_one_body(row_count, features, up, down, clips_in, wg,
                  pre, stats, taps, masks, k1_out, k2_out, vec_out,
                  kf, weight, acc, x, clips, sems, clip_sem, *frames):
    clip_copy = pltpu.make_async_copy(clips_in, clips, clip_sem)
    clip_copy.start()
    wide = x.shape[1] // sems.shape[0]
    fetch = []
    for k in range(sems.shape[0]):
        lanes = pl.ds(k * wide, wide)
        fetch.append(pltpu.make_async_copy(features.at[:, lanes], x.at[:, lanes], sems.at[k]))
        fetch[k].start()
    clip_copy.wait()
    emit_masks(wg.shape[0], clips, masks)
    emit_pair = taps_one_emitter(x, up, down, masks, taps, frames)
    rows = taps.shape[1]
    half = rows - TAIL
    pairs = 2
    rows_one = 9 * C_IN // row_count
    rows_two = 9 * C_MID // row_count
    grps = wg.shape[0] // row_count
    share = C_MID // grps
    for r in range(row_count):
        shard = [
            unpack(wg[g * row_count + r].astype(F32), share, rows_one + rows_two + 4)
            for g in range(grps)
        ]
        shard = jnp.concatenate(shard, axis=0).T
        kf[rows_one * r : rows_one * (r + 1)] = shard[0:rows_one]
        at = 9 * C_IN + rows_two * r
        kf[at : at + rows_two] = shard[rows_one : rows_one + rows_two]
        if r == 0:
            vec_out[...] = shard[rows_one + rows_two : rows_one + rows_two + 4]
    k1_out[...] = kf[0 : 9 * C_IN].astype(BF16)
    k2_out[...] = kf[9 * C_IN :].astype(BF16)
    weight[...] = jnp.zeros(weight.shape, BF16)
    for d in range(3):
        for q in range(4):
            for p in range(2):
                t = q - p
                if 0 <= t < 3:
                    at = d * BOTH + q * C_IN
                    start = (3 * t + d) * C_IN
                    weight[at : at + C_IN, p * 128 : p * 128 + 128] = k1_out[start : start + C_IN]
    acc[...] = jnp.zeros(acc.shape, F32)

    def convolve(c):
        here = range(c * pairs, (c + 1) * pairs)
        out = jnp.dot(near_bins(taps, here, rows), weight[...], preferred_element_type=F32)
        for parity in range(2):
            for q in range(pairs):
                at = (parity * pairs + q) * rows
                pre[2 * (c * pairs + q) + parity] = out[at : at + rows]
        stats_of(out, 2 * pairs, rows, half, acc)

    total = MEL // 2
    for j in range(total):
        if j % (total // len(fetch)) == 0:
            fetch[j // (total // len(fetch))].wait()
        emit_pair(j)
        if j >= pairs and j % pairs == 0:
            convolve(j // pairs - 1)
    convolve(total // pairs - 1)
    spread(fold(acc[0]), fold(acc[1]), stats)


def conv_one(features, up, down, clips, wg, row_count):
    rows = features.shape[0] // 2 + TAIL
    copies = wg.shape[0]
    return call(
        lambda *refs: conv_one_body(row_count, *refs),
        (features, up, down, clips, wg),
        [
            like((MEL, rows, BOTH), F32),
            like((copies, 2, C_MID), F32),
            like((MEL // 2 + 2, rows, WIDE), BF16),
            like((2, rows, LANES), F32),
            like((9 * C_IN, C_MID), BF16),
            like((9 * C_MID, C_MID), BF16),
            like((4, C_MID), F32),
        ],
        [
            pltpu.VMEM((9 * (C_IN + C_MID), C_MID), F32),
            pltpu.VMEM((3 * BOTH, BOTH), BF16),
            pltpu.VMEM((2, 8, BOTH), F32),
            pltpu.VMEM(features.shape, BF16),
            pltpu.VMEM(clips.shape, jnp.int32),
            pltpu.SemaphoreType.DMA((4,)),
            pltpu.SemaphoreType.DMA,
            *[pltpu.VMEM((features.shape[0] + 48, LANES), F32)] * 4,
        ],
        in_specs=[HBM, VMEM, VMEM, HBM, VMEM],
    )


def place_two(k2, weight):
    weight[...] = jnp.zeros(weight.shape, BF16)
    for d in range(3):
        for q in range(4):
            for p in range(2):
                t = q - p
                if 0 <= t < 3:
                    at = d * WIDE + q * 128
                    start = (3 * t + d) * C_MID
                    weight[at : at + 128, p * 128 : p * 128 + 128] = k2[start : start + C_MID]


def place_two_back(k2, weight):
    weight[...] = jnp.zeros(weight.shape, BF16)
    for t in range(3):
        for d in range(3):
            start = (3 * t + d) * C_MID
            turned = (0.5 * k2[start : start + C_MID].astype(F32).T).astype(BF16)
            for p in range(2):
                at = (2 - d) * WIDE + (2 - t + p) * 128
                weight[at : at + 128, p * 128 : p * 128 + 128] = turned


def place_one_back(k1, weight):
    weight[...] = jnp.zeros(weight.shape, BF16)
    for t in range(3):
        for d in range(3):
            start = (3 * t + d) * C_IN
            turned = k1[start : start + C_IN].astype(F32).T.astype(BF16)
            for mo in (1, 2):
                for p in range(2):
                    at = (mo - d + 1) * WIDE + (2 - t + p) * 128
                    to = p * 128 + (mo - 1) * 64
                    weight[at : at + 128, to : to + 64] = turned


def conv_two_body(count, pre_one, stats_one, vec, masks, k2,
                  pre, stats, taps, sums_out, weight_back, acc, weight, *sides):
    place_two(k2, weight)
    rows = masks.shape[1]
    half = rows - TAIL
    mels = 2
    sums = stat_sums(stats_one)
    sums_out[...] = sums
    mean, rstd = norm_terms(sums, count)
    scale = 0.5 * vec[0:1] * rstd
    shift = twice(0.5 * vec[1:2] - mean * scale)
    scale = twice(scale)
    clear_ends(taps)
    acc[...] = jnp.zeros(acc.shape, F32)

    def activate(m):
        def tile(r):
            h = pre_one[m, r : r + TILE] * scale + shift
            return halves_of(h + h * jnp.tanh(h))

        emit_taps(taps.at[1 + m], masks, sides[m % SIDES], sides[SIDES + m % SIDES], tile)

    def convolve(c):
        lhs = [taps[c * mels + d : (c + 1) * mels + d].reshape(mels * rows, WIDE) for d in range(3)]
        out = jnp.dot(jnp.concatenate(lhs, axis=1), weight[...], preferred_element_type=F32)
        pre[c * mels : (c + 1) * mels] = out.reshape(mels, rows, BOTH)
        stats_of(out, mels, rows, half, acc)

    for m in range(MEL):
        activate(m)
        if m >= mels and m % mels == 0:
            convolve(m // mels - 1)
        if m == 8:
            place_two_back(k2, weight_back)
    convolve(MEL // mels - 1)
    spread(fold(acc[0]), fold(acc[1]), stats)


def conv_two(pre_one, stats_one, vec, masks, k2, count):
    copies = stats_one.shape[0]
    rows = masks.shape[1]
    return call(
        lambda *refs: conv_two_body(count, *refs),
        (pre_one, stats_one, vec, masks, k2),
        [
            like((MEL, rows, BOTH), F32),
            like((copies, 2, C_MID), F32),
            like((MEL + 2, rows, WIDE), BF16),
            like((2, C_MID), F32),
            like((3 * WIDE, BOTH), BF16),
        ],
        [pltpu.VMEM((2, 8, BOTH), F32), pltpu.VMEM((3 * WIDE, BOTH), BF16), *side_scratch(rows)],
    )


def norm_two_body(count, pre, stats_two, vec, cot, up, down, pooled, lift, back_stats, sums_out, acc):
    half = cot.shape[0]
    sums = stat_sums(stats_two)
    sums_out[...] = sums
    mean, rstd = norm_terms(sums, count)
    scale = 0.5 * vec[2:3] * rstd
    shift = 0.5 * vec[3:4] - mean * scale
    acc[...] = jnp.zeros(acc.shape, F32)
    row = lax.broadcasted_iota(jnp.int32, (TAIL, LANES), 0)

    factor = 0.125 * vec[2:3] * rstd

    def pair(j):
        lanes = pl.ds(pl.multiple_of(j * LANES, LANES), LANES)
        u = up[:, lanes].astype(F32)
        d = down[:, lanes].astype(F32)
        first = jnp.zeros((8, LANES), F32)
        second = jnp.zeros((8, LANES), F32)
        for r in tiles(half + TAIL):
            span = slice(r, r + TILE)
            if r < half:
                grad = cot[span, lanes].astype(F32) * factor
            else:
                grad = jnp.where(row == 0, d[4:5], jnp.where(row == TAIL - 1, u[4:5], 0.0)) * factor
            total = jnp.zeros((TILE, LANES), F32)
            for m in (2 * j, 2 * j + 1):
                for p in range(2):
                    side = slice(p * C_MID, (p + 1) * C_MID)
                    value = pre[m, span, side]
                    h = value * scale + shift
                    th = jnp.tanh(h)
                    one = 1.0 + th
                    silu = h * one
                    gl = grad * (one + (silu - silu * th))
                    lift[m, span, side] = gl
                    if r < half:
                        total += silu
                        first += partial_sum(gl)
                        second += partial_sum(gl * h)
            if r < half:
                pooled[span, lanes] = (total * 0.25).astype(BF16)
        add_sums(acc, first, second)

    def four_pairs(i, carry):
        for k in range(4):
            pair(4 * i + k)
        return carry

    lax.fori_loop(0, MEL // 8, four_pairs, 0)
    first, second = [jnp.sum(acc[k], axis=0, keepdims=True) for k in range(2)]
    scaled = vec[2:3] * rstd
    first = first / scaled
    spread(first, normed_sum(second / scaled, first, vec[2:3], vec[3:4]), back_stats)


def norm_two(pre, stats_two, vec, cot, up, down, count):
    copies = stats_two.shape[0]
    half, wide = cot.shape
    return call(
        lambda *refs: norm_two_body(count, *refs),
        (pre, stats_two, vec, cot, up, down),
        [
            like((half, wide), BF16),
            like((MEL, half + TAIL, BOTH), F32),
            like((copies, 2, C_MID), F32),
            like((2, C_MID), F32),
        ],
        [pltpu.VMEM((2, 8, LANES), F32)],
    )


def grad_terms(sums, back, gain, count):
    mean, rstd = norm_terms(sums, count)
    a = gain * rstd
    b = -a * rstd * (back[1:2] / count)
    c = -a * (back[0:1] / count) - b * mean
    return twice(a), twice(b), twice(c)


def back_two_body(count, lift, pre_two, sums_two, back_stats, vec, masks, weight, pre_one, sums_one,
                  taps_a, lift_one, two, back_out, sums_out, acc, acc_two, turned, *buffers):
    sides, taps = buffers[: 2 * SIDES], buffers[2 * SIDES :]
    rows = masks.shape[1]
    half = rows - TAIL
    mels = 1
    wide_mels = 4
    back = stat_sums(back_stats)
    sums_out[...] = back
    _, b, c = grad_terms(sums_two[...], back, vec[2:3], count)
    mean, rstd = norm_terms(sums_one[...], count)
    scale = 0.5 * vec[0:1] * rstd
    shift = twice(0.5 * vec[1:2] - mean * scale)
    scale = twice(scale)
    taps[-1][...] = jnp.zeros(taps[-1].shape, BF16)
    acc[...] = jnp.zeros(acc.shape, F32)

    def lower(m):
        def tile(r):
            span = slice(r, r + TILE)
            return halves_of(lift[m, span] + (pre_two[m, span] * b + c))

        emit_taps(ring_slot(taps, m), masks, sides[m % SIDES], sides[SIDES + m % SIDES], tile)

    def convolve(k):
        lhs = [ring_slot(taps, k + d - 1)[...] for d in range(3)]
        out = jnp.dot(jnp.concatenate(lhs, axis=1), weight[...], preferred_element_type=F32)
        first = jnp.zeros((8, BOTH), F32)
        second = jnp.zeros((8, BOTH), F32)
        for i in range(mels):
            m = k * mels + i
            for r in range(0, rows, 8):
                span = slice(r, r + 8)
                h = pre_one[m, span] * scale + shift
                th = jnp.tanh(h)
                one = 1.0 + th
                silu = h * one
                gl = out[i * rows + r : i * rows + r + 8] * (one + (silu - silu * th))
                lift_one[m, span] = gl
                if r < half:
                    first += gl
                    second += gl * h
        add_sums(acc, first, second)

    def correlate(k):
        here = range(k * wide_mels, (k + 1) * wide_mels)
        flat = wide_mels * half
        chosen = stack(taps, here, half, slice(128, 384)).T
        for p in range(2):
            turned[:, p * flat : (p + 1) * flat] = chosen[p * C_MID : (p + 1) * C_MID]
        for p in range(2):
            near = []
            for d in range(3):
                first = here[0] + d
                lanes = slice(p * LANES, p * LANES + 3 * LANES)
                near.append(taps_a[first : first + wide_mels, 0:half, lanes].reshape(flat, 3 * LANES))
            total = jnp.dot(
                turned[:, p * flat : (p + 1) * flat],
                jnp.concatenate(near, axis=1),
                preferred_element_type=F32,
            )
            if k == 0 and p == 0:
                acc_two[...] = total
            else:
                acc_two[...] += total

    for k in range(MEL // mels + 1):
        for m in range(k * mels, (k + 1) * mels):
            if m < MEL:
                lower(m)
        if k > 0:
            convolve(k - 1)
            if k * mels % wide_mels == 0:
                correlate(k * mels // wide_mels - 1)
    plain = fold(acc[0])
    spread(plain, normed_sum(fold(acc[1]), plain, vec[0:1], vec[1:2]), back_out)
    for t in range(3):
        for d in range(3):
            at = (3 * d + t) * 128
            to = (3 * t + d) * 128
            two[:, to : to + 128] = acc_two[:, at : at + 128]


def back_two(lift, pre_two, sums_two, back_stats, vec, masks, weight, pre_one, sums_one, taps_a, count):
    copies = back_stats.shape[0]
    rows = masks.shape[1]
    return call(
        lambda *refs: back_two_body(count, *refs),
        (lift, pre_two, sums_two, back_stats, vec, masks, weight, pre_one, sums_one, taps_a),
        [
            like((MEL, rows, BOTH), F32),
            like((C_MID, 9 * C_MID), F32),
            like((copies, 2, C_MID), F32),
            like((2, C_MID), F32),
        ],
        [
            pltpu.VMEM((2, 8, BOTH), F32),
            pltpu.VMEM((C_MID, 9 * C_MID), F32),
            pltpu.VMEM((C_MID, 8 * (rows - TAIL)), BF16),
            *side_scratch(rows),
            *ring_scratch(17, rows),
        ],

        input_output_aliases={0: 0},
    )


def scatter_blocks(out, tops, two, one, row_count):
    copies, block_rows = out.shape[0:2]
    grps = copies // row_count
    share = C_MID // grps
    size_two = 9 * C_MID // row_count
    size_one = 9 * C_IN // row_count
    ahead = LANES if block_rows == share + 24 and size_two >= LANES else 0

    def first():
        turned = two[...].T
        for r in range(row_count if ahead else 0):
            tops[r] = turned[size_two * r : size_two * r + ahead].T

    def second():
        turned = two[...].T
        turned_one = one().T
        for r in range(row_count):
            rows = [
                turned[size_two * r + ahead : size_two * (r + 1)],
                turned_one[size_one * r : size_one * (r + 1)],
            ]
            back = jnp.concatenate(rows, axis=0).T
            for g in range(grps):
                here = slice(share * g, share * (g + 1))
                if ahead:
                    block = jnp.concatenate([tops[r, here], pack_rest(back[here])], axis=0)
                else:
                    block = pack(back[here], block_rows)
                out[g * row_count + r] = block.astype(BF16)

    return first, second


def kernel_one_step(taps_x, grads, acc, k, pairs):
    half = grads.shape[1] - TAIL
    here = range(k * pairs, (k + 1) * pairs)
    mels = [2 * j + parity for parity in range(2) for j in here]
    chosen = jnp.concatenate([grads[m, 0:half] for m in mels], axis=0)
    total = dot_rows(chosen, near_bins(taps_x, here, half))
    if k == 0:
        acc[...] = total
    else:
        acc[...] += total


def kernel_one_sums(acc):
    pieces = []
    for t in range(3):
        for d in range(3):
            total = jnp.zeros((C_MID, C_IN), F32)
            for p in range(2):
                at = d * BOTH + (t + p) * C_IN
                total += acc[p * C_MID : (p + 1) * C_MID, at : at + C_IN]
            pieces.append(total)
    return jnp.concatenate(pieces, axis=1)


STORED = 640


def grads_body(count, row_count, lift, pre_one, sums_one, back_stats, vec, masks, taps_x, two,
               stored, blocks, sums_out, acc_one, grads, low_masks, tops, sems):
    back = stat_sums(back_stats)
    sums_out[...] = back
    a, b, c = grad_terms(sums_one[...], back, vec[0:1], count)
    rows = masks.shape[1]
    for slot in range(2):
        low_masks[:, slot * LANES : (slot + 1) * LANES] = masks[slot].astype(BF16)
    copies = [pltpu.make_async_copy(low_masks, stored.at[MEL], sems.at[sems.shape[0] - 1])]
    copies[0].start()

    def lower(m):
        for r in tiles(rows):
            span = slice(r, r + TILE)
            grads[m, span] = (lift[m, span] * a + (pre_one[m, span] * b + c)).astype(BF16)

    scatter_ahead, scatter_rest = scatter_blocks(
        blocks, tops, two, lambda: kernel_one_sums(acc_one), row_count
    )
    pairs = 2
    mels = 2 * pairs
    steps = MEL // mels
    for k in range(steps + 1):
        if k == 2:
            scatter_ahead()
        if k < steps:
            for m in range(mels * k, mels * (k + 1)):
                lower(m)
            here = pl.ds(mels * k, mels)
            copies.append(pltpu.make_async_copy(grads.at[here], stored.at[here], sems.at[k]))
            copies[-1].start()
        if k > 0:
            kernel_one_step(taps_x, grads, acc_one, k - 1, pairs)
    scatter_rest()
    for copy in copies:
        copy.wait()


def kernel_grads(lift, pre_one, sums_one, back_stats, vec, masks, taps_x, two, row_count, count):
    copies = back_stats.shape[0]
    rows = masks.shape[1]
    share = C_MID * row_count // copies
    block_rows = packed_rows(share, 9 * (C_IN + C_MID) // row_count)
    return call(
        lambda *refs: grads_body(count, row_count, *refs),
        (lift, pre_one, sums_one, back_stats, vec, masks, taps_x, two),
        [
            like((STORED, rows, BOTH), BF16),
            like((copies, block_rows, LANES), BF16),
            like((2, C_MID), F32),
        ],
        [
            pltpu.VMEM((BOTH, 3 * BOTH), F32),
            pltpu.VMEM((MEL, rows, BOTH), BF16),
            pltpu.VMEM((rows, BOTH), BF16),
            pltpu.VMEM((row_count, C_MID, LANES), F32),
            pltpu.SemaphoreType.DMA((9,)),
        ],
        out_specs=[HBM, VMEM, VMEM],
    )


def features_body(stored, k1, out, grads, low_masks, masks, weight, woven, sems, out_sems, *buffers):
    sides, taps = buffers[: 2 * SIDES], buffers[2 * SIDES :]
    pairs = 4
    rows = grads.shape[1]
    half = rows - TAIL
    groups = sems.shape[0] - 1
    group = MEL // groups
    mask_copy = pltpu.make_async_copy(stored.at[MEL], low_masks, sems.at[groups])
    mask_copy.start()
    fetch = []
    for k in range(groups):
        here = pl.ds(k * group, group)
        fetch.append(pltpu.make_async_copy(stored.at[here], grads.at[here], sems.at[k]))
        fetch[k].start()
    taps[-1][...] = jnp.zeros(taps[-1].shape, BF16)
    place_one_back(k1, weight)
    mask_copy.wait()
    for slot in range(2):
        masks[slot] = low_masks[:, slot * LANES : (slot + 1) * LANES].astype(F32)

    def emit(m):
        def tile(r):
            return halves_of(grads[m, r : r + TILE].astype(F32))

        emit_taps(ring_slot(taps, m), masks, sides[m % SIDES], sides[SIDES + m % SIDES], tile)

    copies = []
    slots = woven.shape[0]

    def convolve(k):
        near = [
            stack(taps, [2 * (k * pairs + q) + i - 1 for q in range(pairs)], half) for i in range(4)
        ]
        part = jnp.dot(jnp.concatenate(near, axis=1), weight[...], preferred_element_type=F32)
        for q in range(pairs):
            j = k * pairs + q
            b = j % slots
            here = slice(q * half, (q + 1) * half)
            if j >= slots:
                copies[j - slots].wait()
            woven[b, pl.ds(0, half, stride=2), :] = part[here, 0:128]
            woven[b, pl.ds(1, half, stride=2), :] = part[here, 128:256]
            copy = pltpu.make_async_copy(
                woven.at[b], out.at[:, pl.ds(j * LANES, LANES)], out_sems.at[b]
            )
            copy.start()
            copies.append(copy)

    for m in range(MEL):
        if m % group == 0:
            fetch[m // group].wait()
        emit(m)
        if m > 0 and m % (2 * pairs) == 0:
            convolve(m // (2 * pairs) - 1)
    convolve(MEL // (2 * pairs) - 1)
    for copy in copies[-slots:]:
        copy.wait()


def features_grad(stored, k1):
    rows = stored.shape[1]
    half = rows - TAIL
    return call(
        features_body,
        (stored, k1),
        [like((2 * half, MEL * C_IN), F32)],
        [
            pltpu.VMEM((MEL, rows, BOTH), BF16),
            pltpu.VMEM((rows, BOTH), BF16),
            pltpu.VMEM((2, rows, LANES), F32),
            pltpu.VMEM((4 * WIDE, BOTH), BF16),
            pltpu.VMEM((8, 2 * half, LANES), F32),
            pltpu.SemaphoreType.DMA((9,)),
            pltpu.SemaphoreType.DMA((8,)),
            *side_scratch(rows),
            *ring_scratch(27, half),
        ],
        limit=24,
        in_specs=[HBM, VMEM],
        out_specs=[ANY],
    )[0]


def finish_body(got, back_one_sums, back_two_sums, own_one, own_two, ga, sa, gb, sb):
    size = own_two.shape[1]
    share = own_two.shape[0]
    total = jnp.sum(got[...].astype(F32), axis=0)
    total = unpack(total, share, size + own_one.shape[1])
    own_two[...] = total[:, 0:size]
    own_one[...] = total[:, size:]
    lane = lax.broadcasted_iota(jnp.int32, (share, C_MID), 1)
    row = lax.broadcasted_iota(jnp.int32, (share, C_MID), 0)
    chosen = lane == lax.axis_index("grp") * share + row
    first = lax.broadcasted_iota(jnp.int32, (share, share), 0)
    second = lax.broadcasted_iota(jnp.int32, (share, share), 1)
    for out, sums, k in (
        (ga, back_one_sums, 1), (sa, back_one_sums, 0), (gb, back_two_sums, 1), (sb, back_two_sums, 0)
    ):
        wide = jnp.broadcast_to(sums[k : k + 1], (share, C_MID))
        column = jnp.sum(jnp.where(chosen, wide, 0.0), axis=1, keepdims=True)
        wide = jnp.broadcast_to(column, (share, share))
        out[...] = jnp.sum(jnp.where(first == second, wide, 0.0), axis=0, keepdims=True)


def finish(got, back_one_sums, back_two_sums, share, rows_one, rows_two):
    shapes = [(share, rows_one), (share, rows_two)] + [(1, share)] * 4
    return call(
        finish_body,
        (got, back_one_sums, back_two_sums),
        [like(s, F32) for s in shapes],
    )


def exchange(blocks):
    return lax.all_to_all(blocks, AXES, 0, 0, tiled=True)


def shards(
    features, clip_starts, kernel_one, kernel_two, gain_one, shift_one, gain_two, shift_two, cotangent
):
    frames = features.shape[0]
    copies = lax.axis_size(AXES)
    row_count = lax.axis_size("row")
    count = float(frames * MEL * copies)
    rows_one, rows_two = kernel_one.shape[0], kernel_two.shape[0]
    share = kernel_one.shape[1]
    vectors = [v.reshape(1, share) for v in (gain_one, shift_one, gain_two, shift_two)]
    clips = clip_starts.reshape(1, -1)
    weights, up, down = setup(kernel_one.T, kernel_two.T, vectors, features, cotangent, copies)
    ends = copies - 1
    up = lax.ppermute(up, AXES, [(i, i + 1) for i in range(ends)])
    down = lax.ppermute(down, AXES, [(i + 1, i) for i in range(ends)])
    weights = exchange(weights)
    pre_one, stats, taps_x, masks, k1, k2, vec = conv_one(
        features, up, down, clips, weights, row_count
    )
    stats = exchange(stats)
    pre_two, stats, taps_a, sums_one, weight_back = conv_two(
        pre_one, stats, vec, masks, k2, count
    )
    stats = exchange(stats)
    block_out, lift, stats, sums_two = norm_two(pre_two, stats, vec, cotangent, up, down, count)
    stats = exchange(stats)
    lift, two, stats, back_two_sums = back_two(
        lift, pre_two, sums_two, stats, vec, masks, weight_back, pre_one, sums_one, taps_a, count
    )
    stats = exchange(stats)
    stored, blocks, back_one_sums = kernel_grads(
        lift, pre_one, sums_one, stats, vec, masks, taps_x, two, row_count, count
    )
    blocks = exchange(blocks)
    grad_features = features_grad(stored, k1)
    own_one, own_two, ga, sa, gb, sb = finish(
        blocks, back_one_sums, back_two_sums, share, rows_one, rows_two
    )
    return (
        block_out,
        grad_features,
        own_one.T,
        own_two.T,
        ga.reshape(share),
        sa.reshape(share),
        gb.reshape(share),
        sb.reshape(share),
    )


def solution(mesh):
    placed = (
        P(AXES, None), P(), P("row", "grp"), P("row", "grp"),
        P("grp"), P("grp"), P("grp"), P("grp"), P(AXES, None),
    )
    return jax.shard_map(
        shards,
        mesh=mesh,
        in_specs=placed,
        out_specs=(
            P(AXES, None), P(AXES, None), P("row", "grp"), P("row", "grp"),
            P("grp"), P("grp"), P("grp"), P("grp"),
        ),
        check_vma=False,
    )
```
